32 devices in a mesh: row: 4 (over x, core), col: 2 (over y), gz: 4 (over z).
Axes of the slice: x: 2, y: 2, z: 4, core: 2. Of those that a mesh axis runs over, the one named last changes fastest.
Arguments:
- volume_field: bfloat16 [128, 32, 16, 512], P(None, 'row', 'col', 'gz'), may hold values from -6 to 6
- volume_load: bfloat16 [128, 32, 16, 512], P(None, 'row', 'col', 'gz'), may hold values from -6 to 6
- coefficient: float32 [32, 16, 512], P('row', 'col', 'gz'), may hold values from 0.25 to 2
- surface_block: bfloat16 [1024, 32768], P('row', 'col'), may hold values from -0.046875 to 0.046875
- trace_cell: int32 [4, 2, 4, 1024], P('row', 'col', 'gz'), may hold values from 0 to 8191, as said below
- flux_cell: int32 [4, 2, 4, 32], P('row', 'col', 'gz'), may hold values from 0 to 8191, as said below
Outputs:
- new_field: bfloat16 [128, 32, 16, 512], P(None, 'row', 'col', 'gz')
- surface_flux: float32 [128, 1024], P('gz', ('row', 'col'))
The draws below stay inside these ranges and needn't reach their ends.
Inputs may be any that keep to these rules, and one draw needn't show every extreme that they name: `trace_cell`: within each device's 1024 entries, entry values are local cell numbers, one from each aligned run of 8 consecutive cells, in a permuted order; the first and last cells of the block are always chosen. `flux_cell`: within each device's 32 entries, entry values are local cell numbers, one from each aligned run of 256 consecutive cells, in a permuted order; the first and last cells of the block are always chosen.
All inputs are finite; a program needn't handle non-finite values.
Results may differ from the reference program's by a relative error of at most 0.0032.
Values may be sent and summed in bfloat16 or wider, within the bound.
No kernel may reach another device: no remote copies, remote signals or barrier semaphores. Data moves between devices by JAX's collectives and lax.ppermute only.
A program may use at most 128 MiB of HBM per device.

```python
import jax
import jax.numpy as jnp
from jax import lax

RHS = 128
VX = 8
VY = 8
VZ = 128
TS = 1024
NS = 32768
NSR = 1024
FS = 32
NX = 32
NY = 16
NZ = 512
N_ROW = 4
N_COL = 2
N_GZ = 4


def spread_cells(key, per_device):
    device_count = N_ROW * N_COL * N_GZ
    stride = VX * VY * VZ // per_device
    offsets = jax.random.randint(key, (device_count, per_device), 0, stride, dtype=jnp.int32)
    column = jnp.arange(per_device, dtype=jnp.int32)[None, :]
    offsets = jnp.where(column == 0, 0, jnp.where(column == per_device - 1, stride - 1, offsets))
    chosen_cells = column * stride + offsets
    sub_keys = jax.random.split(jax.random.fold_in(key, 5), device_count)
    shuffle = jax.vmap(lambda sub: jax.random.permutation(sub, per_device))(sub_keys)
    chosen_cells = jnp.take_along_axis(chosen_cells, shuffle.astype(jnp.int32), axis=1)
    return chosen_cells.reshape(N_ROW, N_COL, N_GZ, per_device).astype(jnp.int32)


def draw_trace_cell(key, part):
    return spread_cells(jax.random.fold_in(key, 11), TS)


def draw_flux_cell(key, part):
    return spread_cells(jax.random.fold_in(key, 23), FS)


def with_spikes(values, own_key, source, target, blocks, factor):
    def block_of(position):
        return (jnp.arange(values.shape[position]) // (values.shape[position] // blocks)).reshape((-1,) + (1,) * (values.ndim - 1 - position))

    first = jax.random.permutation(own_key, blocks)[block_of(target)]
    far = (block_of(target) + blocks // 2) % blocks
    return jnp.where((block_of(source) == first) | (block_of(source) == far), factor * values, values)


def block_scale(own_key, extent, shards, low, top_value):
    level = 1.0
    for dim, parts in shards:
        draws = jax.random.uniform(jax.random.fold_in(jax.random.fold_in(own_key, 6), dim), (parts,), jnp.float32, low / len(shards), top_value / len(shards))
        level = level * jnp.repeat(jnp.exp(draws), extent[dim] // parts).reshape((-1,) + (1,) * (len(extent) - 1 - dim))
    return level


def centred(rng, shape, width, most, shards=(), held_as=jnp.bfloat16):
    entries = width * jax.random.normal(rng, shape, jnp.float32)
    if shards:
        entries = entries * block_scale(rng, shape, shards, -0.22, 0.18)
    return jnp.clip(entries, -most, most).astype(held_as)


def noise_with(key, shape, deviation, most, cuts, heavy, held_as=jnp.bfloat16):
    entries = deviation * jax.random.normal(key, shape, jnp.float32)
    if cuts:
        entries = entries * block_scale(key, shape, cuts, -0.22, 0.18)
    return jnp.clip(with_spikes(entries, jax.random.fold_in(key, 3), *heavy), -most, most).astype(held_as)


def setup_inputs(seed: int = 0) -> dict:
    splits = jax.random.split(jax.random.key(seed), 7)
    return {
        "volume_field": centred(splits[0], (RHS, NX, NY, NZ), 1.0, 6.0, ((1, 4), (2, 2), (3, 4))),
        "volume_load": centred(splits[1], (RHS, NX, NY, NZ), 1.0, 6.0, ((1, 4), (2, 2), (3, 4))),
        "coefficient": jnp.clip(0.25 + 1.75 * jax.random.uniform(splits[2], (NX, NY, NZ), jnp.float32) ** block_scale(splits[2], (NX, NY, NZ), ((0, 4), (1, 2), (2, 4)), -0.2, 0.2), 0.25, 2.0),
        "surface_block": noise_with(splits[3], (NSR, NS), NS ** -0.5, 0.046875, ((0, 4), (1, 2)), (1, 0, 4, 2.0)),
        "trace_cell": draw_trace_cell(jax.random.fold_in(splits[6], 71), 0),
        "flux_cell": draw_flux_cell(jax.random.fold_in(splits[6], 71), 0),
    }


OMEGA = 0.8


def relax(current, source, diagonal):
    centre = current.astype(jnp.float32)
    padded = jnp.pad(centre, 1)
    beside = padded[2:, 1:-1, 1:-1] + padded[:-2, 1:-1, 1:-1]
    beside = beside + padded[1:-1, 2:, 1:-1] + padded[1:-1, :-2, 1:-1]
    beside = beside + padded[1:-1, 1:-1, 2:] + padded[1:-1, 1:-1, :-2]
    return (centre + OMEGA * (source - (diagonal * centre - beside)) / diagonal).astype(jnp.bfloat16)


def reference(volume_field, volume_load, coefficient, surface_block, trace_cell, flux_cell):
    cell_count = VX * VY * VZ
    blocks = volume_field.reshape(RHS, N_ROW, VX, N_COL, VY, N_GZ, VZ)
    blocks = blocks.transpose(0, 1, 3, 5, 2, 4, 6).reshape(RHS, N_ROW, N_COL, N_GZ, cell_count)
    indices = jnp.broadcast_to(trace_cell[None].astype(jnp.int32), (RHS, N_ROW, N_COL, N_GZ, TS))
    traced = jnp.take_along_axis(blocks, indices, axis=4)
    trace_values = traced.transpose(0, 2, 1, 3, 4).reshape(RHS, N_COL * N_ROW * N_GZ * TS)
    surface_flux = jnp.dot(trace_values, surface_block.T, preferred_element_type=jnp.float32)
    flux_parts = surface_flux.reshape(RHS, N_ROW, N_COL, N_GZ, FS).astype(jnp.float32)
    onehot = (flux_cell[..., None].astype(jnp.int32) == jnp.arange(cell_count, dtype=jnp.int32)).astype(jnp.float32)
    placed = jnp.einsum('srcgk,rcgkv->srcgv', flux_parts, onehot, precision=lax.Precision.HIGHEST)
    placed = placed.reshape(RHS, N_ROW, N_COL, N_GZ, VX, VY, VZ).transpose(0, 1, 4, 2, 5, 3, 6)
    placed = placed.reshape(RHS, NX, NY, NZ)
    diagonal = 6.0 + coefficient.astype(jnp.float32)

    def one_side(items):
        current, load_term, extra = items
        source = load_term.astype(jnp.float32) + extra
        for repeat in range(3):
            current = relax(current, source, diagonal)
        return current

    new_field = lax.map(one_side, (volume_field, volume_load, placed))
    return new_field, surface_flux
```

```python
import functools

import jax
import jax.numpy as jnp
from jax import lax
from jax.experimental import pallas as pl
from jax.experimental.pallas import tpu as pltpu
from jax.sharding import PartitionSpec as P

OMEGA = 0.8
BF = jnp.bfloat16
F32 = jnp.float32
VMEM_LIMIT = 40 * 1024 * 1024


def iota(shape, dim):
    return lax.broadcasted_iota(jnp.int32, shape, dim)


def dot(a, b):
    return jnp.dot(a, b, preferred_element_type=F32)


def dot_nt(a, b):
    return lax.dot_general(a, b, (((1,), (1,)), ((), ())), preferred_element_type=F32)


def params():
    return pltpu.CompilerParams(vmem_limit_bytes=VMEM_LIMIT)


def trace_kernel(stride, field_ref, cell_ref, out_ref, perm, pick, rsum, picked):
    step = pl.program_id(0)
    sides, rows, lanes = field_ref.shape
    slots = cell_ref.shape[3]
    per_row = lanes // stride
    group = 16
    width = group * per_row

    @pl.when(step == 0)
    def _():
        cell = cell_ref[0, 0]
        perm[...] = (iota((slots, slots), 0) == cell // stride).astype(BF)
        offset = jnp.broadcast_to((cell % stride).astype(BF), (16, slots))
        sorted_offset = dot_nt(offset, perm[...])[0:1].astype(jnp.int32)
        place = (iota((1, slots), 1) % per_row) * stride + sorted_offset
        pick[...] = (iota((lanes, slots), 0) == place).astype(BF)
        shape = (sides, sides * group)
        rsum[...] = (iota(shape, 1) // group == iota(shape, 0)).astype(BF)

    shape = (sides * group, width)
    own = iota(shape, 0) % group == iota(shape, 1) // per_row
    for part in range(rows // group):
        values = field_ref[:, part * group : (part + 1) * group, :].reshape(sides * group, lanes)
        cols = slice(part * width, (part + 1) * width)
        spread = dot(values, pick[:, cols])
        spread = jnp.where(own, spread, 0.0).astype(BF)
        picked[pl.ds(pl.multiple_of(step * sides, sides), sides), cols] = dot(
            rsum[...], spread
        ).astype(BF)

    @pl.when(step == pl.num_programs(0) - 1)
    def _():
        out_ref[...] = dot(picked[...], perm[...]).astype(BF)


def traces(field, trace_cell, block):
    sides, rows, lanes = field.shape
    slots = trace_cell.shape[3]
    stride = rows * lanes // slots
    return pl.pallas_call(
        functools.partial(trace_kernel, stride),
        grid=(sides // block,),
        in_specs=[
            pl.BlockSpec((block, rows, lanes), lambda i: (i, 0, 0)),
            pl.BlockSpec(trace_cell.shape, lambda i: (0, 0, 0, 0)),
        ],
        out_specs=pl.BlockSpec((sides, slots), lambda i: (0, 0)),
        out_shape=jax.ShapeDtypeStruct((sides, slots), BF),
        scratch_shapes=[
            pltpu.VMEM((slots, slots), BF),
            pltpu.VMEM((lanes, slots), BF),
            pltpu.VMEM((block, block * 16), BF),
            pltpu.VMEM((sides, slots), BF),
        ],
        compiler_params=params(),
        cost_estimate=pl.CostEstimate(
            flops=4 * sides * rows * lanes * 128, bytes_accessed=field.size * 2, transcendentals=0
        ),
    )(field, trace_cell)


def xor_gather(value, axis):
    peers = lax.axis_size(axis)
    held = {0: value}
    bit = peers // 2
    while bit:
        swap = [(i, i ^ bit) for i in range(peers)]
        for key in sorted(held, reverse=True):
            held[key ^ bit] = lax.ppermute(held[key], axis, swap)
        bit //= 2
    return [held[key] for key in range(peers)]


def surface_kernel(row, gz, peers, gzs, cols, *refs):
    parts = refs[:peers]
    block_ref, out_ref, held, sems = refs[peers:]
    sides, slots = parts[0].shape
    me, group = lax.axis_index(row), lax.axis_index(gz)
    copies = []
    for key in range(peers):
        start = pl.multiple_of((jnp.bitwise_xor(me, key) * gzs + group) * slots, slots)
        copies.append(
            pltpu.make_async_copy(block_ref.at[:, pl.ds(start, slots)], held.at[key], sems.at[key])
        )
        copies[-1].start()
    total = None
    for key in range(peers):
        copies[key].wait()
        term = dot_nt(parts[key][...], held[key])
        total = term if total is None else total + term
    turned = total.T
    lines = total.shape[1]
    out_ref[...] = jnp.zeros_like(out_ref)
    s_count, l_count, f_count = sides // gzs, lines // cols, lines // (cols * gzs)
    for c in range(cols):
        for g in range(gzs):
            dest = c * gzs + g
            out_ref[dest, :s_count, :l_count] = total[
                g * s_count : (g + 1) * s_count, c * l_count : (c + 1) * l_count
            ].astype(out_ref.dtype)
            out_ref[dest, s_count : s_count + f_count, :sides] = turned[
                dest * f_count : (dest + 1) * f_count
            ].astype(out_ref.dtype)


def surface(parts, block, dtype):
    peers, gzs, cols = lax.axis_size("row"), lax.axis_size("gz"), lax.axis_size("col")
    sides, slots = parts[0].shape
    lines = block.shape[0]
    depth = sides // gzs + lines // (cols * gzs)
    shape = (cols * gzs, depth, max(sides, lines // cols))
    whole = pl.BlockSpec(memory_space=pltpu.VMEM)
    return pl.pallas_call(
        functools.partial(surface_kernel, "row", "gz", peers, gzs, cols),
        in_specs=[whole] * peers + [pl.BlockSpec(memory_space=pl.ANY)],
        out_specs=whole,
        out_shape=jax.ShapeDtypeStruct(shape, dtype),
        scratch_shapes=[
            pltpu.VMEM((peers, lines, slots), BF),
            pltpu.SemaphoreType.DMA((peers,)),
        ],
        compiler_params=params(),
        cost_estimate=pl.CostEstimate(
            flops=2 * sides * lines * slots * peers,
            bytes_accessed=2 * lines * slots * peers,
            transcendentals=0,
        ),
    )(*parts, block)


class Shape:
    def __init__(self, sides, first, second, lanes, cols, block):
        self.sides, self.x, self.y, self.lanes = sides, first, second, lanes
        self.cells = first * second
        self.paired = cols == 2
        self.block = block
        self.chunk = max(1, 256 // self.cells)
        self.rows = self.chunk * self.cells
        self.faces = 3 if self.paired else 4

    def face_len(self, face):
        return self.y if face < 2 else self.x


def face_select(shape, second, halo):
    dims = (shape.rows, shape.chunk * shape.y * 2 + shape.chunk * shape.x * (shape.faces - 2))
    row = iota(dims, 0)
    side, cell = row // shape.cells, row % shape.cells
    x, y = cell // shape.y, cell % shape.y
    col = iota(dims, 1)
    hit = None
    base = 0
    for face in range(shape.faces):
        length = shape.face_len(face)
        span = shape.chunk * length
        inside = col - base
        if face < 2:
            edge = 0 if face == 0 else shape.x - 1
            place = (x == edge) & (inside == side * length + y)
        else:
            if shape.paired:
                edge = jnp.where(second == 0, shape.y - 1, 0)
            else:
                edge = 0 if face == 2 else shape.y - 1
            place = (y == edge) & (inside == side * length + x)
        hit = place if hit is None else hit | place
        base += span
    return hit.astype(BF)


def z_mask(shape):
    dims = (shape.cells, 2 * shape.cells)
    return iota(dims, 1) % shape.cells == iota(dims, 0)


def build_out(shape, second, faces_m, ends_m, rsum):
    faces_m[...] = face_select(shape, second, False).T
    dims = (shape.lanes, 2 * shape.cells)
    edge = jnp.where(iota(dims, 1) < shape.cells, 0, shape.lanes - 1)
    ends_m[...] = (iota(dims, 0) == edge).astype(BF)
    dims = (shape.block, shape.block * shape.cells)
    rsum[...] = (iota(dims, 1) // shape.cells == iota(dims, 0)).astype(BF)


def emit_faces(shape, index, values, face_refs, faces_m, ends_m, rsum, ends):
    cut = dot(faces_m[...], values).astype(BF)
    base = 0
    for face in range(shape.faces):
        span = shape.chunk * shape.face_len(face)
        face_refs[face][index * span : (index + 1) * span, :] = cut[base : base + span]
        base += span
    tips = dot(values, ends_m[...])
    mask = jnp.concatenate([z_mask(shape)] * shape.chunk, axis=0)
    tips = jnp.where(mask, tips, 0.0).astype(BF)
    part = dot(rsum[:, index * shape.rows : (index + 1) * shape.rows], tips)
    return part if ends is None else ends + part


def faces_kernel(shape, field_ref, *refs):
    face_refs, z_ref = refs[: shape.faces], refs[shape.faces]
    faces_m, ends_m, rsum = refs[shape.faces + 1 :]

    @pl.when(pl.program_id(0) == 0)
    def _():
        build_out(shape, lax.axis_index("col"), faces_m, ends_m, rsum)

    ends = None
    for index in range(shape.block // shape.chunk):
        values = field_ref[index * shape.rows : (index + 1) * shape.rows, :]
        ends = emit_faces(shape, index, values, face_refs, faces_m, ends_m, rsum, ends)
    z_ref[...] = ends.astype(BF)


def face_outputs(shape):
    specs, shapes = [], []
    for face in range(shape.faces):
        length = shape.face_len(face)
        specs.append(pl.BlockSpec((shape.block * length, shape.lanes), lambda i: (i, 0)))
        shapes.append(jax.ShapeDtypeStruct((shape.sides * length, shape.lanes), BF))
    specs.append(pl.BlockSpec((shape.block, 2 * shape.cells), lambda i: (i, 0)))
    shapes.append(jax.ShapeDtypeStruct((shape.sides, 2 * shape.cells), BF))
    return specs, shapes


def face_scratch(shape):
    cut = shape.chunk * shape.y * 2 + shape.chunk * shape.x * (shape.faces - 2)
    return [
        pltpu.VMEM((cut, shape.rows), BF),
        pltpu.VMEM((shape.lanes, 2 * shape.cells), BF),
        pltpu.VMEM((shape.block, shape.block * shape.cells), BF),
    ]


def first_faces(shape, field):
    specs, shapes = face_outputs(shape)
    return pl.pallas_call(
        functools.partial(faces_kernel, shape),
        grid=(shape.sides // shape.block,),
        in_specs=[pl.BlockSpec((shape.block * shape.cells, shape.lanes), lambda i: (i, 0))],
        out_specs=specs,
        out_shape=shapes,
        scratch_shapes=face_scratch(shape),
        compiler_params=params(),
        cost_estimate=pl.CostEstimate(
            flops=4 * field.size * 128, bytes_accessed=4 * field.size, transcendentals=0
        ),
    )(field)


def sweep_kernel(shape, with_flux, last, *refs):
    refs = list(refs)
    take = lambda count: [refs.pop(0) for _ in range(count)]
    field_ref, load_ref, coef_ref = take(3)
    halo_refs = take(shape.faces)
    below_ref, above_ref = take(2)
    if with_flux:
        recv_ref, cell_ref = take(2)
    (out_ref,) = take(1)
    if not last:
        face_refs = take(shape.faces)
        (z_ref,) = take(1)
    if with_flux:
        source_ref, flux_ref = take(2)
    weight, near_m, halo_m, line_m = take(4)
    if not last:
        faces_m, ends_m, rsum = take(3)
    if with_flux:
        phi, cell_m = take(2)

    step = pl.program_id(0)
    cells, lanes = shape.cells, shape.lanes

    @pl.when(step == 0)
    def _():
        second = lax.axis_index("col")
        weight[...] = OMEGA / (6.0 + coef_ref[...])
        dims = (shape.rows, shape.rows)
        row, col = iota(dims, 0), iota(dims, 1)
        x, y = row % cells // shape.y, row % shape.y
        x2, y2 = col % cells // shape.y, col % shape.y
        near = ((x == x2) & (jnp.abs(y - y2) == 1)) | ((y == y2) & (jnp.abs(x - x2) == 1))
        near_m[...] = (near & (row // cells == col // cells)).astype(BF)
        halo_m[...] = face_select(shape, second, True)
        dims = (lanes, lanes)
        line_m[:lanes, :] = (jnp.abs(iota(dims, 0) - iota(dims, 1)) == 1).astype(BF)
        dims = (2 * cells, lanes)
        edge = jnp.where(iota(dims, 0) < cells, lanes - 1, 0)
        line_m[lanes:, :] = (iota(dims, 1) == edge).astype(BF)
        if not last:
            build_out(shape, second, faces_m, ends_m, rsum)
        if with_flux:
            total = recv_ref[0].astype(F32)
            for peer in range(1, recv_ref.shape[0]):
                total = total + recv_ref[peer].astype(F32)
            s_count, l_count = flux_ref.shape
            slots = cell_ref.shape[3]
            flux_ref[...] = total[:s_count, :l_count]
            owned = total[s_count : s_count + slots, : shape.sides]
            high = owned.astype(BF).astype(F32)
            both = jnp.concatenate([high, owned - high], axis=0)
            phi[...] = both.T
            cell = jnp.concatenate([cell_ref[0, 0]] * 2, axis=1)
            cell_m[...] = (iota((lanes, 2 * slots), 0) == cell % lanes).astype(BF)

    mask = z_mask(shape)
    zs = jnp.where(
        iota((shape.block, 2 * cells), 1) < cells,
        above_ref[...].astype(F32),
        below_ref[...].astype(F32),
    )
    if with_flux:
        slots = cell_ref.shape[3]
        cell = jnp.concatenate([cell_ref[0, 0]] * 2, axis=1)
        cell_mask = iota((cells, 2 * slots), 0) == cell // lanes
        phis = phi[pl.ds(pl.multiple_of(step * shape.block, shape.block), shape.block), :]
    weights = jnp.concatenate([weight[...]] * shape.chunk, axis=0)
    ends = None
    for index in range(shape.block // shape.chunk):
        span = slice(index * shape.rows, (index + 1) * shape.rows)
        values = field_ref[span, :]
        halos = []
        for face in range(shape.faces):
            length = shape.chunk * shape.face_len(face)
            halos.append(halo_refs[face][index * length : (index + 1) * length, :])
        spread = []
        for side in range(shape.chunk):
            at = index * shape.chunk + side
            spread.append(jnp.where(mask, jnp.broadcast_to(zs[at : at + 1], mask.shape), 0.0))
        spread = jnp.concatenate(spread, axis=0).astype(BF)
        near = dot(near_m[...], values) + dot(halo_m[...], jnp.concatenate(halos, axis=0))
        near = near + dot(jnp.concatenate([values, spread], axis=1), line_m[...])
        source = load_ref[span, :].astype(F32)
        if with_flux:
            spread = []
            for side in range(shape.chunk):
                at = index * shape.chunk + side
                line = jnp.broadcast_to(phis[at : at + 1], cell_mask.shape)
                spread.append(jnp.where(cell_mask, line, 0.0))
            spread = jnp.concatenate(spread, axis=0).astype(BF)
            source = source + dot_nt(spread, cell_m[...])
            source_ref[span, :] = source.astype(BF)
        fresh = (1.0 - OMEGA) * values.astype(F32) + weights * (source + near)
        fresh = fresh.astype(BF)
        out_ref[span, :] = fresh
        if not last:
            ends = emit_faces(shape, index, fresh, face_refs, faces_m, ends_m, rsum, ends)
    if not last:
        z_ref[...] = ends.astype(BF)


def sweep(shape, field, load, coef, halos, recv=None, flux_cell=None, last=False):
    with_flux = recv is not None
    block, lanes, cells = shape.block, shape.lanes, shape.cells
    big = pl.BlockSpec((block * cells, lanes), lambda i: (i, 0))
    specs, shapes = face_outputs(shape)
    in_specs = [big, big, pl.BlockSpec(coef.shape, lambda i: (0, 0))] + specs + specs[-1:]
    operands = [field, load, coef, *halos]
    out_specs, out_shapes = [big], [jax.ShapeDtypeStruct(field.shape, BF)]
    cut = shape.chunk * shape.y * 2 + shape.chunk * shape.x * (shape.faces - 2)
    scratch = [
        pltpu.VMEM(coef.shape, F32),
        pltpu.VMEM((shape.rows, shape.rows), BF),
        pltpu.VMEM((shape.rows, cut), BF),
        pltpu.VMEM((lanes + 2 * cells, lanes), BF),
    ]
    if not last:
        out_specs, out_shapes = out_specs + specs, out_shapes + shapes
        scratch += face_scratch(shape)
    if with_flux:
        slots = flux_cell.shape[3]
        gzs = lax.axis_size("gz")
        in_specs += [
            pl.BlockSpec(recv.shape, lambda i: (0, 0, 0)),
            pl.BlockSpec(flux_cell.shape, lambda i: (0, 0, 0, 0)),
        ]
        operands += [recv, flux_cell]
        flux_shape = (shape.sides // gzs, slots * gzs)
        out_specs += [big, pl.BlockSpec(flux_shape, lambda i: (0, 0))]
        out_shapes += [
            jax.ShapeDtypeStruct(field.shape, BF),
            jax.ShapeDtypeStruct(flux_shape, F32),
        ]
        scratch += [pltpu.VMEM((shape.sides, 2 * slots), F32), pltpu.VMEM((lanes, 2 * slots), BF)]
    return pl.pallas_call(
        functools.partial(sweep_kernel, shape, with_flux, last),
        grid=(shape.sides // block,),
        in_specs=in_specs,
        out_specs=out_specs,
        out_shape=out_shapes,
        scratch_shapes=scratch,
        compiler_params=params(),
        cost_estimate=pl.CostEstimate(
            flops=10 * field.size * 128, bytes_accessed=8 * field.size, transcendentals=0
        ),
    )(*operands)


def exchange(shape, faces):
    def ways(axis):
        peers = lax.axis_size(axis)
        up = [(i, i + 1) for i in range(peers - 1)]
        return up, [(j, i) for i, j in up]

    *cut, ends = faces
    if shape.paired:
        y = [lax.ppermute(cut[2], "col", [(0, 1), (1, 0)])]
    else:
        up, down = ways("col")
        y = [lax.ppermute(cut[3], "col", up), lax.ppermute(cut[2], "col", down)]
    up, down = ways("row")
    x = [lax.ppermute(cut[1], "row", up), lax.ppermute(cut[0], "row", down)]
    up, down = ways("gz")
    z = [lax.ppermute(ends, "gz", up), lax.ppermute(ends, "gz", down)]
    return x + y + z


def per_device(volume_field, volume_load, coefficient, surface_block, trace_cell, flux_cell):
    sides, first, second, lanes = volume_field.shape
    cells = first * second
    block = min(32, sides)
    shape = Shape(sides, first, second, lanes, lax.axis_size("col"), block)
    field = volume_field.reshape(sides * cells, lanes)
    load = volume_load.reshape(sides * cells, lanes)
    coef = coefficient.reshape(cells, lanes)

    trace = traces(volume_field.reshape(sides, cells, lanes), trace_cell, block)
    parts = xor_gather(trace, "row")
    halos = exchange(shape, first_faces(shape, field))
    sent = surface(parts, surface_block, F32)
    recv = lax.all_to_all(sent, ("col", "gz"), split_axis=0, concat_axis=0, tiled=True)

    current, *faces, source, surface_flux = sweep(
        shape, field, load, coef, halos, recv=recv, flux_cell=flux_cell
    )
    current, *faces = sweep(shape, current, source, coef, exchange(shape, faces))
    (current,) = sweep(shape, current, source, coef, exchange(shape, faces), last=True)
    return current.reshape(volume_field.shape), surface_flux


def solution(mesh):
    in_specs = (
        P(None, "row", "col", "gz"),
        P(None, "row", "col", "gz"),
        P("row", "col", "gz"),
        P("row", "col"),
        P("row", "col", "gz", None),
        P("row", "col", "gz", None),
    )
    out_specs = (P(None, "row", "col", "gz"), P("gz", ("row", "col")))
    return jax.shard_map(
        per_device, mesh=mesh, in_specs=in_specs, out_specs=out_specs, check_vma=False
    )
```

```python
import functools

import jax
import jax.numpy as jnp
from jax import lax
from jax.experimental import pallas as pl
from jax.experimental.pallas import tpu as pltpu
from jax.sharding import PartitionSpec as P

OMEGA = 0.8
BF = jnp.bfloat16
F32 = jnp.float32
WHOLE = pl.BlockSpec(memory_space=pltpu.VMEM)


def iota(shape, dim):
    return lax.broadcasted_iota(jnp.int32, shape, dim)


def dot(a, b):
    return jnp.dot(a, b, preferred_element_type=F32)


def dot_nt(a, b):
    return lax.dot_general(a, b, (((1,), (1,)), ((), ())), preferred_element_type=F32)


def params(mebibytes=24):
    return pltpu.CompilerParams(vmem_limit_bytes=mebibytes * 1024 * 1024)


def trace_kernel(stride, block, field_ref, cell_ref, out_ref, field, cell_v, perm, pick, rsum, sems):
    sides, rows, lanes = field.shape
    slots = cell_ref.shape[3]
    per_row = lanes // stride
    group = 16
    width = group * per_row
    cell_copy = pltpu.make_async_copy(cell_ref, cell_v, sems.at[sides // block])
    cell_copy.start()
    copies = []
    for step in range(sides // block):
        span = pl.ds(step * block, block)
        copies.append(pltpu.make_async_copy(field_ref.at[span], field.at[span], sems.at[step]))
        copies[-1].start()

    shape = (block, block * group)
    rsum[...] = (iota(shape, 1) // group == iota(shape, 0)).astype(BF)
    cell_copy.wait()
    cell = cell_v[0, 0]
    perm[...] = (iota((slots, slots), 0) == cell // stride).astype(BF)
    offset = jnp.broadcast_to((cell % stride).astype(BF), (16, slots))
    sorted_offset = dot_nt(offset, perm[...])[0:1].astype(jnp.int32)
    place = (iota((1, slots), 1) % per_row) * stride + sorted_offset
    pick[...] = (iota((lanes, slots), 0) == place).astype(BF)

    shape = (block * group, width)
    own = iota(shape, 0) % group == iota(shape, 1) // per_row
    picked = []
    for step in range(sides // block):
        copies[step].wait()
        parts = []
        for part in range(rows // group):
            values = field[step * block : (step + 1) * block, part * group : (part + 1) * group, :]
            cols = slice(part * width, (part + 1) * width)
            spread = dot(values.reshape(block * group, lanes), pick[:, cols])
            spread = jnp.where(own, spread, 0.0).astype(BF)
            parts.append(dot(rsum[...], spread).astype(BF))
        picked.append(jnp.concatenate(parts, axis=1))
    out_ref[...] = dot(jnp.concatenate(picked, axis=0), perm[...]).astype(BF)


def traces(field, trace_cell, block):
    sides, rows, lanes = field.shape
    slots = trace_cell.shape[3]
    stride = rows * lanes // slots
    hbm = pl.BlockSpec(memory_space=pltpu.HBM)
    return pl.pallas_call(
        functools.partial(trace_kernel, stride, block),
        in_specs=[hbm, hbm],
        out_specs=WHOLE,
        out_shape=jax.ShapeDtypeStruct((sides, slots), BF),
        scratch_shapes=[
            pltpu.VMEM(field.shape, BF),
            pltpu.VMEM(trace_cell.shape, jnp.int32),
            pltpu.VMEM((slots, slots), BF),
            pltpu.VMEM((lanes, slots), BF),
            pltpu.VMEM((block, block * 16), BF),
            pltpu.SemaphoreType.DMA((sides // block + 1,)),
        ],
        compiler_params=params(62),
        cost_estimate=pl.CostEstimate(
            flops=4 * sides * rows * lanes * 128, bytes_accessed=field.size * 2, transcendentals=0
        ),
    )(field, trace_cell)


def surface_kernel(row, gz, peers, gzs, cols, *refs):
    parts = refs[:peers]
    block_ref, out_ref, held, sems = refs[peers:]
    sides, slots = parts[0].shape
    me, group = lax.axis_index(row), lax.axis_index(gz)
    copies = []
    for key in range(peers):
        start = pl.multiple_of((jnp.bitwise_xor(me, key) * gzs + group) * slots, slots)
        copies.append(
            pltpu.make_async_copy(block_ref.at[:, pl.ds(start, slots)], held.at[key], sems.at[key])
        )
        copies[-1].start()
    total = None
    for key in range(peers):
        copies[key].wait()
        term = dot_nt(parts[key][...], held[key])
        total = term if total is None else total + term
    turned = total.T
    lines = total.shape[1]
    out_ref[...] = jnp.zeros_like(out_ref)
    s_count, l_count, f_count = sides // gzs, lines // cols, lines // (cols * gzs)
    for c in range(cols):
        for g in range(gzs):
            dest = c * gzs + g
            out_ref[dest, :s_count, :l_count] = total[
                g * s_count : (g + 1) * s_count, c * l_count : (c + 1) * l_count
            ].astype(out_ref.dtype)
            out_ref[dest, s_count : s_count + f_count, :sides] = turned[
                dest * f_count : (dest + 1) * f_count
            ].astype(out_ref.dtype)


def surface(parts, block, dtype):
    peers, gzs, cols = lax.axis_size("row"), lax.axis_size("gz"), lax.axis_size("col")
    sides, slots = parts[0].shape
    lines = block.shape[0]
    depth = sides // gzs + lines // (cols * gzs)
    shape = (cols * gzs, depth, max(sides, lines // cols))
    return pl.pallas_call(
        functools.partial(surface_kernel, "row", "gz", peers, gzs, cols),
        in_specs=[WHOLE] * peers + [pl.BlockSpec(memory_space=pltpu.HBM)],
        out_specs=WHOLE,
        out_shape=jax.ShapeDtypeStruct(shape, dtype),
        scratch_shapes=[
            pltpu.VMEM((peers, lines, slots), BF),
            pltpu.SemaphoreType.DMA((peers,)),
        ],
        compiler_params=params(58),
        cost_estimate=pl.CostEstimate(
            flops=2 * sides * lines * slots * peers,
            bytes_accessed=2 * lines * slots * peers,
            transcendentals=0,
        ),
    )(*parts, block)


def swaps(peers):
    pairs = [[(i, i + 1) for i in range(first, peers - 1, 2)] for first in (0, 1)]
    return [[(i, j) for i, j in part] + [(j, i) for i, j in part] for part in pairs if part]


class Shape:
    def __init__(self, sides, first, second, lanes):
        self.sides, self.x, self.y, self.lanes = sides, first, second, lanes
        self.cells = first * second
        self.chunk = max(1, 256 // self.cells)
        self.rows = self.chunk * self.cells
        self.block = min(sides, 16)
        self.faces = [("row", i) for i in range(len(swaps(lax.axis_size("row"))))]
        self.faces += [("col", i) for i in range(len(swaps(lax.axis_size("col"))))]
        self.ends = len(swaps(lax.axis_size("gz")))

    def face_len(self, face):
        return self.y if face[0] == "row" else self.x

    def halo_rows(self):
        return sum(self.chunk * self.face_len(face) for face in self.faces)

    def edge(self, face):
        axis, turn = face
        last = (self.x if axis == "row" else self.y) - 1
        return jnp.where(lax.axis_index(axis) % 2 == turn, last, 0)


def halo_place(shape):
    dims = (shape.rows, shape.halo_rows())
    row, col = iota(dims, 0), iota(dims, 1)
    side, cell = row // shape.cells, row % shape.cells
    x, y = cell // shape.y, cell % shape.y
    hit, base = None, 0
    for face in shape.faces:
        length = shape.face_len(face)
        along, across = (y, x) if face[0] == "row" else (x, y)
        place = (across == shape.edge(face)) & (col - base == side * length + along)
        hit = place if hit is None else hit | place
        base += shape.chunk * length
    return hit.astype(BF)


def z_mask(shape, count):
    dims = (count * shape.cells, 2 * shape.cells)
    return iota(dims, 1) % shape.cells == iota(dims, 0) % shape.cells


def build_out(shape, ends_m, rsum):
    dims = (shape.lanes, 2 * shape.cells)
    edge = jnp.where(iota(dims, 1) < shape.cells, 0, shape.lanes - 1)
    ends_m[...] = (iota(dims, 0) == edge).astype(BF)
    dims = (shape.block, shape.block * shape.cells)
    rsum[...] = (iota(dims, 1) // shape.cells == iota(dims, 0)).astype(BF)


def emit_faces(shape, at, values, tall, face_refs, z_ref, ends_m, rsum):
    for face, ref in zip(shape.faces, face_refs):
        length, edge = shape.face_len(face), shape.edge(face)
        lines = []
        for side in range(shape.block):
            start = side * shape.cells
            if face[0] == "row":
                lines.append(tall[pl.ds(pl.multiple_of(start + edge * length, 8), length), :])
            else:
                lines.append(tall[pl.ds(start + edge, length, stride=shape.y), :])
        span = shape.block * length
        ref[pl.ds(pl.multiple_of(at * length, span), span), :] = jnp.concatenate(
            lines, axis=0
        ).astype(BF)
    tips = jnp.where(z_mask(shape, shape.block), dot(values, ends_m[...]), 0.0).astype(BF)
    z_ref[pl.ds(pl.multiple_of(at, shape.block), shape.block), :] = dot(rsum[...], tips).astype(BF)


def faces_kernel(shape, field_ref, *refs):
    *face_refs, z_ref, tall, ends_m, rsum = refs
    build_out(shape, ends_m, rsum)

    @pl.loop(0, shape.sides // shape.block)
    def _(step):
        size = shape.block * shape.cells
        values = field_ref[pl.ds(pl.multiple_of(step * size, size), size), :]
        tall[...] = values.astype(F32)
        emit_faces(shape, step * shape.block, values, tall, face_refs, z_ref, ends_m, rsum)


def face_outputs(shape):
    shapes = [
        jax.ShapeDtypeStruct((shape.sides * shape.face_len(face), shape.lanes), BF)
        for face in shape.faces
    ]
    return shapes + [jax.ShapeDtypeStruct((shape.sides, 2 * shape.cells), BF)]


def face_scratch(shape):
    return [
        pltpu.VMEM((shape.block * shape.cells, shape.lanes), F32),
        pltpu.VMEM((shape.lanes, 2 * shape.cells), BF),
        pltpu.VMEM((shape.block, shape.block * shape.cells), BF),
    ]


def first_faces(shape, field):
    shapes = face_outputs(shape)
    return pl.pallas_call(
        functools.partial(faces_kernel, shape),
        in_specs=[WHOLE],
        out_specs=[WHOLE] * len(shapes),
        out_shape=shapes,
        scratch_shapes=face_scratch(shape),
        compiler_params=params(),
        cost_estimate=pl.CostEstimate(
            flops=field.size * 128, bytes_accessed=4 * field.size, transcendentals=0
        ),
    )(field)


def sweep_kernel(shape, with_flux, last, *refs):
    refs = list(refs)
    take = lambda count: [refs.pop(0) for _ in range(count)]
    field_ref, load_ref, coef_ref = take(3)
    halo_refs = take(len(shape.faces))
    end_refs = take(shape.ends)
    if with_flux:
        recv_ref, cell_ref = take(2)
    (out_ref,) = take(1)
    if not last:
        face_refs = take(len(shape.faces))
        (z_ref,) = take(1)
    if with_flux:
        source_ref, flux_ref = take(2)
    weight, near_m, line_m = take(3)
    if not last:
        tall, ends_m, rsum = take(3)
    if with_flux:
        phi, cell_m = take(2)

    grid_step = pl.program_id(0)
    cells, lanes = shape.cells, shape.lanes

    @pl.when(grid_step == 0)
    def _():
        weight[...] = OMEGA / (6.0 + coef_ref[...])
        dims = (shape.rows, shape.rows)
        row, col = iota(dims, 0), iota(dims, 1)
        x, y = row % cells // shape.y, row % shape.y
        x2, y2 = col % cells // shape.y, col % shape.y
        near = ((x == x2) & (jnp.abs(y - y2) == 1)) | ((y == y2) & (jnp.abs(x - x2) == 1))
        near_m[:, : shape.rows] = (near & (row // cells == col // cells)).astype(BF)
        near_m[:, shape.rows :] = halo_place(shape)
        dims = (lanes, lanes)
        line_m[:lanes, :] = (jnp.abs(iota(dims, 0) - iota(dims, 1)) == 1).astype(BF)
        dims = (2 * cells, lanes)
        edge = jnp.where(iota(dims, 0) < cells, lanes - 1, 0)
        line_m[lanes:, :] = (iota(dims, 1) == edge).astype(BF)
        if not last:
            build_out(shape, ends_m, rsum)
        if with_flux:
            total = recv_ref[0].astype(F32)
            for peer in range(1, recv_ref.shape[0]):
                total = total + recv_ref[peer].astype(F32)
            s_count, l_count = flux_ref.shape
            slots = cell_ref.shape[3]
            flux_ref[...] = total[:s_count, :l_count]
            owned = total[s_count : s_count + slots, : shape.sides]
            high = owned.astype(BF).astype(F32)
            both = jnp.concatenate([high, owned - high], axis=0)
            phi[...] = both.T
            cell = jnp.concatenate([cell_ref[0, 0]] * 2, axis=1)
            cell_m[...] = (iota((lanes, 2 * slots), 0) == cell % lanes).astype(BF)

    mask = z_mask(shape, 1)
    even = lax.axis_index("gz") % 2 == 0
    first_swap = (iota((shape.block, 2 * cells), 1) < cells) == even
    if with_flux:
        slots = cell_ref.shape[3]
        cell = jnp.concatenate([cell_ref[0, 0]] * 2, axis=1)
        cell_mask = iota((cells, 2 * slots), 0) == cell // lanes
    weights = jnp.concatenate([weight[...]] * shape.chunk, axis=0)
    out_sides = out_ref.shape[0] // cells

    @pl.loop(0, out_sides // shape.block)
    def _(step):
        local = step * shape.block
        at = grid_step * out_sides + local
        sides = pl.ds(pl.multiple_of(at, shape.block), shape.block)
        zs = end_refs[0][sides, :].astype(F32)
        other = end_refs[1][sides, :].astype(F32) if shape.ends > 1 else 0.0
        zs = jnp.where(first_swap, zs, other)
        if with_flux:
            phis = phi[sides, :]
        for index in range(shape.block // shape.chunk):
            offset = index * shape.rows
            span = pl.ds(pl.multiple_of(at * cells + offset, shape.rows), shape.rows)
            values = field_ref[span, :]
            stack = [values]
            for face, ref in zip(shape.faces, halo_refs):
                length = shape.face_len(face)
                size = shape.chunk * length
                start = pl.multiple_of(at * length + index * size, size)
                stack.append(ref[pl.ds(start, size), :])
            spread = []
            for side in range(index * shape.chunk, (index + 1) * shape.chunk):
                line = jnp.broadcast_to(zs[side : side + 1], mask.shape)
                spread.append(jnp.where(mask, line, 0.0))
            spread = jnp.concatenate(spread, axis=0).astype(BF)
            near = dot(near_m[...], jnp.concatenate(stack, axis=0))
            near = near + dot(jnp.concatenate([values, spread], axis=1), line_m[...])
            source = load_ref[span, :].astype(F32)
            if with_flux:
                spread = []
                for side in range(index * shape.chunk, (index + 1) * shape.chunk):
                    line = jnp.broadcast_to(phis[side : side + 1], cell_mask.shape)
                    spread.append(jnp.where(cell_mask, line, 0.0))
                spread = jnp.concatenate(spread, axis=0).astype(BF)
                source = source + dot_nt(spread, cell_m[...])
                source_ref[span, :] = source.astype(BF)
            fresh = (1.0 - OMEGA) * values.astype(F32) + weights * (source + near)
            out_span = pl.ds(pl.multiple_of(local * cells + offset, shape.rows), shape.rows)
            out_ref[out_span, :] = fresh.astype(BF)
            if not last:
                tall[offset : offset + shape.rows, :] = fresh
        if not last:
            size = shape.block * cells
            values = out_ref[pl.ds(pl.multiple_of(local * cells, size), size), :]
            emit_faces(shape, at, values, tall, face_refs, z_ref, ends_m, rsum)


def sweep(shape, field, load, coef, halos, recv=None, flux_cell=None, last=False):
    with_flux = recv is not None
    lanes, cells = shape.lanes, shape.cells
    operands = [field, load, coef, *halos]
    out_shapes = [jax.ShapeDtypeStruct(field.shape, BF)]
    scratch = [
        pltpu.VMEM(coef.shape, F32),
        pltpu.VMEM((shape.rows, shape.rows + shape.halo_rows()), BF),
        pltpu.VMEM((lanes + 2 * cells, lanes), BF),
    ]
    if not last:
        out_shapes += face_outputs(shape)
        scratch += face_scratch(shape)
    if with_flux:
        slots = flux_cell.shape[3]
        gzs = lax.axis_size("gz")
        operands += [recv, flux_cell]
        out_shapes += [
            jax.ShapeDtypeStruct(field.shape, BF),
            jax.ShapeDtypeStruct((shape.sides // gzs, slots * gzs), F32),
        ]
        scratch += [pltpu.VMEM((shape.sides, 2 * slots), F32), pltpu.VMEM((lanes, 2 * slots), BF)]
    steps = max(1, shape.sides // (2 * shape.block)) if last else 1
    out_specs = [WHOLE] * len(out_shapes)
    if last:
        out_specs = [pl.BlockSpec((field.shape[0] // steps, lanes), lambda i: (i, 0))]
    return pl.pallas_call(
        functools.partial(sweep_kernel, shape, with_flux, last),
        grid=(steps,),
        in_specs=[WHOLE] * len(operands),
        out_specs=out_specs,
        out_shape=out_shapes,
        scratch_shapes=scratch,
        compiler_params=params(),
        cost_estimate=pl.CostEstimate(
            flops=6 * field.size * 128, bytes_accessed=8 * field.size, transcendentals=0
        ),
    )(*operands)


def exchange(shape, faces):
    *cut, ends = faces
    halos = {}
    for face, value in sorted(zip(shape.faces, cut), key=lambda item: item[0][0]):
        pairs = swaps(lax.axis_size(face[0]))[face[1]]
        halos[face] = lax.ppermute(value, face[0], pairs)
    tips = [lax.ppermute(ends, "gz", pairs) for pairs in swaps(lax.axis_size("gz"))]
    return [halos[face] for face in shape.faces] + tips


def xor_gather(value, axis, hidden):
    peers = lax.axis_size(axis)
    held = {0: value}
    bit = peers // 2
    while bit:
        swap = [(i, i ^ bit) for i in range(peers)]
        fresh = {key ^ bit: lax.ppermute(held[key], axis, swap) for key in sorted(held, reverse=True)}
        held.update(fresh)
        if bit == peers // 2:
            held[bit], hidden = lax.optimization_barrier((held[bit], hidden))
        bit //= 2
    return [held[key] for key in range(peers)], hidden


def per_device(volume_field, volume_load, coefficient, surface_block, trace_cell, flux_cell):
    sides, first, second, lanes = volume_field.shape
    cells = first * second
    shape = Shape(sides, first, second, lanes)
    field = volume_field.reshape(sides * cells, lanes)
    load = volume_load.reshape(sides * cells, lanes)
    coef = coefficient.reshape(cells, lanes)

    trace = traces(volume_field.reshape(sides, cells, lanes), trace_cell, min(32, sides))
    parts, faces = xor_gather(trace, "row", first_faces(shape, field))
    halos = exchange(shape, faces)
    sent = surface(parts, surface_block, F32)
    recv = lax.all_to_all(sent, ("col", "gz"), split_axis=0, concat_axis=0, tiled=True)

    current, *faces, source, surface_flux = sweep(
        shape, field, load, coef, halos, recv=recv, flux_cell=flux_cell
    )
    current, *faces = sweep(shape, current, source, coef, exchange(shape, faces))
    (current,) = sweep(shape, current, source, coef, exchange(shape, faces), last=True)
    return current.reshape(volume_field.shape), surface_flux


def solution(mesh):
    in_specs = (
        P(None, "row", "col", "gz"),
        P(None, "row", "col", "gz"),
        P("row", "col", "gz"),
        P("row", "col"),
        P("row", "col", "gz", None),
        P("row", "col", "gz", None),
    )
    out_specs = (P(None, "row", "col", "gz"), P("gz", ("row", "col")))
    return jax.shard_map(
        per_device, mesh=mesh, in_specs=in_specs, out_specs=out_specs, check_vma=False
    )
```

```python
import functools

import jax
import jax.numpy as jnp
from jax import lax
from jax.experimental import pallas as pl
from jax.experimental.pallas import tpu as pltpu
from jax.sharding import PartitionSpec as P

OMEGA = 0.8
BF = jnp.bfloat16
F32 = jnp.float32
WHOLE = pl.BlockSpec(memory_space=pltpu.VMEM)


def iota(shape, dim):
    return lax.broadcasted_iota(jnp.int32, shape, dim)


def dot(a, b):
    return jnp.dot(a, b, preferred_element_type=F32)


def dot_nt(a, b):
    return lax.dot_general(a, b, (((1,), (1,)), ((), ())), preferred_element_type=F32)


FACES_MIB = 50


def params(mebibytes=24):
    return pltpu.CompilerParams(vmem_limit_bytes=mebibytes * 1024 * 1024)


def trace_kernel(stride, block, field_ref, cell_ref, out_ref, field, cell_v, perm, pick, rsum, sems):
    sides, rows, lanes = field.shape
    slots = cell_ref.shape[3]
    per_row = lanes // stride
    group = 16
    width = group * per_row
    cell_copy = pltpu.make_async_copy(cell_ref, cell_v, sems.at[sides // block])
    cell_copy.start()
    copies = []
    for step in range(sides // block):
        span = pl.ds(step * block, block)
        copies.append(pltpu.make_async_copy(field_ref.at[span], field.at[span], sems.at[step]))
        copies[-1].start()

    shape = (block, block * group)
    rsum[...] = (iota(shape, 1) // group == iota(shape, 0)).astype(BF)
    cell_copy.wait()
    cell = cell_v[0, 0]
    perm[...] = (iota((slots, slots), 0) == cell // stride).astype(BF)
    offset = jnp.broadcast_to((cell % stride).astype(BF), (16, slots))
    sorted_offset = dot_nt(offset, perm[...])[0:1].astype(jnp.int32)
    place = (iota((1, slots), 1) % per_row) * stride + sorted_offset
    pick[...] = (iota((lanes, slots), 0) == place).astype(BF)

    shape = (block * group, width)
    own = iota(shape, 0) % group == iota(shape, 1) // per_row
    picked = []
    for step in range(sides // block):
        copies[step].wait()
        parts = []
        for part in range(rows // group):
            values = field[step * block : (step + 1) * block, part * group : (part + 1) * group, :]
            cols = slice(part * width, (part + 1) * width)
            spread = dot(values.reshape(block * group, lanes), pick[:, cols])
            spread = jnp.where(own, spread, 0.0).astype(BF)
            parts.append(dot(rsum[...], spread).astype(BF))
        picked.append(jnp.concatenate(parts, axis=1))
    out_ref[...] = dot(jnp.concatenate(picked, axis=0), perm[...]).T.astype(BF)


def traces(field, trace_cell, block):
    sides, rows, lanes = field.shape
    slots = trace_cell.shape[3]
    stride = rows * lanes // slots
    hbm = pl.BlockSpec(memory_space=pltpu.HBM)
    return pl.pallas_call(
        functools.partial(trace_kernel, stride, block),
        in_specs=[hbm, hbm],
        out_specs=WHOLE,
        out_shape=jax.ShapeDtypeStruct((slots, sides), BF),
        scratch_shapes=[
            pltpu.VMEM(field.shape, BF),
            pltpu.VMEM(trace_cell.shape, jnp.int32),
            pltpu.VMEM((slots, slots), BF),
            pltpu.VMEM((lanes, slots), BF),
            pltpu.VMEM((block, block * 16), BF),
            pltpu.SemaphoreType.DMA((sides // block + 1,)),
        ],
        compiler_params=params(62),
        cost_estimate=pl.CostEstimate(
            flops=4 * sides * rows * lanes * 128, bytes_accessed=field.size * 2, transcendentals=0
        ),
    )(field, trace_cell)


def fetch_columns(block_ref, held, sems, slots):
    me, group, gzs = lax.axis_index("row"), lax.axis_index("gz"), lax.axis_size("gz")
    copies = []
    for key in range(held.shape[0]):
        start = pl.multiple_of((jnp.bitwise_xor(me, key) * gzs + group) * slots, slots)
        copies.append(
            pltpu.make_async_copy(block_ref.at[:, pl.ds(start, slots)], held.at[key], sems.at[key])
        )
        copies[-1].start()
    return copies


def surface_kernel(gzs, cols, *refs):
    *parts, held, out_ref = refs
    sides = parts[0].shape[1]
    total = None
    for key, part in enumerate(parts):
        term = dot(held[key], part[...])
        total = term if total is None else total + term
    turned = total.T
    lines = total.shape[0]
    if out_ref.shape[2] != sides or lines // cols != sides:
        out_ref[...] = jnp.zeros_like(out_ref)
    s_count, l_count, f_count = sides // gzs, lines // cols, lines // (cols * gzs)
    for c in range(cols):
        for g in range(gzs):
            dest = c * gzs + g
            out_ref[dest, :s_count, :l_count] = turned[
                g * s_count : (g + 1) * s_count, c * l_count : (c + 1) * l_count
            ].astype(out_ref.dtype)
            out_ref[dest, s_count : s_count + f_count, :sides] = total[
                dest * f_count : (dest + 1) * f_count
            ].astype(out_ref.dtype)


def surface(parts, held, dtype):
    gzs, cols = lax.axis_size("gz"), lax.axis_size("col")
    sides = parts[0].shape[1]
    lines = held.shape[1]
    depth = sides // gzs + lines // (cols * gzs)
    shape = (cols * gzs, depth, max(sides, lines // cols))
    return pl.pallas_call(
        functools.partial(surface_kernel, gzs, cols),
        in_specs=[WHOLE] * (len(parts) + 1),
        out_specs=WHOLE,
        out_shape=jax.ShapeDtypeStruct(shape, dtype),
        compiler_params=params(),
        cost_estimate=pl.CostEstimate(
            flops=2 * sides * held.size, bytes_accessed=2 * held.size, transcendentals=0
        ),
    )(*parts, held)


def swaps(peers):
    turns = [[(i, i + 1) for i in range(first, peers - 1, 2)] for first in (0, 1)]
    if turns[1] and peers % 2 == 0:
        turns[1].append((peers - 1, 0))
    return [[(i, j) for i, j in part] + [(j, i) for i, j in part] for part in turns if part]


def has_neighbour(axis, turn):
    index = lax.axis_index(axis)
    other = jnp.where(index % 2 == turn, index + 1, index - 1)
    return (other >= 0) & (other < lax.axis_size(axis))


class Shape:
    def __init__(self, sides, first, second, lanes):
        self.sides, self.x, self.y, self.lanes = sides, first, second, lanes
        self.cells = first * second
        self.chunk = max(1, 128 // self.cells)
        self.rows = self.chunk * self.cells
        self.block = min(sides, 16)
        self.half = self.block // 2
        self.half_rows = self.half * self.cells
        self.faces = [("row", i) for i in range(len(swaps(lax.axis_size("row"))))]
        self.faces += [("col", i) for i in range(len(swaps(lax.axis_size("col"))))]
        self.ends = len(swaps(lax.axis_size("gz")))

    def face_len(self, face):
        return self.y if face[0] == "row" else self.x

    def halo_rows(self):
        return sum(self.chunk * self.face_len(face) for face in self.faces)

    def edge(self, face):
        axis, turn = face
        last = (self.x if axis == "row" else self.y) - 1
        return jnp.where(lax.axis_index(axis) % 2 == turn, last, 0)


def halo_place(shape):
    dims = (shape.rows, shape.halo_rows())
    row, col = iota(dims, 0), iota(dims, 1)
    side, cell = row // shape.cells, row % shape.cells
    x, y = cell // shape.y, cell % shape.y
    hit, base = None, 0
    for face in shape.faces:
        length = shape.face_len(face)
        along, across = (y, x) if face[0] == "row" else (x, y)
        place = (across == shape.edge(face)) & (col - base == side * length + along)
        place = place & has_neighbour(*face)
        hit = place if hit is None else hit | place
        base += shape.chunk * length
    return hit.astype(BF)


def z_mask(shape, count):
    dims = (count * shape.cells, 2 * shape.cells)
    return iota(dims, 1) % shape.cells == iota(dims, 0) % shape.cells


def twice(matrix):
    zero = jnp.zeros_like(matrix)
    return jnp.concatenate(
        [jnp.concatenate([matrix, zero], axis=1), jnp.concatenate([zero, matrix], axis=1)], axis=0
    )


def beside(values):
    half = values.shape[0] // 2
    return jnp.concatenate([values[:half], values[half:]], axis=1)


def build_out(shape, ends_m, rsum):
    dims = (shape.lanes, 2 * shape.cells)
    edge = jnp.where(iota(dims, 1) < shape.cells, 0, shape.lanes - 1)
    ends_m[...] = twice((iota(dims, 0) == edge).astype(F32)).astype(BF)
    dims = rsum.shape
    rsum[...] = (iota(dims, 1) // shape.cells == iota(dims, 0)).astype(BF)


def emit_faces(shape, at, values, tall, face_refs, z_ref, ends_m, rsum):
    for face, ref in zip(shape.faces, face_refs):
        length, edge = shape.face_len(face), shape.edge(face)
        lines = []
        for side in range(shape.block):
            start = side * shape.cells
            if face[0] == "row":
                lines.append(tall[pl.ds(pl.multiple_of(start + edge * length, 8), length), :])
            else:
                lines.append(tall[pl.ds(start + edge, length, stride=shape.y), :])
        span = shape.block * length
        ref[pl.ds(pl.multiple_of(at * length, span), span), :] = jnp.concatenate(
            lines, axis=0
        ).astype(BF)
    mask = jnp.concatenate([z_mask(shape, shape.half)] * 2, axis=1)
    tips = jnp.where(mask, dot(beside(values), ends_m[...]), 0.0).astype(BF)
    tips = dot(rsum[...], tips)[: shape.half]
    tips = jnp.concatenate([tips[:, : 2 * shape.cells], tips[:, 2 * shape.cells :]], axis=0)
    z_ref[pl.ds(pl.multiple_of(at, shape.block), shape.block), :] = tips.astype(BF)


def faces_kernel(shape, slots, field_ref, block_ref, *refs):
    *face_refs, z_ref, held, tall, ends_m, rsum, sems = refs
    copies = fetch_columns(block_ref, held, sems, slots)
    build_out(shape, ends_m, rsum)

    @pl.loop(0, shape.sides // shape.block)
    def _(step):
        size = shape.block * shape.cells
        values = field_ref[pl.ds(pl.multiple_of(step * size, size), size), :]
        tall[...] = values.astype(F32)
        emit_faces(shape, step * shape.block, values, tall, face_refs, z_ref, ends_m, rsum)

    for copy in copies:
        copy.wait()


def face_outputs(shape):
    shapes = [
        jax.ShapeDtypeStruct((shape.sides * shape.face_len(face), shape.lanes), BF)
        for face in shape.faces
    ]
    return shapes + [jax.ShapeDtypeStruct((shape.sides, 2 * shape.cells), BF)]


def face_scratch(shape):
    return [
        pltpu.VMEM((shape.block * shape.cells, shape.lanes), F32),
        pltpu.VMEM((2 * shape.lanes, 4 * shape.cells), BF),
        pltpu.VMEM((max(8, shape.half), shape.half_rows), BF),
    ]


def first_faces(shape, field, block, slots):
    peers = lax.axis_size("row")
    shapes = face_outputs(shape)
    shapes.append(jax.ShapeDtypeStruct((peers, block.shape[0], slots), BF))
    return pl.pallas_call(
        functools.partial(faces_kernel, shape, slots),
        in_specs=[WHOLE, pl.BlockSpec(memory_space=pltpu.HBM)],
        out_specs=[WHOLE] * len(shapes),
        out_shape=shapes,
        scratch_shapes=face_scratch(shape) + [pltpu.SemaphoreType.DMA((peers,))],
        compiler_params=params(FACES_MIB),
        cost_estimate=pl.CostEstimate(
            flops=field.size * 128, bytes_accessed=4 * field.size, transcendentals=0
        ),
    )(field, block)


def sweep_kernel(shape, with_flux, last, *refs):
    refs = list(refs)
    take = lambda count: [refs.pop(0) for _ in range(count)]
    field_ref, load_ref, coef_ref = take(3)
    halo_refs = take(len(shape.faces))
    end_refs = take(shape.ends)
    if with_flux:
        recv_ref, cell_ref = take(2)
    (out_ref,) = take(1)
    if not last:
        face_refs = take(len(shape.faces))
        (z_ref,) = take(1)
    if with_flux:
        source_ref, flux_ref = take(2)
    weight, near_m, line_m, lines = take(4)
    if not last:
        tall, ends_m, rsum = take(3)
    if with_flux:
        phi, cell_m, placed = take(3)

    grid_step = pl.program_id(0)
    cells, lanes = shape.cells, shape.lanes

    @pl.when(grid_step == 0)
    def _():
        weight[...] = OMEGA / (6.0 + coef_ref[...])
        dims = (shape.rows, shape.rows)
        row, col = iota(dims, 0), iota(dims, 1)
        x, y = row % cells // shape.y, row % shape.y
        x2, y2 = col % cells // shape.y, col % shape.y
        near = ((x == x2) & (jnp.abs(y - y2) == 1)) | ((y == y2) & (jnp.abs(x - x2) == 1))
        near_m[:, : shape.rows] = (near & (row // cells == col // cells)).astype(BF)
        near_m[:, shape.rows :] = halo_place(shape)
        dims = (lanes, lanes)
        line = (jnp.abs(iota(dims, 0) - iota(dims, 1)) == 1).astype(F32)
        line_m[: 2 * lanes, :] = twice(line).astype(BF)
        dims = (2 * cells, lanes)
        edge = jnp.where(iota(dims, 0) < cells, lanes - 1, 0)
        line_m[2 * lanes :, :] = twice((iota(dims, 1) == edge).astype(F32)).astype(BF)
        if not last:
            build_out(shape, ends_m, rsum)
        if with_flux:
            total = recv_ref[0].astype(F32)
            for peer in range(1, recv_ref.shape[0]):
                total = total + recv_ref[peer].astype(F32)
            s_count, l_count = flux_ref.shape
            slots = cell_ref.shape[3]
            flux_ref[...] = total[:s_count, :l_count]
            owned = total[s_count : s_count + slots, : shape.sides]
            high = owned.astype(BF).astype(F32)
            both = jnp.concatenate([high, owned - high], axis=0)
            phi[...] = both.T
            cell = jnp.concatenate([cell_ref[0, 0]] * 2, axis=1)
            cell_m[...] = twice((iota((lanes, 2 * slots), 0) == cell % lanes).astype(F32)).astype(BF)

    mask = z_mask(shape, 1)
    even = lax.axis_index("gz") % 2 == 0
    filled = (iota((shape.block, 2 * cells), 1) < cells) == even
    if with_flux:
        slots = cell_ref.shape[3]
        cell = jnp.concatenate([cell_ref[0, 0]] * 2, axis=1)
        cell_mask = iota((cells, 2 * slots), 0) == cell // lanes
    weights = jnp.concatenate([weight[...]] * shape.chunk, axis=0)
    out_sides = out_ref.shape[0] // cells

    def expand(lines, where, first):
        rows = []
        for side in range(first, first + shape.half):
            line = jnp.broadcast_to(lines[side : side + 1], where.shape)
            rows.append(jnp.where(where, line, 0.0))
        return jnp.concatenate(rows, axis=0).astype(BF)

    @pl.loop(0, out_sides // shape.block)
    def _(step):
        local = step * shape.block
        at = grid_step * out_sides + local
        sides = pl.ds(pl.multiple_of(at, shape.block), shape.block)
        size = shape.block * cells
        zs = 0.0
        for turn in range(shape.ends):
            wanted = (filled == (turn == 0)) & has_neighbour("gz", turn)
            zs = jnp.where(wanted, end_refs[turn][sides, :].astype(F32), zs)
        values = field_ref[pl.ds(pl.multiple_of(at * cells, size), size), :]
        left = [beside(values), expand(zs, mask, 0), expand(zs, mask, shape.half)]
        lines[...] = dot(jnp.concatenate(left, axis=1), line_m[...])
        if with_flux:
            phis = phi[sides, :]
            left = [expand(phis, cell_mask, 0), expand(phis, cell_mask, shape.half)]
            placed[...] = dot_nt(jnp.concatenate(left, axis=1), cell_m[...])
        for index in range(shape.half // shape.chunk):
            offset = index * shape.rows
            starts = (offset, offset + shape.half_rows)
            stacks = []
            for start in starts:
                rows = pl.ds(pl.multiple_of(at * cells + start, shape.rows), shape.rows)
                stack = [field_ref[rows, :]]
                for face, ref in zip(shape.faces, halo_refs):
                    length = shape.face_len(face)
                    count = shape.chunk * length
                    first = pl.multiple_of(at * length + start // cells * length, count)
                    stack.append(ref[pl.ds(first, count), :])
                stacks.append(jnp.concatenate(stack, axis=0))
            near = dot(near_m[...], jnp.concatenate(stacks, axis=1))
            near = near + lines[offset : offset + shape.rows, :]
            for part, start in enumerate(starts):
                cols = slice(part * lanes, (part + 1) * lanes)
                rows = pl.ds(pl.multiple_of(at * cells + start, shape.rows), shape.rows)
                source = load_ref[rows, :].astype(F32)
                if with_flux:
                    source = source + placed[offset : offset + shape.rows, cols]
                    source_ref[rows, :] = source.astype(BF)
                centre = field_ref[rows, :].astype(F32)
                fresh = (1.0 - OMEGA) * centre + weights * (source + near[:, cols])
                to = pl.ds(pl.multiple_of(local * cells + start, shape.rows), shape.rows)
                out_ref[to, :] = fresh.astype(BF)
                if not last:
                    tall[start : start + shape.rows, :] = fresh
        if not last:
            fresh = out_ref[pl.ds(pl.multiple_of(local * cells, size), size), :]
            emit_faces(shape, at, fresh, tall, face_refs, z_ref, ends_m, rsum)


def sweep(shape, field, load, coef, halos, recv=None, flux_cell=None, last=False):
    with_flux = recv is not None
    lanes, cells = shape.lanes, shape.cells
    operands = [field, load, coef, *halos]
    out_shapes = [jax.ShapeDtypeStruct(field.shape, BF)]
    scratch = [
        pltpu.VMEM(coef.shape, F32),
        pltpu.VMEM((shape.rows, shape.rows + shape.halo_rows()), BF),
        pltpu.VMEM((2 * lanes + 4 * cells, 2 * lanes), BF),
        pltpu.VMEM((shape.half_rows, 2 * lanes), F32),
    ]
    if not last:
        out_shapes += face_outputs(shape)
        scratch += face_scratch(shape)
    if with_flux:
        slots = flux_cell.shape[3]
        gzs = lax.axis_size("gz")
        operands += [recv, flux_cell]
        out_shapes += [
            jax.ShapeDtypeStruct(field.shape, BF),
            jax.ShapeDtypeStruct((shape.sides // gzs, slots * gzs), F32),
        ]
        scratch += [
            pltpu.VMEM((shape.sides, 2 * slots), F32),
            pltpu.VMEM((2 * lanes, 4 * slots), BF),
            pltpu.VMEM((shape.half_rows, 2 * lanes), F32),
        ]
    steps = max(1, shape.sides // (2 * shape.block)) if last else 1
    out_specs = [WHOLE] * len(out_shapes)
    if last:
        out_specs = [pl.BlockSpec((field.shape[0] // steps, lanes), lambda i: (i, 0))]
    return pl.pallas_call(
        functools.partial(sweep_kernel, shape, with_flux, last),
        grid=(steps,),
        in_specs=[WHOLE] * len(operands),
        out_specs=out_specs,
        out_shape=out_shapes,
        scratch_shapes=scratch,
        compiler_params=params(),
        cost_estimate=pl.CostEstimate(
            flops=6 * field.size * 128, bytes_accessed=8 * field.size, transcendentals=0
        ),
    )(*operands)


def exchange(shape, faces):
    *cut, ends = faces
    halos = {}
    for face, value in sorted(zip(shape.faces, cut), key=lambda item: item[0][0]):
        pairs = swaps(lax.axis_size(face[0]))[face[1]]
        halos[face] = lax.ppermute(value, face[0], pairs)
    tips = [lax.ppermute(ends, "gz", pairs) for pairs in swaps(lax.axis_size("gz"))]
    return [halos[face] for face in shape.faces] + tips


def xor_gather(value, axis, hidden):
    peers = lax.axis_size(axis)
    held = {0: value}
    bit = peers // 2
    while bit:
        swap = [(i, i ^ bit) for i in range(peers)]
        fresh = {key ^ bit: lax.ppermute(held[key], axis, swap) for key in sorted(held, reverse=True)}
        held.update(fresh)
        if bit == peers // 2:
            held[bit], hidden = lax.optimization_barrier((held[bit], hidden))
        bit //= 2
    return [held[key] for key in range(peers)], hidden


def per_device(volume_field, volume_load, coefficient, surface_block, trace_cell, flux_cell):
    sides, first, second, lanes = volume_field.shape
    cells = first * second
    shape = Shape(sides, first, second, lanes)
    field = volume_field.reshape(sides * cells, lanes)
    load = volume_load.reshape(sides * cells, lanes)
    coef = coefficient.reshape(cells, lanes)

    slots = trace_cell.shape[3]
    trace = traces(volume_field.reshape(sides, cells, lanes), trace_cell, min(32, sides))
    *faces, held = first_faces(shape, field, surface_block, slots)
    parts, _ = xor_gather(trace, "row", faces)
    halos = exchange(shape, faces)
    parts, halos = lax.optimization_barrier((parts, halos))
    sent = surface(parts, held, F32)
    recv = lax.all_to_all(sent, ("col", "gz"), split_axis=0, concat_axis=0, tiled=True)

    current, *faces, source, surface_flux = sweep(
        shape, field, load, coef, halos, recv=recv, flux_cell=flux_cell
    )
    current, *faces = sweep(shape, current, source, coef, exchange(shape, faces))
    (current,) = sweep(shape, current, source, coef, exchange(shape, faces), last=True)
    return current.reshape(volume_field.shape), surface_flux


def solution(mesh):
    in_specs = (
        P(None, "row", "col", "gz"),
        P(None, "row", "col", "gz"),
        P("row", "col", "gz"),
        P("row", "col"),
        P("row", "col", "gz", None),
        P("row", "col", "gz", None),
    )
    out_specs = (P(None, "row", "col", "gz"), P("gz", ("row", "col")))
    return jax.shard_map(
        per_device, mesh=mesh, in_specs=in_specs, out_specs=out_specs, check_vma=False
    )
```

```python
import functools

import jax
import jax.numpy as jnp
from jax import lax
from jax.experimental import pallas as pl
from jax.experimental.pallas import tpu as pltpu
from jax.sharding import PartitionSpec as P

OMEGA = 0.8
BF = jnp.bfloat16
F32 = jnp.float32
WHOLE = pl.BlockSpec(memory_space=pltpu.VMEM)


def iota(shape, dim):
    return lax.broadcasted_iota(jnp.int32, shape, dim)


def dot(a, b):
    return jnp.dot(a, b, preferred_element_type=F32)


def dot_nt(a, b):
    return lax.dot_general(a, b, (((1,), (1,)), ((), ())), preferred_element_type=F32)


FACES_MIB = 50


def params(mebibytes=24):
    return pltpu.CompilerParams(vmem_limit_bytes=mebibytes * 1024 * 1024)


def trace_kernel(stride, block, field_ref, cell_ref, out_ref, field, cell_v, near, pick, rsum, sems):
    sides, rows, lanes = field.shape
    slots = cell_ref.shape[3]
    per_row = lanes // stride
    group = 16
    width = group * per_row
    parts = rows // group
    cell_copy = pltpu.make_async_copy(cell_ref, cell_v, sems.at[sides // block])
    cell_copy.start()
    copies = []
    for step in range(sides // block):
        span = pl.ds(step * block, block)
        copies.append(pltpu.make_async_copy(field_ref.at[span], field.at[span], sems.at[step]))
        copies[-1].start()

    shape = (block, block * group)
    rsum[...] = (iota(shape, 1) // group == iota(shape, 0)).astype(BF)
    cell_copy.wait()
    cell = cell_v[0, 0]
    run = cell // stride
    digit = jnp.zeros_like(cell)
    for part in range(parts):
        digit = jnp.where(run // width == part, (cell % stride) * stride**part, digit)
    hit = iota((width, slots), 0) == run % width
    near[...] = hit.astype(BF)
    digits = jnp.sum(jnp.where(hit, digit.astype(F32), 0.0), axis=1, keepdims=True)
    digits = digits.astype(jnp.int32)
    for part in range(parts):
        offset = digits // stride**part % stride
        place = iota((width, lanes), 0) % per_row * stride + offset
        pick[part] = (iota((width, lanes), 1) == place).astype(BF)

    shape = (block * group, width)
    own = iota(shape, 0) % group == iota(shape, 1) // per_row
    picked = [[] for _ in range(parts)]
    for step in range(sides // block):
        copies[step].wait()
        for part in range(parts):
            values = field[step * block : (step + 1) * block, part * group : (part + 1) * group, :]
            spread = dot_nt(values.reshape(block * group, lanes), pick[part])
            spread = jnp.where(own, spread, 0.0).astype(BF)
            picked[part].append(dot(rsum[...], spread).astype(BF))
    total = jnp.zeros((sides, slots), F32)
    for part in range(parts):
        placed = dot(jnp.concatenate(picked[part], axis=0), near[...])
        total = jnp.where(run // width == part, placed, total)
    out_ref[...] = total.T.astype(BF)


def traces(field, trace_cell, block):
    sides, rows, lanes = field.shape
    slots = trace_cell.shape[3]
    stride = rows * lanes // slots
    width = 16 * lanes // stride
    hbm = pl.BlockSpec(memory_space=pltpu.HBM)
    return pl.pallas_call(
        functools.partial(trace_kernel, stride, block),
        in_specs=[hbm, hbm],
        out_specs=WHOLE,
        out_shape=jax.ShapeDtypeStruct((slots, sides), BF),
        scratch_shapes=[
            pltpu.VMEM(field.shape, BF),
            pltpu.VMEM(trace_cell.shape, jnp.int32),
            pltpu.VMEM((width, slots), BF),
            pltpu.VMEM((slots // width, width, lanes), BF),
            pltpu.VMEM((block, block * 16), BF),
            pltpu.SemaphoreType.DMA((sides // block + 1,)),
        ],
        compiler_params=params(62),
        cost_estimate=pl.CostEstimate(
            flops=4 * sides * rows * lanes * 128, bytes_accessed=field.size * 2, transcendentals=0
        ),
    )(field, trace_cell)


def fetch_columns(block_ref, held, sems, slots):
    me, group, gzs = lax.axis_index("row"), lax.axis_index("gz"), lax.axis_size("gz")
    copies = []
    for key in range(held.shape[0]):
        start = pl.multiple_of((jnp.bitwise_xor(me, key) * gzs + group) * slots, slots)
        copies.append(
            pltpu.make_async_copy(block_ref.at[:, pl.ds(start, slots)], held.at[key], sems.at[key])
        )
        copies[-1].start()
    return copies


def surface_kernel(gzs, cols, *refs):
    *parts, held, out_ref = refs
    sides = parts[0].shape[1]
    total = None
    for key, part in enumerate(parts):
        term = dot(held[key], part[...])
        total = term if total is None else total + term
    turned = total.T
    lines = total.shape[0]
    if out_ref.shape[2] != sides or lines // cols != sides:
        out_ref[...] = jnp.zeros_like(out_ref)
    s_count, l_count, f_count = sides // gzs, lines // cols, lines // (cols * gzs)
    for c in range(cols):
        for g in range(gzs):
            dest = c * gzs + g
            out_ref[dest, :s_count, :l_count] = turned[
                g * s_count : (g + 1) * s_count, c * l_count : (c + 1) * l_count
            ].astype(out_ref.dtype)
            out_ref[dest, s_count : s_count + f_count, :sides] = total[
                dest * f_count : (dest + 1) * f_count
            ].astype(out_ref.dtype)


def surface(parts, held, dtype):
    gzs, cols = lax.axis_size("gz"), lax.axis_size("col")
    sides = parts[0].shape[1]
    lines = held.shape[1]
    depth = sides // gzs + lines // (cols * gzs)
    shape = (cols * gzs, depth, max(sides, lines // cols))
    return pl.pallas_call(
        functools.partial(surface_kernel, gzs, cols),
        in_specs=[WHOLE] * (len(parts) + 1),
        out_specs=WHOLE,
        out_shape=jax.ShapeDtypeStruct(shape, dtype),
        compiler_params=params(),
        cost_estimate=pl.CostEstimate(
            flops=2 * sides * held.size, bytes_accessed=2 * held.size, transcendentals=0
        ),
    )(*parts, held)


def swaps(peers):
    turns = []
    for turn in (0, 1):
        partner = {i: i + 1 if i % 2 == turn else i - 1 for i in range(peers)}
        pairs = [(i, j if 0 <= j < peers else i) for i, j in partner.items()]
        if any(i != j for i, j in pairs):
            turns.append(pairs)
    return turns


def has_neighbour(axis, turn):
    index = lax.axis_index(axis)
    other = jnp.where(index % 2 == turn, index + 1, index - 1)
    return (other >= 0) & (other < lax.axis_size(axis))


class Shape:
    def __init__(self, sides, first, second, lanes):
        self.sides, self.x, self.y, self.lanes = sides, first, second, lanes
        self.cells = first * second
        self.chunk = max(1, 128 // self.cells)
        self.rows = self.chunk * self.cells
        self.block = min(sides, 32)
        self.half = self.block // 2
        self.half_rows = self.half * self.cells
        self.faces = [("row", i) for i in range(len(swaps(lax.axis_size("row"))))]
        self.faces += [("col", i) for i in range(len(swaps(lax.axis_size("col"))))]
        self.ends = len(swaps(lax.axis_size("gz")))

    def face_len(self, face):
        return self.y if face[0] == "row" else self.x

    def halo_rows(self):
        return sum(self.chunk * self.face_len(face) for face in self.faces)

    def edge(self, face):
        axis, turn = face
        last = (self.x if axis == "row" else self.y) - 1
        return jnp.where(lax.axis_index(axis) % 2 == turn, last, 0)


def halo_place(shape):
    dims = (shape.rows, shape.halo_rows())
    row, col = iota(dims, 0), iota(dims, 1)
    side, cell = row // shape.cells, row % shape.cells
    x, y = cell // shape.y, cell % shape.y
    hit, base = None, 0
    for face in shape.faces:
        length = shape.face_len(face)
        along, across = (y, x) if face[0] == "row" else (x, y)
        place = (across == shape.edge(face)) & (col - base == side * length + along)
        place = place & has_neighbour(*face)
        hit = place if hit is None else hit | place
        base += shape.chunk * length
    return hit.astype(BF)


def z_mask(shape, count):
    dims = (count * shape.cells, 2 * shape.cells)
    return iota(dims, 1) % shape.cells == iota(dims, 0) % shape.cells


def twice(matrix):
    zero = jnp.zeros_like(matrix)
    return jnp.concatenate(
        [jnp.concatenate([matrix, zero], axis=1), jnp.concatenate([zero, matrix], axis=1)], axis=0
    )


def beside(values):
    half = values.shape[0] // 2
    return jnp.concatenate([values[:half], values[half:]], axis=1)


def build_out(shape, ends_m, rsum):
    dims = (shape.lanes, 2 * shape.cells)
    edge = jnp.where(iota(dims, 1) < shape.cells, 0, shape.lanes - 1)
    ends_m[...] = twice((iota(dims, 0) == edge).astype(F32)).astype(BF)
    dims = rsum.shape
    rsum[...] = (iota(dims, 1) // shape.cells == iota(dims, 0)).astype(BF)


def emit_faces(shape, at, values, tall, face_refs, z_ref, ends_m, rsum):
    for face, ref in zip(shape.faces, face_refs):
        length, edge = shape.face_len(face), shape.edge(face)
        lines = []
        for side in range(shape.block):
            start = side * shape.cells
            if face[0] == "row":
                lines.append(tall[pl.ds(pl.multiple_of(start + edge * length, 8), length), :])
            else:
                lines.append(tall[pl.ds(start + edge, length, stride=shape.y), :])
        span = shape.block * length
        ref[pl.ds(pl.multiple_of(at * length, span), span), :] = jnp.concatenate(
            lines, axis=0
        ).astype(BF)
    mask = jnp.concatenate([z_mask(shape, shape.half)] * 2, axis=1)
    tips = jnp.where(mask, dot(beside(values), ends_m[...]), 0.0).astype(BF)
    tips = dot(rsum[...], tips)[: shape.half]
    tips = jnp.concatenate([tips[:, : 2 * shape.cells], tips[:, 2 * shape.cells :]], axis=0)
    z_ref[pl.ds(pl.multiple_of(at, shape.block), shape.block), :] = tips.astype(BF)


def faces_kernel(shape, slots, field_ref, block_ref, *refs):
    *face_refs, z_ref, held, tall, ends_m, rsum, sems = refs
    copies = fetch_columns(block_ref, held, sems, slots)
    build_out(shape, ends_m, rsum)

    @pl.loop(0, shape.sides // shape.block)
    def _(step):
        size = shape.block * shape.cells
        values = field_ref[pl.ds(pl.multiple_of(step * size, size), size), :]
        tall[...] = values.astype(F32)
        emit_faces(shape, step * shape.block, values, tall, face_refs, z_ref, ends_m, rsum)

    for copy in copies:
        copy.wait()


def face_outputs(shape):
    shapes = [
        jax.ShapeDtypeStruct((shape.sides * shape.face_len(face), shape.lanes), BF)
        for face in shape.faces
    ]
    return shapes + [jax.ShapeDtypeStruct((shape.sides, 2 * shape.cells), BF)]


def face_scratch(shape):
    return [
        pltpu.VMEM((shape.block * shape.cells, shape.lanes), F32),
        pltpu.VMEM((2 * shape.lanes, 4 * shape.cells), BF),
        pltpu.VMEM((max(8, shape.half), shape.half_rows), BF),
    ]


def first_faces(shape, field, block, slots):
    peers = lax.axis_size("row")
    shapes = face_outputs(shape)
    shapes.append(jax.ShapeDtypeStruct((peers, block.shape[0], slots), BF))
    return pl.pallas_call(
        functools.partial(faces_kernel, shape, slots),
        in_specs=[WHOLE, pl.BlockSpec(memory_space=pltpu.HBM)],
        out_specs=[WHOLE] * len(shapes),
        out_shape=shapes,
        scratch_shapes=face_scratch(shape) + [pltpu.SemaphoreType.DMA((peers,))],
        compiler_params=params(FACES_MIB),
        cost_estimate=pl.CostEstimate(
            flops=field.size * 128, bytes_accessed=4 * field.size, transcendentals=0
        ),
    )(field, block)


def sweep_kernel(shape, with_flux, last, *refs):
    refs = list(refs)
    take = lambda count: [refs.pop(0) for _ in range(count)]
    field_ref, load_ref, coef_ref = take(3)
    halo_refs = take(len(shape.faces))
    end_refs = take(shape.ends)
    if with_flux:
        recv_ref, cell_ref = take(2)
    (out_ref,) = take(1)
    if not last:
        face_refs = take(len(shape.faces))
        (z_ref,) = take(1)
    if with_flux:
        source_ref, flux_ref = take(2)
    weight, near_m, line_m, lines = take(4)
    if not last:
        tall, ends_m, rsum = take(3)
    if with_flux:
        phi, cell_m, placed = take(3)

    grid_step = pl.program_id(0)
    cells, lanes = shape.cells, shape.lanes

    @pl.when(grid_step == 0)
    def _():
        weight[...] = OMEGA / (6.0 + coef_ref[...])
        dims = (shape.rows, shape.rows)
        row, col = iota(dims, 0), iota(dims, 1)
        x, y = row % cells // shape.y, row % shape.y
        x2, y2 = col % cells // shape.y, col % shape.y
        near = ((x == x2) & (jnp.abs(y - y2) == 1)) | ((y == y2) & (jnp.abs(x - x2) == 1))
        near_m[:, : shape.rows] = (near & (row // cells == col // cells)).astype(BF)
        near_m[:, shape.rows :] = halo_place(shape)
        dims = (lanes, lanes)
        line = (jnp.abs(iota(dims, 0) - iota(dims, 1)) == 1).astype(F32)
        line_m[: 2 * lanes, :] = twice(line).astype(BF)
        dims = (2 * cells, lanes)
        edge = jnp.where(iota(dims, 0) < cells, lanes - 1, 0)
        line_m[2 * lanes :, :] = twice((iota(dims, 1) == edge).astype(F32)).astype(BF)
        if not last:
            build_out(shape, ends_m, rsum)
        if with_flux:
            total = recv_ref[0].astype(F32)
            for peer in range(1, recv_ref.shape[0]):
                total = total + recv_ref[peer].astype(F32)
            s_count, l_count = flux_ref.shape
            slots = cell_ref.shape[3]
            flux_ref[...] = total[:s_count, :l_count]
            owned = total[s_count : s_count + slots, : shape.sides]
            high = owned.astype(BF).astype(F32)
            both = jnp.concatenate([high, owned - high], axis=0)
            phi[...] = both.T
            cell = jnp.concatenate([cell_ref[0, 0]] * 2, axis=1)
            cell_m[...] = twice((iota((lanes, 2 * slots), 0) == cell % lanes).astype(F32)).astype(BF)

    mask = z_mask(shape, 1)
    even = lax.axis_index("gz") % 2 == 0
    filled = (iota((shape.block, 2 * cells), 1) < cells) == even
    if with_flux:
        slots = cell_ref.shape[3]
        cell = jnp.concatenate([cell_ref[0, 0]] * 2, axis=1)
        cell_mask = iota((cells, 2 * slots), 0) == cell // lanes
    weights = jnp.concatenate([weight[...]] * shape.chunk, axis=0)
    out_sides = out_ref.shape[0] // cells

    def expand(lines, where, first):
        rows = []
        for side in range(first, first + shape.half):
            line = jnp.broadcast_to(lines[side : side + 1], where.shape)
            rows.append(jnp.where(where, line, 0.0))
        return jnp.concatenate(rows, axis=0).astype(BF)

    @pl.loop(0, out_sides // shape.block)
    def _(step):
        local = step * shape.block
        at = grid_step * out_sides + local
        sides = pl.ds(pl.multiple_of(at, shape.block), shape.block)
        size = shape.block * cells
        zs = 0.0
        for turn in range(shape.ends):
            wanted = (filled == (turn == 0)) & has_neighbour("gz", turn)
            zs = jnp.where(wanted, end_refs[turn][sides, :].astype(F32), zs)
        values = field_ref[pl.ds(pl.multiple_of(at * cells, size), size), :]
        left = [beside(values), expand(zs, mask, 0), expand(zs, mask, shape.half)]
        lines[...] = dot(jnp.concatenate(left, axis=1), line_m[...])
        if with_flux:
            phis = phi[sides, :]
            left = [expand(phis, cell_mask, 0), expand(phis, cell_mask, shape.half)]
            placed[...] = dot_nt(jnp.concatenate(left, axis=1), cell_m[...])
        for index in range(shape.half // shape.chunk):
            offset = index * shape.rows
            starts = (offset, offset + shape.half_rows)
            stacks = []
            for start in starts:
                rows = pl.ds(pl.multiple_of(at * cells + start, shape.rows), shape.rows)
                stack = [field_ref[rows, :]]
                for face, ref in zip(shape.faces, halo_refs):
                    length = shape.face_len(face)
                    count = shape.chunk * length
                    first = pl.multiple_of(at * length + start // cells * length, count)
                    stack.append(ref[pl.ds(first, count), :])
                stacks.append(jnp.concatenate(stack, axis=0))
            near = dot(near_m[...], jnp.concatenate(stacks, axis=1))
            near = near + lines[offset : offset + shape.rows, :]
            for part, start in enumerate(starts):
                cols = slice(part * lanes, (part + 1) * lanes)
                rows = pl.ds(pl.multiple_of(at * cells + start, shape.rows), shape.rows)
                source = load_ref[rows, :].astype(F32)
                if with_flux:
                    source = source + placed[offset : offset + shape.rows, cols]
                    source_ref[rows, :] = source.astype(BF)
                centre = field_ref[rows, :].astype(F32)
                fresh = (1.0 - OMEGA) * centre + weights * (source + near[:, cols])
                to = pl.ds(pl.multiple_of(local * cells + start, shape.rows), shape.rows)
                out_ref[to, :] = fresh.astype(BF)
                if not last:
                    tall[start : start + shape.rows, :] = fresh
        if not last:
            fresh = out_ref[pl.ds(pl.multiple_of(local * cells, size), size), :]
            emit_faces(shape, at, fresh, tall, face_refs, z_ref, ends_m, rsum)


def sweep(shape, field, load, coef, halos, recv=None, flux_cell=None, last=False):
    with_flux = recv is not None
    lanes, cells = shape.lanes, shape.cells
    operands = [field, load, coef, *halos]
    out_shapes = [jax.ShapeDtypeStruct(field.shape, BF)]
    scratch = [
        pltpu.VMEM(coef.shape, F32),
        pltpu.VMEM((shape.rows, shape.rows + shape.halo_rows()), BF),
        pltpu.VMEM((2 * lanes + 4 * cells, 2 * lanes), BF),
        pltpu.VMEM((shape.half_rows, 2 * lanes), F32),
    ]
    if not last:
        out_shapes += face_outputs(shape)
        scratch += face_scratch(shape)
    if with_flux:
        slots = flux_cell.shape[3]
        gzs = lax.axis_size("gz")
        operands += [recv, flux_cell]
        out_shapes += [
            jax.ShapeDtypeStruct(field.shape, BF),
            jax.ShapeDtypeStruct((shape.sides // gzs, slots * gzs), F32),
        ]
        scratch += [
            pltpu.VMEM((shape.sides, 2 * slots), F32),
            pltpu.VMEM((2 * lanes, 4 * slots), BF),
            pltpu.VMEM((shape.half_rows, 2 * lanes), F32),
        ]
    steps = max(1, shape.sides // (2 * shape.block)) if last else 1
    out_specs = [WHOLE] * len(out_shapes)
    if last:
        out_specs = [pl.BlockSpec((field.shape[0] // steps, lanes), lambda i: (i, 0))]
    return pl.pallas_call(
        functools.partial(sweep_kernel, shape, with_flux, last),
        grid=(steps,),
        in_specs=[WHOLE] * len(operands),
        out_specs=out_specs,
        out_shape=out_shapes,
        scratch_shapes=scratch,
        compiler_params=params(),
        cost_estimate=pl.CostEstimate(
            flops=6 * field.size * 128, bytes_accessed=8 * field.size, transcendentals=0
        ),
    )(*operands)


def exchange(shape, faces):
    *cut, ends = faces
    halos = {}
    for face, value in sorted(zip(shape.faces, cut), key=lambda item: item[0][0]):
        pairs = swaps(lax.axis_size(face[0]))[face[1]]
        halos[face] = lax.ppermute(value, face[0], pairs)
    tips = [lax.ppermute(ends, "gz", pairs) for pairs in swaps(lax.axis_size("gz"))]
    return [halos[face] for face in shape.faces] + tips


def xor_gather(value, axis, hidden):
    peers = lax.axis_size(axis)
    held = {0: value}
    bit = peers // 2
    while bit:
        swap = [(i, i ^ bit) for i in range(peers)]
        fresh = {key ^ bit: lax.ppermute(held[key], axis, swap) for key in sorted(held, reverse=True)}
        held.update(fresh)
        if bit == peers // 2:
            held[bit], hidden = lax.optimization_barrier((held[bit], hidden))
        bit //= 2
    return [held[key] for key in range(peers)], hidden


def per_device(volume_field, volume_load, coefficient, surface_block, trace_cell, flux_cell):
    sides, first, second, lanes = volume_field.shape
    cells = first * second
    shape = Shape(sides, first, second, lanes)
    field = volume_field.reshape(sides * cells, lanes)
    load = volume_load.reshape(sides * cells, lanes)
    coef = coefficient.reshape(cells, lanes)

    slots = trace_cell.shape[3]
    trace = traces(volume_field.reshape(sides, cells, lanes), trace_cell, min(32, sides))
    *faces, held = first_faces(shape, field, surface_block, slots)
    parts, _ = xor_gather(trace, "row", faces)
    halos = exchange(shape, faces)
    parts, halos = lax.optimization_barrier((parts, halos))
    sent = surface(parts, held, F32)
    recv = lax.all_to_all(sent, ("col", "gz"), split_axis=0, concat_axis=0, tiled=True)

    current, *faces, source, surface_flux = sweep(
        shape, field, load, coef, halos, recv=recv, flux_cell=flux_cell
    )
    current, *faces = sweep(shape, current, source, coef, exchange(shape, faces))
    (current,) = sweep(shape, current, source, coef, exchange(shape, faces), last=True)
    return current.reshape(volume_field.shape), surface_flux


def solution(mesh):
    in_specs = (
        P(None, "row", "col", "gz"),
        P(None, "row", "col", "gz"),
        P("row", "col", "gz"),
        P("row", "col"),
        P("row", "col", "gz", None),
        P("row", "col", "gz", None),
    )
    out_specs = (P(None, "row", "col", "gz"), P("gz", ("row", "col")))
    return jax.shard_map(
        per_device, mesh=mesh, in_specs=in_specs, out_specs=out_specs, check_vma=False
    )
```

```python
import functools

import jax
import jax.numpy as jnp
from jax import lax
from jax.experimental import pallas as pl
from jax.experimental.pallas import tpu as pltpu
from jax.sharding import PartitionSpec as P

OMEGA = 0.8
BF = jnp.bfloat16
F32 = jnp.float32
WHOLE = pl.BlockSpec(memory_space=pltpu.VMEM)


def iota(shape, dim):
    return lax.broadcasted_iota(jnp.int32, shape, dim)


def dot(a, b):
    return jnp.dot(a, b, preferred_element_type=F32)


def dot_nt(a, b):
    return lax.dot_general(a, b, (((1,), (1,)), ((), ())), preferred_element_type=F32)


FACES_MIB = 50


def params(mebibytes=24):
    return pltpu.CompilerParams(vmem_limit_bytes=mebibytes * 1024 * 1024)


def trace_kernel(stride, block, field_ref, cell_ref, out_ref, field, cell_v, tall, near, place, picked, sems):
    sides, rows, lanes = field.shape
    slots = cell_ref.shape[3]
    per_row = lanes // stride
    width = near.shape[0]
    parts = slots // width
    cell_copy = pltpu.make_async_copy(cell_ref, cell_v, sems.at[sides // block])
    cell_copy.start()
    copies = []
    for step in range(sides // block):
        span = pl.ds(step * block, block)
        copies.append(pltpu.make_async_copy(field_ref.at[span], field.at[span], sems.at[step]))
        copies[-1].start()

    cell_copy.wait()
    cell = cell_v[0, 0]
    run = cell // stride
    digit = jnp.zeros_like(cell)
    for part in range(parts):
        digit = jnp.where(run // width == part, (cell % stride) * stride**part, digit)
    hit = iota((width, slots), 0) == run % width
    near[...] = hit.astype(BF)
    digits = jnp.sum(jnp.where(hit, digit.astype(F32), 0.0), axis=1, keepdims=True)
    digits = jnp.broadcast_to(digits, (width, 128)).T[0:8].astype(jnp.int32)
    first = iota((8, width), 1) % per_row * stride
    for part in range(parts):
        place[:, part * width : (part + 1) * width] = first + digits // stride**part % stride

    together = 128 // per_row
    group = iota((8, 128), 1) // per_row
    for step in range(sides // block):
        copies[step].wait()
        span = field[step * block : (step + 1) * block]
        tall[...] = span.reshape(block * rows, lanes).astype(F32)

        @pl.loop(0, block // 8)
        def _(batch):
            for tile in range(rows // together):
                cols = slice(tile * 128, (tile + 1) * 128)
                where = place[:, cols]
                found = None
                for row in range(together):
                    start = batch * 8 * rows + tile * together + row
                    line = tall[pl.ds(start, 8, stride=rows), :]
                    line = jnp.take_along_axis(line, where, axis=1)
                    found = line if found is None else jnp.where(group == row, line, found)
                at = pl.multiple_of(step * block + batch * 8, 8)
                picked[pl.ds(at, 8), cols] = found

    total = jnp.zeros((sides, slots), F32)
    for part in range(parts):
        sorted_runs = picked[:, part * width : (part + 1) * width].astype(BF)
        total = jnp.where(run // width == part, dot(sorted_runs, near[...]), total)
    out_ref[...] = total.T.astype(BF)


def traces(field, trace_cell, block):
    sides, rows, lanes = field.shape
    slots = trace_cell.shape[3]
    stride = rows * lanes // slots
    width = min(slots, 256)
    hbm = pl.BlockSpec(memory_space=pltpu.HBM)
    return pl.pallas_call(
        functools.partial(trace_kernel, stride, block),
        in_specs=[hbm, hbm],
        out_specs=WHOLE,
        out_shape=jax.ShapeDtypeStruct((slots, sides), BF),
        scratch_shapes=[
            pltpu.VMEM(field.shape, BF),
            pltpu.VMEM(trace_cell.shape, jnp.int32),
            pltpu.VMEM((block * rows, lanes), F32),
            pltpu.VMEM((width, slots), BF),
            pltpu.VMEM((8, slots), jnp.int32),
            pltpu.VMEM((sides, slots), F32),
            pltpu.SemaphoreType.DMA((sides // block + 1,)),
        ],
        compiler_params=params(62),
        cost_estimate=pl.CostEstimate(
            flops=4 * sides * rows * lanes * 128, bytes_accessed=field.size * 2, transcendentals=0
        ),
    )(field, trace_cell)


def fetch_columns(block_ref, held, sems, slots):
    me, group, gzs = lax.axis_index("row"), lax.axis_index("gz"), lax.axis_size("gz")
    copies = []
    for key in range(held.shape[0]):
        start = pl.multiple_of((jnp.bitwise_xor(me, key) * gzs + group) * slots, slots)
        copies.append(
            pltpu.make_async_copy(block_ref.at[:, pl.ds(start, slots)], held.at[key], sems.at[key])
        )
        copies[-1].start()
    return copies


def surface_kernel(direct, *refs):
    *ins, total = refs
    outs = ins[len(ins) - direct :]
    *parts, held = ins[: len(ins) - direct]
    value = None
    for key, part in enumerate(parts):
        term = dot(held[key], part[...])
        value = term if value is None else value + term
    if direct == 1:
        outs[0][...] = value
        return
    total[...] = value
    count = outs[0].shape[0]
    me = lax.axis_index("col") * lax.axis_size("gz") + lax.axis_index("gz")
    for key, out in enumerate(outs):
        start = pl.multiple_of(jnp.bitwise_xor(me, key) * count, 8)
        out[...] = total[pl.ds(start, count), :]


def surface(parts, held):
    owners = lax.axis_size("gz") * lax.axis_size("col")
    sides = parts[0].shape[1]
    lines = held.shape[1]
    few = owners <= 8 and owners & (owners - 1) == 0 and lines // owners % 8 == 0
    count = owners if few else 1
    return pl.pallas_call(
        functools.partial(surface_kernel, count),
        in_specs=[WHOLE] * (len(parts) + 1),
        out_specs=[WHOLE] * count,
        out_shape=[jax.ShapeDtypeStruct((lines // count, sides), F32)] * count,
        scratch_shapes=[pltpu.VMEM((lines, sides), F32)],
        compiler_params=params(),
        cost_estimate=pl.CostEstimate(
            flops=2 * sides * held.size, bytes_accessed=2 * held.size, transcendentals=0
        ),
    )(*parts, held)


def send_to_owners(shares, late):
    owners = lax.axis_size("gz") * lax.axis_size("col")
    if len(shares) == 1:
        share = shares[0]
        share = share.reshape(owners, share.shape[0] // owners, share.shape[1])
        return [lax.all_to_all(share, ("col", "gz"), split_axis=0, concat_axis=0, tiled=True)], late
    got = [shares[0]]
    order = sorted(range(1, owners), key=lambda key: -(key % lax.axis_size("gz")))
    for place, key in enumerate(order):
        if place == len(order) // 2:
            held, late = lax.optimization_barrier(([shares[k] for k in order[place:]], late))
            shares = [held[order.index(k) - place] if k in order[place:] else s for k, s in enumerate(shares)]
        pairs = [(i, i ^ key) for i in range(owners)]
        got.append(lax.ppermute(shares[key], ("col", "gz"), pairs))
    return got, late


def turns(axis):
    return 1 if lax.axis_size(axis) == 2 else 2


def partner(index, turn):
    return jnp.where(index % 2 == turn, index + 1, index - 1)


def has_neighbour(axis, turn):
    other = partner(lax.axis_index(axis), turn)
    return (other >= 0) & (other < lax.axis_size(axis))


def swap(value, axis, turn):
    axes = ("row", "col", "gz")
    sizes = [lax.axis_size(name) for name in axes]
    along = axes.index(axis)
    spare = 0 if axis == "gz" else 2
    pairs = []
    for r in range(sizes[0]):
        for c in range(sizes[1]):
            for g in range(sizes[2]):
                here = [r, c, g]
                there = [r, c, g]
                there[along] += 1 if here[along] % 2 == turn else -1
                if not 0 <= there[along] < sizes[along]:
                    there[along] = here[along]
                    if here[spare] ^ 1 < sizes[spare]:
                        there[spare] ^= 1
                flat = [(at[0] * sizes[1] + at[1]) * sizes[2] + at[2] for at in (here, there)]
                pairs.append(tuple(flat))
    return lax.ppermute(value, axes, pairs)


class Shape:
    def __init__(self, sides, first, second, lanes):
        self.sides, self.x, self.y, self.lanes = sides, first, second, lanes
        self.cells = first * second
        self.chunk = max(1, 128 // self.cells)
        self.rows = self.chunk * self.cells
        self.block = min(sides, 32)
        self.half = self.block // 2
        self.half_rows = self.half * self.cells
        self.faces = [("col", i) for i in range(turns("col"))]
        self.faces += [("row", i) for i in reversed(range(turns("row")))]
        self.ends = turns("gz")

    def face_len(self, face):
        return self.y if face[0] == "row" else self.x

    def halo_rows(self):
        return sum(self.chunk * self.face_len(face) for face in self.faces)

    def edge(self, face):
        axis, turn = face
        last = (self.x if axis == "row" else self.y) - 1
        return jnp.where(lax.axis_index(axis) % 2 == turn, last, 0)


def halo_place(shape):
    dims = (shape.rows, shape.halo_rows())
    row, col = iota(dims, 0), iota(dims, 1)
    side, cell = row // shape.cells, row % shape.cells
    x, y = cell // shape.y, cell % shape.y
    hit, base = None, 0
    for face in shape.faces:
        length = shape.face_len(face)
        along, across = (y, x) if face[0] == "row" else (x, y)
        place = (across == shape.edge(face)) & (col - base == side * length + along)
        place = place & has_neighbour(*face)
        hit = place if hit is None else hit | place
        base += shape.chunk * length
    return hit.astype(BF)


def z_mask(shape, count):
    dims = (count * shape.cells, 2 * shape.cells)
    return iota(dims, 1) % shape.cells == iota(dims, 0) % shape.cells


def twice(matrix):
    zero = jnp.zeros_like(matrix)
    return jnp.concatenate(
        [jnp.concatenate([matrix, zero], axis=1), jnp.concatenate([zero, matrix], axis=1)], axis=0
    )


def beside(values):
    half = values.shape[0] // 2
    return jnp.concatenate([values[:half], values[half:]], axis=1)


def build_out(shape, ends_m, rsum):
    dims = (shape.lanes, 2 * shape.cells)
    edge = jnp.where(iota(dims, 1) < shape.cells, 0, shape.lanes - 1)
    ends_m[...] = twice((iota(dims, 0) == edge).astype(F32)).astype(BF)
    dims = rsum.shape
    rsum[...] = (iota(dims, 1) // shape.cells == iota(dims, 0)).astype(BF)


def emit_faces(shape, at, values, tall, face_refs, z_ref, ends_m, rsum):
    for face, ref in zip(shape.faces, face_refs):
        length, edge = shape.face_len(face), shape.edge(face)
        lines = []
        for side in range(shape.block):
            start = side * shape.cells
            if face[0] == "row":
                lines.append(tall[pl.ds(pl.multiple_of(start + edge * length, 8), length), :])
            else:
                lines.append(tall[pl.ds(start + edge, length, stride=shape.y), :])
        span = shape.block * length
        ref[pl.ds(pl.multiple_of(at * length, span), span), :] = jnp.concatenate(
            lines, axis=0
        ).astype(BF)
    mask = jnp.concatenate([z_mask(shape, shape.half)] * 2, axis=1)
    tips = jnp.where(mask, dot(beside(values), ends_m[...]), 0.0).astype(BF)
    tips = dot(rsum[...], tips)[: shape.half]
    tips = jnp.concatenate([tips[:, : 2 * shape.cells], tips[:, 2 * shape.cells :]], axis=0)
    z_ref[pl.ds(pl.multiple_of(at, shape.block), shape.block), :] = tips.astype(BF)


def faces_kernel(shape, slots, field_ref, block_ref, *refs):
    *face_refs, z_ref, held, tall, ends_m, rsum, sems = refs
    copies = fetch_columns(block_ref, held, sems, slots)
    build_out(shape, ends_m, rsum)

    @pl.loop(0, shape.sides // shape.block)
    def _(step):
        size = shape.block * shape.cells
        values = field_ref[pl.ds(pl.multiple_of(step * size, size), size), :]
        tall[...] = values.astype(F32)
        emit_faces(shape, step * shape.block, values, tall, face_refs, z_ref, ends_m, rsum)

    for copy in copies:
        copy.wait()


def face_outputs(shape):
    shapes = [
        jax.ShapeDtypeStruct((shape.sides * shape.face_len(face), shape.lanes), BF)
        for face in shape.faces
    ]
    return shapes + [jax.ShapeDtypeStruct((shape.sides, 2 * shape.cells), BF)]


def face_scratch(shape):
    return [
        pltpu.VMEM((shape.block * shape.cells, shape.lanes), F32),
        pltpu.VMEM((2 * shape.lanes, 4 * shape.cells), BF),
        pltpu.VMEM((max(8, shape.half), shape.half_rows), BF),
    ]


def first_faces(shape, field, block, slots):
    peers = lax.axis_size("row")
    shapes = face_outputs(shape)
    shapes.append(jax.ShapeDtypeStruct((peers, block.shape[0], slots), BF))
    return pl.pallas_call(
        functools.partial(faces_kernel, shape, slots),
        in_specs=[WHOLE, pl.BlockSpec(memory_space=pltpu.HBM)],
        out_specs=[WHOLE] * len(shapes),
        out_shape=shapes,
        scratch_shapes=face_scratch(shape) + [pltpu.SemaphoreType.DMA((peers,))],
        compiler_params=params(FACES_MIB),
        cost_estimate=pl.CostEstimate(
            flops=field.size * 128, bytes_accessed=4 * field.size, transcendentals=0
        ),
    )(field, block)


def sweep_kernel(shape, recvs, fluxes, by_xor, *refs):
    with_flux, last = recvs > 0, fluxes > 0
    refs = list(refs)
    take = lambda count: [refs.pop(0) for _ in range(count)]
    field_ref, load_ref, coef_ref = take(3)
    halo_refs = take(len(shape.faces))
    end_refs = take(shape.ends)
    if with_flux:
        recv_refs = take(recvs)
        (cell_ref,) = take(1)
    flux_refs = take(fluxes)
    (out_ref,) = take(1)
    if last:
        (flux_ref,) = take(1)
    else:
        face_refs = take(len(shape.faces))
        (z_ref,) = take(1)
    if with_flux:
        source_ref, owned_ref = take(2)
    weight, near_m, line_m, lines = take(4)
    if last:
        window, turned = take(2)
    else:
        tall, ends_m, rsum = take(3)
    if with_flux:
        phi, cell_m, placed = take(3)

    grid_step = pl.program_id(0)
    cells, lanes = shape.cells, shape.lanes

    @pl.when(grid_step == 0)
    def _():
        weight[...] = OMEGA / (6.0 + coef_ref[...])
        dims = (shape.rows, shape.rows)
        row, col = iota(dims, 0), iota(dims, 1)
        x, y = row % cells // shape.y, row % shape.y
        x2, y2 = col % cells // shape.y, col % shape.y
        near = ((x == x2) & (jnp.abs(y - y2) == 1)) | ((y == y2) & (jnp.abs(x - x2) == 1))
        near_m[:, : shape.rows] = (near & (row // cells == col // cells)).astype(BF)
        near_m[:, shape.rows :] = halo_place(shape)
        dims = (lanes, lanes)
        line = (jnp.abs(iota(dims, 0) - iota(dims, 1)) == 1).astype(F32)
        line_m[: 2 * lanes, :] = twice(line).astype(BF)
        dims = (2 * cells, lanes)
        edge = jnp.where(iota(dims, 0) < cells, lanes - 1, 0)
        line_m[2 * lanes :, :] = twice((iota(dims, 1) == edge).astype(F32)).astype(BF)
        if last:
            group = lax.axis_index("gz")
            count = flux_refs[0].shape[0]
            for key, ref in enumerate(flux_refs):
                place = jnp.bitwise_xor(group, key) if by_xor else key
                window[pl.ds(place * count, count), :] = ref[...]
            turned[...] = window[...].T
            count = flux_ref.shape[0]
            flux_ref[...] = turned[pl.ds(pl.multiple_of(group * count, count), count), :]
        else:
            build_out(shape, ends_m, rsum)
        if with_flux:
            slots = cell_ref.shape[3]
            if recvs == 1:
                owned = recv_refs[0][0]
                for peer in range(1, recv_refs[0].shape[0]):
                    owned = owned + recv_refs[0][peer]
            else:
                owned = recv_refs[0][...]
                for ref in recv_refs[1:]:
                    owned = owned + ref[...]
            owned_ref[...] = owned
            high = owned.astype(BF).astype(F32)
            both = jnp.concatenate([high, owned - high], axis=0)
            phi[...] = both.T
            cell = jnp.concatenate([cell_ref[0, 0]] * 2, axis=1)
            cell_m[...] = twice((iota((lanes, 2 * slots), 0) == cell % lanes).astype(F32)).astype(BF)

    mask = z_mask(shape, 1)
    even = lax.axis_index("gz") % 2 == 0
    filled = (iota((shape.block, 2 * cells), 1) < cells) == even
    if with_flux:
        slots = cell_ref.shape[3]
        cell = jnp.concatenate([cell_ref[0, 0]] * 2, axis=1)
        cell_mask = iota((cells, 2 * slots), 0) == cell // lanes
    weights = jnp.concatenate([weight[...]] * shape.chunk, axis=0)
    out_sides = out_ref.shape[0] // cells

    def expand(lines, where, first):
        rows = []
        for side in range(first, first + shape.half):
            line = jnp.broadcast_to(lines[side : side + 1], where.shape)
            rows.append(jnp.where(where, line, 0.0))
        return jnp.concatenate(rows, axis=0).astype(BF)

    @pl.loop(0, out_sides // shape.block)
    def _(step):
        local = step * shape.block
        at = grid_step * out_sides + local
        sides = pl.ds(pl.multiple_of(at, shape.block), shape.block)
        size = shape.block * cells
        zs = 0.0
        for turn in range(shape.ends):
            wanted = (filled == (turn == 0)) & has_neighbour("gz", turn)
            zs = jnp.where(wanted, end_refs[turn][sides, :].astype(F32), zs)
        values = field_ref[pl.ds(pl.multiple_of(at * cells, size), size), :]
        left = [beside(values), expand(zs, mask, 0), expand(zs, mask, shape.half)]
        lines[...] = dot(jnp.concatenate(left, axis=1), line_m[...])
        if with_flux:
            phis = phi[sides, :]
            left = [expand(phis, cell_mask, 0), expand(phis, cell_mask, shape.half)]
            placed[...] = dot_nt(jnp.concatenate(left, axis=1), cell_m[...])
        for index in range(shape.half // shape.chunk):
            offset = index * shape.rows
            starts = (offset, offset + shape.half_rows)
            stacks = []
            for start in starts:
                rows = pl.ds(pl.multiple_of(at * cells + start, shape.rows), shape.rows)
                stack = [field_ref[rows, :]]
                for face, ref in zip(shape.faces, halo_refs):
                    length = shape.face_len(face)
                    count = shape.chunk * length
                    first = pl.multiple_of(at * length + start // cells * length, count)
                    stack.append(ref[pl.ds(first, count), :])
                stacks.append(jnp.concatenate(stack, axis=0))
            near = dot(near_m[...], jnp.concatenate(stacks, axis=1))
            near = near + lines[offset : offset + shape.rows, :]
            for part, start in enumerate(starts):
                cols = slice(part * lanes, (part + 1) * lanes)
                rows = pl.ds(pl.multiple_of(at * cells + start, shape.rows), shape.rows)
                source = load_ref[rows, :].astype(F32)
                if with_flux:
                    source = source + placed[offset : offset + shape.rows, cols]
                    source_ref[rows, :] = source.astype(BF)
                centre = field_ref[rows, :].astype(F32)
                fresh = (1.0 - OMEGA) * centre + weights * (source + near[:, cols])
                to = pl.ds(pl.multiple_of(local * cells + start, shape.rows), shape.rows)
                out_ref[to, :] = fresh.astype(BF)
                if not last:
                    tall[start : start + shape.rows, :] = fresh
        if not last:
            fresh = out_ref[pl.ds(pl.multiple_of(local * cells, size), size), :]
            emit_faces(shape, at, fresh, tall, face_refs, z_ref, ends_m, rsum)


def sweep(shape, field, load, coef, halos, recv=(), flux_cell=None, flux=(), by_xor=True, last=False):
    lanes, cells = shape.lanes, shape.cells
    operands = [field, load, coef, *halos, *recv]
    out_shapes = [jax.ShapeDtypeStruct(field.shape, BF)]
    scratch = [
        pltpu.VMEM(coef.shape, F32),
        pltpu.VMEM((shape.rows, shape.rows + shape.halo_rows()), BF),
        pltpu.VMEM((2 * lanes + 4 * cells, 2 * lanes), BF),
        pltpu.VMEM((shape.half_rows, 2 * lanes), F32),
    ]
    if last:
        operands += flux
        gzs = len(flux)
        slots = flux[0].shape[0]
        flux_shape = (shape.sides // gzs, slots * gzs)
        out_shapes.append(jax.ShapeDtypeStruct(flux_shape, F32))
        scratch += [
            pltpu.VMEM((slots * gzs, shape.sides), F32),
            pltpu.VMEM((shape.sides, slots * gzs), F32),
        ]
    else:
        out_shapes += face_outputs(shape)
        scratch += face_scratch(shape)
    if recv:
        slots = flux_cell.shape[3]
        operands.append(flux_cell)
        out_shapes += [
            jax.ShapeDtypeStruct(field.shape, BF),
            jax.ShapeDtypeStruct((slots, shape.sides), F32),
        ]
        scratch += [
            pltpu.VMEM((shape.sides, 2 * slots), F32),
            pltpu.VMEM((2 * lanes, 4 * slots), BF),
            pltpu.VMEM((shape.half_rows, 2 * lanes), F32),
        ]
    steps = shape.sides // shape.block if last else 1
    out_specs = [WHOLE] * len(out_shapes)
    if last:
        out_specs = [
            pl.BlockSpec((field.shape[0] // steps, lanes), lambda i: (i, 0)),
            pl.BlockSpec(flux_shape, lambda i: (0, 0)),
        ]
    return pl.pallas_call(
        functools.partial(sweep_kernel, shape, len(recv), len(flux), by_xor),
        grid=(steps,),
        in_specs=[WHOLE] * len(operands),
        out_specs=out_specs,
        out_shape=out_shapes,
        scratch_shapes=scratch,
        compiler_params=params(),
        cost_estimate=pl.CostEstimate(
            flops=6 * field.size * 128, bytes_accessed=8 * field.size, transcendentals=0
        ),
    )(*operands)


def exchange(shape, faces):
    *cut, ends = faces
    halos = [swap(value, *face) for face, value in zip(shape.faces, cut)]
    return halos + [swap(ends, "gz", turn) for turn in range(shape.ends)]


def row_gather(trace, faces):
    peers = lax.axis_size("row")
    held = {0: trace}
    bit = peers // 2
    while bit:
        pairs = [(i, i ^ bit) for i in range(peers)]
        fresh = {key ^ bit: lax.ppermute(held[key], "row", pairs) for key in sorted(held, reverse=True)}
        if bit == peers // 2:
            held, fresh, _ = lax.optimization_barrier((held, fresh, faces))
        held.update(fresh)
        bit //= 2
    return [held[key] for key in range(peers)]


def gz_gather(value):
    peers = lax.axis_size("gz")
    if peers & (peers - 1):
        return list(lax.all_gather(value, "gz")), False
    got = [value]
    for key in range(1, peers):
        got.append(lax.ppermute(value, "gz", [(i, i ^ key) for i in range(peers)]))
    return got, True


def per_device(volume_field, volume_load, coefficient, surface_block, trace_cell, flux_cell):
    sides, first, second, lanes = volume_field.shape
    cells = first * second
    shape = Shape(sides, first, second, lanes)
    field = volume_field.reshape(sides * cells, lanes)
    load = volume_load.reshape(sides * cells, lanes)
    coef = coefficient.reshape(cells, lanes)

    slots = trace_cell.shape[3]
    trace = traces(volume_field.reshape(sides, cells, lanes), trace_cell, min(32, sides))
    *faces, held = first_faces(shape, field, surface_block, slots)
    parts = row_gather(trace, faces)
    halos = exchange(shape, faces)
    early = len([face for face in shape.faces if face[0] == "col"])
    parts, halos[early:] = lax.optimization_barrier((parts, halos[early:]))
    recv, halos[:early] = send_to_owners(surface(parts, held), halos[:early])

    current, *faces, source, owned = sweep(
        shape, field, load, coef, halos, recv=recv, flux_cell=flux_cell
    )
    current, *faces = sweep(shape, current, source, coef, exchange(shape, faces))
    flux, by_xor = gz_gather(owned)
    current, surface_flux = sweep(
        shape, current, source, coef, exchange(shape, faces), flux=flux, by_xor=by_xor, last=True
    )
    return current.reshape(volume_field.shape), surface_flux


def solution(mesh):
    in_specs = (
        P(None, "row", "col", "gz"),
        P(None, "row", "col", "gz"),
        P("row", "col", "gz"),
        P("row", "col"),
        P("row", "col", "gz", None),
        P("row", "col", "gz", None),
    )
    out_specs = (P(None, "row", "col", "gz"), P("gz", ("row", "col")))
    return jax.shard_map(
        per_device, mesh=mesh, in_specs=in_specs, out_specs=out_specs, check_vma=False
    )
```

```python
import functools

import jax
import jax.numpy as jnp
from jax import lax
from jax.experimental import pallas as pl
from jax.experimental.pallas import tpu as pltpu
from jax.sharding import PartitionSpec as P

OMEGA = 0.8
BF = jnp.bfloat16
F32 = jnp.float32
WHOLE = pl.BlockSpec(memory_space=pltpu.VMEM)


def aligned(start, unit):
    return start if isinstance(start, int) else pl.multiple_of(start, unit)


def iota(shape, dim):
    return lax.broadcasted_iota(jnp.int32, shape, dim)


def dot(a, b):
    return jnp.dot(a, b, preferred_element_type=F32)


def dot_nt(a, b):
    return lax.dot_general(a, b, (((1,), (1,)), ((), ())), preferred_element_type=F32)


FACES_MIB = 50


def params(mebibytes=24):
    return pltpu.CompilerParams(vmem_limit_bytes=mebibytes * 1024 * 1024)


def trace_kernel(stride, block, field_ref, cell_ref, out_ref, field, cell_v, tall, near, place, picked, sems):
    sides, rows, lanes = field.shape
    slots = cell_ref.shape[3]
    per_row = lanes // stride
    width = near.shape[0]
    parts = slots // width
    cell_copy = pltpu.make_async_copy(cell_ref, cell_v, sems.at[sides // block])
    cell_copy.start()
    copies = []
    for step in range(sides // block):
        span = pl.ds(step * block, block)
        copies.append(pltpu.make_async_copy(field_ref.at[span], field.at[span], sems.at[step]))
        copies[-1].start()

    cell_copy.wait()
    cell = cell_v[0, 0]
    run = cell // stride
    digit = jnp.zeros_like(cell)
    for part in range(parts):
        digit = jnp.where(run // width == part, (cell % stride) * stride**part, digit)
    hit = iota((width, slots), 0) == run % width
    near[...] = hit.astype(BF)
    digits = jnp.sum(jnp.where(hit, digit.astype(F32), 0.0), axis=1, keepdims=True)
    digits = jnp.broadcast_to(digits, (width, 128)).T[0:8].astype(jnp.int32)
    first = iota((8, width), 1) % per_row * stride
    for part in range(parts):
        place[:, part * width : (part + 1) * width] = first + digits // stride**part % stride

    together = 128 // per_row
    group = iota((8, 128), 1) // per_row
    for step in range(sides // block):
        copies[step].wait()
        span = field[step * block : (step + 1) * block]
        tall[...] = span.reshape(block * rows, lanes).astype(F32)

        @pl.loop(0, block // 8)
        def _(batch):
            for tile in range(rows // together):
                cols = slice(tile * 128, (tile + 1) * 128)
                where = place[:, cols]
                found = None
                for row in range(together):
                    start = batch * 8 * rows + tile * together + row
                    line = tall[pl.ds(start, 8, stride=rows), :]
                    line = jnp.take_along_axis(line, where, axis=1)
                    found = line if found is None else jnp.where(group == row, line, found)
                at = pl.multiple_of(step * block + batch * 8, 8)
                picked[pl.ds(at, 8), cols] = found

    total = jnp.zeros((sides, slots), F32)
    for part in range(parts):
        sorted_runs = picked[:, part * width : (part + 1) * width].astype(BF)
        total = jnp.where(run // width == part, dot(sorted_runs, near[...]), total)
    out_ref[...] = total.T.astype(BF)


def traces(field, trace_cell, block):
    sides, rows, lanes = field.shape
    slots = trace_cell.shape[3]
    stride = rows * lanes // slots
    width = min(slots, 256)
    hbm = pl.BlockSpec(memory_space=pltpu.HBM)
    return pl.pallas_call(
        functools.partial(trace_kernel, stride, block),
        in_specs=[hbm, hbm],
        out_specs=WHOLE,
        out_shape=jax.ShapeDtypeStruct((slots, sides), BF),
        scratch_shapes=[
            pltpu.VMEM(field.shape, BF),
            pltpu.VMEM(trace_cell.shape, jnp.int32),
            pltpu.VMEM((block * rows, lanes), F32),
            pltpu.VMEM((width, slots), BF),
            pltpu.VMEM((8, slots), jnp.int32),
            pltpu.VMEM((sides, slots), F32),
            pltpu.SemaphoreType.DMA((sides // block + 1,)),
        ],
        compiler_params=params(62),
        cost_estimate=pl.CostEstimate(
            flops=4 * sides * rows * lanes * 128, bytes_accessed=field.size * 2, transcendentals=0
        ),
    )(field, trace_cell)


def fetch_columns(block_ref, held, sems, slots):
    me, group, gzs = lax.axis_index("row"), lax.axis_index("gz"), lax.axis_size("gz")
    copies = []
    for key in range(held.shape[0]):
        start = pl.multiple_of((jnp.bitwise_xor(me, key) * gzs + group) * slots, slots)
        copies.append(
            pltpu.make_async_copy(block_ref.at[:, pl.ds(start, slots)], held.at[key], sems.at[key])
        )
        copies[-1].start()
    return copies


def surface_kernel(halves, *refs):
    ins, total = refs[:-1], refs[-1]
    outs = ins[len(ins) - halves :]
    *parts, held = ins[: len(ins) - halves]
    value = None
    for key, part in enumerate(parts):
        term = dot(held[key], part[...])
        value = term if value is None else value + term
    if halves == 1:
        outs[0][...] = value
        return
    total[...] = value
    count = outs[0].shape[0]
    mine = lax.axis_index("col")
    for key, out in enumerate(outs):
        out[...] = total[pl.ds(pl.multiple_of((mine ^ key) * count, 8), count), :]


def surface(parts, held, halves):
    sides = parts[0].shape[1]
    lines = held.shape[1]
    return pl.pallas_call(
        functools.partial(surface_kernel, halves),
        in_specs=[WHOLE] * (len(parts) + 1),
        out_specs=[WHOLE] * halves,
        out_shape=[jax.ShapeDtypeStruct((lines // halves, sides), F32)] * halves,
        scratch_shapes=[pltpu.VMEM((lines, sides), F32)],
        compiler_params=params(),
        cost_estimate=pl.CostEstimate(
            flops=2 * sides * held.size, bytes_accessed=2 * held.size, transcendentals=0
        ),
    )(*parts, held)


def share_kernel(peers, mine_ref, other_ref, *refs):
    *outs, total, turned = refs
    total[...] = mine_ref[...] + other_ref[...]
    turned[...] = total[...].T
    lines, sides = total.shape
    group = lax.axis_index("gz")
    for key, out in enumerate(outs):
        peer = group ^ key
        rows, some = lines // peers, sides // peers
        out[:rows, :] = total[pl.ds(pl.multiple_of(peer * rows, 8), rows), :]
        out[rows:, :] = turned[pl.ds(pl.multiple_of(peer * some, 8), some), :]


def shares(mine, other):
    peers = lax.axis_size("gz")
    lines, sides = mine.shape
    out = jax.ShapeDtypeStruct(((lines + sides) // peers, sides), F32)
    return pl.pallas_call(
        functools.partial(share_kernel, peers),
        in_specs=[WHOLE] * 2,
        out_specs=[WHOLE] * peers,
        out_shape=[out] * peers,
        scratch_shapes=[pltpu.VMEM((lines, sides), F32), pltpu.VMEM((sides, lines), F32)],
        compiler_params=params(),
        cost_estimate=pl.CostEstimate(
            flops=lines * sides, bytes_accessed=16 * lines * sides, transcendentals=0
        ),
    )(mine, other)


def flux_sums(parts, held, late):
    cols, gzs = lax.axis_size("col"), lax.axis_size("gz")
    sides = parts[0].shape[1]
    lines = held.shape[1]
    if cols == 2 and gzs & (gzs - 1) == 0 and lines // cols == sides and sides // gzs % 8 == 0:
        mine, other = surface(parts, held, 2)
        other = lax.ppermute(other, "col", [(0, 1), (1, 0)])
        sent = shares(mine, other)
        sent, late = lax.optimization_barrier((sent, late))
        recv = [sent[0]]
        for key in range(gzs - 1, 0, -1):
            recv.append(lax.ppermute(sent[key], "gz", [(i, i ^ key) for i in range(gzs)]))
        return recv, late
    (total,) = surface(parts, held, 1)
    rows = lax.psum_scatter(total, "col", scatter_dimension=0, tiled=True)
    owned = lax.psum_scatter(rows, "gz", scatter_dimension=0, tiled=True)
    flux = lax.psum_scatter(rows.T, "gz", scatter_dimension=0, tiled=True)
    flux = jnp.pad(flux, ((0, 0), (0, sides - flux.shape[1])))
    return [jnp.concatenate([owned, flux], axis=0)], late


def turns(axis):
    return 1 if lax.axis_size(axis) == 2 else 2


def partner(index, turn):
    return jnp.where(index % 2 == turn, index + 1, index - 1)


def has_neighbour(axis, turn):
    other = partner(lax.axis_index(axis), turn)
    return (other >= 0) & (other < lax.axis_size(axis))


def swap(value, axis, turn):
    axes = ("row", "col", "gz")
    sizes = [lax.axis_size(name) for name in axes]
    along = axes.index(axis)
    spare = 0 if axis == "gz" else 2
    pairs = []
    for r in range(sizes[0]):
        for c in range(sizes[1]):
            for g in range(sizes[2]):
                here = [r, c, g]
                there = [r, c, g]
                there[along] += 1 if here[along] % 2 == turn else -1
                if not 0 <= there[along] < sizes[along]:
                    there[along] = here[along]
                    if here[spare] ^ 1 < sizes[spare]:
                        there[spare] ^= 1
                flat = [(at[0] * sizes[1] + at[1]) * sizes[2] + at[2] for at in (here, there)]
                pairs.append(tuple(flat))
    return lax.ppermute(value, axes, pairs)


class Shape:
    def __init__(self, sides, first, second, lanes):
        self.sides, self.x, self.y, self.lanes = sides, first, second, lanes
        self.cells = first * second
        self.chunk = max(1, 128 // self.cells)
        self.rows = self.chunk * self.cells
        self.block = min(sides, 32)
        self.half = self.block // 2
        self.half_rows = self.half * self.cells
        self.faces = [("col", i) for i in range(turns("col"))]
        self.faces += [("row", i) for i in reversed(range(turns("row")))]
        self.ends = turns("gz")

    def face_len(self, face):
        return self.y if face[0] == "row" else self.x

    def halo_rows(self):
        return sum(self.chunk * self.face_len(face) for face in self.faces)

    def edge(self, face):
        axis, turn = face
        last = (self.x if axis == "row" else self.y) - 1
        return jnp.where(lax.axis_index(axis) % 2 == turn, last, 0)


def halo_place(shape):
    dims = (shape.rows, shape.halo_rows())
    row, col = iota(dims, 0), iota(dims, 1)
    side, cell = row // shape.cells, row % shape.cells
    x, y = cell // shape.y, cell % shape.y
    hit, base = None, 0
    for face in shape.faces:
        length = shape.face_len(face)
        along, across = (y, x) if face[0] == "row" else (x, y)
        place = (across == shape.edge(face)) & (col - base == side * length + along)
        place = place & has_neighbour(*face)
        hit = place if hit is None else hit | place
        base += shape.chunk * length
    return hit.astype(BF)


def z_mask(shape, count):
    dims = (count * shape.cells, 2 * shape.cells)
    return iota(dims, 1) % shape.cells == iota(dims, 0) % shape.cells


def twice(matrix):
    zero = jnp.zeros_like(matrix)
    return jnp.concatenate(
        [jnp.concatenate([matrix, zero], axis=1), jnp.concatenate([zero, matrix], axis=1)], axis=0
    )


def beside(values):
    half = values.shape[0] // 2
    return jnp.concatenate([values[:half], values[half:]], axis=1)


def build_out(shape, ends_m, rsum):
    dims = (shape.lanes, 2 * shape.cells)
    edge = jnp.where(iota(dims, 1) < shape.cells, 0, shape.lanes - 1)
    ends_m[...] = twice((iota(dims, 0) == edge).astype(F32)).astype(BF)
    dims = rsum.shape
    rsum[...] = (iota(dims, 1) // shape.cells == iota(dims, 0)).astype(BF)


def emit_faces(shape, at, values, tall, face_refs, z_ref, ends_m, rsum):
    for face, ref in zip(shape.faces, face_refs):
        length, edge = shape.face_len(face), shape.edge(face)
        lines = []
        for side in range(shape.block):
            start = side * shape.cells
            if face[0] == "row":
                lines.append(tall[pl.ds(aligned(start + edge * length, 8), length), :])
            else:
                lines.append(tall[pl.ds(start + edge, length, stride=shape.y), :])
        span = shape.block * length
        ref[pl.ds(aligned(at * length, span), span), :] = jnp.concatenate(
            lines, axis=0
        ).astype(BF)
    mask = jnp.concatenate([z_mask(shape, shape.half)] * 2, axis=1)
    tips = jnp.where(mask, dot(beside(values), ends_m[...]), 0.0).astype(BF)
    tips = dot(rsum[...], tips)[: shape.half]
    tips = jnp.concatenate([tips[:, : 2 * shape.cells], tips[:, 2 * shape.cells :]], axis=0)
    z_ref[pl.ds(aligned(at, shape.block), shape.block), :] = tips.astype(BF)


def faces_kernel(shape, slots, field_ref, block_ref, *refs):
    *face_refs, z_ref, held, tall, ends_m, rsum, sems = refs
    copies = fetch_columns(block_ref, held, sems, slots)
    build_out(shape, ends_m, rsum)

    @pl.loop(0, shape.sides // shape.block)
    def _(step):
        size = shape.block * shape.cells
        values = field_ref[pl.ds(aligned(step * size, size), size), :]
        tall[...] = values.astype(F32)
        emit_faces(shape, step * shape.block, values, tall, face_refs, z_ref, ends_m, rsum)

    for copy in copies:
        copy.wait()


def face_outputs(shape):
    shapes = [
        jax.ShapeDtypeStruct((shape.sides * shape.face_len(face), shape.lanes), BF)
        for face in shape.faces
    ]
    return shapes + [jax.ShapeDtypeStruct((shape.sides, 2 * shape.cells), BF)]


def face_scratch(shape):
    return [
        pltpu.VMEM((shape.block * shape.cells, shape.lanes), F32),
        pltpu.VMEM((2 * shape.lanes, 4 * shape.cells), BF),
        pltpu.VMEM((max(8, shape.half), shape.half_rows), BF),
    ]


def first_faces(shape, field, block, slots):
    peers = lax.axis_size("row")
    shapes = face_outputs(shape)
    shapes.append(jax.ShapeDtypeStruct((peers, block.shape[0], slots), BF))
    return pl.pallas_call(
        functools.partial(faces_kernel, shape, slots),
        in_specs=[WHOLE, pl.BlockSpec(memory_space=pltpu.HBM)],
        out_specs=[WHOLE] * len(shapes),
        out_shape=shapes,
        scratch_shapes=face_scratch(shape) + [pltpu.SemaphoreType.DMA((peers,))],
        compiler_params=params(FACES_MIB),
        cost_estimate=pl.CostEstimate(
            flops=field.size * 128, bytes_accessed=4 * field.size, transcendentals=0
        ),
    )(field, block)


def sweep_kernel(shape, recvs, last, *refs):
    with_flux = recvs > 0
    refs = list(refs)
    take = lambda count: [refs.pop(0) for _ in range(count)]
    field_ref, load_ref, coef_ref = take(3)
    halo_refs = take(len(shape.faces))
    end_refs = take(shape.ends)
    if with_flux:
        recv_refs = take(recvs)
        (cell_ref,) = take(1)
    (out_ref,) = take(1)
    if not last:
        face_refs = take(len(shape.faces))
        (z_ref,) = take(1)
    if with_flux:
        source_ref, flux_ref = take(2)
    weight, near_m, line_m, lines = take(4)
    if not last:
        tall, ends_m, rsum = take(3)
    if with_flux:
        phi, cell_m, placed = take(3)

    grid_step = pl.program_id(0)
    cells, lanes = shape.cells, shape.lanes

    @pl.when(grid_step == 0)
    def _():
        weight[...] = OMEGA / (6.0 + coef_ref[...])
        dims = (shape.rows, shape.rows)
        row, col = iota(dims, 0), iota(dims, 1)
        x, y = row % cells // shape.y, row % shape.y
        x2, y2 = col % cells // shape.y, col % shape.y
        near = ((x == x2) & (jnp.abs(y - y2) == 1)) | ((y == y2) & (jnp.abs(x - x2) == 1))
        near_m[:, : shape.rows] = (near & (row // cells == col // cells)).astype(BF)
        near_m[:, shape.rows :] = halo_place(shape)
        dims = (lanes, lanes)
        line = (jnp.abs(iota(dims, 0) - iota(dims, 1)) == 1).astype(F32)
        line_m[: 2 * lanes, :] = twice(line).astype(BF)
        dims = (2 * cells, lanes)
        edge = jnp.where(iota(dims, 0) < cells, lanes - 1, 0)
        line_m[2 * lanes :, :] = twice((iota(dims, 1) == edge).astype(F32)).astype(BF)
        if not last:
            build_out(shape, ends_m, rsum)
        if with_flux:
            slots = cell_ref.shape[3]
            owned = recv_refs[0][...]
            for ref in recv_refs[1:]:
                owned = owned + ref[...]
            flux_ref[...] = owned[slots:, : flux_ref.shape[1]]
            owned = owned[:slots]
            high = owned.astype(BF).astype(F32)
            both = jnp.concatenate([high, owned - high], axis=0)
            phi[...] = both.T
            cell = jnp.concatenate([cell_ref[0, 0]] * 2, axis=1)
            cell_m[...] = twice((iota((lanes, 2 * slots), 0) == cell % lanes).astype(F32)).astype(BF)

    mask = z_mask(shape, 1)
    even = lax.axis_index("gz") % 2 == 0
    filled = (iota((shape.block, 2 * cells), 1) < cells) == even
    if with_flux:
        slots = cell_ref.shape[3]
        cell = jnp.concatenate([cell_ref[0, 0]] * 2, axis=1)
        cell_mask = iota((cells, 2 * slots), 0) == cell // lanes
    weights = jnp.concatenate([weight[...]] * shape.chunk, axis=0)
    out_sides = out_ref.shape[0] // cells

    def expand(lines, where, first):
        rows = []
        for side in range(first, first + shape.half):
            line = jnp.broadcast_to(lines[side : side + 1], where.shape)
            rows.append(jnp.where(where, line, 0.0))
        return jnp.concatenate(rows, axis=0).astype(BF)

    def work(step):
        local = step * shape.block
        at = local if out_sides == shape.sides else grid_step * out_sides + local
        sides = pl.ds(aligned(at, shape.block), shape.block)
        size = shape.block * cells
        zs = 0.0
        for turn in range(shape.ends):
            wanted = (filled == (turn == 0)) & has_neighbour("gz", turn)
            zs = jnp.where(wanted, end_refs[turn][sides, :].astype(F32), zs)
        values = field_ref[pl.ds(aligned(at * cells, size), size), :]
        left = [beside(values), expand(zs, mask, 0), expand(zs, mask, shape.half)]
        lines[step] = dot(jnp.concatenate(left, axis=1), line_m[...])
        if with_flux:
            phis = phi[sides, :]
            left = [expand(phis, cell_mask, 0), expand(phis, cell_mask, shape.half)]
            placed[step] = dot_nt(jnp.concatenate(left, axis=1), cell_m[...])
        for index in range(shape.half // shape.chunk):
            offset = index * shape.rows
            starts = (offset, offset + shape.half_rows)
            stacks = []
            for start in starts:
                rows = pl.ds(aligned(at * cells + start, shape.rows), shape.rows)
                stack = [field_ref[rows, :]]
                for face, ref in zip(shape.faces, halo_refs):
                    length = shape.face_len(face)
                    count = shape.chunk * length
                    first = aligned(at * length + start // cells * length, count)
                    stack.append(ref[pl.ds(first, count), :])
                stacks.append(jnp.concatenate(stack, axis=0))
            near = dot(near_m[...], jnp.concatenate(stacks, axis=1))
            near = near + lines[step, offset : offset + shape.rows, :]
            for part, start in enumerate(starts):
                cols = slice(part * lanes, (part + 1) * lanes)
                rows = pl.ds(aligned(at * cells + start, shape.rows), shape.rows)
                source = load_ref[rows, :].astype(F32)
                if with_flux:
                    source = source + placed[step, offset : offset + shape.rows, cols]
                    source_ref[rows, :] = source.astype(BF)
                centre = field_ref[rows, :].astype(F32)
                fresh = (1.0 - OMEGA) * centre + weights * (source + near[:, cols])
                to = pl.ds(aligned(local * cells + start, shape.rows), shape.rows)
                out_ref[to, :] = fresh.astype(BF)
                if not last:
                    tall[step, start : start + shape.rows, :] = fresh

    def emit(step):
        at, size = step * shape.block, shape.block * cells
        fresh = out_ref[at * cells : at * cells + size, :]
        emit_faces(shape, at, fresh, tall.at[step], face_refs, z_ref, ends_m, rsum)

    steps = out_sides // shape.block
    for step in range(steps):
        work(step)
        if not last and step > 0:
            emit(step - 1)
    if not last:
        emit(steps - 1)


def sweep(shape, field, load, coef, halos, recv=(), flux_cell=None, last=False):
    lanes, cells = shape.lanes, shape.cells
    steps = shape.sides // shape.block
    grid = steps if last else 1
    half = (steps // grid, shape.half_rows, 2 * lanes)
    operands = [field, load, coef, *halos, *recv]
    out_shapes = [jax.ShapeDtypeStruct(field.shape, BF)]
    scratch = [
        pltpu.VMEM(coef.shape, F32),
        pltpu.VMEM((shape.rows, shape.rows + shape.halo_rows()), BF),
        pltpu.VMEM((2 * lanes + 4 * cells, 2 * lanes), BF),
        pltpu.VMEM(half, F32),
    ]
    if not last:
        out_shapes += face_outputs(shape)
        tall, *others = face_scratch(shape)
        scratch += [pltpu.VMEM((steps, *tall.shape), F32), *others]
    if recv:
        slots = flux_cell.shape[3]
        operands.append(flux_cell)
        out_shapes += [
            jax.ShapeDtypeStruct(field.shape, BF),
            jax.ShapeDtypeStruct((recv[0].shape[0] - slots, slots * lax.axis_size("gz")), F32),
        ]
        scratch += [
            pltpu.VMEM((shape.sides, 2 * slots), F32),
            pltpu.VMEM((2 * lanes, 4 * slots), BF),
            pltpu.VMEM(half, F32),
        ]
    out_specs = [WHOLE] * len(out_shapes)
    if last:
        out_specs = [pl.BlockSpec((field.shape[0] // grid, lanes), lambda i: (i, 0))]
    return pl.pallas_call(
        functools.partial(sweep_kernel, shape, len(recv), last),
        grid=(grid,),
        in_specs=[WHOLE] * len(operands),
        out_specs=out_specs,
        out_shape=out_shapes,
        scratch_shapes=scratch,
        compiler_params=params(),
        cost_estimate=pl.CostEstimate(
            flops=6 * field.size * 128, bytes_accessed=8 * field.size, transcendentals=0
        ),
    )(*operands)


def exchange(shape, faces):
    *cut, ends = faces
    halos = [swap(value, *face) for face, value in zip(shape.faces, cut)]
    return halos + [swap(ends, "gz", turn) for turn in range(shape.ends)]


def row_gather(trace, faces):
    peers = lax.axis_size("row")
    held = {0: trace}
    bit = peers // 2
    while bit:
        pairs = [(i, i ^ bit) for i in range(peers)]
        fresh = {key ^ bit: lax.ppermute(held[key], "row", pairs) for key in sorted(held, reverse=True)}
        if bit == peers // 2:
            held, fresh, _ = lax.optimization_barrier((held, fresh, faces))
        held.update(fresh)
        bit //= 2
    return [held[key] for key in range(peers)]


def per_device(volume_field, volume_load, coefficient, surface_block, trace_cell, flux_cell):
    sides, first, second, lanes = volume_field.shape
    cells = first * second
    shape = Shape(sides, first, second, lanes)
    field = volume_field.reshape(sides * cells, lanes)
    load = volume_load.reshape(sides * cells, lanes)
    coef = coefficient.reshape(cells, lanes)

    slots = trace_cell.shape[3]
    trace = traces(volume_field.reshape(sides, cells, lanes), trace_cell, min(32, sides))
    *faces, held = first_faces(shape, field, surface_block, slots)
    parts = row_gather(trace, faces)
    halos = exchange(shape, faces)
    early = len([face for face in shape.faces if face[0] == "col"])
    parts, halos[:early] = lax.optimization_barrier((parts, halos[:early]))
    recv, halos[early:] = flux_sums(parts, held, halos[early:])

    current, *faces, source, surface_flux = sweep(
        shape, field, load, coef, halos, recv=recv, flux_cell=flux_cell
    )
    current, *faces = sweep(shape, current, source, coef, exchange(shape, faces))
    (current,) = sweep(shape, current, source, coef, exchange(shape, faces), last=True)
    return current.reshape(volume_field.shape), surface_flux


def solution(mesh):
    in_specs = (
        P(None, "row", "col", "gz"),
        P(None, "row", "col", "gz"),
        P("row", "col", "gz"),
        P("row", "col"),
        P("row", "col", "gz", None),
        P("row", "col", "gz", None),
    )
    out_specs = (P(None, "row", "col", "gz"), P("gz", ("row", "col")))
    return jax.shard_map(
        per_device, mesh=mesh, in_specs=in_specs, out_specs=out_specs, check_vma=False
    )
```

```python
import functools

import jax
import jax.numpy as jnp
from jax import lax
from jax.experimental import pallas as pl
from jax.experimental.pallas import tpu as pltpu
from jax.sharding import PartitionSpec as P

OMEGA = 0.8
BF = jnp.bfloat16
F32 = jnp.float32
WHOLE = pl.BlockSpec(memory_space=pltpu.VMEM)


def aligned(start, unit):
    return start if isinstance(start, int) else pl.multiple_of(start, unit)


def iota(shape, dim):
    return lax.broadcasted_iota(jnp.int32, shape, dim)


def dot(a, b):
    return jnp.dot(a, b, preferred_element_type=F32)


def dot_nt(a, b):
    return lax.dot_general(a, b, (((1,), (1,)), ((), ())), preferred_element_type=F32)


FACES_MIB = 50


def params(mebibytes=24):
    return pltpu.CompilerParams(vmem_limit_bytes=mebibytes * 1024 * 1024)


def trace_kernel(stride, block, field_ref, cell_ref, out_ref, field, cell_v, tall, near, place, picked, sems):
    sides, rows, lanes = field.shape
    slots = cell_ref.shape[3]
    per_row = lanes // stride
    width = near.shape[0]
    parts = slots // width
    cell_copy = pltpu.make_async_copy(cell_ref, cell_v, sems.at[sides // block])
    cell_copy.start()
    copies = []
    for step in range(sides // block):
        span = pl.ds(step * block, block)
        copies.append(pltpu.make_async_copy(field_ref.at[span], field.at[span], sems.at[step]))
        copies[-1].start()

    cell_copy.wait()
    cell = cell_v[0, 0]
    run = cell // stride
    digit = jnp.zeros_like(cell)
    for part in range(parts):
        digit = jnp.where(run // width == part, (cell % stride) * stride**part, digit)
    hit = iota((width, slots), 0) == run % width
    near[...] = hit.astype(BF)
    digits = jnp.sum(jnp.where(hit, digit.astype(F32), 0.0), axis=1, keepdims=True)
    digits = jnp.broadcast_to(digits, (width, 128)).T[0:8].astype(jnp.int32)
    first = iota((8, width), 1) % per_row * stride
    for part in range(parts):
        place[:, part * width : (part + 1) * width] = first + digits // stride**part % stride

    together = 128 // per_row
    group = iota((8, 128), 1) // per_row
    for step in range(sides // block):
        copies[step].wait()
        span = field[step * block : (step + 1) * block]
        tall[step] = span.reshape(block * rows, lanes).astype(F32)

        for batch in range(block // 8):
            for tile in range(rows // together):
                cols = slice(tile * 128, (tile + 1) * 128)
                where = place[:, cols]
                found = None
                for row in range(together):
                    start = batch * 8 * rows + tile * together + row
                    line = tall[step, pl.ds(start, 8, stride=rows), :]
                    line = jnp.take_along_axis(line, where, axis=1)
                    found = line if found is None else jnp.where(group == row, line, found)
                at = step * block + batch * 8
                picked[at : at + 8, cols] = found

    total = jnp.zeros((sides, slots), F32)
    for part in range(parts):
        sorted_runs = picked[:, part * width : (part + 1) * width].astype(BF)
        total = jnp.where(run // width == part, dot(sorted_runs, near[...]), total)
    out_ref[...] = total.T.astype(BF)


def traces(field, trace_cell, block):
    sides, rows, lanes = field.shape
    slots = trace_cell.shape[3]
    stride = rows * lanes // slots
    width = min(slots, 256)
    hbm = pl.BlockSpec(memory_space=pltpu.HBM)
    return pl.pallas_call(
        functools.partial(trace_kernel, stride, block),
        in_specs=[hbm, hbm],
        out_specs=WHOLE,
        out_shape=jax.ShapeDtypeStruct((slots, sides), BF),
        scratch_shapes=[
            pltpu.VMEM(field.shape, BF),
            pltpu.VMEM(trace_cell.shape, jnp.int32),
            pltpu.VMEM((sides // block, block * rows, lanes), F32),
            pltpu.VMEM((width, slots), BF),
            pltpu.VMEM((8, slots), jnp.int32),
            pltpu.VMEM((sides, slots), F32),
            pltpu.SemaphoreType.DMA((sides // block + 1,)),
        ],
        compiler_params=params(62),
        cost_estimate=pl.CostEstimate(
            flops=4 * sides * rows * lanes * 128, bytes_accessed=field.size * 2, transcendentals=0
        ),
    )(field, trace_cell)


def fetch_columns(block_ref, held, sems, slots):
    me, group, gzs = lax.axis_index("row"), lax.axis_index("gz"), lax.axis_size("gz")
    copies = []
    for key in range(held.shape[0]):
        start = pl.multiple_of((jnp.bitwise_xor(me, key) * gzs + group) * slots, slots)
        copies.append(
            pltpu.make_async_copy(block_ref.at[:, pl.ds(start, slots)], held.at[key], sems.at[key])
        )
        copies[-1].start()
    return copies


def surface_kernel(halves, *refs):
    ins, total = refs[:-1], refs[-1]
    outs = ins[len(ins) - halves :]
    *parts, held = ins[: len(ins) - halves]
    value = None
    for key, part in enumerate(parts):
        term = dot(held[key], part[...])
        value = term if value is None else value + term
    if halves == 1:
        outs[0][...] = value
        return
    total[...] = value
    count = outs[0].shape[0]
    mine = lax.axis_index("col")
    for key, out in enumerate(outs):
        out[...] = total[pl.ds(pl.multiple_of((mine ^ key) * count, 8), count), :]


def surface(parts, held, halves):
    sides = parts[0].shape[1]
    lines = held.shape[1]
    return pl.pallas_call(
        functools.partial(surface_kernel, halves),
        in_specs=[WHOLE] * (len(parts) + 1),
        out_specs=[WHOLE] * halves,
        out_shape=[jax.ShapeDtypeStruct((lines // halves, sides), F32)] * halves,
        scratch_shapes=[pltpu.VMEM((lines, sides), F32)],
        compiler_params=params(),
        cost_estimate=pl.CostEstimate(
            flops=2 * sides * held.size, bytes_accessed=2 * held.size, transcendentals=0
        ),
    )(*parts, held)


def share_kernel(peers, mine_ref, other_ref, *refs):
    *outs, total, turned = refs
    total[...] = mine_ref[...] + other_ref[...]
    turned[...] = total[...].T
    lines, sides = total.shape
    group = lax.axis_index("gz")
    for key, out in enumerate(outs):
        peer = group ^ key
        rows, some = lines // peers, sides // peers
        out[:rows, :] = total[pl.ds(pl.multiple_of(peer * rows, 8), rows), :]
        out[rows:, :] = turned[pl.ds(pl.multiple_of(peer * some, 8), some), :]


def shares(mine, other):
    peers = lax.axis_size("gz")
    lines, sides = mine.shape
    out = jax.ShapeDtypeStruct(((lines + sides) // peers, sides), F32)
    return pl.pallas_call(
        functools.partial(share_kernel, peers),
        in_specs=[WHOLE] * 2,
        out_specs=[WHOLE] * peers,
        out_shape=[out] * peers,
        scratch_shapes=[pltpu.VMEM((lines, sides), F32), pltpu.VMEM((sides, lines), F32)],
        compiler_params=params(),
        cost_estimate=pl.CostEstimate(
            flops=lines * sides, bytes_accessed=16 * lines * sides, transcendentals=0
        ),
    )(mine, other)


def flux_sums(parts, held, late):
    cols, gzs = lax.axis_size("col"), lax.axis_size("gz")
    sides = parts[0].shape[1]
    lines = held.shape[1]
    if cols == 2 and gzs & (gzs - 1) == 0 and lines // cols == sides and sides // gzs % 8 == 0:
        mine, other = surface(parts, held, 2)
        other = lax.ppermute(other, "col", [(0, 1), (1, 0)])
        sent = shares(mine, other)
        sent, late = lax.optimization_barrier((sent, late))
        recv = [sent[0]]
        for key in range(gzs - 1, 0, -1):
            recv.append(lax.ppermute(sent[key], "gz", [(i, i ^ key) for i in range(gzs)]))
        return recv, late
    (total,) = surface(parts, held, 1)
    rows = lax.psum_scatter(total, "col", scatter_dimension=0, tiled=True)
    owned = lax.psum_scatter(rows, "gz", scatter_dimension=0, tiled=True)
    flux = lax.psum_scatter(rows.T, "gz", scatter_dimension=0, tiled=True)
    flux = jnp.pad(flux, ((0, 0), (0, sides - flux.shape[1])))
    return [jnp.concatenate([owned, flux], axis=0)], late


def turns(axis):
    return 1 if lax.axis_size(axis) == 2 else 2


def partner(index, turn):
    return jnp.where(index % 2 == turn, index + 1, index - 1)


def has_neighbour(axis, turn):
    other = partner(lax.axis_index(axis), turn)
    return (other >= 0) & (other < lax.axis_size(axis))


def swap(value, axis, turn):
    axes = ("row", "col", "gz")
    sizes = [lax.axis_size(name) for name in axes]
    along = axes.index(axis)
    spare = 0 if axis == "gz" else 2
    pairs = []
    for r in range(sizes[0]):
        for c in range(sizes[1]):
            for g in range(sizes[2]):
                here = [r, c, g]
                there = [r, c, g]
                there[along] += 1 if here[along] % 2 == turn else -1
                if not 0 <= there[along] < sizes[along]:
                    there[along] = here[along]
                    if here[spare] ^ 1 < sizes[spare]:
                        there[spare] ^= 1
                flat = [(at[0] * sizes[1] + at[1]) * sizes[2] + at[2] for at in (here, there)]
                pairs.append(tuple(flat))
    return lax.ppermute(value, axes, pairs)


class Shape:
    def __init__(self, sides, first, second, lanes):
        self.sides, self.x, self.y, self.lanes = sides, first, second, lanes
        self.cells = first * second
        self.chunk = max(1, 128 // self.cells)
        self.rows = self.chunk * self.cells
        self.block = min(sides, 32)
        self.half = self.block // 2
        self.half_rows = self.half * self.cells
        self.faces = [("col", i) for i in range(turns("col"))]
        self.faces += [("row", i) for i in reversed(range(turns("row")))]
        self.ends = turns("gz")

    def face_len(self, face):
        return self.y if face[0] == "row" else self.x

    def halo_rows(self):
        return sum(self.chunk * self.face_len(face) for face in self.faces)

    def edge(self, face):
        axis, turn = face
        last = (self.x if axis == "row" else self.y) - 1
        return jnp.where(lax.axis_index(axis) % 2 == turn, last, 0)


def halo_place(shape):
    dims = (shape.rows, shape.halo_rows())
    row, col = iota(dims, 0), iota(dims, 1)
    side, cell = row // shape.cells, row % shape.cells
    x, y = cell // shape.y, cell % shape.y
    hit, base = None, 0
    for face in shape.faces:
        length = shape.face_len(face)
        along, across = (y, x) if face[0] == "row" else (x, y)
        place = (across == shape.edge(face)) & (col - base == side * length + along)
        place = place & has_neighbour(*face)
        hit = place if hit is None else hit | place
        base += shape.chunk * length
    return hit.astype(BF)


def z_mask(shape, count):
    dims = (count * shape.cells, 2 * shape.cells)
    return iota(dims, 1) % shape.cells == iota(dims, 0) % shape.cells


def twice(matrix):
    zero = jnp.zeros_like(matrix)
    return jnp.concatenate(
        [jnp.concatenate([matrix, zero], axis=1), jnp.concatenate([zero, matrix], axis=1)], axis=0
    )


def beside(values):
    half = values.shape[0] // 2
    return jnp.concatenate([values[:half], values[half:]], axis=1)


def build_out(shape, ends_m, rsum):
    dims = (shape.lanes, 2 * shape.cells)
    edge = jnp.where(iota(dims, 1) < shape.cells, 0, shape.lanes - 1)
    ends_m[...] = twice((iota(dims, 0) == edge).astype(F32)).astype(BF)
    dims = rsum.shape
    rsum[...] = (iota(dims, 1) // shape.cells == iota(dims, 0)).astype(BF)


def emit_faces(shape, at, values, tall, face_refs, z_ref, ends_m, rsum):
    for face, ref in zip(shape.faces, face_refs):
        length, edge = shape.face_len(face), shape.edge(face)
        lines = []
        for side in range(shape.block):
            start = side * shape.cells
            if face[0] == "row":
                lines.append(tall[pl.ds(aligned(start + edge * length, 8), length), :])
            else:
                lines.append(tall[pl.ds(start + edge, length, stride=shape.y), :])
        span = shape.block * length
        ref[pl.ds(aligned(at * length, span), span), :] = jnp.concatenate(
            lines, axis=0
        ).astype(BF)
    mask = jnp.concatenate([z_mask(shape, shape.half)] * 2, axis=1)
    tips = jnp.where(mask, dot(beside(values), ends_m[...]), 0.0).astype(BF)
    tips = dot(rsum[...], tips)[: shape.half]
    tips = jnp.concatenate([tips[:, : 2 * shape.cells], tips[:, 2 * shape.cells :]], axis=0)
    z_ref[pl.ds(aligned(at, shape.block), shape.block), :] = tips.astype(BF)


def faces_kernel(shape, slots, field_ref, block_ref, *refs):
    *face_refs, z_ref, held, field, tall, ends_m, rsum, sems, field_sems = refs
    size = shape.block * shape.cells
    steps = shape.sides // shape.block
    copies = []
    for step in range(steps):
        span = pl.ds(step * size, size)
        copies.append(
            pltpu.make_async_copy(field_ref.at[span], field.at[span], field_sems.at[step])
        )
        copies[-1].start()
    columns = fetch_columns(block_ref, held, sems, slots)
    build_out(shape, ends_m, rsum)
    for step in range(steps):
        copies[step].wait()
        values = field[step * size : (step + 1) * size, :]
        tall[step] = values.astype(F32)
        emit_faces(shape, step * shape.block, values, tall.at[step], face_refs, z_ref, ends_m, rsum)
    for copy in columns:
        copy.wait()


def face_outputs(shape):
    shapes = [
        jax.ShapeDtypeStruct((shape.sides * shape.face_len(face), shape.lanes), BF)
        for face in shape.faces
    ]
    return shapes + [jax.ShapeDtypeStruct((shape.sides, 2 * shape.cells), BF)]


def face_scratch(shape):
    return [
        pltpu.VMEM((shape.block * shape.cells, shape.lanes), F32),
        pltpu.VMEM((2 * shape.lanes, 4 * shape.cells), BF),
        pltpu.VMEM((max(8, shape.half), shape.half_rows), BF),
    ]


def first_faces(shape, field, block, slots):
    peers = lax.axis_size("row")
    steps = shape.sides // shape.block
    shapes = face_outputs(shape)
    shapes.append(jax.ShapeDtypeStruct((peers, block.shape[0], slots), BF))
    tall, *others = face_scratch(shape)
    return pl.pallas_call(
        functools.partial(faces_kernel, shape, slots),
        in_specs=[pl.BlockSpec(memory_space=pltpu.HBM)] * 2,
        out_specs=[WHOLE] * len(shapes),
        out_shape=shapes,
        scratch_shapes=[
            pltpu.VMEM(field.shape, BF),
            pltpu.VMEM((steps, *tall.shape), F32),
            *others,
            pltpu.SemaphoreType.DMA((peers,)),
            pltpu.SemaphoreType.DMA((steps,)),
        ],
        compiler_params=params(FACES_MIB),
        cost_estimate=pl.CostEstimate(
            flops=field.size * 128, bytes_accessed=4 * field.size, transcendentals=0
        ),
    )(field, block)


def sweep_kernel(shape, recvs, last, *refs):
    with_flux = recvs > 0
    refs = list(refs)
    take = lambda count: [refs.pop(0) for _ in range(count)]
    field_ref, load_ref, coef_ref = take(3)
    halo_refs = take(len(shape.faces))
    end_refs = take(shape.ends)
    if with_flux:
        recv_refs = take(recvs)
        (cell_ref,) = take(1)
    (out_ref,) = take(1)
    if not last:
        face_refs = take(len(shape.faces))
        (z_ref,) = take(1)
    if with_flux:
        source_ref, flux_ref = take(2)
    weight, near_m, line_m, lines = take(4)
    if last:
        result_ref = out_ref
        out_ref, out_sems = take(2)
    else:
        tall, ends_m, rsum = take(3)
    if with_flux:
        phi, cell_m, placed = take(3)

    cells, lanes = shape.cells, shape.lanes

    def prepare():
        weight[...] = OMEGA / (6.0 + coef_ref[...])
        dims = (shape.rows, shape.rows)
        row, col = iota(dims, 0), iota(dims, 1)
        x, y = row % cells // shape.y, row % shape.y
        x2, y2 = col % cells // shape.y, col % shape.y
        near = ((x == x2) & (jnp.abs(y - y2) == 1)) | ((y == y2) & (jnp.abs(x - x2) == 1))
        near_m[:, : shape.rows] = (near & (row // cells == col // cells)).astype(BF)
        near_m[:, shape.rows :] = halo_place(shape)
        dims = (lanes, lanes)
        line = (jnp.abs(iota(dims, 0) - iota(dims, 1)) == 1).astype(F32)
        line_m[: 2 * lanes, :] = twice(line).astype(BF)
        dims = (2 * cells, lanes)
        edge = jnp.where(iota(dims, 0) < cells, lanes - 1, 0)
        line_m[2 * lanes :, :] = twice((iota(dims, 1) == edge).astype(F32)).astype(BF)
        if not last:
            build_out(shape, ends_m, rsum)
        if with_flux:
            slots = cell_ref.shape[3]
            owned = recv_refs[0][...]
            for ref in recv_refs[1:]:
                owned = owned + ref[...]
            flux_ref[...] = owned[slots:, : flux_ref.shape[1]]
            owned = owned[:slots]
            high = owned.astype(BF).astype(F32)
            both = jnp.concatenate([high, owned - high], axis=0)
            phi[...] = both.T
            cell = jnp.concatenate([cell_ref[0, 0]] * 2, axis=1)
            cell_m[...] = twice((iota((lanes, 2 * slots), 0) == cell % lanes).astype(F32)).astype(BF)

    prepare()
    mask = z_mask(shape, 1)
    even = lax.axis_index("gz") % 2 == 0
    filled = (iota((shape.block, 2 * cells), 1) < cells) == even
    if with_flux:
        slots = cell_ref.shape[3]
        cell = jnp.concatenate([cell_ref[0, 0]] * 2, axis=1)
        cell_mask = iota((cells, 2 * slots), 0) == cell // lanes
    weights = jnp.concatenate([weight[...]] * shape.chunk, axis=0)

    def expand(lines, where, first):
        rows = []
        for side in range(first, first + shape.half):
            line = jnp.broadcast_to(lines[side : side + 1], where.shape)
            rows.append(jnp.where(where, line, 0.0))
        return jnp.concatenate(rows, axis=0).astype(BF)

    def work(step):
        at = step * shape.block
        sides = pl.ds(aligned(at, shape.block), shape.block)
        size = shape.block * cells
        zs = 0.0
        for turn in range(shape.ends):
            wanted = (filled == (turn == 0)) & has_neighbour("gz", turn)
            zs = jnp.where(wanted, end_refs[turn][sides, :].astype(F32), zs)
        values = field_ref[pl.ds(aligned(at * cells, size), size), :]
        left = [beside(values), expand(zs, mask, 0), expand(zs, mask, shape.half)]
        lines[step] = dot(jnp.concatenate(left, axis=1), line_m[...])
        if with_flux:
            phis = phi[sides, :]
            left = [expand(phis, cell_mask, 0), expand(phis, cell_mask, shape.half)]
            placed[step] = dot_nt(jnp.concatenate(left, axis=1), cell_m[...])
        for index in range(shape.half // shape.chunk):
            offset = index * shape.rows
            starts = (offset, offset + shape.half_rows)
            stacks = []
            for start in starts:
                rows = pl.ds(aligned(at * cells + start, shape.rows), shape.rows)
                stack = [field_ref[rows, :]]
                for face, ref in zip(shape.faces, halo_refs):
                    length = shape.face_len(face)
                    count = shape.chunk * length
                    first = aligned(at * length + start // cells * length, count)
                    stack.append(ref[pl.ds(first, count), :])
                stacks.append(jnp.concatenate(stack, axis=0))
            near = dot(near_m[...], jnp.concatenate(stacks, axis=1))
            near = near + lines[step, offset : offset + shape.rows, :]
            for part, start in enumerate(starts):
                cols = slice(part * lanes, (part + 1) * lanes)
                rows = pl.ds(aligned(at * cells + start, shape.rows), shape.rows)
                source = load_ref[rows, :].astype(F32)
                if with_flux:
                    source = source + placed[step, offset : offset + shape.rows, cols]
                    source_ref[rows, :] = source.astype(BF)
                centre = field_ref[rows, :].astype(F32)
                fresh = (1.0 - OMEGA) * centre + weights * (source + near[:, cols])
                out_ref[rows, :] = fresh.astype(BF)
                if not last:
                    tall[step, start : start + shape.rows, :] = fresh

    def emit(step):
        at, size = step * shape.block, shape.block * cells
        fresh = out_ref[at * cells : at * cells + size, :]
        emit_faces(shape, at, fresh, tall.at[step], face_refs, z_ref, ends_m, rsum)

    steps = shape.sides // shape.block
    copies = []
    for step in range(steps):
        work(step)
        if last:
            span = pl.ds(step * shape.block * cells, shape.block * cells)
            copies.append(
                pltpu.make_async_copy(out_ref.at[span], result_ref.at[span], out_sems.at[step])
            )
            copies[-1].start()
        elif step > 0:
            emit(step - 1)
    for copy in copies:
        copy.wait()
    if not last:
        emit(steps - 1)


def sweep(shape, field, load, coef, halos, recv=(), flux_cell=None, last=False):
    lanes, cells = shape.lanes, shape.cells
    steps = shape.sides // shape.block
    half = (steps, shape.half_rows, 2 * lanes)
    operands = [field, load, coef, *halos, *recv]
    out_shapes = [jax.ShapeDtypeStruct(field.shape, BF)]
    scratch = [
        pltpu.VMEM(coef.shape, F32),
        pltpu.VMEM((shape.rows, shape.rows + shape.halo_rows()), BF),
        pltpu.VMEM((2 * lanes + 4 * cells, 2 * lanes), BF),
        pltpu.VMEM(half, F32),
    ]
    if last:
        scratch += [pltpu.VMEM(field.shape, BF), pltpu.SemaphoreType.DMA((steps,))]
    else:
        out_shapes += face_outputs(shape)
        tall, *others = face_scratch(shape)
        scratch += [pltpu.VMEM((steps, *tall.shape), F32), *others]
    if recv:
        slots = flux_cell.shape[3]
        operands.append(flux_cell)
        out_shapes += [
            jax.ShapeDtypeStruct(field.shape, BF),
            jax.ShapeDtypeStruct((recv[0].shape[0] - slots, slots * lax.axis_size("gz")), F32),
        ]
        scratch += [
            pltpu.VMEM((shape.sides, 2 * slots), F32),
            pltpu.VMEM((2 * lanes, 4 * slots), BF),
            pltpu.VMEM(half, F32),
        ]
    out_specs = [WHOLE] * len(out_shapes)
    if last:
        out_specs = [pl.BlockSpec(memory_space=pltpu.HBM)]
    return pl.pallas_call(
        functools.partial(sweep_kernel, shape, len(recv), last),
        in_specs=[WHOLE] * len(operands),
        out_specs=out_specs,
        out_shape=out_shapes,
        scratch_shapes=scratch,
        compiler_params=params(),
        cost_estimate=pl.CostEstimate(
            flops=6 * field.size * 128, bytes_accessed=8 * field.size, transcendentals=0
        ),
    )(*operands)


def exchange(shape, faces):
    *cut, ends = faces
    halos = [swap(value, *face) for face, value in zip(shape.faces, cut)]
    return halos + [swap(ends, "gz", turn) for turn in range(shape.ends)]


def row_gather(trace, faces):
    peers = lax.axis_size("row")
    held = {0: trace}
    bit = peers // 2
    while bit:
        pairs = [(i, i ^ bit) for i in range(peers)]
        fresh = {key ^ bit: lax.ppermute(held[key], "row", pairs) for key in sorted(held, reverse=True)}
        if bit == peers // 2:
            held, fresh, _ = lax.optimization_barrier((held, fresh, faces))
        held.update(fresh)
        bit //= 2
    return [held[key] for key in range(peers)]


def per_device(volume_field, volume_load, coefficient, surface_block, trace_cell, flux_cell):
    sides, first, second, lanes = volume_field.shape
    cells = first * second
    shape = Shape(sides, first, second, lanes)
    field = volume_field.reshape(sides * cells, lanes)
    load = volume_load.reshape(sides * cells, lanes)
    coef = coefficient.reshape(cells, lanes)

    slots = trace_cell.shape[3]
    trace = traces(volume_field.reshape(sides, cells, lanes), trace_cell, min(32, sides))
    *faces, held = first_faces(shape, field, surface_block, slots)
    parts = row_gather(trace, faces)
    halos = exchange(shape, faces)
    late = shape.faces.index(("row", 1)) if ("row", 1) in shape.faces else 0
    rest = [halo for place, halo in enumerate(halos) if place != late]
    parts, rest = lax.optimization_barrier((parts, rest))
    recv, halo = flux_sums(parts, held, halos[late])
    halos = rest[:late] + [halo] + rest[late:]

    current, *faces, source, surface_flux = sweep(
        shape, field, load, coef, halos, recv=recv, flux_cell=flux_cell
    )
    current, *faces = sweep(shape, current, source, coef, exchange(shape, faces))
    (current,) = sweep(shape, current, source, coef, exchange(shape, faces), last=True)
    return current.reshape(volume_field.shape), surface_flux


def solution(mesh):
    in_specs = (
        P(None, "row", "col", "gz"),
        P(None, "row", "col", "gz"),
        P("row", "col", "gz"),
        P("row", "col"),
        P("row", "col", "gz", None),
        P("row", "col", "gz", None),
    )
    out_specs = (P(None, "row", "col", "gz"), P("gz", ("row", "col")))
    return jax.shard_map(
        per_device, mesh=mesh, in_specs=in_specs, out_specs=out_specs, check_vma=False
    )
```

```python
import functools

import jax
import jax.numpy as jnp
from jax import lax
from jax.experimental import pallas as pl
from jax.experimental.pallas import tpu as pltpu
from jax.sharding import PartitionSpec as P

OMEGA = 0.8
BF = jnp.bfloat16
F32 = jnp.float32
WHOLE = pl.BlockSpec(memory_space=pltpu.VMEM)


def aligned(start, unit):
    return start if isinstance(start, int) else pl.multiple_of(start, unit)


def iota(shape, dim):
    return lax.broadcasted_iota(jnp.int32, shape, dim)


def dot(a, b):
    return jnp.dot(a, b, preferred_element_type=F32)


def dot_nt(a, b):
    return lax.dot_general(a, b, (((1,), (1,)), ((), ())), preferred_element_type=F32)


FACES_MIB = 50


def params(mebibytes=24):
    return pltpu.CompilerParams(vmem_limit_bytes=mebibytes * 1024 * 1024)


def trace_kernel(stride, block, field_ref, cell_ref, out_ref, field, cell_v, tall, near, place, picked, sems):
    sides, rows, lanes = field.shape
    slots = cell_ref.shape[3]
    per_row = lanes // stride
    width = near.shape[0]
    parts = slots // width
    cell_copy = pltpu.make_async_copy(cell_ref, cell_v, sems.at[sides // block])
    cell_copy.start()
    copies = []
    for step in range(sides // block):
        span = pl.ds(step * block, block)
        copies.append(pltpu.make_async_copy(field_ref.at[span], field.at[span], sems.at[step]))
        copies[-1].start()

    cell_copy.wait()
    cell = cell_v[0, 0]
    run = cell // stride
    digit = jnp.zeros_like(cell)
    for part in range(parts):
        digit = jnp.where(run // width == part, (cell % stride) * stride**part, digit)
    hit = iota((width, slots), 0) == run % width
    near[...] = hit.astype(BF)
    digits = jnp.sum(jnp.where(hit, digit.astype(F32), 0.0), axis=1, keepdims=True)
    digits = jnp.broadcast_to(digits, (width, 128)).T[0:8].astype(jnp.int32)
    first = iota((8, width), 1) % per_row * stride
    for part in range(parts):
        place[:, part * width : (part + 1) * width] = first + digits // stride**part % stride

    together = 128 // per_row
    group = iota((8, 128), 1) // per_row
    for step in range(sides // block):
        copies[step].wait()
        span = field[step * block : (step + 1) * block]
        tall[step] = span.reshape(block * rows, lanes).astype(F32)

        for batch in range(block // 8):
            for tile in range(rows // together):
                cols = slice(tile * 128, (tile + 1) * 128)
                where = place[:, cols]
                found = None
                for row in range(together):
                    start = batch * 8 * rows + tile * together + row
                    line = tall[step, pl.ds(start, 8, stride=rows), :]
                    line = jnp.take_along_axis(line, where, axis=1)
                    found = line if found is None else jnp.where(group == row, line, found)
                at = step * block + batch * 8
                picked[at : at + 8, cols] = found

    total = jnp.zeros((sides, slots), F32)
    for part in range(parts):
        sorted_runs = picked[:, part * width : (part + 1) * width].astype(BF)
        total = jnp.where(run // width == part, dot(sorted_runs, near[...]), total)
    out_ref[...] = total.T.astype(BF)


def traces(field, trace_cell, block):
    sides, rows, lanes = field.shape
    slots = trace_cell.shape[3]
    stride = rows * lanes // slots
    width = min(slots, 256)
    hbm = pl.BlockSpec(memory_space=pltpu.HBM)
    return pl.pallas_call(
        functools.partial(trace_kernel, stride, block),
        in_specs=[hbm, hbm],
        out_specs=WHOLE,
        out_shape=jax.ShapeDtypeStruct((slots, sides), BF),
        scratch_shapes=[
            pltpu.VMEM(field.shape, BF),
            pltpu.VMEM(trace_cell.shape, jnp.int32),
            pltpu.VMEM((sides // block, block * rows, lanes), F32),
            pltpu.VMEM((width, slots), BF),
            pltpu.VMEM((8, slots), jnp.int32),
            pltpu.VMEM((sides, slots), F32),
            pltpu.SemaphoreType.DMA((sides // block + 1,)),
        ],
        compiler_params=params(62),
        cost_estimate=pl.CostEstimate(
            flops=4 * sides * rows * lanes * 128, bytes_accessed=field.size * 2, transcendentals=0
        ),
    )(field, trace_cell)


def fetch_columns(block_ref, held, sems, slots):
    me, group, gzs = lax.axis_index("row"), lax.axis_index("gz"), lax.axis_size("gz")
    copies = []
    for key in range(held.shape[0]):
        start = pl.multiple_of((jnp.bitwise_xor(me, key) * gzs + group) * slots, slots)
        copies.append(
            pltpu.make_async_copy(block_ref.at[:, pl.ds(start, slots)], held.at[key], sems.at[key])
        )
        copies[-1].start()
    return copies


def surface_kernel(halves, *refs):
    ins, total = refs[:-1], refs[-1]
    outs = ins[len(ins) - halves :]
    *parts, held = ins[: len(ins) - halves]
    value = None
    for key, part in enumerate(parts):
        term = dot(held[key], part[...])
        value = term if value is None else value + term
    if halves == 1:
        outs[0][...] = value
        return
    total[...] = value
    count = outs[0].shape[0]
    mine = lax.axis_index("col")
    for key, out in enumerate(outs):
        out[...] = total[pl.ds(pl.multiple_of((mine ^ key) * count, 8), count), :]


def surface(parts, held, halves):
    sides = parts[0].shape[1]
    lines = held.shape[1]
    return pl.pallas_call(
        functools.partial(surface_kernel, halves),
        in_specs=[WHOLE] * (len(parts) + 1),
        out_specs=[WHOLE] * halves,
        out_shape=[jax.ShapeDtypeStruct((lines // halves, sides), F32)] * halves,
        scratch_shapes=[pltpu.VMEM((lines, sides), F32)],
        compiler_params=params(),
        cost_estimate=pl.CostEstimate(
            flops=2 * sides * held.size, bytes_accessed=2 * held.size, transcendentals=0
        ),
    )(*parts, held)


def share_kernel(peers, mine_ref, other_ref, *refs):
    *outs, total, turned = refs
    total[...] = mine_ref[...] + other_ref[...]
    turned[...] = total[...].T
    lines, sides = total.shape
    group = lax.axis_index("gz")
    for key, out in enumerate(outs):
        peer = group ^ key
        rows, some = lines // peers, sides // peers
        out[:rows, :] = total[pl.ds(pl.multiple_of(peer * rows, 8), rows), :]
        out[rows:, :] = turned[pl.ds(pl.multiple_of(peer * some, 8), some), :]


def shares(mine, other):
    peers = lax.axis_size("gz")
    lines, sides = mine.shape
    out = jax.ShapeDtypeStruct(((lines + sides) // peers, sides), F32)
    return pl.pallas_call(
        functools.partial(share_kernel, peers),
        in_specs=[WHOLE] * 2,
        out_specs=[WHOLE] * peers,
        out_shape=[out] * peers,
        scratch_shapes=[pltpu.VMEM((lines, sides), F32), pltpu.VMEM((sides, lines), F32)],
        compiler_params=params(),
        cost_estimate=pl.CostEstimate(
            flops=lines * sides, bytes_accessed=16 * lines * sides, transcendentals=0
        ),
    )(mine, other)


def flux_sums(parts, held, late):
    cols, gzs = lax.axis_size("col"), lax.axis_size("gz")
    sides = parts[0].shape[1]
    lines = held.shape[1]
    if cols == 2 and gzs & (gzs - 1) == 0 and lines // cols == sides and sides // gzs % 8 == 0:
        mine, other = surface(parts, held, 2)
        other = lax.ppermute(other, "col", [(0, 1), (1, 0)])
        other, late = lax.optimization_barrier((other, late))
        sent = shares(mine, other)
        recv = [sent[0]]
        for key in range(gzs - 1, 0, -1):
            recv.append(lax.ppermute(sent[key], "gz", [(i, i ^ key) for i in range(gzs)]))
        return recv, late
    (total,) = surface(parts, held, 1)
    rows = lax.psum_scatter(total, "col", scatter_dimension=0, tiled=True)
    owned = lax.psum_scatter(rows, "gz", scatter_dimension=0, tiled=True)
    flux = lax.psum_scatter(rows.T, "gz", scatter_dimension=0, tiled=True)
    flux = jnp.pad(flux, ((0, 0), (0, sides - flux.shape[1])))
    return [jnp.concatenate([owned, flux], axis=0)], late


def turns(axis):
    return 1 if lax.axis_size(axis) == 2 else 2


def partner(index, turn):
    return jnp.where(index % 2 == turn, index + 1, index - 1)


def has_neighbour(axis, turn):
    other = partner(lax.axis_index(axis), turn)
    return (other >= 0) & (other < lax.axis_size(axis))


def swap(value, axis, turn):
    axes = ("row", "col", "gz")
    sizes = [lax.axis_size(name) for name in axes]
    along = axes.index(axis)
    spare = 0 if axis == "gz" else 2
    pairs = []
    for r in range(sizes[0]):
        for c in range(sizes[1]):
            for g in range(sizes[2]):
                here = [r, c, g]
                there = [r, c, g]
                there[along] += 1 if here[along] % 2 == turn else -1
                if not 0 <= there[along] < sizes[along]:
                    there[along] = here[along]
                    if here[spare] ^ 1 < sizes[spare]:
                        there[spare] ^= 1
                flat = [(at[0] * sizes[1] + at[1]) * sizes[2] + at[2] for at in (here, there)]
                pairs.append(tuple(flat))
    return lax.ppermute(value, axes, pairs)


class Shape:
    def __init__(self, sides, first, second, lanes):
        self.sides, self.x, self.y, self.lanes = sides, first, second, lanes
        self.cells = first * second
        self.chunk = max(1, 128 // self.cells)
        self.rows = self.chunk * self.cells
        self.block = min(sides, 32)
        self.half = self.block // 2
        self.half_rows = self.half * self.cells
        self.faces = [("col", i) for i in range(turns("col"))]
        self.faces += [("row", i) for i in reversed(range(turns("row")))]
        self.ends = turns("gz")

    def face_len(self, face):
        return self.y if face[0] == "row" else self.x

    def halo_rows(self):
        return sum(self.chunk * self.face_len(face) for face in self.faces)

    def edge(self, face):
        axis, turn = face
        last = (self.x if axis == "row" else self.y) - 1
        return jnp.where(lax.axis_index(axis) % 2 == turn, last, 0)


def halo_place(shape):
    dims = (shape.rows, shape.halo_rows())
    row, col = iota(dims, 0), iota(dims, 1)
    side, cell = row // shape.cells, row % shape.cells
    x, y = cell // shape.y, cell % shape.y
    hit, base = None, 0
    for face in shape.faces:
        length = shape.face_len(face)
        along, across = (y, x) if face[0] == "row" else (x, y)
        place = (across == shape.edge(face)) & (col - base == side * length + along)
        place = place & has_neighbour(*face)
        hit = place if hit is None else hit | place
        base += shape.chunk * length
    return hit.astype(BF)


def z_mask(shape, count):
    dims = (count * shape.cells, 2 * shape.cells)
    return iota(dims, 1) % shape.cells == iota(dims, 0) % shape.cells


def twice(matrix):
    zero = jnp.zeros_like(matrix)
    return jnp.concatenate(
        [jnp.concatenate([matrix, zero], axis=1), jnp.concatenate([zero, matrix], axis=1)], axis=0
    )


def beside(values):
    half = values.shape[0] // 2
    return jnp.concatenate([values[:half], values[half:]], axis=1)


def build_out(shape, ends_m, rsum):
    dims = (shape.lanes, 2 * shape.cells)
    edge = jnp.where(iota(dims, 1) < shape.cells, 0, shape.lanes - 1)
    ends_m[...] = twice((iota(dims, 0) == edge).astype(F32)).astype(BF)
    dims = rsum.shape
    rsum[...] = (iota(dims, 1) // shape.cells == iota(dims, 0)).astype(BF)


def emit_faces(shape, at, values, tall, face_refs, z_ref, ends_m, rsum):
    for face, ref in zip(shape.faces, face_refs):
        length, edge = shape.face_len(face), shape.edge(face)
        lines = []
        for side in range(shape.block):
            start = side * shape.cells
            if face[0] == "row":
                lines.append(tall[pl.ds(aligned(start + edge * length, 8), length), :])
            else:
                lines.append(tall[pl.ds(start + edge, length, stride=shape.y), :])
        span = shape.block * length
        ref[pl.ds(aligned(at * length, span), span), :] = jnp.concatenate(
            lines, axis=0
        ).astype(BF)
    mask = jnp.concatenate([z_mask(shape, shape.half)] * 2, axis=1)
    tips = jnp.where(mask, dot(beside(values), ends_m[...]), 0.0).astype(BF)
    tips = dot(rsum[...], tips)[: shape.half]
    tips = jnp.concatenate([tips[:, : 2 * shape.cells], tips[:, 2 * shape.cells :]], axis=0)
    z_ref[pl.ds(aligned(at, shape.block), shape.block), :] = tips.astype(BF)


def faces_kernel(shape, slots, field_ref, block_ref, *refs):
    *face_refs, z_ref, held, field, tall, ends_m, rsum, sems, field_sems = refs
    size = shape.block * shape.cells
    steps = shape.sides // shape.block
    copies = []
    for step in range(steps):
        span = pl.ds(step * size, size)
        copies.append(
            pltpu.make_async_copy(field_ref.at[span], field.at[span], field_sems.at[step])
        )
        copies[-1].start()
    columns = fetch_columns(block_ref, held, sems, slots)
    build_out(shape, ends_m, rsum)
    for step in range(steps):
        copies[step].wait()
        values = field[step * size : (step + 1) * size, :]
        tall[step] = values.astype(F32)
        emit_faces(shape, step * shape.block, values, tall.at[step], face_refs, z_ref, ends_m, rsum)
    for copy in columns:
        copy.wait()


def face_outputs(shape):
    shapes = [
        jax.ShapeDtypeStruct((shape.sides * shape.face_len(face), shape.lanes), BF)
        for face in shape.faces
    ]
    return shapes + [jax.ShapeDtypeStruct((shape.sides, 2 * shape.cells), BF)]


def face_scratch(shape):
    return [
        pltpu.VMEM((shape.block * shape.cells, shape.lanes), F32),
        pltpu.VMEM((2 * shape.lanes, 4 * shape.cells), BF),
        pltpu.VMEM((max(8, shape.half), shape.half_rows), BF),
    ]


def first_faces(shape, field, block, slots):
    peers = lax.axis_size("row")
    steps = shape.sides // shape.block
    shapes = face_outputs(shape)
    shapes.append(jax.ShapeDtypeStruct((peers, block.shape[0], slots), BF))
    tall, *others = face_scratch(shape)
    return pl.pallas_call(
        functools.partial(faces_kernel, shape, slots),
        in_specs=[pl.BlockSpec(memory_space=pltpu.HBM)] * 2,
        out_specs=[WHOLE] * len(shapes),
        out_shape=shapes,
        scratch_shapes=[
            pltpu.VMEM(field.shape, BF),
            pltpu.VMEM((steps, *tall.shape), F32),
            *others,
            pltpu.SemaphoreType.DMA((peers,)),
            pltpu.SemaphoreType.DMA((steps,)),
        ],
        compiler_params=params(FACES_MIB),
        cost_estimate=pl.CostEstimate(
            flops=field.size * 128, bytes_accessed=4 * field.size, transcendentals=0
        ),
    )(field, block)


def sweep_kernel(shape, recvs, last, *refs):
    with_flux = recvs > 0
    refs = list(refs)
    take = lambda count: [refs.pop(0) for _ in range(count)]
    field_ref, load_ref, coef_ref = take(3)
    halo_refs = take(len(shape.faces))
    end_refs = take(shape.ends)
    if with_flux:
        recv_refs = take(recvs)
        (cell_ref,) = take(1)
    (out_ref,) = take(1)
    if not last:
        face_refs = take(len(shape.faces))
        (z_ref,) = take(1)
    if with_flux:
        source_ref, flux_ref = take(2)
    weight, near_m, line_m, lines = take(4)
    if last:
        result_ref = out_ref
        out_ref, out_sems = take(2)
    else:
        tall, ends_m, rsum = take(3)
    if with_flux:
        phi, cell_m, placed = take(3)

    cells, lanes = shape.cells, shape.lanes

    def prepare():
        weight[...] = OMEGA / (6.0 + coef_ref[...])
        dims = (shape.rows, shape.rows)
        row, col = iota(dims, 0), iota(dims, 1)
        x, y = row % cells // shape.y, row % shape.y
        x2, y2 = col % cells // shape.y, col % shape.y
        near = ((x == x2) & (jnp.abs(y - y2) == 1)) | ((y == y2) & (jnp.abs(x - x2) == 1))
        near_m[:, : shape.rows] = (near & (row // cells == col // cells)).astype(BF)
        near_m[:, shape.rows :] = halo_place(shape)
        dims = (lanes, lanes)
        line = (jnp.abs(iota(dims, 0) - iota(dims, 1)) == 1).astype(F32)
        line_m[: 2 * lanes, :] = twice(line).astype(BF)
        dims = (2 * cells, lanes)
        edge = jnp.where(iota(dims, 0) < cells, lanes - 1, 0)
        line_m[2 * lanes :, :] = twice((iota(dims, 1) == edge).astype(F32)).astype(BF)
        if not last:
            build_out(shape, ends_m, rsum)
        if with_flux:
            slots = cell_ref.shape[3]
            owned = recv_refs[0][...]
            for ref in recv_refs[1:]:
                owned = owned + ref[...]
            flux_ref[...] = owned[slots:, : flux_ref.shape[1]]
            owned = owned[:slots]
            high = owned.astype(BF).astype(F32)
            both = jnp.concatenate([high, owned - high], axis=0)
            phi[...] = both.T
            cell = jnp.concatenate([cell_ref[0, 0]] * 2, axis=1)
            cell_m[...] = twice((iota((lanes, 2 * slots), 0) == cell % lanes).astype(F32)).astype(BF)

    prepare()
    mask = z_mask(shape, 1)
    even = lax.axis_index("gz") % 2 == 0
    filled = (iota((shape.block, 2 * cells), 1) < cells) == even
    if with_flux:
        slots = cell_ref.shape[3]
        cell = jnp.concatenate([cell_ref[0, 0]] * 2, axis=1)
        cell_mask = iota((cells, 2 * slots), 0) == cell // lanes
    weights = jnp.concatenate([weight[...]] * shape.chunk, axis=0)

    def expand(lines, where, first):
        rows = []
        for side in range(first, first + shape.half):
            line = jnp.broadcast_to(lines[side : side + 1], where.shape)
            rows.append(jnp.where(where, line, 0.0))
        return jnp.concatenate(rows, axis=0).astype(BF)

    def work(step):
        at = step * shape.block
        sides = pl.ds(aligned(at, shape.block), shape.block)
        size = shape.block * cells
        zs = 0.0
        for turn in range(shape.ends):
            wanted = (filled == (turn == 0)) & has_neighbour("gz", turn)
            zs = jnp.where(wanted, end_refs[turn][sides, :].astype(F32), zs)
        values = field_ref[pl.ds(aligned(at * cells, size), size), :]
        left = [beside(values), expand(zs, mask, 0), expand(zs, mask, shape.half)]
        lines[step] = dot(jnp.concatenate(left, axis=1), line_m[...])
        if with_flux:
            phis = phi[sides, :]
            left = [expand(phis, cell_mask, 0), expand(phis, cell_mask, shape.half)]
            placed[step] = dot_nt(jnp.concatenate(left, axis=1), cell_m[...])
        for index in range(shape.half // shape.chunk):
            offset = index * shape.rows
            starts = (offset, offset + shape.half_rows)
            stacks = []
            for start in starts:
                rows = pl.ds(aligned(at * cells + start, shape.rows), shape.rows)
                stack = [field_ref[rows, :]]
                for face, ref in zip(shape.faces, halo_refs):
                    length = shape.face_len(face)
                    count = shape.chunk * length
                    first = aligned(at * length + start // cells * length, count)
                    stack.append(ref[pl.ds(first, count), :])
                stacks.append(jnp.concatenate(stack, axis=0))
            near = dot(near_m[...], jnp.concatenate(stacks, axis=1))
            near = near + lines[step, offset : offset + shape.rows, :]
            for part, start in enumerate(starts):
                cols = slice(part * lanes, (part + 1) * lanes)
                rows = pl.ds(aligned(at * cells + start, shape.rows), shape.rows)
                source = load_ref[rows, :].astype(F32)
                if with_flux:
                    source = source + placed[step, offset : offset + shape.rows, cols]
                    source_ref[rows, :] = source.astype(BF)
                centre = field_ref[rows, :].astype(F32)
                fresh = (1.0 - OMEGA) * centre + weights * (source + near[:, cols])
                out_ref[rows, :] = fresh.astype(BF)
                if not last:
                    tall[step, start : start + shape.rows, :] = fresh

    def emit(step):
        at, size = step * shape.block, shape.block * cells
        fresh = out_ref[at * cells : at * cells + size, :]
        emit_faces(shape, at, fresh, tall.at[step], face_refs, z_ref, ends_m, rsum)

    steps = shape.sides // shape.block
    copies = []
    for step in range(steps):
        work(step)
        if last:
            span = pl.ds(step * shape.block * cells, shape.block * cells)
            copies.append(
                pltpu.make_async_copy(out_ref.at[span], result_ref.at[span], out_sems.at[step])
            )
            copies[-1].start()
        elif step > 0:
            emit(step - 1)
    for copy in copies:
        copy.wait()
    if not last:
        emit(steps - 1)


def sweep(shape, field, load, coef, halos, recv=(), flux_cell=None, last=False):
    lanes, cells = shape.lanes, shape.cells
    steps = shape.sides // shape.block
    half = (steps, shape.half_rows, 2 * lanes)
    operands = [field, load, coef, *halos, *recv]
    out_shapes = [jax.ShapeDtypeStruct(field.shape, BF)]
    scratch = [
        pltpu.VMEM(coef.shape, F32),
        pltpu.VMEM((shape.rows, shape.rows + shape.halo_rows()), BF),
        pltpu.VMEM((2 * lanes + 4 * cells, 2 * lanes), BF),
        pltpu.VMEM(half, F32),
    ]
    if last:
        scratch += [pltpu.VMEM(field.shape, BF), pltpu.SemaphoreType.DMA((steps,))]
    else:
        out_shapes += face_outputs(shape)
        tall, *others = face_scratch(shape)
        scratch += [pltpu.VMEM((steps, *tall.shape), F32), *others]
    if recv:
        slots = flux_cell.shape[3]
        operands.append(flux_cell)
        out_shapes += [
            jax.ShapeDtypeStruct(field.shape, BF),
            jax.ShapeDtypeStruct((recv[0].shape[0] - slots, slots * lax.axis_size("gz")), F32),
        ]
        scratch += [
            pltpu.VMEM((shape.sides, 2 * slots), F32),
            pltpu.VMEM((2 * lanes, 4 * slots), BF),
            pltpu.VMEM(half, F32),
        ]
    out_specs = [WHOLE] * len(out_shapes)
    if last:
        out_specs = [pl.BlockSpec(memory_space=pltpu.HBM)]
    return pl.pallas_call(
        functools.partial(sweep_kernel, shape, len(recv), last),
        in_specs=[WHOLE] * len(operands),
        out_specs=out_specs,
        out_shape=out_shapes,
        scratch_shapes=scratch,
        compiler_params=params(),
        cost_estimate=pl.CostEstimate(
            flops=6 * field.size * 128, bytes_accessed=8 * field.size, transcendentals=0
        ),
    )(*operands)


def exchange(shape, faces):
    *cut, ends = faces
    halos = [swap(value, *face) for face, value in zip(shape.faces, cut)]
    return halos + [swap(ends, "gz", turn) for turn in range(shape.ends)]


def row_gather(trace, hidden):
    peers = lax.axis_size("row")
    held = {0: trace}
    bit = peers // 2
    while bit:
        pairs = [(i, i ^ bit) for i in range(peers)]
        fresh = {key ^ bit: lax.ppermute(held[key], "row", pairs) for key in sorted(held, reverse=True)}
        if bit == peers // 2:
            held, fresh, hidden = lax.optimization_barrier((held, fresh, hidden))
        held.update(fresh)
        bit //= 2
    return [held[key] for key in range(peers)], hidden


def per_device(volume_field, volume_load, coefficient, surface_block, trace_cell, flux_cell):
    sides, first, second, lanes = volume_field.shape
    cells = first * second
    shape = Shape(sides, first, second, lanes)
    field = volume_field.reshape(sides * cells, lanes)
    load = volume_load.reshape(sides * cells, lanes)
    coef = coefficient.reshape(cells, lanes)

    slots = trace_cell.shape[3]
    trace = traces(volume_field.reshape(sides, cells, lanes), trace_cell, min(32, sides))
    *faces, held = first_faces(shape, field, surface_block, slots)
    halos = exchange(shape, faces)
    layers = len(shape.faces)
    parts, (_, ends) = row_gather(trace, (faces, halos[layers:]))
    early = len([face for face in shape.faces if face[0] == "col"])
    parts, along_col = lax.optimization_barrier((parts, halos[:early]))
    recv, along_row = flux_sums(parts, held, halos[early:layers])
    halos = along_col + along_row + ends

    current, *faces, source, surface_flux = sweep(
        shape, field, load, coef, halos, recv=recv, flux_cell=flux_cell
    )
    current, *faces = sweep(shape, current, source, coef, exchange(shape, faces))
    (current,) = sweep(shape, current, source, coef, exchange(shape, faces), last=True)
    return current.reshape(volume_field.shape), surface_flux


def solution(mesh):
    in_specs = (
        P(None, "row", "col", "gz"),
        P(None, "row", "col", "gz"),
        P("row", "col", "gz"),
        P("row", "col"),
        P("row", "col", "gz", None),
        P("row", "col", "gz", None),
    )
    out_specs = (P(None, "row", "col", "gz"), P("gz", ("row", "col")))
    return jax.shard_map(
        per_device, mesh=mesh, in_specs=in_specs, out_specs=out_specs, check_vma=False
    )
```

```python
import functools

import jax
import jax.numpy as jnp
from jax import lax
from jax.experimental import pallas as pl
from jax.experimental.pallas import tpu as pltpu
from jax.sharding import PartitionSpec as P

OMEGA = 0.8
BF = jnp.bfloat16
F32 = jnp.float32
WHOLE = pl.BlockSpec(memory_space=pltpu.VMEM)


def aligned(start, unit):
    return start if isinstance(start, int) else pl.multiple_of(start, unit)


def iota(shape, dim):
    return lax.broadcasted_iota(jnp.int32, shape, dim)


def dot(a, b):
    return jnp.dot(a, b, preferred_element_type=F32)


def dot_nt(a, b):
    return lax.dot_general(a, b, (((1,), (1,)), ((), ())), preferred_element_type=F32)


FACES_MIB = 50


def params(mebibytes=24):
    return pltpu.CompilerParams(vmem_limit_bytes=mebibytes * 1024 * 1024)


def trace_kernel(shape, stride, block, field_ref, cell_ref, out_ref, *refs):
    *face_refs, field, cell_v, tall, near, place, picked, sems = refs
    sides, rows, lanes = field.shape
    slots = cell_ref.shape[3]
    per_row = lanes // stride
    width = near.shape[0]
    parts = slots // width
    cell_copy = pltpu.make_async_copy(cell_ref, cell_v, sems.at[sides // block])
    cell_copy.start()
    copies = []
    for step in range(sides // block):
        span = pl.ds(step * block, block)
        copies.append(pltpu.make_async_copy(field_ref.at[span], field.at[span], sems.at[step]))
        copies[-1].start()

    cell_copy.wait()
    cell = cell_v[0, 0]
    run = cell // stride
    digit = jnp.zeros_like(cell)
    for part in range(parts):
        digit = jnp.where(run // width == part, (cell % stride) * stride**part, digit)
    hit = iota((width, slots), 0) == run % width
    near[...] = hit.astype(BF)
    digits = jnp.sum(jnp.where(hit, digit.astype(F32), 0.0), axis=1, keepdims=True)
    digits = jnp.broadcast_to(digits, (width, 128)).T[0:8].astype(jnp.int32)
    first = iota((8, width), 1) % per_row * stride
    for part in range(parts):
        place[:, part * width : (part + 1) * width] = first + digits // stride**part % stride

    together = 128 // per_row
    group = iota((8, 128), 1) // per_row
    for step in range(sides // block):
        copies[step].wait()
        span = field[step * block : (step + 1) * block]
        tall[step] = span.reshape(block * rows, lanes).astype(F32)
        cut_faces(shape, shape.outer, step * block, block, tall.at[step], face_refs)

        for batch in range(block // 8):
            for tile in range(rows // together):
                cols = slice(tile * 128, (tile + 1) * 128)
                where = place[:, cols]
                found = None
                for row in range(together):
                    start = batch * 8 * rows + tile * together + row
                    line = tall[step, pl.ds(start, 8, stride=rows), :]
                    line = jnp.take_along_axis(line, where, axis=1)
                    found = line if found is None else jnp.where(group == row, line, found)
                at = step * block + batch * 8
                picked[at : at + 8, cols] = found

    total = jnp.zeros((sides, slots), F32)
    for part in range(parts):
        sorted_runs = picked[:, part * width : (part + 1) * width].astype(BF)
        total = jnp.where(run // width == part, dot(sorted_runs, near[...]), total)
    out_ref[...] = total.T.astype(BF)


def traces(shape, field, trace_cell, block):
    sides, rows, lanes = field.shape
    slots = trace_cell.shape[3]
    stride = rows * lanes // slots
    width = min(slots, 256)
    hbm = pl.BlockSpec(memory_space=pltpu.HBM)
    return pl.pallas_call(
        functools.partial(trace_kernel, shape, stride, block),
        in_specs=[hbm, hbm],
        out_specs=[WHOLE] * (1 + len(shape.outer)),
        out_shape=[jax.ShapeDtypeStruct((slots, sides), BF)] + face_shapes(shape, shape.outer),
        scratch_shapes=[
            pltpu.VMEM(field.shape, BF),
            pltpu.VMEM(trace_cell.shape, jnp.int32),
            pltpu.VMEM((sides // block, block * rows, lanes), F32),
            pltpu.VMEM((width, slots), BF),
            pltpu.VMEM((8, slots), jnp.int32),
            pltpu.VMEM((sides, slots), F32),
            pltpu.SemaphoreType.DMA((sides // block + 1,)),
        ],
        compiler_params=params(62),
        cost_estimate=pl.CostEstimate(
            flops=4 * sides * rows * lanes * 128, bytes_accessed=field.size * 2, transcendentals=0
        ),
    )(field, trace_cell)


def fetch_columns(block_ref, held, sems, slots):
    me, group, gzs = lax.axis_index("row"), lax.axis_index("gz"), lax.axis_size("gz")
    copies = []
    for key in range(held.shape[0]):
        start = pl.multiple_of((jnp.bitwise_xor(me, key) * gzs + group) * slots, slots)
        copies.append(
            pltpu.make_async_copy(block_ref.at[:, pl.ds(start, slots)], held.at[key], sems.at[key])
        )
        copies[-1].start()
    return copies


def surface_kernel(halves, *refs):
    ins, total = refs[:-1], refs[-1]
    outs = ins[len(ins) - halves :]
    *parts, held = ins[: len(ins) - halves]
    value = None
    for key, part in enumerate(parts):
        term = dot(held[key], part[...])
        value = term if value is None else value + term
    if halves == 1:
        outs[0][...] = value
        return
    total[...] = value
    count = outs[0].shape[0]
    mine = lax.axis_index("col")
    for key, out in enumerate(outs):
        out[...] = total[pl.ds(pl.multiple_of((mine ^ key) * count, 8), count), :]


def surface(parts, held, halves):
    sides = parts[0].shape[1]
    lines = held.shape[1]
    return pl.pallas_call(
        functools.partial(surface_kernel, halves),
        in_specs=[WHOLE] * (len(parts) + 1),
        out_specs=[WHOLE] * halves,
        out_shape=[jax.ShapeDtypeStruct((lines // halves, sides), F32)] * halves,
        scratch_shapes=[pltpu.VMEM((lines, sides), F32)],
        compiler_params=params(),
        cost_estimate=pl.CostEstimate(
            flops=2 * sides * held.size, bytes_accessed=2 * held.size, transcendentals=0
        ),
    )(*parts, held)


def share_kernel(peers, mine_ref, other_ref, *refs):
    *outs, total, turned = refs
    total[...] = mine_ref[...] + other_ref[...]
    turned[...] = total[...].T
    lines, sides = total.shape
    group = lax.axis_index("gz")
    for key, out in enumerate(outs):
        peer = group ^ key
        rows, some = lines // peers, sides // peers
        out[:rows, :] = total[pl.ds(pl.multiple_of(peer * rows, 8), rows), :]
        out[rows:, :] = turned[pl.ds(pl.multiple_of(peer * some, 8), some), :]


def shares(mine, other):
    peers = lax.axis_size("gz")
    lines, sides = mine.shape
    out = jax.ShapeDtypeStruct(((lines + sides) // peers, sides), F32)
    return pl.pallas_call(
        functools.partial(share_kernel, peers),
        in_specs=[WHOLE] * 2,
        out_specs=[WHOLE] * peers,
        out_shape=[out] * peers,
        scratch_shapes=[pltpu.VMEM((lines, sides), F32), pltpu.VMEM((sides, lines), F32)],
        compiler_params=params(),
        cost_estimate=pl.CostEstimate(
            flops=lines * sides, bytes_accessed=16 * lines * sides, transcendentals=0
        ),
    )(mine, other)


def flux_sums(parts, held, late):
    cols, gzs = lax.axis_size("col"), lax.axis_size("gz")
    sides = parts[0].shape[1]
    lines = held.shape[1]
    if cols == 2 and gzs & (gzs - 1) == 0 and lines // cols == sides and sides // gzs % 8 == 0:
        mine, other = surface(parts, held, 2)
        other = lax.ppermute(other, "col", [(0, 1), (1, 0)])
        other, late = lax.optimization_barrier((other, late))
        sent = shares(mine, other)
        recv = [sent[0]]
        for key in range(gzs - 1, 0, -1):
            recv.append(lax.ppermute(sent[key], "gz", [(i, i ^ key) for i in range(gzs)]))
        return recv, late
    (total,) = surface(parts, held, 1)
    rows = lax.psum_scatter(total, "col", scatter_dimension=0, tiled=True)
    owned = lax.psum_scatter(rows, "gz", scatter_dimension=0, tiled=True)
    flux = lax.psum_scatter(rows.T, "gz", scatter_dimension=0, tiled=True)
    flux = jnp.pad(flux, ((0, 0), (0, sides - flux.shape[1])))
    return [jnp.concatenate([owned, flux], axis=0)], late


def turns(axis):
    return 1 if lax.axis_size(axis) == 2 else 2


def partner(index, turn):
    return jnp.where(index % 2 == turn, index + 1, index - 1)


def has_neighbour(axis, turn):
    other = partner(lax.axis_index(axis), turn)
    return (other >= 0) & (other < lax.axis_size(axis))


def swap(value, axis, turn):
    axes = ("row", "col", "gz")
    sizes = [lax.axis_size(name) for name in axes]
    along = axes.index(axis)
    spare = 0 if axis == "gz" else 2
    pairs = []
    for r in range(sizes[0]):
        for c in range(sizes[1]):
            for g in range(sizes[2]):
                here = [r, c, g]
                there = [r, c, g]
                there[along] += 1 if here[along] % 2 == turn else -1
                if not 0 <= there[along] < sizes[along]:
                    there[along] = here[along]
                    if here[spare] ^ 1 < sizes[spare]:
                        there[spare] ^= 1
                flat = [(at[0] * sizes[1] + at[1]) * sizes[2] + at[2] for at in (here, there)]
                pairs.append(tuple(flat))
    return lax.ppermute(value, axes, pairs)


class Shape:
    def __init__(self, sides, first, second, lanes):
        self.sides, self.x, self.y, self.lanes = sides, first, second, lanes
        self.cells = first * second
        self.chunk = max(1, 128 // self.cells)
        self.rows = self.chunk * self.cells
        self.block = min(sides, 32)
        self.half = self.block // 2
        self.half_rows = self.half * self.cells
        self.outer = [("col", i) for i in range(turns("col"))]
        self.inner = [("row", i) for i in reversed(range(turns("row")))]
        self.faces = self.outer + self.inner
        self.ends = turns("gz")

    def face_len(self, face):
        return self.y if face[0] == "row" else self.x

    def halo_rows(self):
        return sum(self.chunk * self.face_len(face) for face in self.faces)

    def edge(self, face):
        axis, turn = face
        last = (self.x if axis == "row" else self.y) - 1
        return jnp.where(lax.axis_index(axis) % 2 == turn, last, 0)


def halo_place(shape):
    dims = (shape.rows, shape.halo_rows())
    row, col = iota(dims, 0), iota(dims, 1)
    side, cell = row // shape.cells, row % shape.cells
    x, y = cell // shape.y, cell % shape.y
    hit, base = None, 0
    for face in shape.faces:
        length = shape.face_len(face)
        along, across = (y, x) if face[0] == "row" else (x, y)
        place = (across == shape.edge(face)) & (col - base == side * length + along)
        place = place & has_neighbour(*face)
        hit = place if hit is None else hit | place
        base += shape.chunk * length
    return hit.astype(BF)


def z_mask(shape, count):
    dims = (count * shape.cells, 2 * shape.cells)
    return iota(dims, 1) % shape.cells == iota(dims, 0) % shape.cells


def twice(matrix):
    zero = jnp.zeros_like(matrix)
    return jnp.concatenate(
        [jnp.concatenate([matrix, zero], axis=1), jnp.concatenate([zero, matrix], axis=1)], axis=0
    )


def beside(values):
    half = values.shape[0] // 2
    return jnp.concatenate([values[:half], values[half:]], axis=1)


def build_out(shape, ends_m, rsum):
    dims = (shape.lanes, 2 * shape.cells)
    edge = jnp.where(iota(dims, 1) < shape.cells, 0, shape.lanes - 1)
    ends_m[...] = twice((iota(dims, 0) == edge).astype(F32)).astype(BF)
    dims = rsum.shape
    rsum[...] = (iota(dims, 1) // shape.cells == iota(dims, 0)).astype(BF)


def cut_faces(shape, faces, at, block, tall, face_refs):
    for face, ref in zip(faces, face_refs):
        length, edge = shape.face_len(face), shape.edge(face)
        lines = []
        for side in range(block):
            start = side * shape.cells
            if face[0] == "row":
                lines.append(tall[pl.ds(aligned(start + edge * length, 8), length), :])
            else:
                lines.append(tall[pl.ds(start + edge, length, stride=shape.y), :])
        span = slice(at * length, (at + block) * length)
        ref[span, :] = jnp.concatenate(lines, axis=0).astype(BF)


def cut_ends(shape, at, values, z_ref, ends_m, rsum):
    mask = jnp.concatenate([z_mask(shape, shape.half)] * 2, axis=1)
    tips = jnp.where(mask, dot(beside(values), ends_m[...]), 0.0).astype(BF)
    tips = dot(rsum[...], tips)[: shape.half]
    tips = jnp.concatenate([tips[:, : 2 * shape.cells], tips[:, 2 * shape.cells :]], axis=0)
    z_ref[at : at + shape.block, :] = tips.astype(BF)


def build_tables(shape, coef_ref, weight, near_m, line_m, ends_m, rsum):
    cells, lanes = shape.cells, shape.lanes
    weight[...] = jnp.concatenate([OMEGA / (6.0 + coef_ref[...])] * shape.chunk, axis=0)
    dims = (shape.rows, shape.rows)
    row, col = iota(dims, 0), iota(dims, 1)
    x, y = row % cells // shape.y, row % shape.y
    x2, y2 = col % cells // shape.y, col % shape.y
    near = ((x == x2) & (jnp.abs(y - y2) == 1)) | ((y == y2) & (jnp.abs(x - x2) == 1))
    near_m[:, : shape.rows] = (near & (row // cells == col // cells)).astype(BF)
    near_m[:, shape.rows :] = halo_place(shape)
    dims = (lanes, lanes)
    line = (jnp.abs(iota(dims, 0) - iota(dims, 1)) == 1).astype(F32)
    line_m[: 2 * lanes, :] = twice(line).astype(BF)
    dims = (2 * cells, lanes)
    edge = jnp.where(iota(dims, 0) < cells, lanes - 1, 0)
    line_m[2 * lanes :, :] = twice((iota(dims, 1) == edge).astype(F32)).astype(BF)
    build_out(shape, ends_m, rsum)


def table_shapes(shape):
    lanes, cells = shape.lanes, shape.cells
    return [
        jax.ShapeDtypeStruct((shape.rows, lanes), F32),
        jax.ShapeDtypeStruct((shape.rows, shape.rows + shape.halo_rows()), BF),
        jax.ShapeDtypeStruct((2 * lanes + 4 * cells, 2 * lanes), BF),
        jax.ShapeDtypeStruct((2 * lanes, 4 * cells), BF),
        jax.ShapeDtypeStruct((max(8, shape.half), shape.half_rows), BF),
    ]


def faces_kernel(shape, slots, field_ref, block_ref, coef_ref, *refs):
    refs = list(refs)
    face_refs = [refs.pop(0) for _ in shape.inner]
    z_ref, held, *tables, field, tall, sems, field_sems = refs
    size = shape.block * shape.cells
    steps = shape.sides // shape.block
    copies = []
    for step in range(steps):
        span = pl.ds(step * size, size)
        copies.append(
            pltpu.make_async_copy(field_ref.at[span], field.at[span], field_sems.at[step])
        )
        copies[-1].start()
    columns = fetch_columns(block_ref, held, sems, slots)
    build_tables(shape, coef_ref, *tables)
    ends_m, rsum = tables[-2:]
    for step in range(steps):
        copies[step].wait()
        values = field[step * size : (step + 1) * size, :]
        tall[step] = values.astype(F32)
        cut_faces(shape, shape.inner, step * shape.block, shape.block, tall.at[step], face_refs)
        cut_ends(shape, step * shape.block, values, z_ref, ends_m, rsum)
    for copy in columns:
        copy.wait()


def face_shapes(shape, faces):
    return [
        jax.ShapeDtypeStruct((shape.sides * shape.face_len(face), shape.lanes), BF)
        for face in faces
    ]


def first_faces(shape, field, block, coef, slots):
    peers = lax.axis_size("row")
    steps = shape.sides // shape.block
    shapes = face_shapes(shape, shape.inner)
    shapes.append(jax.ShapeDtypeStruct((shape.sides, 2 * shape.cells), BF))
    shapes.append(jax.ShapeDtypeStruct((peers, block.shape[0], slots), BF))
    shapes += table_shapes(shape)
    hbm = pl.BlockSpec(memory_space=pltpu.HBM)
    return pl.pallas_call(
        functools.partial(faces_kernel, shape, slots),
        in_specs=[hbm, hbm, WHOLE],
        out_specs=[WHOLE] * len(shapes),
        out_shape=shapes,
        scratch_shapes=[
            pltpu.VMEM(field.shape, BF),
            pltpu.VMEM((steps, shape.block * shape.cells, shape.lanes), F32),
            pltpu.SemaphoreType.DMA((peers,)),
            pltpu.SemaphoreType.DMA((steps,)),
        ],
        compiler_params=params(FACES_MIB),
        cost_estimate=pl.CostEstimate(
            flops=field.size * 128, bytes_accessed=4 * field.size, transcendentals=0
        ),
    )(field, block, coef)


def sweep_kernel(shape, recvs, last, *refs):
    with_flux = recvs > 0
    refs = list(refs)
    take = lambda count: [refs.pop(0) for _ in range(count)]
    field_ref, load_ref, weight, near_m, line_m, ends_m, rsum = take(7)
    halo_refs = take(len(shape.faces))
    end_refs = take(shape.ends)
    if with_flux:
        recv_refs = take(recvs)
        (cell_ref,) = take(1)
    (out_ref,) = take(1)
    if not last:
        face_refs = take(len(shape.faces))
        (z_ref,) = take(1)
    if with_flux:
        source_ref, flux_ref = take(2)
    (lines,) = take(1)
    if last:
        result_ref = out_ref
        out_ref, out_sems = take(2)
    else:
        (tall,) = take(1)
    if with_flux:
        phi, cell_m, placed = take(3)

    cells, lanes = shape.cells, shape.lanes

    if with_flux:
        slots = cell_ref.shape[3]
        owned = recv_refs[0][...]
        for ref in recv_refs[1:]:
            owned = owned + ref[...]
        flux_ref[...] = owned[slots:, : flux_ref.shape[1]]
        owned = owned[:slots]
        high = owned.astype(BF).astype(F32)
        both = jnp.concatenate([high, owned - high], axis=0)
        phi[...] = both.T
        cell = jnp.concatenate([cell_ref[0, 0]] * 2, axis=1)
        cell_m[...] = twice((iota((lanes, 2 * slots), 0) == cell % lanes).astype(F32)).astype(BF)

    mask = z_mask(shape, 1)
    even = lax.axis_index("gz") % 2 == 0
    filled = (iota((shape.block, 2 * cells), 1) < cells) == even
    if with_flux:
        slots = cell_ref.shape[3]
        cell = jnp.concatenate([cell_ref[0, 0]] * 2, axis=1)
        cell_mask = iota((cells, 2 * slots), 0) == cell // lanes
    weights = weight[...]

    def expand(lines, where, first):
        rows = []
        for side in range(first, first + shape.half):
            line = jnp.broadcast_to(lines[side : side + 1], where.shape)
            rows.append(jnp.where(where, line, 0.0))
        return jnp.concatenate(rows, axis=0).astype(BF)

    def work(step):
        at = step * shape.block
        sides = pl.ds(aligned(at, shape.block), shape.block)
        size = shape.block * cells
        zs = 0.0
        for turn in range(shape.ends):
            wanted = (filled == (turn == 0)) & has_neighbour("gz", turn)
            zs = jnp.where(wanted, end_refs[turn][sides, :].astype(F32), zs)
        values = field_ref[pl.ds(aligned(at * cells, size), size), :]
        left = [beside(values), expand(zs, mask, 0), expand(zs, mask, shape.half)]
        lines[step] = dot(jnp.concatenate(left, axis=1), line_m[...])
        if with_flux:
            phis = phi[sides, :]
            left = [expand(phis, cell_mask, 0), expand(phis, cell_mask, shape.half)]
            placed[step] = dot_nt(jnp.concatenate(left, axis=1), cell_m[...])
        for index in range(shape.half // shape.chunk):
            offset = index * shape.rows
            starts = (offset, offset + shape.half_rows)
            stacks = []
            for start in starts:
                rows = pl.ds(aligned(at * cells + start, shape.rows), shape.rows)
                stack = [field_ref[rows, :]]
                for face, ref in zip(shape.faces, halo_refs):
                    length = shape.face_len(face)
                    count = shape.chunk * length
                    first = aligned(at * length + start // cells * length, count)
                    stack.append(ref[pl.ds(first, count), :])
                stacks.append(jnp.concatenate(stack, axis=0))
            near = dot(near_m[...], jnp.concatenate(stacks, axis=1))
            near = near + lines[step, offset : offset + shape.rows, :]
            for part, start in enumerate(starts):
                cols = slice(part * lanes, (part + 1) * lanes)
                rows = pl.ds(aligned(at * cells + start, shape.rows), shape.rows)
                source = load_ref[rows, :].astype(F32)
                if with_flux:
                    source = source + placed[step, offset : offset + shape.rows, cols]
                    source_ref[rows, :] = source.astype(BF)
                centre = field_ref[rows, :].astype(F32)
                fresh = (1.0 - OMEGA) * centre + weights * (source + near[:, cols])
                out_ref[rows, :] = fresh.astype(BF)
                if not last:
                    tall[step, start : start + shape.rows, :] = fresh

    def emit(step):
        at, size = step * shape.block, shape.block * cells
        fresh = out_ref[at * cells : at * cells + size, :]
        cut_faces(shape, shape.faces, at, shape.block, tall.at[step], face_refs)
        cut_ends(shape, at, fresh, z_ref, ends_m, rsum)

    steps = shape.sides // shape.block
    copies = []
    for step in range(steps):
        work(step)
        if last:
            span = pl.ds(step * shape.block * cells, shape.block * cells)
            copies.append(
                pltpu.make_async_copy(out_ref.at[span], result_ref.at[span], out_sems.at[step])
            )
            copies[-1].start()
        elif step > 0:
            emit(step - 1)
    for copy in copies:
        copy.wait()
    if not last:
        emit(steps - 1)


def sweep(shape, field, load, tables, halos, recv=(), flux_cell=None, last=False):
    lanes, cells = shape.lanes, shape.cells
    steps = shape.sides // shape.block
    half = (steps, shape.half_rows, 2 * lanes)
    operands = [field, load, *tables, *halos, *recv]
    out_shapes = [jax.ShapeDtypeStruct(field.shape, BF)]
    scratch = [pltpu.VMEM(half, F32)]
    if last:
        scratch += [pltpu.VMEM(field.shape, BF), pltpu.SemaphoreType.DMA((steps,))]
    else:
        out_shapes += face_shapes(shape, shape.faces)
        out_shapes.append(jax.ShapeDtypeStruct((shape.sides, 2 * cells), BF))
        scratch.append(pltpu.VMEM((steps, shape.block * cells, lanes), F32))
    if recv:
        slots = flux_cell.shape[3]
        operands.append(flux_cell)
        out_shapes += [
            jax.ShapeDtypeStruct(field.shape, BF),
            jax.ShapeDtypeStruct((recv[0].shape[0] - slots, slots * lax.axis_size("gz")), F32),
        ]
        scratch += [
            pltpu.VMEM((shape.sides, 2 * slots), F32),
            pltpu.VMEM((2 * lanes, 4 * slots), BF),
            pltpu.VMEM(half, F32),
        ]
    out_specs = [WHOLE] * len(out_shapes)
    if last:
        out_specs = [pl.BlockSpec(memory_space=pltpu.HBM)]
    return pl.pallas_call(
        functools.partial(sweep_kernel, shape, len(recv), last),
        in_specs=[WHOLE] * len(operands),
        out_specs=out_specs,
        out_shape=out_shapes,
        scratch_shapes=scratch,
        compiler_params=params(),
        cost_estimate=pl.CostEstimate(
            flops=6 * field.size * 128, bytes_accessed=8 * field.size, transcendentals=0
        ),
    )(*operands)


def exchange(shape, faces):
    *cut, ends = faces
    halos = [swap(value, *face) for face, value in zip(shape.faces, cut)]
    return halos + [swap(ends, "gz", turn) for turn in range(shape.ends)]


def row_gather(trace, hidden):
    peers = lax.axis_size("row")
    held = {0: trace}
    bit = peers // 2
    while bit:
        pairs = [(i, i ^ bit) for i in range(peers)]
        fresh = {key ^ bit: lax.ppermute(held[key], "row", pairs) for key in sorted(held, reverse=True)}
        if bit == peers // 2:
            held, fresh, hidden = lax.optimization_barrier((held, fresh, hidden))
        held.update(fresh)
        bit //= 2
    return [held[key] for key in range(peers)], hidden


def per_device(volume_field, volume_load, coefficient, surface_block, trace_cell, flux_cell):
    sides, first, second, lanes = volume_field.shape
    cells = first * second
    shape = Shape(sides, first, second, lanes)
    field = volume_field.reshape(sides * cells, lanes)
    load = volume_load.reshape(sides * cells, lanes)
    coef = coefficient.reshape(cells, lanes)

    slots = trace_cell.shape[3]
    trace, *outer = traces(
        shape, volume_field.reshape(sides, cells, lanes), trace_cell, min(32, sides)
    )
    firsts = first_faces(shape, field, surface_block, coef, slots)
    layers = len(shape.faces)
    count = len(shape.inner) + 1
    inner, held, tables = firsts[:count], firsts[count], firsts[count + 1 :]
    halos = exchange(shape, [*outer, *inner])
    early = len(shape.outer)
    parts, (_, along_col, ends) = row_gather(trace, (inner, halos[:early], halos[layers:]))
    recv, along_row = flux_sums(parts, held, halos[early:layers])
    halos = along_col + along_row + ends

    current, *faces, source, surface_flux = sweep(
        shape, field, load, tables, halos, recv=recv, flux_cell=flux_cell
    )
    current, *faces = sweep(shape, current, source, tables, exchange(shape, faces))
    (current,) = sweep(shape, current, source, tables, exchange(shape, faces), last=True)
    return current.reshape(volume_field.shape), surface_flux


def solution(mesh):
    in_specs = (
        P(None, "row", "col", "gz"),
        P(None, "row", "col", "gz"),
        P("row", "col", "gz"),
        P("row", "col"),
        P("row", "col", "gz", None),
        P("row", "col", "gz", None),
    )
    out_specs = (P(None, "row", "col", "gz"), P("gz", ("row", "col")))
    return jax.shard_map(
        per_device, mesh=mesh, in_specs=in_specs, out_specs=out_specs, check_vma=False
    )
```

```python
import functools

import jax
import jax.numpy as jnp
from jax import lax
from jax.experimental import pallas as pl
from jax.experimental.pallas import tpu as pltpu
from jax.sharding import PartitionSpec as P

OMEGA = 0.8
BF = jnp.bfloat16
F32 = jnp.float32
WHOLE = pl.BlockSpec(memory_space=pltpu.VMEM)


def aligned(start, unit):
    return start if isinstance(start, int) else pl.multiple_of(start, unit)


def iota(shape, dim):
    return lax.broadcasted_iota(jnp.int32, shape, dim)


def dot(a, b):
    return jnp.dot(a, b, preferred_element_type=F32)


def dot_nt(a, b):
    return lax.dot_general(a, b, (((1,), (1,)), ((), ())), preferred_element_type=F32)


FACES_MIB = 50


def params(mebibytes=24):
    return pltpu.CompilerParams(vmem_limit_bytes=mebibytes * 1024 * 1024)


def trace_kernel(shape, stride, block, field_ref, cell_ref, out_ref, *refs):
    *face_refs, field, cell_v, tall, near, place, picked, sems = refs
    sides, rows, lanes = field.shape
    slots = cell_ref.shape[3]
    per_row = lanes // stride
    width = near.shape[0]
    parts = slots // width
    cell_copy = pltpu.make_async_copy(cell_ref, cell_v, sems.at[sides // block])
    cell_copy.start()
    copies = []
    for step in range(sides // block):
        span = pl.ds(step * block, block)
        copies.append(pltpu.make_async_copy(field_ref.at[span], field.at[span], sems.at[step]))
        copies[-1].start()

    cell_copy.wait()
    cell = cell_v[0, 0]
    run = cell // stride
    digit = jnp.zeros_like(cell)
    for part in range(parts):
        digit = jnp.where(run // width == part, (cell % stride) * stride**part, digit)
    hit = iota((width, slots), 0) == run % width
    near[...] = hit.astype(BF)
    digits = jnp.sum(jnp.where(hit, digit.astype(F32), 0.0), axis=1, keepdims=True)
    digits = jnp.broadcast_to(digits, (width, 128)).T[0:8].astype(jnp.int32)
    first = iota((8, width), 1) % per_row * stride
    for part in range(parts):
        place[:, part * width : (part + 1) * width] = first + digits // stride**part % stride

    together = 128 // per_row
    group = iota((8, 128), 1) // per_row
    for step in range(sides // block):
        copies[step].wait()
        span = field[step * block : (step + 1) * block]
        tall[step] = span.reshape(block * rows, lanes).astype(F32)
        cut_faces(shape, shape.outer, step * block, block, tall.at[step], face_refs)

        for batch in range(block // 8):
            for tile in range(rows // together):
                cols = slice(tile * 128, (tile + 1) * 128)
                where = place[:, cols]
                found = None
                for row in range(together):
                    start = batch * 8 * rows + tile * together + row
                    line = tall[step, pl.ds(start, 8, stride=rows), :]
                    line = jnp.take_along_axis(line, where, axis=1)
                    found = line if found is None else jnp.where(group == row, line, found)
                at = step * block + batch * 8
                picked[at : at + 8, cols] = found

    total = jnp.zeros((sides, slots), F32)
    for part in range(parts):
        sorted_runs = picked[:, part * width : (part + 1) * width].astype(BF)
        total = jnp.where(run // width == part, dot(sorted_runs, near[...]), total)
    out_ref[...] = total.T.astype(BF)


def traces(shape, field, trace_cell, block):
    sides, rows, lanes = field.shape
    slots = trace_cell.shape[3]
    stride = rows * lanes // slots
    width = min(slots, 256)
    hbm = pl.BlockSpec(memory_space=pltpu.HBM)
    return pl.pallas_call(
        functools.partial(trace_kernel, shape, stride, block),
        in_specs=[hbm, hbm],
        out_specs=[WHOLE] * (1 + len(shape.outer)),
        out_shape=[jax.ShapeDtypeStruct((slots, sides), BF)] + face_shapes(shape, shape.outer),
        scratch_shapes=[
            pltpu.VMEM(field.shape, BF),
            pltpu.VMEM(trace_cell.shape, jnp.int32),
            pltpu.VMEM((sides // block, block * rows, lanes), F32),
            pltpu.VMEM((width, slots), BF),
            pltpu.VMEM((8, slots), jnp.int32),
            pltpu.VMEM((sides, slots), F32),
            pltpu.SemaphoreType.DMA((sides // block + 1,)),
        ],
        compiler_params=params(62),
        cost_estimate=pl.CostEstimate(
            flops=4 * sides * rows * lanes * 128, bytes_accessed=field.size * 2, transcendentals=0
        ),
    )(field, trace_cell)


def fetch_columns(block_ref, held, sems, slots):
    me, group, gzs = lax.axis_index("row"), lax.axis_index("gz"), lax.axis_size("gz")
    copies = []
    for key in range(held.shape[0]):
        start = pl.multiple_of((jnp.bitwise_xor(me, key) * gzs + group) * slots, slots)
        copies.append(
            pltpu.make_async_copy(block_ref.at[:, pl.ds(start, slots)], held.at[key], sems.at[key])
        )
        copies[-1].start()
    return copies


def surface_kernel(halves, *refs):
    ins, total = refs[:-1], refs[-1]
    outs = ins[len(ins) - halves :]
    *parts, held = ins[: len(ins) - halves]
    value = None
    for key, part in enumerate(parts):
        term = dot(held[key], part[...])
        value = term if value is None else value + term
    if halves == 1:
        outs[0][...] = value
        return
    total[...] = value
    count = outs[0].shape[0]
    mine = lax.axis_index("col")
    for key, out in enumerate(outs):
        out[...] = total[pl.ds(pl.multiple_of((mine ^ key) * count, 8), count), :]


def surface(parts, held, halves):
    sides = parts[0].shape[1]
    lines = held.shape[1]
    return pl.pallas_call(
        functools.partial(surface_kernel, halves),
        in_specs=[WHOLE] * (len(parts) + 1),
        out_specs=[WHOLE] * halves,
        out_shape=[jax.ShapeDtypeStruct((lines // halves, sides), F32)] * halves,
        scratch_shapes=[pltpu.VMEM((lines, sides), F32)],
        compiler_params=params(),
        cost_estimate=pl.CostEstimate(
            flops=2 * sides * held.size, bytes_accessed=2 * held.size, transcendentals=0
        ),
    )(*parts, held)


def share_kernel(peers, mine_ref, other_ref, *refs):
    *outs, total, turned = refs
    total[...] = mine_ref[...] + other_ref[...]
    turned[...] = total[...].T
    lines, sides = total.shape
    group = lax.axis_index("gz")
    for key, out in enumerate(outs):
        peer = group ^ key
        rows, some = lines // peers, sides // peers
        out[:rows, :] = total[pl.ds(pl.multiple_of(peer * rows, 8), rows), :]
        out[rows:, :] = turned[pl.ds(pl.multiple_of(peer * some, 8), some), :]


def shares(mine, other):
    peers = lax.axis_size("gz")
    lines, sides = mine.shape
    out = jax.ShapeDtypeStruct(((lines + sides) // peers, sides), F32)
    return pl.pallas_call(
        functools.partial(share_kernel, peers),
        in_specs=[WHOLE] * 2,
        out_specs=[WHOLE] * peers,
        out_shape=[out] * peers,
        scratch_shapes=[pltpu.VMEM((lines, sides), F32), pltpu.VMEM((sides, lines), F32)],
        compiler_params=params(),
        cost_estimate=pl.CostEstimate(
            flops=lines * sides, bytes_accessed=16 * lines * sides, transcendentals=0
        ),
    )(mine, other)


def flux_sums(parts, held, late, after):
    cols, gzs = lax.axis_size("col"), lax.axis_size("gz")
    sides = parts[0].shape[1]
    lines = held.shape[1]
    if cols == 2 and gzs & (gzs - 1) == 0 and lines // cols == sides and sides // gzs % 8 == 0:
        mine, other = surface(parts, held, 2)
        mine, other, after = lax.optimization_barrier((mine, other, after))
        other = lax.ppermute(other, "col", [(0, 1), (1, 0)])
        other, late = lax.optimization_barrier((other, late))
        sent = shares(mine, other)
        recv = [sent[0]]
        for key in range(gzs - 1, 0, -1):
            recv.append(lax.ppermute(sent[key], "gz", [(i, i ^ key) for i in range(gzs)]))
        return recv, after
    (total,) = surface(parts, held, 1)
    rows = lax.psum_scatter(total, "col", scatter_dimension=0, tiled=True)
    owned = lax.psum_scatter(rows, "gz", scatter_dimension=0, tiled=True)
    flux = lax.psum_scatter(rows.T, "gz", scatter_dimension=0, tiled=True)
    flux = jnp.pad(flux, ((0, 0), (0, sides - flux.shape[1])))
    return [jnp.concatenate([owned, flux], axis=0)], after


def turns(axis):
    return 1 if lax.axis_size(axis) == 2 else 2


def partner(index, turn):
    return jnp.where(index % 2 == turn, index + 1, index - 1)


def has_neighbour(axis, turn):
    other = partner(lax.axis_index(axis), turn)
    return (other >= 0) & (other < lax.axis_size(axis))


def swap(value, axis, turn):
    axes = ("row", "col", "gz")
    sizes = [lax.axis_size(name) for name in axes]
    along = axes.index(axis)
    spare = 0 if axis == "gz" else 2
    pairs = []
    for r in range(sizes[0]):
        for c in range(sizes[1]):
            for g in range(sizes[2]):
                here = [r, c, g]
                there = [r, c, g]
                there[along] += 1 if here[along] % 2 == turn else -1
                if not 0 <= there[along] < sizes[along]:
                    there[along] = here[along]
                    if here[spare] ^ 1 < sizes[spare]:
                        there[spare] ^= 1
                flat = [(at[0] * sizes[1] + at[1]) * sizes[2] + at[2] for at in (here, there)]
                pairs.append(tuple(flat))
    return lax.ppermute(value, axes, pairs)


class Shape:
    def __init__(self, sides, first, second, lanes):
        self.sides, self.x, self.y, self.lanes = sides, first, second, lanes
        self.cells = first * second
        self.chunk = max(1, 128 // self.cells)
        self.rows = self.chunk * self.cells
        self.block = min(sides, 32)
        self.half = self.block // 2
        self.half_rows = self.half * self.cells
        self.outer = [("col", i) for i in range(turns("col"))]
        self.inner = [("row", i) for i in reversed(range(turns("row")))]
        self.faces = self.outer + self.inner
        self.ends = turns("gz")

    def face_len(self, face):
        return self.y if face[0] == "row" else self.x

    def halo_rows(self):
        return sum(self.chunk * self.face_len(face) for face in self.faces)

    def edge(self, face):
        axis, turn = face
        last = (self.x if axis == "row" else self.y) - 1
        return jnp.where(lax.axis_index(axis) % 2 == turn, last, 0)


def halo_place(shape):
    dims = (shape.rows, shape.halo_rows())
    row, col = iota(dims, 0), iota(dims, 1)
    side, cell = row // shape.cells, row % shape.cells
    x, y = cell // shape.y, cell % shape.y
    hit, base = None, 0
    for face in shape.faces:
        length = shape.face_len(face)
        along, across = (y, x) if face[0] == "row" else (x, y)
        place = (across == shape.edge(face)) & (col - base == side * length + along)
        place = place & has_neighbour(*face)
        hit = place if hit is None else hit | place
        base += shape.chunk * length
    return hit.astype(BF)


def z_mask(shape, count):
    dims = (count * shape.cells, 2 * shape.cells)
    return iota(dims, 1) % shape.cells == iota(dims, 0) % shape.cells


def twice(matrix):
    zero = jnp.zeros_like(matrix)
    return jnp.concatenate(
        [jnp.concatenate([matrix, zero], axis=1), jnp.concatenate([zero, matrix], axis=1)], axis=0
    )


def beside(values):
    half = values.shape[0] // 2
    return jnp.concatenate([values[:half], values[half:]], axis=1)


def build_out(shape, ends_m, rsum):
    dims = (shape.lanes, 2 * shape.cells)
    edge = jnp.where(iota(dims, 1) < shape.cells, 0, shape.lanes - 1)
    ends_m[...] = twice((iota(dims, 0) == edge).astype(F32)).astype(BF)
    dims = rsum.shape
    rsum[...] = (iota(dims, 1) // shape.cells == iota(dims, 0)).astype(BF)


def cut_faces(shape, faces, at, block, tall, face_refs):
    for face, ref in zip(faces, face_refs):
        length, edge = shape.face_len(face), shape.edge(face)
        lines = []
        for side in range(block):
            start = side * shape.cells
            if face[0] == "row":
                lines.append(tall[pl.ds(aligned(start + edge * length, 8), length), :])
            else:
                lines.append(tall[pl.ds(start + edge, length, stride=shape.y), :])
        span = slice(at * length, (at + block) * length)
        ref[span, :] = jnp.concatenate(lines, axis=0).astype(BF)


def cut_ends(shape, at, values, z_ref, ends_m, rsum):
    mask = jnp.concatenate([z_mask(shape, shape.half)] * 2, axis=1)
    tips = jnp.where(mask, dot(beside(values), ends_m[...]), 0.0).astype(BF)
    tips = dot(rsum[...], tips)[: shape.half]
    tips = jnp.concatenate([tips[:, : 2 * shape.cells], tips[:, 2 * shape.cells :]], axis=0)
    z_ref[at : at + shape.block, :] = tips.astype(BF)


def build_tables(shape, coef_ref, weight, near_m, line_m, ends_m, rsum):
    cells, lanes = shape.cells, shape.lanes
    weight[...] = jnp.concatenate([OMEGA / (6.0 + coef_ref[...])] * shape.chunk, axis=0)
    dims = (shape.rows, shape.rows)
    row, col = iota(dims, 0), iota(dims, 1)
    x, y = row % cells // shape.y, row % shape.y
    x2, y2 = col % cells // shape.y, col % shape.y
    near = ((x == x2) & (jnp.abs(y - y2) == 1)) | ((y == y2) & (jnp.abs(x - x2) == 1))
    near_m[:, : shape.rows] = (near & (row // cells == col // cells)).astype(BF)
    near_m[:, shape.rows :] = halo_place(shape)
    dims = (lanes, lanes)
    line = (jnp.abs(iota(dims, 0) - iota(dims, 1)) == 1).astype(F32)
    line_m[: 2 * lanes, :] = twice(line).astype(BF)
    dims = (2 * cells, lanes)
    edge = jnp.where(iota(dims, 0) < cells, lanes - 1, 0)
    line_m[2 * lanes :, :] = twice((iota(dims, 1) == edge).astype(F32)).astype(BF)
    build_out(shape, ends_m, rsum)


def table_shapes(shape):
    lanes, cells = shape.lanes, shape.cells
    return [
        jax.ShapeDtypeStruct((shape.rows, lanes), F32),
        jax.ShapeDtypeStruct((shape.rows, shape.rows + shape.halo_rows()), BF),
        jax.ShapeDtypeStruct((2 * lanes + 4 * cells, 2 * lanes), BF),
        jax.ShapeDtypeStruct((2 * lanes, 4 * cells), BF),
        jax.ShapeDtypeStruct((max(8, shape.half), shape.half_rows), BF),
    ]


def faces_kernel(shape, slots, field_ref, block_ref, coef_ref, *refs):
    refs = list(refs)
    face_refs = [refs.pop(0) for _ in shape.inner]
    z_ref, held, *tables, field, tall, sems, field_sems = refs
    size = shape.block * shape.cells
    steps = shape.sides // shape.block
    copies = []
    for step in range(steps):
        span = pl.ds(step * size, size)
        copies.append(
            pltpu.make_async_copy(field_ref.at[span], field.at[span], field_sems.at[step])
        )
        copies[-1].start()
    columns = fetch_columns(block_ref, held, sems, slots)
    build_tables(shape, coef_ref, *tables)
    ends_m, rsum = tables[-2:]
    for step in range(steps):
        copies[step].wait()
        values = field[step * size : (step + 1) * size, :]
        tall[step] = values.astype(F32)
        cut_faces(shape, shape.inner, step * shape.block, shape.block, tall.at[step], face_refs)
        cut_ends(shape, step * shape.block, values, z_ref, ends_m, rsum)
    for copy in columns:
        copy.wait()


def face_shapes(shape, faces):
    return [
        jax.ShapeDtypeStruct((shape.sides * shape.face_len(face), shape.lanes), BF)
        for face in faces
    ]


def first_faces(shape, field, block, coef, slots):
    peers = lax.axis_size("row")
    steps = shape.sides // shape.block
    shapes = face_shapes(shape, shape.inner)
    shapes.append(jax.ShapeDtypeStruct((shape.sides, 2 * shape.cells), BF))
    shapes.append(jax.ShapeDtypeStruct((peers, block.shape[0], slots), BF))
    shapes += table_shapes(shape)
    hbm = pl.BlockSpec(memory_space=pltpu.HBM)
    return pl.pallas_call(
        functools.partial(faces_kernel, shape, slots),
        in_specs=[hbm, hbm, WHOLE],
        out_specs=[WHOLE] * len(shapes),
        out_shape=shapes,
        scratch_shapes=[
            pltpu.VMEM(field.shape, BF),
            pltpu.VMEM((steps, shape.block * shape.cells, shape.lanes), F32),
            pltpu.SemaphoreType.DMA((peers,)),
            pltpu.SemaphoreType.DMA((steps,)),
        ],
        compiler_params=params(FACES_MIB),
        cost_estimate=pl.CostEstimate(
            flops=field.size * 128, bytes_accessed=4 * field.size, transcendentals=0
        ),
    )(field, block, coef)


def sweep_kernel(shape, recvs, last, *refs):
    with_flux = recvs > 0
    refs = list(refs)
    take = lambda count: [refs.pop(0) for _ in range(count)]
    field_ref, load_ref, weight, near_m, line_m, ends_m, rsum = take(7)
    halo_refs = take(len(shape.faces))
    end_refs = take(shape.ends)
    if with_flux:
        recv_refs = take(recvs)
        (cell_ref,) = take(1)
    (out_ref,) = take(1)
    if not last:
        face_refs = take(len(shape.faces))
        (z_ref,) = take(1)
    if with_flux:
        source_ref, flux_ref = take(2)
    (lines,) = take(1)
    if last:
        result_ref = out_ref
        out_ref, out_sems = take(2)
    else:
        (tall,) = take(1)
    if with_flux:
        phi, cell_m, placed = take(3)

    cells, lanes = shape.cells, shape.lanes

    if with_flux:
        slots = cell_ref.shape[3]
        owned = recv_refs[0][...]
        for ref in recv_refs[1:]:
            owned = owned + ref[...]
        flux_ref[...] = owned[slots:, : flux_ref.shape[1]]
        owned = owned[:slots]
        high = owned.astype(BF).astype(F32)
        both = jnp.concatenate([high, owned - high], axis=0)
        phi[...] = both.T
        cell = jnp.concatenate([cell_ref[0, 0]] * 2, axis=1)
        cell_m[...] = twice((iota((lanes, 2 * slots), 0) == cell % lanes).astype(F32)).astype(BF)

    mask = z_mask(shape, 1)
    even = lax.axis_index("gz") % 2 == 0
    filled = (iota((shape.block, 2 * cells), 1) < cells) == even
    if with_flux:
        slots = cell_ref.shape[3]
        cell = jnp.concatenate([cell_ref[0, 0]] * 2, axis=1)
        cell_mask = iota((cells, 2 * slots), 0) == cell // lanes
    weights = weight[...]

    def expand(lines, where, first):
        rows = []
        for side in range(first, first + shape.half):
            line = jnp.broadcast_to(lines[side : side + 1], where.shape)
            rows.append(jnp.where(where, line, 0.0))
        return jnp.concatenate(rows, axis=0).astype(BF)

    def work(step):
        at = step * shape.block
        sides = pl.ds(aligned(at, shape.block), shape.block)
        size = shape.block * cells
        zs = 0.0
        for turn in range(shape.ends):
            wanted = (filled == (turn == 0)) & has_neighbour("gz", turn)
            zs = jnp.where(wanted, end_refs[turn][sides, :].astype(F32), zs)
        values = field_ref[pl.ds(aligned(at * cells, size), size), :]
        left = [beside(values), expand(zs, mask, 0), expand(zs, mask, shape.half)]
        lines[step] = dot(jnp.concatenate(left, axis=1), line_m[...])
        if with_flux:
            phis = phi[sides, :]
            left = [expand(phis, cell_mask, 0), expand(phis, cell_mask, shape.half)]
            placed[step] = dot_nt(jnp.concatenate(left, axis=1), cell_m[...])
        for index in range(shape.half // shape.chunk):
            offset = index * shape.rows
            starts = (offset, offset + shape.half_rows)
            stacks = []
            for start in starts:
                rows = pl.ds(aligned(at * cells + start, shape.rows), shape.rows)
                stack = [field_ref[rows, :]]
                for face, ref in zip(shape.faces, halo_refs):
                    length = shape.face_len(face)
                    count = shape.chunk * length
                    first = aligned(at * length + start // cells * length, count)
                    stack.append(ref[pl.ds(first, count), :])
                stacks.append(jnp.concatenate(stack, axis=0))
            near = dot(near_m[...], jnp.concatenate(stacks, axis=1))
            near = near + lines[step, offset : offset + shape.rows, :]
            for part, start in enumerate(starts):
                cols = slice(part * lanes, (part + 1) * lanes)
                rows = pl.ds(aligned(at * cells + start, shape.rows), shape.rows)
                source = load_ref[rows, :].astype(F32)
                if with_flux:
                    source = source + placed[step, offset : offset + shape.rows, cols]
                    source_ref[rows, :] = source.astype(BF)
                centre = field_ref[rows, :].astype(F32)
                fresh = (1.0 - OMEGA) * centre + weights * (source + near[:, cols])
                out_ref[rows, :] = fresh.astype(BF)
                if not last:
                    tall[step, start : start + shape.rows, :] = fresh

    def emit(step):
        at, size = step * shape.block, shape.block * cells
        fresh = out_ref[at * cells : at * cells + size, :]
        cut_faces(shape, shape.faces, at, shape.block, tall.at[step], face_refs)
        cut_ends(shape, at, fresh, z_ref, ends_m, rsum)

    steps = shape.sides // shape.block
    copies = []
    for step in range(steps):
        work(step)
        if last:
            span = pl.ds(step * shape.block * cells, shape.block * cells)
            copies.append(
                pltpu.make_async_copy(out_ref.at[span], result_ref.at[span], out_sems.at[step])
            )
            copies[-1].start()
        elif step > 0:
            emit(step - 1)
    for copy in copies:
        copy.wait()
    if not last:
        emit(steps - 1)


def sweep(shape, field, load, tables, halos, recv=(), flux_cell=None, last=False):
    lanes, cells = shape.lanes, shape.cells
    steps = shape.sides // shape.block
    half = (steps, shape.half_rows, 2 * lanes)
    operands = [field, load, *tables, *halos, *recv]
    out_shapes = [jax.ShapeDtypeStruct(field.shape, BF)]
    scratch = [pltpu.VMEM(half, F32)]
    if last:
        scratch += [pltpu.VMEM(field.shape, BF), pltpu.SemaphoreType.DMA((steps,))]
    else:
        out_shapes += face_shapes(shape, shape.faces)
        out_shapes.append(jax.ShapeDtypeStruct((shape.sides, 2 * cells), BF))
        scratch.append(pltpu.VMEM((steps, shape.block * cells, lanes), F32))
    if recv:
        slots = flux_cell.shape[3]
        operands.append(flux_cell)
        out_shapes += [
            jax.ShapeDtypeStruct(field.shape, BF),
            jax.ShapeDtypeStruct((recv[0].shape[0] - slots, slots * lax.axis_size("gz")), F32),
        ]
        scratch += [
            pltpu.VMEM((shape.sides, 2 * slots), F32),
            pltpu.VMEM((2 * lanes, 4 * slots), BF),
            pltpu.VMEM(half, F32),
        ]
    out_specs = [WHOLE] * len(out_shapes)
    if last:
        out_specs = [pl.BlockSpec(memory_space=pltpu.HBM)]
    return pl.pallas_call(
        functools.partial(sweep_kernel, shape, len(recv), last),
        in_specs=[WHOLE] * len(operands),
        out_specs=out_specs,
        out_shape=out_shapes,
        scratch_shapes=scratch,
        compiler_params=params(),
        cost_estimate=pl.CostEstimate(
            flops=6 * field.size * 128, bytes_accessed=8 * field.size, transcendentals=0
        ),
    )(*operands)


def swap_faces(faces, values):
    return [swap(value, *face) for face, value in zip(faces, values)]


def swap_ends(shape, ends):
    return [swap(ends, "gz", turn) for turn in range(shape.ends)]


def exchange(shape, faces):
    *cut, ends = faces
    return swap_faces(shape.faces, cut) + swap_ends(shape, ends)


def row_gather(trace, hidden):
    peers = lax.axis_size("row")
    held = {0: trace}
    bit = peers // 2
    while bit:
        pairs = [(i, i ^ bit) for i in range(peers)]
        fresh = {key ^ bit: lax.ppermute(held[key], "row", pairs) for key in sorted(held, reverse=True)}
        if bit == peers // 2:
            held, fresh, hidden = lax.optimization_barrier((held, fresh, hidden))
        held.update(fresh)
        bit //= 2
    return [held[key] for key in range(peers)], hidden


def per_device(volume_field, volume_load, coefficient, surface_block, trace_cell, flux_cell):
    sides, first, second, lanes = volume_field.shape
    cells = first * second
    shape = Shape(sides, first, second, lanes)
    field = volume_field.reshape(sides * cells, lanes)
    load = volume_load.reshape(sides * cells, lanes)
    coef = coefficient.reshape(cells, lanes)

    slots = trace_cell.shape[3]
    trace, *outer = traces(
        shape, volume_field.reshape(sides, cells, lanes), trace_cell, min(32, sides)
    )
    firsts = first_faces(shape, field, surface_block, coef, slots)
    layers = len(shape.faces)
    count = len(shape.inner) + 1
    inner, held, tables = firsts[:count], firsts[count], firsts[count + 1 :]
    *inner, ends = inner
    along_col = swap_faces(shape.outer, outer)
    parts, (inner, along_col) = row_gather(trace, (inner, along_col))
    along_row = swap_faces(shape.inner, inner)
    recv, ends = flux_sums(parts, held, along_row, ends)
    halos = along_col + along_row + swap_ends(shape, ends)

    current, *faces, source, surface_flux = sweep(
        shape, field, load, tables, halos, recv=recv, flux_cell=flux_cell
    )
    current, *faces = sweep(shape, current, source, tables, exchange(shape, faces))
    (current,) = sweep(shape, current, source, tables, exchange(shape, faces), last=True)
    return current.reshape(volume_field.shape), surface_flux


def solution(mesh):
    in_specs = (
        P(None, "row", "col", "gz"),
        P(None, "row", "col", "gz"),
        P("row", "col", "gz"),
        P("row", "col"),
        P("row", "col", "gz", None),
        P("row", "col", "gz", None),
    )
    out_specs = (P(None, "row", "col", "gz"), P("gz", ("row", "col")))
    return jax.shard_map(
        per_device, mesh=mesh, in_specs=in_specs, out_specs=out_specs, check_vma=False
    )
```

```python
import functools

import jax
import jax.numpy as jnp
from jax import lax
from jax.experimental import pallas as pl
from jax.experimental.pallas import tpu as pltpu
from jax.sharding import PartitionSpec as P

OMEGA = 0.8
BF = jnp.bfloat16
F32 = jnp.float32
WHOLE = pl.BlockSpec(memory_space=pltpu.VMEM)


def aligned(start, unit):
    return start if isinstance(start, int) else pl.multiple_of(start, unit)


def iota(shape, dim):
    return lax.broadcasted_iota(jnp.int32, shape, dim)


def dot(a, b):
    return jnp.dot(a, b, preferred_element_type=F32)


def dot_nt(a, b):
    return lax.dot_general(a, b, (((1,), (1,)), ((), ())), preferred_element_type=F32)


FACES_MIB = 50


def params(mebibytes=24):
    return pltpu.CompilerParams(vmem_limit_bytes=mebibytes * 1024 * 1024)


def trace_kernel(shape, stride, block, field_ref, cell_ref, out_ref, *refs):
    *face_refs, field, cell_v, tall, near, place, picked, sems = refs
    sides, rows, lanes = field.shape
    slots = cell_ref.shape[3]
    per_row = lanes // stride
    width = near.shape[0]
    parts = slots // width
    cell_copy = pltpu.make_async_copy(cell_ref, cell_v, sems.at[sides // block])
    cell_copy.start()
    copies = []
    for step in range(sides // block):
        span = pl.ds(step * block, block)
        copies.append(pltpu.make_async_copy(field_ref.at[span], field.at[span], sems.at[step]))
        copies[-1].start()

    cell_copy.wait()
    cell = cell_v[0, 0]
    run = cell // stride
    digit = jnp.zeros_like(cell)
    for part in range(parts):
        digit = jnp.where(run // width == part, (cell % stride) * stride**part, digit)
    hit = iota((width, slots), 0) == run % width
    near[...] = hit.astype(BF)
    digits = jnp.sum(jnp.where(hit, digit.astype(F32), 0.0), axis=1, keepdims=True)
    digits = jnp.broadcast_to(digits, (width, 128)).T[0:8].astype(jnp.int32)
    first = iota((8, width), 1) % per_row * stride
    for part in range(parts):
        place[:, part * width : (part + 1) * width] = first + digits // stride**part % stride

    together = 128 // per_row
    group = iota((8, 128), 1) // per_row
    for step in range(sides // block):
        copies[step].wait()
        span = field[step * block : (step + 1) * block]
        tall[step] = span.reshape(block * rows, lanes).astype(F32)
        cut_faces(shape, shape.outer, step * block, block, tall.at[step], face_refs)

        for batch in range(block // 8):
            for tile in range(rows // together):
                cols = slice(tile * 128, (tile + 1) * 128)
                where = place[:, cols]
                found = None
                for row in range(together):
                    start = batch * 8 * rows + tile * together + row
                    line = tall[step, pl.ds(start, 8, stride=rows), :]
                    line = jnp.take_along_axis(line, where, axis=1)
                    found = line if found is None else jnp.where(group == row, line, found)
                at = step * block + batch * 8
                picked[at : at + 8, cols] = found

    total = jnp.zeros((sides, slots), F32)
    for part in range(parts):
        sorted_runs = picked[:, part * width : (part + 1) * width].astype(BF)
        total = jnp.where(run // width == part, dot(sorted_runs, near[...]), total)
    out_ref[...] = total.T.astype(BF)


def traces(shape, field, trace_cell, block):
    sides, rows, lanes = field.shape
    slots = trace_cell.shape[3]
    stride = rows * lanes // slots
    width = min(slots, 256)
    hbm = pl.BlockSpec(memory_space=pltpu.HBM)
    return pl.pallas_call(
        functools.partial(trace_kernel, shape, stride, block),
        in_specs=[hbm, hbm],
        out_specs=[WHOLE] * (1 + len(shape.outer)),
        out_shape=[jax.ShapeDtypeStruct((slots, sides), BF)] + face_shapes(shape, shape.outer),
        scratch_shapes=[
            pltpu.VMEM(field.shape, BF),
            pltpu.VMEM(trace_cell.shape, jnp.int32),
            pltpu.VMEM((sides // block, block * rows, lanes), F32),
            pltpu.VMEM((width, slots), BF),
            pltpu.VMEM((8, slots), jnp.int32),
            pltpu.VMEM((sides, slots), F32),
            pltpu.SemaphoreType.DMA((sides // block + 1,)),
        ],
        compiler_params=params(62),
        cost_estimate=pl.CostEstimate(
            flops=4 * sides * rows * lanes * 128, bytes_accessed=field.size * 2, transcendentals=0
        ),
    )(field, trace_cell)


def fetch_columns(block_ref, held, sems, slots):
    me, group, gzs = lax.axis_index("row"), lax.axis_index("gz"), lax.axis_size("gz")
    copies = []
    for key in range(held.shape[0]):
        start = pl.multiple_of((jnp.bitwise_xor(me, key) * gzs + group) * slots, slots)
        copies.append(
            pltpu.make_async_copy(block_ref.at[:, pl.ds(start, slots)], held.at[key], sems.at[key])
        )
        copies[-1].start()
    return copies


def surface_kernel(halves, *refs):
    ins, total = refs[:-1], refs[-1]
    outs = ins[len(ins) - halves :]
    *parts, held = ins[: len(ins) - halves]
    value = None
    for key, part in enumerate(parts):
        term = dot(held[key], part[...])
        value = term if value is None else value + term
    if halves == 1:
        outs[0][...] = value
        return
    total[...] = value
    count = outs[0].shape[0]
    mine = lax.axis_index("col")
    for key, out in enumerate(outs):
        out[...] = total[pl.ds(pl.multiple_of((mine ^ key) * count, 8), count), :]


def surface(parts, held, halves):
    sides = parts[0].shape[1]
    lines = held.shape[1]
    return pl.pallas_call(
        functools.partial(surface_kernel, halves),
        in_specs=[WHOLE] * (len(parts) + 1),
        out_specs=[WHOLE] * halves,
        out_shape=[jax.ShapeDtypeStruct((lines // halves, sides), F32)] * halves,
        scratch_shapes=[pltpu.VMEM((lines, sides), F32)],
        compiler_params=params(),
        cost_estimate=pl.CostEstimate(
            flops=2 * sides * held.size, bytes_accessed=2 * held.size, transcendentals=0
        ),
    )(*parts, held)


def share_kernel(peers, mine_ref, other_ref, keep_ref, send_ref, total, turned):
    total[...] = mine_ref[...] + other_ref[...]
    turned[...] = total[...].T
    lines, sides = total.shape
    rows, some = lines // peers, sides // peers
    group = lax.axis_index("gz")
    for key in range(peers):
        peer = group ^ key
        out = send_ref if key % 2 else keep_ref
        base = key // 2 * (rows + some)
        out[base : base + rows, :] = total[pl.ds(pl.multiple_of(peer * rows, 8), rows), :]
        base += rows
        out[base : base + some, :] = turned[pl.ds(pl.multiple_of(peer * some, 8), some), :]


def shares(mine, other):
    peers = lax.axis_size("gz")
    lines, sides = mine.shape
    out = jax.ShapeDtypeStruct(((lines + sides) // 2, sides), F32)
    return pl.pallas_call(
        functools.partial(share_kernel, peers),
        in_specs=[WHOLE] * 2,
        out_specs=[WHOLE] * 2,
        out_shape=[out] * 2,
        scratch_shapes=[pltpu.VMEM((lines, sides), F32), pltpu.VMEM((sides, lines), F32)],
        compiler_params=params(),
        cost_estimate=pl.CostEstimate(
            flops=lines * sides, bytes_accessed=16 * lines * sides, transcendentals=0
        ),
    )(mine, other)


def halve_kernel(kept_ref, got_ref, keep_ref, send_ref):
    half = keep_ref.shape[0]
    keep_ref[...] = kept_ref[:half, :] + got_ref[:half, :]
    send_ref[...] = kept_ref[half:, :] + got_ref[half:, :]


def halve(kept, got):
    out = jax.ShapeDtypeStruct((kept.shape[0] // 2, kept.shape[1]), F32)
    return pl.pallas_call(
        halve_kernel,
        in_specs=[WHOLE] * 2,
        out_specs=[WHOLE] * 2,
        out_shape=[out] * 2,
        compiler_params=params(),
        cost_estimate=pl.CostEstimate(
            flops=kept.size, bytes_accessed=16 * kept.size, transcendentals=0
        ),
    )(kept, got)


def flux_sums(parts, held, late, swap_z, ends):
    cols, gzs = lax.axis_size("col"), lax.axis_size("gz")
    sides = parts[0].shape[1]
    lines = held.shape[1]
    if cols == 2 and gzs == 4 and lines // cols == sides and sides // gzs % 8 == 0:
        mine, other = surface(parts, held, 2)
        mine, other, late, ends = lax.optimization_barrier((mine, other, late, ends))
        other = lax.ppermute(other, "col", [(0, 1), (1, 0)])
        other, tips = lax.optimization_barrier((other, swap_z(ends)))
        keep, send = shares(mine, other)
        for bit in (1, 2):
            got = lax.ppermute(send, "gz", [(i, i ^ bit) for i in range(gzs)])
            if bit == 1:
                keep, send = halve(keep, got)
        return [keep, got], late, tips
    (total,) = surface(parts, held, 1)
    rows = lax.psum_scatter(total, "col", scatter_dimension=0, tiled=True)
    owned = lax.psum_scatter(rows, "gz", scatter_dimension=0, tiled=True)
    flux = lax.psum_scatter(rows.T, "gz", scatter_dimension=0, tiled=True)
    flux = jnp.pad(flux, ((0, 0), (0, sides - flux.shape[1])))
    return [jnp.concatenate([owned, flux], axis=0)], late, swap_z(ends)


def turns(axis):
    return 1 if lax.axis_size(axis) == 2 else 2


def partner(index, turn):
    return jnp.where(index % 2 == turn, index + 1, index - 1)


def has_neighbour(axis, turn):
    other = partner(lax.axis_index(axis), turn)
    return (other >= 0) & (other < lax.axis_size(axis))


def swap(value, axis, turn):
    axes = ("row", "col", "gz")
    sizes = [lax.axis_size(name) for name in axes]
    along = axes.index(axis)
    spare = 0 if axis == "gz" else 2
    pairs = []
    for r in range(sizes[0]):
        for c in range(sizes[1]):
            for g in range(sizes[2]):
                here = [r, c, g]
                there = [r, c, g]
                there[along] += 1 if here[along] % 2 == turn else -1
                if not 0 <= there[along] < sizes[along]:
                    there[along] = here[along]
                    if here[spare] ^ 1 < sizes[spare]:
                        there[spare] ^= 1
                flat = [(at[0] * sizes[1] + at[1]) * sizes[2] + at[2] for at in (here, there)]
                pairs.append(tuple(flat))
    return lax.ppermute(value, axes, pairs)


class Shape:
    def __init__(self, sides, first, second, lanes):
        self.sides, self.x, self.y, self.lanes = sides, first, second, lanes
        self.cells = first * second
        self.chunk = max(1, 128 // self.cells)
        self.rows = self.chunk * self.cells
        self.block = min(sides, 32)
        self.half = self.block // 2
        self.half_rows = self.half * self.cells
        self.outer = [("col", i) for i in range(turns("col"))]
        self.inner = [("row", i) for i in reversed(range(turns("row")))]
        self.faces = self.outer + self.inner
        self.ends = turns("gz")

    def face_len(self, face):
        return self.y if face[0] == "row" else self.x

    def halo_rows(self):
        return sum(self.chunk * self.face_len(face) for face in self.faces)

    def edge(self, face):
        axis, turn = face
        last = (self.x if axis == "row" else self.y) - 1
        return jnp.where(lax.axis_index(axis) % 2 == turn, last, 0)


def halo_place(shape):
    dims = (shape.rows, shape.halo_rows())
    row, col = iota(dims, 0), iota(dims, 1)
    side, cell = row // shape.cells, row % shape.cells
    x, y = cell // shape.y, cell % shape.y
    hit, base = None, 0
    for face in shape.faces:
        length = shape.face_len(face)
        along, across = (y, x) if face[0] == "row" else (x, y)
        place = (across == shape.edge(face)) & (col - base == side * length + along)
        place = place & has_neighbour(*face)
        hit = place if hit is None else hit | place
        base += shape.chunk * length
    return hit.astype(BF)


def z_mask(shape, count):
    dims = (count * shape.cells, 2 * shape.cells)
    return iota(dims, 1) % shape.cells == iota(dims, 0) % shape.cells


def twice(matrix):
    zero = jnp.zeros_like(matrix)
    return jnp.concatenate(
        [jnp.concatenate([matrix, zero], axis=1), jnp.concatenate([zero, matrix], axis=1)], axis=0
    )


def beside(values):
    half = values.shape[0] // 2
    return jnp.concatenate([values[:half], values[half:]], axis=1)


def build_out(shape, ends_m, rsum):
    dims = (shape.lanes, 2 * shape.cells)
    edge = jnp.where(iota(dims, 1) < shape.cells, 0, shape.lanes - 1)
    ends_m[...] = twice((iota(dims, 0) == edge).astype(F32)).astype(BF)
    dims = rsum.shape
    rsum[...] = (iota(dims, 1) // shape.cells == iota(dims, 0)).astype(BF)


def cut_faces(shape, faces, at, block, tall, face_refs):
    for face, ref in zip(faces, face_refs):
        length, edge = shape.face_len(face), shape.edge(face)
        lines = []
        for side in range(block):
            start = side * shape.cells
            if face[0] == "row":
                lines.append(tall[pl.ds(aligned(start + edge * length, 8), length), :])
            else:
                lines.append(tall[pl.ds(start + edge, length, stride=shape.y), :])
        span = slice(at * length, (at + block) * length)
        ref[span, :] = jnp.concatenate(lines, axis=0).astype(BF)


def cut_ends(shape, at, values, z_ref, ends_m, rsum):
    mask = jnp.concatenate([z_mask(shape, shape.half)] * 2, axis=1)
    tips = jnp.where(mask, dot(beside(values), ends_m[...]), 0.0).astype(BF)
    tips = dot(rsum[...], tips)[: shape.half]
    tips = jnp.concatenate([tips[:, : 2 * shape.cells], tips[:, 2 * shape.cells :]], axis=0)
    z_ref[at : at + shape.block, :] = tips.astype(BF)


def build_tables(shape, coef_ref, weight, near_m, line_m, ends_m, rsum):
    cells, lanes = shape.cells, shape.lanes
    weight[...] = jnp.concatenate([OMEGA / (6.0 + coef_ref[...])] * shape.chunk, axis=0)
    dims = (shape.rows, shape.rows)
    row, col = iota(dims, 0), iota(dims, 1)
    x, y = row % cells // shape.y, row % shape.y
    x2, y2 = col % cells // shape.y, col % shape.y
    near = ((x == x2) & (jnp.abs(y - y2) == 1)) | ((y == y2) & (jnp.abs(x - x2) == 1))
    near_m[:, : shape.rows] = (near & (row // cells == col // cells)).astype(BF)
    near_m[:, shape.rows :] = halo_place(shape)
    dims = (lanes, lanes)
    line = (jnp.abs(iota(dims, 0) - iota(dims, 1)) == 1).astype(F32)
    line_m[: 2 * lanes, :] = twice(line).astype(BF)
    dims = (2 * cells, lanes)
    edge = jnp.where(iota(dims, 0) < cells, lanes - 1, 0)
    line_m[2 * lanes :, :] = twice((iota(dims, 1) == edge).astype(F32)).astype(BF)
    build_out(shape, ends_m, rsum)


def table_shapes(shape):
    lanes, cells = shape.lanes, shape.cells
    return [
        jax.ShapeDtypeStruct((shape.rows, lanes), F32),
        jax.ShapeDtypeStruct((shape.rows, shape.rows + shape.halo_rows()), BF),
        jax.ShapeDtypeStruct((2 * lanes + 4 * cells, 2 * lanes), BF),
        jax.ShapeDtypeStruct((2 * lanes, 4 * cells), BF),
        jax.ShapeDtypeStruct((max(8, shape.half), shape.half_rows), BF),
    ]


def faces_kernel(shape, slots, field_ref, block_ref, coef_ref, *refs):
    refs = list(refs)
    face_refs = [refs.pop(0) for _ in shape.inner]
    z_ref, held, *tables, field, tall, sems, field_sems = refs
    size = shape.block * shape.cells
    steps = shape.sides // shape.block
    copies = []
    for step in range(steps):
        span = pl.ds(step * size, size)
        copies.append(
            pltpu.make_async_copy(field_ref.at[span], field.at[span], field_sems.at[step])
        )
        copies[-1].start()
    columns = fetch_columns(block_ref, held, sems, slots)
    build_tables(shape, coef_ref, *tables)
    ends_m, rsum = tables[-2:]
    for step in range(steps):
        copies[step].wait()
        values = field[step * size : (step + 1) * size, :]
        tall[step] = values.astype(F32)
        cut_faces(shape, shape.inner, step * shape.block, shape.block, tall.at[step], face_refs)
        cut_ends(shape, step * shape.block, values, z_ref, ends_m, rsum)
    for copy in columns:
        copy.wait()


def face_shapes(shape, faces):
    return [
        jax.ShapeDtypeStruct((shape.sides * shape.face_len(face), shape.lanes), BF)
        for face in faces
    ]


def first_faces(shape, field, block, coef, slots):
    peers = lax.axis_size("row")
    steps = shape.sides // shape.block
    shapes = face_shapes(shape, shape.inner)
    shapes.append(jax.ShapeDtypeStruct((shape.sides, 2 * shape.cells), BF))
    shapes.append(jax.ShapeDtypeStruct((peers, block.shape[0], slots), BF))
    shapes += table_shapes(shape)
    hbm = pl.BlockSpec(memory_space=pltpu.HBM)
    return pl.pallas_call(
        functools.partial(faces_kernel, shape, slots),
        in_specs=[hbm, hbm, WHOLE],
        out_specs=[WHOLE] * len(shapes),
        out_shape=shapes,
        scratch_shapes=[
            pltpu.VMEM(field.shape, BF),
            pltpu.VMEM((steps, shape.block * shape.cells, shape.lanes), F32),
            pltpu.SemaphoreType.DMA((peers,)),
            pltpu.SemaphoreType.DMA((steps,)),
        ],
        compiler_params=params(FACES_MIB),
        cost_estimate=pl.CostEstimate(
            flops=field.size * 128, bytes_accessed=4 * field.size, transcendentals=0
        ),
    )(field, block, coef)


def sweep_kernel(shape, recvs, last, *refs):
    with_flux = recvs > 0
    refs = list(refs)
    take = lambda count: [refs.pop(0) for _ in range(count)]
    field_ref, load_ref, weight, near_m, line_m, ends_m, rsum = take(7)
    halo_refs = take(len(shape.faces))
    end_refs = take(shape.ends)
    if with_flux:
        recv_refs = take(recvs)
        (cell_ref,) = take(1)
    (out_ref,) = take(1)
    if not last:
        face_refs = take(len(shape.faces))
        (z_ref,) = take(1)
    if with_flux:
        source_ref, flux_ref = take(2)
    (lines,) = take(1)
    if last:
        result_ref = out_ref
        out_ref, out_sems = take(2)
    else:
        (tall,) = take(1)
    if with_flux:
        phi, cell_m, placed = take(3)

    cells, lanes = shape.cells, shape.lanes

    if with_flux:
        slots = cell_ref.shape[3]
        owned = recv_refs[0][...]
        for ref in recv_refs[1:]:
            owned = owned + ref[...]
        flux_ref[...] = owned[slots:, : flux_ref.shape[1]]
        owned = owned[:slots]
        high = owned.astype(BF).astype(F32)
        both = jnp.concatenate([high, owned - high], axis=0)
        phi[...] = both.T
        cell = jnp.concatenate([cell_ref[0, 0]] * 2, axis=1)
        cell_m[...] = twice((iota((lanes, 2 * slots), 0) == cell % lanes).astype(F32)).astype(BF)

    mask = z_mask(shape, 1)
    even = lax.axis_index("gz") % 2 == 0
    filled = (iota((shape.block, 2 * cells), 1) < cells) == even
    if with_flux:
        slots = cell_ref.shape[3]
        cell = jnp.concatenate([cell_ref[0, 0]] * 2, axis=1)
        cell_mask = iota((cells, 2 * slots), 0) == cell // lanes
    weights = weight[...]

    def expand(lines, where, first):
        rows = []
        for side in range(first, first + shape.half):
            line = jnp.broadcast_to(lines[side : side + 1], where.shape)
            rows.append(jnp.where(where, line, 0.0))
        return jnp.concatenate(rows, axis=0).astype(BF)

    def work(step):
        at = step * shape.block
        sides = pl.ds(aligned(at, shape.block), shape.block)
        size = shape.block * cells
        zs = 0.0
        for turn in range(shape.ends):
            wanted = (filled == (turn == 0)) & has_neighbour("gz", turn)
            zs = jnp.where(wanted, end_refs[turn][sides, :].astype(F32), zs)
        values = field_ref[pl.ds(aligned(at * cells, size), size), :]
        left = [beside(values), expand(zs, mask, 0), expand(zs, mask, shape.half)]
        lines[step] = dot(jnp.concatenate(left, axis=1), line_m[...])
        if with_flux:
            phis = phi[sides, :]
            left = [expand(phis, cell_mask, 0), expand(phis, cell_mask, shape.half)]
            placed[step] = dot_nt(jnp.concatenate(left, axis=1), cell_m[...])
        for index in range(shape.half // shape.chunk):
            offset = index * shape.rows
            starts = (offset, offset + shape.half_rows)
            stacks = []
            for start in starts:
                rows = pl.ds(aligned(at * cells + start, shape.rows), shape.rows)
                stack = [field_ref[rows, :]]
                for face, ref in zip(shape.faces, halo_refs):
                    length = shape.face_len(face)
                    count = shape.chunk * length
                    first = aligned(at * length + start // cells * length, count)
                    stack.append(ref[pl.ds(first, count), :])
                stacks.append(jnp.concatenate(stack, axis=0))
            near = dot(near_m[...], jnp.concatenate(stacks, axis=1))
            near = near + lines[step, offset : offset + shape.rows, :]
            for part, start in enumerate(starts):
                cols = slice(part * lanes, (part + 1) * lanes)
                rows = pl.ds(aligned(at * cells + start, shape.rows), shape.rows)
                source = load_ref[rows, :].astype(F32)
                if with_flux:
                    source = source + placed[step, offset : offset + shape.rows, cols]
                    source_ref[rows, :] = source.astype(BF)
                centre = field_ref[rows, :].astype(F32)
                fresh = (1.0 - OMEGA) * centre + weights * (source + near[:, cols])
                out_ref[rows, :] = fresh.astype(BF)
                if not last:
                    tall[step, start : start + shape.rows, :] = fresh

    def emit(step):
        at, size = step * shape.block, shape.block * cells
        fresh = out_ref[at * cells : at * cells + size, :]
        cut_faces(shape, shape.faces, at, shape.block, tall.at[step], face_refs)
        cut_ends(shape, at, fresh, z_ref, ends_m, rsum)

    steps = shape.sides // shape.block
    copies = []
    for step in range(steps):
        work(step)
        if last:
            span = pl.ds(step * shape.block * cells, shape.block * cells)
            copies.append(
                pltpu.make_async_copy(out_ref.at[span], result_ref.at[span], out_sems.at[step])
            )
            copies[-1].start()
        elif step > 0:
            emit(step - 1)
    for copy in copies:
        copy.wait()
    if not last:
        emit(steps - 1)


def sweep(shape, field, load, tables, halos, recv=(), flux_cell=None, last=False):
    lanes, cells = shape.lanes, shape.cells
    steps = shape.sides // shape.block
    half = (steps, shape.half_rows, 2 * lanes)
    operands = [field, load, *tables, *halos, *recv]
    out_shapes = [jax.ShapeDtypeStruct(field.shape, BF)]
    scratch = [pltpu.VMEM(half, F32)]
    if last:
        scratch += [pltpu.VMEM(field.shape, BF), pltpu.SemaphoreType.DMA((steps,))]
    else:
        out_shapes += face_shapes(shape, shape.faces)
        out_shapes.append(jax.ShapeDtypeStruct((shape.sides, 2 * cells), BF))
        scratch.append(pltpu.VMEM((steps, shape.block * cells, lanes), F32))
    if recv:
        slots = flux_cell.shape[3]
        operands.append(flux_cell)
        out_shapes += [
            jax.ShapeDtypeStruct(field.shape, BF),
            jax.ShapeDtypeStruct((recv[0].shape[0] - slots, slots * lax.axis_size("gz")), F32),
        ]
        scratch += [
            pltpu.VMEM((shape.sides, 2 * slots), F32),
            pltpu.VMEM((2 * lanes, 4 * slots), BF),
            pltpu.VMEM(half, F32),
        ]
    out_specs = [WHOLE] * len(out_shapes)
    if last:
        out_specs = [pl.BlockSpec(memory_space=pltpu.HBM)]
    return pl.pallas_call(
        functools.partial(sweep_kernel, shape, len(recv), last),
        in_specs=[WHOLE] * len(operands),
        out_specs=out_specs,
        out_shape=out_shapes,
        scratch_shapes=scratch,
        compiler_params=params(),
        cost_estimate=pl.CostEstimate(
            flops=6 * field.size * 128, bytes_accessed=8 * field.size, transcendentals=0
        ),
    )(*operands)


def swap_faces(faces, values):
    return [swap(value, *face) for face, value in zip(faces, values)]


def swap_ends(shape, ends):
    return [swap(ends, "gz", turn) for turn in range(shape.ends)]


def exchange(shape, faces):
    *cut, ends = faces
    return swap_faces(shape.faces, cut) + swap_ends(shape, ends)


def row_gather(trace, hidden):
    peers = lax.axis_size("row")
    held = {0: trace}
    bit = peers // 2
    while bit:
        pairs = [(i, i ^ bit) for i in range(peers)]
        fresh = {key ^ bit: lax.ppermute(held[key], "row", pairs) for key in sorted(held, reverse=True)}
        if bit == peers // 2:
            held, fresh, hidden = lax.optimization_barrier((held, fresh, hidden))
        held.update(fresh)
        bit //= 2
    return [held[key] for key in range(peers)], hidden


def per_device(volume_field, volume_load, coefficient, surface_block, trace_cell, flux_cell):
    sides, first, second, lanes = volume_field.shape
    cells = first * second
    shape = Shape(sides, first, second, lanes)
    field = volume_field.reshape(sides * cells, lanes)
    load = volume_load.reshape(sides * cells, lanes)
    coef = coefficient.reshape(cells, lanes)

    slots = trace_cell.shape[3]
    trace, *outer = traces(
        shape, volume_field.reshape(sides, cells, lanes), trace_cell, min(32, sides)
    )
    firsts = first_faces(shape, field, surface_block, coef, slots)
    layers = len(shape.faces)
    count = len(shape.inner) + 1
    inner, held, tables = firsts[:count], firsts[count], firsts[count + 1 :]
    *inner, ends = inner
    along_col = swap_faces(shape.outer, outer)
    along_row = swap_faces(shape.inner, inner)
    parts, (_, along_col) = row_gather(trace, (inner, along_col))
    parts, along_row = lax.optimization_barrier((parts, along_row))
    swap_z = functools.partial(swap_ends, shape)
    recv, along_row, tips = flux_sums(parts, held, along_row, swap_z, ends)
    halos = along_col + along_row + tips

    current, *faces, source, surface_flux = sweep(
        shape, field, load, tables, halos, recv=recv, flux_cell=flux_cell
    )
    current, *faces = sweep(shape, current, source, tables, exchange(shape, faces))
    (current,) = sweep(shape, current, source, tables, exchange(shape, faces), last=True)
    return current.reshape(volume_field.shape), surface_flux


def solution(mesh):
    in_specs = (
        P(None, "row", "col", "gz"),
        P(None, "row", "col", "gz"),
        P("row", "col", "gz"),
        P("row", "col"),
        P("row", "col", "gz", None),
        P("row", "col", "gz", None),
    )
    out_specs = (P(None, "row", "col", "gz"), P("gz", ("row", "col")))
    return jax.shard_map(
        per_device, mesh=mesh, in_specs=in_specs, out_specs=out_specs, check_vma=False
    )
```

```python
import functools

import jax
import jax.numpy as jnp
from jax import lax
from jax.experimental import pallas as pl
from jax.experimental.pallas import tpu as pltpu
from jax.sharding import PartitionSpec as P

OMEGA = 0.8
BF = jnp.bfloat16
F32 = jnp.float32
WHOLE = pl.BlockSpec(memory_space=pltpu.VMEM)


def aligned(start, unit):
    return start if isinstance(start, int) else pl.multiple_of(start, unit)


def iota(shape, dim):
    return lax.broadcasted_iota(jnp.int32, shape, dim)


def dot(a, b):
    return jnp.dot(a, b, preferred_element_type=F32)


def dot_nt(a, b):
    return lax.dot_general(a, b, (((1,), (1,)), ((), ())), preferred_element_type=F32)


FACES_MIB = 50


def params(mebibytes=24):
    return pltpu.CompilerParams(vmem_limit_bytes=mebibytes * 1024 * 1024)


def trace_kernel(shape, stride, block, field_ref, cell_ref, out_ref, *refs):
    *face_refs, field, cell_v, tall, near, place, picked, sems = refs
    sides, rows, lanes = field.shape
    slots = cell_ref.shape[3]
    per_row = lanes // stride
    width = near.shape[0]
    parts = slots // width
    cell_copy = pltpu.make_async_copy(cell_ref, cell_v, sems.at[sides // block])
    cell_copy.start()
    copies = []
    for step in range(sides // block):
        span = pl.ds(step * block, block)
        copies.append(pltpu.make_async_copy(field_ref.at[span], field.at[span], sems.at[step]))
        copies[-1].start()

    cell_copy.wait()
    cell = cell_v[0, 0]
    run = cell // stride
    digit = jnp.zeros_like(cell)
    for part in range(parts):
        digit = jnp.where(run // width == part, (cell % stride) * stride**part, digit)
    hit = iota((width, slots), 0) == run % width
    near[...] = hit.astype(BF)
    digits = jnp.sum(jnp.where(hit, digit.astype(F32), 0.0), axis=1, keepdims=True)
    digits = jnp.broadcast_to(digits, (width, 128)).T[0:8].astype(jnp.int32)
    first = iota((8, width), 1) % per_row * stride
    for part in range(parts):
        place[:, part * width : (part + 1) * width] = first + digits // stride**part % stride

    together = 128 // per_row
    group = iota((8, 128), 1) // per_row
    for step in range(sides // block):
        copies[step].wait()
        span = field[step * block : (step + 1) * block]
        tall[step] = span.reshape(block * rows, lanes).astype(F32)
        cut_faces(shape, shape.outer, step * block, block, tall.at[step], face_refs)

        for batch in range(block // 8):
            for tile in range(rows // together):
                cols = slice(tile * 128, (tile + 1) * 128)
                where = place[:, cols]
                found = None
                for row in range(together):
                    start = batch * 8 * rows + tile * together + row
                    line = tall[step, pl.ds(start, 8, stride=rows), :]
                    line = jnp.take_along_axis(line, where, axis=1)
                    found = line if found is None else jnp.where(group == row, line, found)
                at = step * block + batch * 8
                picked[at : at + 8, cols] = found

    total = jnp.zeros((sides, slots), F32)
    for part in range(parts):
        sorted_runs = picked[:, part * width : (part + 1) * width].astype(BF)
        total = jnp.where(run // width == part, dot(sorted_runs, near[...]), total)
    out_ref[...] = total.T.astype(BF)


def traces(shape, field, trace_cell, block):
    sides, rows, lanes = field.shape
    slots = trace_cell.shape[3]
    stride = rows * lanes // slots
    width = min(slots, 256)
    hbm = pl.BlockSpec(memory_space=pltpu.HBM)
    return pl.pallas_call(
        functools.partial(trace_kernel, shape, stride, block),
        in_specs=[hbm, hbm],
        out_specs=[WHOLE] * (1 + len(shape.outer)),
        out_shape=[jax.ShapeDtypeStruct((slots, sides), BF)] + face_shapes(shape, shape.outer),
        scratch_shapes=[
            pltpu.VMEM(field.shape, BF),
            pltpu.VMEM(trace_cell.shape, jnp.int32),
            pltpu.VMEM((sides // block, block * rows, lanes), F32),
            pltpu.VMEM((width, slots), BF),
            pltpu.VMEM((8, slots), jnp.int32),
            pltpu.VMEM((sides, slots), F32),
            pltpu.SemaphoreType.DMA((sides // block + 1,)),
        ],
        compiler_params=params(62),
        cost_estimate=pl.CostEstimate(
            flops=4 * sides * rows * lanes * 128, bytes_accessed=field.size * 2, transcendentals=0
        ),
    )(field, trace_cell)


def fetch_columns(block_ref, held, sems, slots):
    me, group, gzs = lax.axis_index("row"), lax.axis_index("gz"), lax.axis_size("gz")
    copies = []
    for key in range(held.shape[0]):
        start = pl.multiple_of((jnp.bitwise_xor(me, key) * gzs + group) * slots, slots)
        copies.append(
            pltpu.make_async_copy(block_ref.at[:, pl.ds(start, slots)], held.at[key], sems.at[key])
        )
        copies[-1].start()
    return copies


def surface_kernel(halves, *refs):
    ins, total = refs[:-1], refs[-1]
    outs = ins[len(ins) - halves :]
    *parts, held = ins[: len(ins) - halves]
    value = None
    for key, part in enumerate(parts):
        term = dot(held[key], part[...])
        value = term if value is None else value + term
    if halves == 1:
        outs[0][...] = value
        return
    total[...] = value
    count = outs[0].shape[0]
    mine = lax.axis_index("col")
    for key, out in enumerate(outs):
        out[...] = total[pl.ds(pl.multiple_of((mine ^ key) * count, 8), count), :]


def surface(parts, held, halves):
    sides = parts[0].shape[1]
    lines = held.shape[1]
    return pl.pallas_call(
        functools.partial(surface_kernel, halves),
        in_specs=[WHOLE] * (len(parts) + 1),
        out_specs=[WHOLE] * halves,
        out_shape=[jax.ShapeDtypeStruct((lines // halves, sides), F32)] * halves,
        scratch_shapes=[pltpu.VMEM((lines, sides), F32)],
        compiler_params=params(),
        cost_estimate=pl.CostEstimate(
            flops=2 * sides * held.size, bytes_accessed=2 * held.size, transcendentals=0
        ),
    )(*parts, held)


def share_kernel(peers, mine_ref, other_ref, *refs):
    *outs, total, turned = refs
    total[...] = mine_ref[...] + other_ref[...]
    turned[...] = total[...].T
    lines, sides = total.shape
    group = lax.axis_index("gz")
    for key, out in enumerate(outs):
        peer = group ^ key
        rows, some = lines // peers, sides // peers
        out[:rows, :] = total[pl.ds(pl.multiple_of(peer * rows, 8), rows), :]
        out[rows:, :] = turned[pl.ds(pl.multiple_of(peer * some, 8), some), :]


def shares(mine, other):
    peers = lax.axis_size("gz")
    lines, sides = mine.shape
    out = jax.ShapeDtypeStruct(((lines + sides) // peers, sides), F32)
    return pl.pallas_call(
        functools.partial(share_kernel, peers),
        in_specs=[WHOLE] * 2,
        out_specs=[WHOLE] * peers,
        out_shape=[out] * peers,
        scratch_shapes=[pltpu.VMEM((lines, sides), F32), pltpu.VMEM((sides, lines), F32)],
        compiler_params=params(),
        cost_estimate=pl.CostEstimate(
            flops=lines * sides, bytes_accessed=16 * lines * sides, transcendentals=0
        ),
    )(mine, other)


def flux_sums(parts, held, late, after):
    cols, gzs = lax.axis_size("col"), lax.axis_size("gz")
    sides = parts[0].shape[1]
    lines = held.shape[1]
    if cols == 2 and gzs & (gzs - 1) == 0 and lines // cols == sides and sides // gzs % 8 == 0:
        mine, other = surface(parts, held, 2)
        mine, other, after = lax.optimization_barrier((mine, other, after))
        other = lax.ppermute(other, "col", [(0, 1), (1, 0)])
        other, late = lax.optimization_barrier((other, late))
        sent = shares(mine, other)
        recv = [sent[0]]
        for key in range(gzs - 1, 0, -1):
            recv.append(lax.ppermute(sent[key], "gz", [(i, i ^ key) for i in range(gzs)]))
        return recv, after
    (total,) = surface(parts, held, 1)
    rows = lax.psum_scatter(total, "col", scatter_dimension=0, tiled=True)
    owned = lax.psum_scatter(rows, "gz", scatter_dimension=0, tiled=True)
    flux = lax.psum_scatter(rows.T, "gz", scatter_dimension=0, tiled=True)
    flux = jnp.pad(flux, ((0, 0), (0, sides - flux.shape[1])))
    return [jnp.concatenate([owned, flux], axis=0)], after


def turns(axis):
    return 1 if lax.axis_size(axis) == 2 else 2


def partner(index, turn):
    return jnp.where(index % 2 == turn, index + 1, index - 1)


def has_neighbour(axis, turn):
    other = partner(lax.axis_index(axis), turn)
    return (other >= 0) & (other < lax.axis_size(axis))


def swap(value, axis, turn):
    axes = ("row", "col", "gz")
    sizes = [lax.axis_size(name) for name in axes]
    along = axes.index(axis)
    spare = 0 if axis == "gz" else 2
    pairs = []
    for r in range(sizes[0]):
        for c in range(sizes[1]):
            for g in range(sizes[2]):
                here = [r, c, g]
                there = [r, c, g]
                there[along] += 1 if here[along] % 2 == turn else -1
                if not 0 <= there[along] < sizes[along]:
                    there[along] = here[along]
                    if here[spare] ^ 1 < sizes[spare]:
                        there[spare] ^= 1
                flat = [(at[0] * sizes[1] + at[1]) * sizes[2] + at[2] for at in (here, there)]
                pairs.append(tuple(flat))
    return lax.ppermute(value, axes, pairs)


class Shape:
    def __init__(self, sides, first, second, lanes):
        self.sides, self.x, self.y, self.lanes = sides, first, second, lanes
        self.cells = first * second
        self.chunk = max(1, 128 // self.cells)
        self.rows = self.chunk * self.cells
        self.block = min(sides, 32)
        self.half = self.block // 2
        self.half_rows = self.half * self.cells
        self.outer = [("col", i) for i in range(turns("col"))]
        self.inner = [("row", i) for i in reversed(range(turns("row")))]
        self.faces = self.outer + self.inner
        self.ends = turns("gz")

    def face_len(self, face):
        return self.y if face[0] == "row" else self.x

    def halo_rows(self):
        return sum(self.chunk * self.face_len(face) for face in self.faces)

    def edge(self, face):
        axis, turn = face
        last = (self.x if axis == "row" else self.y) - 1
        return jnp.where(lax.axis_index(axis) % 2 == turn, last, 0)


def halo_place(shape):
    dims = (shape.rows, shape.halo_rows())
    row, col = iota(dims, 0), iota(dims, 1)
    side, cell = row // shape.cells, row % shape.cells
    x, y = cell // shape.y, cell % shape.y
    hit, base = None, 0
    for face in shape.faces:
        length = shape.face_len(face)
        along, across = (y, x) if face[0] == "row" else (x, y)
        place = (across == shape.edge(face)) & (col - base == side * length + along)
        place = place & has_neighbour(*face)
        hit = place if hit is None else hit | place
        base += shape.chunk * length
    return hit.astype(BF)


def z_mask(shape, count):
    dims = (count * shape.cells, 2 * shape.cells)
    return iota(dims, 1) % shape.cells == iota(dims, 0) % shape.cells


def twice(matrix):
    zero = jnp.zeros_like(matrix)
    return jnp.concatenate(
        [jnp.concatenate([matrix, zero], axis=1), jnp.concatenate([zero, matrix], axis=1)], axis=0
    )


def beside(values):
    half = values.shape[0] // 2
    return jnp.concatenate([values[:half], values[half:]], axis=1)


def build_out(shape, ends_m, rsum):
    dims = (shape.lanes, 2 * shape.cells)
    edge = jnp.where(iota(dims, 1) < shape.cells, 0, shape.lanes - 1)
    ends_m[...] = twice((iota(dims, 0) == edge).astype(F32)).astype(BF)
    dims = rsum.shape
    rsum[...] = (iota(dims, 1) // shape.cells == iota(dims, 0)).astype(BF)


def cut_faces(shape, faces, at, block, tall, face_refs):
    for face, ref in zip(faces, face_refs):
        length, edge = shape.face_len(face), shape.edge(face)
        lines = []
        for side in range(block):
            start = side * shape.cells
            if face[0] == "row":
                lines.append(tall[pl.ds(aligned(start + edge * length, 8), length), :])
            else:
                lines.append(tall[pl.ds(start + edge, length, stride=shape.y), :])
        span = slice(at * length, (at + block) * length)
        ref[span, :] = jnp.concatenate(lines, axis=0).astype(BF)


def cut_ends(shape, at, values, z_ref, ends_m, rsum):
    mask = jnp.concatenate([z_mask(shape, shape.half)] * 2, axis=1)
    tips = jnp.where(mask, dot(beside(values), ends_m[...]), 0.0).astype(BF)
    tips = dot(rsum[...], tips)[: shape.half]
    tips = jnp.concatenate([tips[:, : 2 * shape.cells], tips[:, 2 * shape.cells :]], axis=0)
    z_ref[at : at + shape.block, :] = tips.astype(BF)


def build_tables(shape, coef_ref, weight, near_m, line_m, ends_m, rsum):
    cells, lanes = shape.cells, shape.lanes
    weight[...] = jnp.concatenate([OMEGA / (6.0 + coef_ref[...])] * shape.chunk, axis=0)
    dims = (shape.rows, shape.rows)
    row, col = iota(dims, 0), iota(dims, 1)
    x, y = row % cells // shape.y, row % shape.y
    x2, y2 = col % cells // shape.y, col % shape.y
    near = ((x == x2) & (jnp.abs(y - y2) == 1)) | ((y == y2) & (jnp.abs(x - x2) == 1))
    near_m[:, : shape.rows] = (near & (row // cells == col // cells)).astype(BF)
    near_m[:, shape.rows :] = halo_place(shape)
    dims = (lanes, lanes)
    line = (jnp.abs(iota(dims, 0) - iota(dims, 1)) == 1).astype(F32)
    line_m[: 2 * lanes, :] = twice(line).astype(BF)
    dims = (2 * cells, lanes)
    edge = jnp.where(iota(dims, 0) < cells, lanes - 1, 0)
    line_m[2 * lanes :, :] = twice((iota(dims, 1) == edge).astype(F32)).astype(BF)
    build_out(shape, ends_m, rsum)


def table_shapes(shape):
    lanes, cells = shape.lanes, shape.cells
    return [
        jax.ShapeDtypeStruct((shape.rows, lanes), F32),
        jax.ShapeDtypeStruct((shape.rows, shape.rows + shape.halo_rows()), BF),
        jax.ShapeDtypeStruct((2 * lanes + 4 * cells, 2 * lanes), BF),
        jax.ShapeDtypeStruct((2 * lanes, 4 * cells), BF),
        jax.ShapeDtypeStruct((max(8, shape.half), shape.half_rows), BF),
    ]


def faces_kernel(shape, slots, field_ref, block_ref, coef_ref, *refs):
    refs = list(refs)
    face_refs = [refs.pop(0) for _ in shape.inner]
    z_ref, held, *tables, field, tall, sems, field_sems = refs
    size = shape.block * shape.cells
    steps = shape.sides // shape.block
    copies = []
    for step in range(steps):
        span = pl.ds(step * size, size)
        copies.append(
            pltpu.make_async_copy(field_ref.at[span], field.at[span], field_sems.at[step])
        )
        copies[-1].start()
    columns = fetch_columns(block_ref, held, sems, slots)
    build_tables(shape, coef_ref, *tables)
    ends_m, rsum = tables[-2:]
    for step in range(steps):
        copies[step].wait()
        values = field[step * size : (step + 1) * size, :]
        tall[step] = values.astype(F32)
        cut_faces(shape, shape.inner, step * shape.block, shape.block, tall.at[step], face_refs)
        cut_ends(shape, step * shape.block, values, z_ref, ends_m, rsum)
    for copy in columns:
        copy.wait()


def face_shapes(shape, faces):
    return [
        jax.ShapeDtypeStruct((shape.sides * shape.face_len(face), shape.lanes), BF)
        for face in faces
    ]


def first_faces(shape, field, block, coef, slots):
    peers = lax.axis_size("row")
    steps = shape.sides // shape.block
    shapes = face_shapes(shape, shape.inner)
    shapes.append(jax.ShapeDtypeStruct((shape.sides, 2 * shape.cells), BF))
    shapes.append(jax.ShapeDtypeStruct((peers, block.shape[0], slots), BF))
    shapes += table_shapes(shape)
    hbm = pl.BlockSpec(memory_space=pltpu.HBM)
    return pl.pallas_call(
        functools.partial(faces_kernel, shape, slots),
        in_specs=[hbm, hbm, WHOLE],
        out_specs=[WHOLE] * len(shapes),
        out_shape=shapes,
        scratch_shapes=[
            pltpu.VMEM(field.shape, BF),
            pltpu.VMEM((steps, shape.block * shape.cells, shape.lanes), F32),
            pltpu.SemaphoreType.DMA((peers,)),
            pltpu.SemaphoreType.DMA((steps,)),
        ],
        compiler_params=params(FACES_MIB),
        cost_estimate=pl.CostEstimate(
            flops=field.size * 128, bytes_accessed=4 * field.size, transcendentals=0
        ),
    )(field, block, coef)


def base_kernel(shape, field_ref, load_ref, weight, near_m, line_m, base_ref, lines):
    cells, lanes = shape.cells, shape.lanes
    weights = weight[...]
    for step in range(shape.sides // shape.block):
        at = step * shape.block * cells
        values = field_ref[at : at + shape.block * cells, :]
        lines[step] = dot(beside(values), line_m[: 2 * lanes, :])
        for index in range(shape.half // shape.chunk):
            offset = index * shape.rows
            spans = [
                slice(at + start, at + start + shape.rows)
                for start in (offset, offset + shape.half_rows)
            ]
            stack = jnp.concatenate([field_ref[span, :] for span in spans], axis=1)
            near = dot(near_m[:, : shape.rows], stack) + lines[step, offset : offset + shape.rows, :]
            for part, span in enumerate(spans):
                source = load_ref[span, :].astype(F32)
                centre = field_ref[span, :].astype(F32)
                near_part = near[:, part * lanes : (part + 1) * lanes]
                base_ref[span, :] = (1.0 - OMEGA) * centre + weights * (source + near_part)


def sweep_base(shape, field, load, tables):
    steps = shape.sides // shape.block
    return pl.pallas_call(
        functools.partial(base_kernel, shape),
        in_specs=[WHOLE] * 5,
        out_specs=WHOLE,
        out_shape=jax.ShapeDtypeStruct(field.shape, F32),
        scratch_shapes=[pltpu.VMEM((steps, shape.half_rows, 2 * shape.lanes), F32)],
        compiler_params=params(),
        cost_estimate=pl.CostEstimate(
            flops=6 * field.size * 128, bytes_accessed=8 * field.size, transcendentals=0
        ),
    )(field, load, *tables[:3])


def finish_kernel(shape, recvs, last, *refs):
    with_flux = recvs > 0
    refs = list(refs)
    take = lambda count: [refs.pop(0) for _ in range(count)]
    base_ref, weight, near_m, line_m, ends_m, rsum = take(6)
    halo_refs = take(len(shape.faces))
    end_refs = take(shape.ends)
    if with_flux:
        load_ref, cell_ref = take(2)
        recv_refs = take(recvs)
    (out_ref,) = take(1)
    if not last:
        face_refs = take(len(shape.faces))
        (z_ref,) = take(1)
    if with_flux:
        source_ref, flux_ref = take(2)
    (lines,) = take(1)
    if last:
        result_ref = out_ref
        out_ref, out_sems = take(2)
    else:
        (tall,) = take(1)
    if with_flux:
        phi, cell_m, placed = take(3)

    cells, lanes = shape.cells, shape.lanes

    if with_flux:
        slots = cell_ref.shape[3]
        owned = recv_refs[0][...]
        for ref in recv_refs[1:]:
            owned = owned + ref[...]
        flux_ref[...] = owned[slots:, : flux_ref.shape[1]]
        owned = owned[:slots]
        high = owned.astype(BF).astype(F32)
        both = jnp.concatenate([high, owned - high], axis=0)
        phi[...] = both.T
        cell = jnp.concatenate([cell_ref[0, 0]] * 2, axis=1)
        cell_m[...] = twice((iota((lanes, 2 * slots), 0) == cell % lanes).astype(F32)).astype(BF)
        cell_mask = iota((cells, 2 * slots), 0) == cell // lanes

    mask = z_mask(shape, 1)
    even = lax.axis_index("gz") % 2 == 0
    filled = (iota((shape.block, 2 * cells), 1) < cells) == even
    weights = weight[...]

    def expand(lines, where):
        rows = []
        for side in range(shape.block):
            line = jnp.broadcast_to(lines[side : side + 1], where.shape)
            rows.append(jnp.where(where, line, 0.0))
        return beside(jnp.concatenate(rows, axis=0).astype(BF))

    def work(step):
        at = step * shape.block
        sides = slice(at, at + shape.block)
        zs = 0.0
        for turn in range(shape.ends):
            wanted = (filled == (turn == 0)) & has_neighbour("gz", turn)
            zs = jnp.where(wanted, end_refs[turn][sides, :].astype(F32), zs)
        lines[step] = dot(expand(zs, mask), line_m[2 * lanes :, :])
        if with_flux:
            placed[step] = dot_nt(expand(phi[sides, :], cell_mask), cell_m[...])
        for index in range(shape.half // shape.chunk):
            offset = index * shape.rows
            starts = (offset, offset + shape.half_rows)
            stacks = []
            for start in starts:
                stack = []
                for face, ref in zip(shape.faces, halo_refs):
                    length = shape.face_len(face)
                    first = at * length + start // cells * length
                    stack.append(ref[first : first + shape.chunk * length, :])
                stacks.append(jnp.concatenate(stack, axis=0))
            near = dot(near_m[:, shape.rows :], jnp.concatenate(stacks, axis=1))
            near = near + lines[step, offset : offset + shape.rows, :]
            if with_flux:
                near = near + placed[step, offset : offset + shape.rows, :]
            for part, start in enumerate(starts):
                cols = slice(part * lanes, (part + 1) * lanes)
                rows = slice(at * cells + start, at * cells + start + shape.rows)
                if with_flux:
                    flux = placed[step, offset : offset + shape.rows, cols]
                    source_ref[rows, :] = (load_ref[rows, :].astype(F32) + flux).astype(BF)
                fresh = base_ref[rows, :] + weights * near[:, cols]
                out_ref[rows, :] = fresh.astype(BF)
                if not last:
                    tall[step, start : start + shape.rows, :] = fresh

    def emit(step):
        at, size = step * shape.block, shape.block * cells
        fresh = out_ref[at * cells : at * cells + size, :]
        cut_faces(shape, shape.faces, at, shape.block, tall.at[step], face_refs)
        cut_ends(shape, at, fresh, z_ref, ends_m, rsum)

    steps = shape.sides // shape.block
    copies = []
    for step in range(steps):
        work(step)
        if last:
            span = pl.ds(step * shape.block * cells, shape.block * cells)
            copies.append(
                pltpu.make_async_copy(out_ref.at[span], result_ref.at[span], out_sems.at[step])
            )
            copies[-1].start()
        elif step > 0:
            emit(step - 1)
    for copy in copies:
        copy.wait()
    if not last:
        emit(steps - 1)


def sweep_finish(shape, base, tables, halos, load=None, flux_cell=None, recv=(), last=False):
    lanes, cells = shape.lanes, shape.cells
    steps = shape.sides // shape.block
    half = (steps, shape.half_rows, 2 * lanes)
    operands = [base, *tables, *halos]
    out_shapes = [jax.ShapeDtypeStruct(base.shape, BF)]
    scratch = [pltpu.VMEM(half, F32)]
    if last:
        scratch += [pltpu.VMEM(base.shape, BF), pltpu.SemaphoreType.DMA((steps,))]
    else:
        out_shapes += face_shapes(shape, shape.faces)
        out_shapes.append(jax.ShapeDtypeStruct((shape.sides, 2 * cells), BF))
        scratch.append(pltpu.VMEM((steps, shape.block * cells, lanes), F32))
    if recv:
        slots = flux_cell.shape[3]
        operands += [load, flux_cell, *recv]
        out_shapes += [
            jax.ShapeDtypeStruct(base.shape, BF),
            jax.ShapeDtypeStruct((recv[0].shape[0] - slots, slots * lax.axis_size("gz")), F32),
        ]
        scratch += [
            pltpu.VMEM((shape.sides, 2 * slots), F32),
            pltpu.VMEM((2 * lanes, 4 * slots), BF),
            pltpu.VMEM(half, F32),
        ]
    out_specs = [WHOLE] * len(out_shapes)
    if last:
        out_specs = [pl.BlockSpec(memory_space=pltpu.HBM)]
    return pl.pallas_call(
        functools.partial(finish_kernel, shape, len(recv), last),
        in_specs=[WHOLE] * len(operands),
        out_specs=out_specs,
        out_shape=out_shapes,
        scratch_shapes=scratch,
        compiler_params=params(),
        cost_estimate=pl.CostEstimate(
            flops=4 * base.size * 128, bytes_accessed=8 * base.size, transcendentals=0
        ),
    )(*operands)


def swap_faces(faces, values):
    return [swap(value, *face) for face, value in zip(faces, values)]


def swap_ends(shape, ends):
    return [swap(ends, "gz", turn) for turn in range(shape.ends)]


def exchange(shape, faces):
    *cut, ends = faces
    return swap_faces(shape.faces, cut) + swap_ends(shape, ends)


def row_gather(trace, hidden):
    peers = lax.axis_size("row")
    held = {0: trace}
    bit = peers // 2
    while bit:
        pairs = [(i, i ^ bit) for i in range(peers)]
        fresh = {key ^ bit: lax.ppermute(held[key], "row", pairs) for key in sorted(held, reverse=True)}
        if bit == peers // 2:
            held, fresh, hidden = lax.optimization_barrier((held, fresh, hidden))
        held.update(fresh)
        bit //= 2
    return [held[key] for key in range(peers)], hidden


def per_device(volume_field, volume_load, coefficient, surface_block, trace_cell, flux_cell):
    sides, first, second, lanes = volume_field.shape
    cells = first * second
    shape = Shape(sides, first, second, lanes)
    field = volume_field.reshape(sides * cells, lanes)
    load = volume_load.reshape(sides * cells, lanes)
    coef = coefficient.reshape(cells, lanes)

    slots = trace_cell.shape[3]
    trace, *outer = traces(
        shape, volume_field.reshape(sides, cells, lanes), trace_cell, min(32, sides)
    )
    firsts = first_faces(shape, field, surface_block, coef, slots)
    layers = len(shape.faces)
    count = len(shape.inner) + 1
    inner, held, tables = firsts[:count], firsts[count], firsts[count + 1 :]
    *inner, ends = inner
    along_col = swap_faces(shape.outer, outer)
    parts, (inner, along_col) = row_gather(trace, (inner, along_col))
    along_row = swap_faces(shape.inner, inner)
    recv, ends = flux_sums(parts, held, along_row, ends)
    halos = along_col + along_row + swap_ends(shape, ends)

    base = sweep_base(shape, field, load, tables)
    current, *faces, source, surface_flux = sweep_finish(
        shape, base, tables, halos, load=load, flux_cell=flux_cell, recv=recv
    )
    for last in (False, True):
        halos = exchange(shape, faces)
        base = sweep_base(shape, current, source, tables)
        current, *faces = sweep_finish(shape, base, tables, halos, last=last)
    return current.reshape(volume_field.shape), surface_flux


def solution(mesh):
    in_specs = (
        P(None, "row", "col", "gz"),
        P(None, "row", "col", "gz"),
        P("row", "col", "gz"),
        P("row", "col"),
        P("row", "col", "gz", None),
        P("row", "col", "gz", None),
    )
    out_specs = (P(None, "row", "col", "gz"), P("gz", ("row", "col")))
    return jax.shard_map(
        per_device, mesh=mesh, in_specs=in_specs, out_specs=out_specs, check_vma=False
    )
```

```python
import functools

import jax
import jax.numpy as jnp
from jax import lax
from jax.experimental import pallas as pl
from jax.experimental.pallas import tpu as pltpu
from jax.sharding import PartitionSpec as P

OMEGA = 0.8
BF = jnp.bfloat16
F32 = jnp.float32
WHOLE = pl.BlockSpec(memory_space=pltpu.VMEM)


def aligned(start, unit):
    return start if isinstance(start, int) else pl.multiple_of(start, unit)


def iota(shape, dim):
    return lax.broadcasted_iota(jnp.int32, shape, dim)


def dot(a, b):
    return jnp.dot(a, b, preferred_element_type=F32)


def dot_nt(a, b):
    return lax.dot_general(a, b, (((1,), (1,)), ((), ())), preferred_element_type=F32)


FACES_MIB = 50


def params(mebibytes=24):
    return pltpu.CompilerParams(vmem_limit_bytes=mebibytes * 1024 * 1024)


def trace_kernel(shape, stride, block, field_ref, cell_ref, out_ref, *refs):
    *face_refs, field, cell_v, tall, near, place, picked, sems = refs
    sides, rows, lanes = field.shape
    slots = cell_ref.shape[3]
    per_row = lanes // stride
    width = near.shape[0]
    parts = slots // width
    cell_copy = pltpu.make_async_copy(cell_ref, cell_v, sems.at[sides // block])
    cell_copy.start()
    copies = []
    for step in range(sides // block):
        span = pl.ds(step * block, block)
        copies.append(pltpu.make_async_copy(field_ref.at[span], field.at[span], sems.at[step]))
        copies[-1].start()

    cell_copy.wait()
    cell = cell_v[0, 0]
    run = cell // stride
    digit = jnp.zeros_like(cell)
    for part in range(parts):
        digit = jnp.where(run // width == part, (cell % stride) * stride**part, digit)
    hit = iota((width, slots), 0) == run % width
    near[...] = hit.astype(BF)
    digits = jnp.sum(jnp.where(hit, digit.astype(F32), 0.0), axis=1, keepdims=True)
    digits = jnp.broadcast_to(digits, (width, 128)).T[0:8].astype(jnp.int32)
    first = iota((8, width), 1) % per_row * stride
    for part in range(parts):
        place[:, part * width : (part + 1) * width] = first + digits // stride**part % stride

    together = 128 // per_row
    group = iota((8, 128), 1) // per_row
    for step in range(sides // block):
        copies[step].wait()
        span = field[step * block : (step + 1) * block]
        tall[step] = span.reshape(block * rows, lanes).astype(F32)
        cut_faces(shape, shape.outer, step * block, block, tall.at[step], face_refs)

        for batch in range(block // 8):
            for tile in range(rows // together):
                cols = slice(tile * 128, (tile + 1) * 128)
                where = place[:, cols]
                found = None
                for row in range(together):
                    start = batch * 8 * rows + tile * together + row
                    line = tall[step, pl.ds(start, 8, stride=rows), :]
                    line = jnp.take_along_axis(line, where, axis=1)
                    found = line if found is None else jnp.where(group == row, line, found)
                at = step * block + batch * 8
                picked[at : at + 8, cols] = found

    total = jnp.zeros((sides, slots), F32)
    for part in range(parts):
        sorted_runs = picked[:, part * width : (part + 1) * width].astype(BF)
        total = jnp.where(run // width == part, dot(sorted_runs, near[...]), total)
    out_ref[...] = total.T.astype(BF)


def traces(shape, field, trace_cell, block):
    sides, rows, lanes = field.shape
    slots = trace_cell.shape[3]
    stride = rows * lanes // slots
    width = min(slots, 256)
    hbm = pl.BlockSpec(memory_space=pltpu.HBM)
    return pl.pallas_call(
        functools.partial(trace_kernel, shape, stride, block),
        in_specs=[hbm, hbm],
        out_specs=[WHOLE] * (1 + len(shape.outer)),
        out_shape=[jax.ShapeDtypeStruct((slots, sides), BF)] + face_shapes(shape, shape.outer),
        scratch_shapes=[
            pltpu.VMEM(field.shape, BF),
            pltpu.VMEM(trace_cell.shape, jnp.int32),
            pltpu.VMEM((sides // block, block * rows, lanes), F32),
            pltpu.VMEM((width, slots), BF),
            pltpu.VMEM((8, slots), jnp.int32),
            pltpu.VMEM((sides, slots), F32),
            pltpu.SemaphoreType.DMA((sides // block + 1,)),
        ],
        compiler_params=params(62),
        cost_estimate=pl.CostEstimate(
            flops=4 * sides * rows * lanes * 128, bytes_accessed=field.size * 2, transcendentals=0
        ),
    )(field, trace_cell)


def fetch_columns(block_ref, held, sems, slots):
    me, group, gzs = lax.axis_index("row"), lax.axis_index("gz"), lax.axis_size("gz")
    copies = []
    for key in range(held.shape[0]):
        start = pl.multiple_of((jnp.bitwise_xor(me, key) * gzs + group) * slots, slots)
        copies.append(
            pltpu.make_async_copy(block_ref.at[:, pl.ds(start, slots)], held.at[key], sems.at[key])
        )
        copies[-1].start()
    return copies


def surface_kernel(halves, *refs):
    ins, total = refs[:-1], refs[-1]
    outs = ins[len(ins) - halves :]
    *parts, held = ins[: len(ins) - halves]
    value = None
    for key, part in enumerate(parts):
        term = dot(held[key], part[...])
        value = term if value is None else value + term
    if halves == 1:
        outs[0][...] = value
        return
    total[...] = value
    count = outs[0].shape[0]
    mine = lax.axis_index("col")
    for key, out in enumerate(outs):
        out[...] = total[pl.ds(pl.multiple_of((mine ^ key) * count, 8), count), :]


def surface(parts, held, halves):
    sides = parts[0].shape[1]
    lines = held.shape[1]
    return pl.pallas_call(
        functools.partial(surface_kernel, halves),
        in_specs=[WHOLE] * (len(parts) + 1),
        out_specs=[WHOLE] * halves,
        out_shape=[jax.ShapeDtypeStruct((lines // halves, sides), F32)] * halves,
        scratch_shapes=[pltpu.VMEM((lines, sides), F32)],
        compiler_params=params(),
        cost_estimate=pl.CostEstimate(
            flops=2 * sides * held.size, bytes_accessed=2 * held.size, transcendentals=0
        ),
    )(*parts, held)


def share_kernel(peers, mine_ref, other_ref, *refs):
    *outs, total, turned = refs
    total[...] = mine_ref[...] + other_ref[...]
    turned[...] = total[...].T
    lines, sides = total.shape
    group = lax.axis_index("gz")
    for key, out in enumerate(outs):
        peer = group ^ key
        rows, some = lines // peers, sides // peers
        out[:rows, :] = total[pl.ds(pl.multiple_of(peer * rows, 8), rows), :]
        out[rows:, :] = turned[pl.ds(pl.multiple_of(peer * some, 8), some), :]


def shares(mine, other):
    peers = lax.axis_size("gz")
    lines, sides = mine.shape
    out = jax.ShapeDtypeStruct(((lines + sides) // peers, sides), F32)
    return pl.pallas_call(
        functools.partial(share_kernel, peers),
        in_specs=[WHOLE] * 2,
        out_specs=[WHOLE] * peers,
        out_shape=[out] * peers,
        scratch_shapes=[pltpu.VMEM((lines, sides), F32), pltpu.VMEM((sides, lines), F32)],
        compiler_params=params(),
        cost_estimate=pl.CostEstimate(
            flops=lines * sides, bytes_accessed=16 * lines * sides, transcendentals=0
        ),
    )(mine, other)


def flux_sums(parts, held, late, after):
    cols, gzs = lax.axis_size("col"), lax.axis_size("gz")
    sides = parts[0].shape[1]
    lines = held.shape[1]
    if cols == 2 and gzs & (gzs - 1) == 0 and lines // cols == sides and sides // gzs % 8 == 0:
        mine, other = surface(parts, held, 2)
        mine, other, after = lax.optimization_barrier((mine, other, after))
        other = lax.ppermute(other, "col", [(0, 1), (1, 0)])
        other, late = lax.optimization_barrier((other, late))
        sent = shares(mine, other)
        recv = [sent[0]]
        for key in range(gzs - 1, 0, -1):
            recv.append(lax.ppermute(sent[key], "gz", [(i, i ^ key) for i in range(gzs)]))
        return recv, after
    (total,) = surface(parts, held, 1)
    rows = lax.psum_scatter(total, "col", scatter_dimension=0, tiled=True)
    owned = lax.psum_scatter(rows, "gz", scatter_dimension=0, tiled=True)
    flux = lax.psum_scatter(rows.T, "gz", scatter_dimension=0, tiled=True)
    flux = jnp.pad(flux, ((0, 0), (0, sides - flux.shape[1])))
    return [jnp.concatenate([owned, flux], axis=0)], after


def turns(axis):
    return 1 if lax.axis_size(axis) == 2 else 2


def partner(index, turn):
    return jnp.where(index % 2 == turn, index + 1, index - 1)


def has_neighbour(axis, turn):
    other = partner(lax.axis_index(axis), turn)
    return (other >= 0) & (other < lax.axis_size(axis))


def swap(value, axis, turn):
    axes = ("row", "col", "gz")
    sizes = [lax.axis_size(name) for name in axes]
    along = axes.index(axis)
    spare = 0 if axis == "gz" else 2
    pairs = []
    for r in range(sizes[0]):
        for c in range(sizes[1]):
            for g in range(sizes[2]):
                here = [r, c, g]
                there = [r, c, g]
                there[along] += 1 if here[along] % 2 == turn else -1
                if not 0 <= there[along] < sizes[along]:
                    there[along] = here[along]
                    if here[spare] ^ 1 < sizes[spare]:
                        there[spare] ^= 1
                flat = [(at[0] * sizes[1] + at[1]) * sizes[2] + at[2] for at in (here, there)]
                pairs.append(tuple(flat))
    return lax.ppermute(value, axes, pairs)


class Shape:
    def __init__(self, sides, first, second, lanes):
        self.sides, self.x, self.y, self.lanes = sides, first, second, lanes
        self.cells = first * second
        self.chunk = max(1, 128 // self.cells)
        self.rows = self.chunk * self.cells
        self.block = min(sides, 32)
        self.half = self.block // 2
        self.half_rows = self.half * self.cells
        self.outer = [("col", i) for i in range(turns("col"))]
        self.inner = [("row", i) for i in reversed(range(turns("row")))]
        self.faces = self.outer + self.inner
        self.ends = turns("gz")

    def face_len(self, face):
        return self.y if face[0] == "row" else self.x

    def halo_rows(self):
        return sum(self.chunk * self.face_len(face) for face in self.faces)

    def edge(self, face):
        axis, turn = face
        last = (self.x if axis == "row" else self.y) - 1
        return jnp.where(lax.axis_index(axis) % 2 == turn, last, 0)


def halo_place(shape):
    dims = (shape.rows, shape.halo_rows())
    row, col = iota(dims, 0), iota(dims, 1)
    side, cell = row // shape.cells, row % shape.cells
    x, y = cell // shape.y, cell % shape.y
    hit, base = None, 0
    for face in shape.faces:
        length = shape.face_len(face)
        along, across = (y, x) if face[0] == "row" else (x, y)
        place = (across == shape.edge(face)) & (col - base == side * length + along)
        place = place & has_neighbour(*face)
        hit = place if hit is None else hit | place
        base += shape.chunk * length
    return hit.astype(BF)


def z_mask(shape, count):
    dims = (count * shape.cells, 2 * shape.cells)
    return iota(dims, 1) % shape.cells == iota(dims, 0) % shape.cells


def twice(matrix):
    zero = jnp.zeros_like(matrix)
    return jnp.concatenate(
        [jnp.concatenate([matrix, zero], axis=1), jnp.concatenate([zero, matrix], axis=1)], axis=0
    )


def beside(values):
    half = values.shape[0] // 2
    return jnp.concatenate([values[:half], values[half:]], axis=1)


def build_out(shape, ends_m, rsum):
    dims = (shape.lanes, 2 * shape.cells)
    edge = jnp.where(iota(dims, 1) < shape.cells, 0, shape.lanes - 1)
    ends_m[...] = twice((iota(dims, 0) == edge).astype(F32)).astype(BF)
    dims = rsum.shape
    rsum[...] = (iota(dims, 1) // shape.cells == iota(dims, 0)).astype(BF)


def cut_faces(shape, faces, at, block, tall, face_refs):
    for face, ref in zip(faces, face_refs):
        length, edge = shape.face_len(face), shape.edge(face)
        lines = []
        for side in range(block):
            start = side * shape.cells
            if face[0] == "row":
                lines.append(tall[pl.ds(aligned(start + edge * length, 8), length), :])
            else:
                lines.append(tall[pl.ds(start + edge, length, stride=shape.y), :])
        span = slice(at * length, (at + block) * length)
        ref[span, :] = jnp.concatenate(lines, axis=0).astype(BF)


def cut_ends(shape, at, values, z_ref, ends_m, rsum):
    mask = jnp.concatenate([z_mask(shape, shape.half)] * 2, axis=1)
    tips = jnp.where(mask, dot(beside(values), ends_m[...]), 0.0).astype(BF)
    tips = dot(rsum[...], tips)[: shape.half]
    tips = jnp.concatenate([tips[:, : 2 * shape.cells], tips[:, 2 * shape.cells :]], axis=0)
    z_ref[at : at + shape.block, :] = tips.astype(BF)


def build_tables(shape, coef_ref, weight, near_m, line_m, ends_m, rsum):
    cells, lanes = shape.cells, shape.lanes
    weight[...] = jnp.concatenate([OMEGA / (6.0 + coef_ref[...])] * shape.chunk, axis=0)
    dims = (shape.rows, shape.rows)
    row, col = iota(dims, 0), iota(dims, 1)
    x, y = row % cells // shape.y, row % shape.y
    x2, y2 = col % cells // shape.y, col % shape.y
    near = ((x == x2) & (jnp.abs(y - y2) == 1)) | ((y == y2) & (jnp.abs(x - x2) == 1))
    near_m[:, : shape.rows] = (near & (row // cells == col // cells)).astype(BF)
    near_m[:, shape.rows :] = halo_place(shape)
    dims = (lanes, lanes)
    line = (jnp.abs(iota(dims, 0) - iota(dims, 1)) == 1).astype(F32)
    line_m[: 2 * lanes, :] = twice(line).astype(BF)
    dims = (2 * cells, lanes)
    edge = jnp.where(iota(dims, 0) < cells, lanes - 1, 0)
    line_m[2 * lanes :, :] = twice((iota(dims, 1) == edge).astype(F32)).astype(BF)
    build_out(shape, ends_m, rsum)


def table_shapes(shape):
    lanes, cells = shape.lanes, shape.cells
    return [
        jax.ShapeDtypeStruct((shape.rows, lanes), F32),
        jax.ShapeDtypeStruct((shape.rows, shape.rows + shape.halo_rows()), BF),
        jax.ShapeDtypeStruct((2 * lanes + 4 * cells, 2 * lanes), BF),
        jax.ShapeDtypeStruct((2 * lanes, 4 * cells), BF),
        jax.ShapeDtypeStruct((max(8, shape.half), shape.half_rows), BF),
    ]


def faces_kernel(shape, slots, field_ref, block_ref, coef_ref, *refs):
    refs = list(refs)
    face_refs = [refs.pop(0) for _ in shape.inner]
    z_ref, held, *tables, field, tall, sems, field_sems = refs
    size = shape.block * shape.cells
    steps = shape.sides // shape.block
    copies = []
    for step in range(steps):
        span = pl.ds(step * size, size)
        copies.append(
            pltpu.make_async_copy(field_ref.at[span], field.at[span], field_sems.at[step])
        )
        copies[-1].start()
    columns = fetch_columns(block_ref, held, sems, slots)
    build_tables(shape, coef_ref, *tables)
    ends_m, rsum = tables[-2:]
    for step in range(steps):
        copies[step].wait()
        values = field[step * size : (step + 1) * size, :]
        tall[step] = values.astype(F32)
        cut_faces(shape, shape.inner, step * shape.block, shape.block, tall.at[step], face_refs)
        cut_ends(shape, step * shape.block, values, z_ref, ends_m, rsum)
    for copy in columns:
        copy.wait()


def face_shapes(shape, faces):
    return [
        jax.ShapeDtypeStruct((shape.sides * shape.face_len(face), shape.lanes), BF)
        for face in faces
    ]


def first_faces(shape, field, block, coef, slots):
    peers = lax.axis_size("row")
    steps = shape.sides // shape.block
    shapes = face_shapes(shape, shape.inner)
    shapes.append(jax.ShapeDtypeStruct((shape.sides, 2 * shape.cells), BF))
    shapes.append(jax.ShapeDtypeStruct((peers, block.shape[0], slots), BF))
    shapes += table_shapes(shape)
    hbm = pl.BlockSpec(memory_space=pltpu.HBM)
    return pl.pallas_call(
        functools.partial(faces_kernel, shape, slots),
        in_specs=[hbm, hbm, WHOLE],
        out_specs=[WHOLE] * len(shapes),
        out_shape=shapes,
        scratch_shapes=[
            pltpu.VMEM(field.shape, BF),
            pltpu.VMEM((steps, shape.block * shape.cells, shape.lanes), F32),
            pltpu.SemaphoreType.DMA((peers,)),
            pltpu.SemaphoreType.DMA((steps,)),
        ],
        compiler_params=params(FACES_MIB),
        cost_estimate=pl.CostEstimate(
            flops=field.size * 128, bytes_accessed=4 * field.size, transcendentals=0
        ),
    )(field, block, coef)


def expand(shape, lines, where):
    rows = []
    for side in range(shape.block):
        line = jnp.broadcast_to(lines[side : side + 1], where.shape)
        rows.append(jnp.where(where, line, 0.0))
    return beside(jnp.concatenate(rows, axis=0).astype(BF))


def build_cells(shape, cell_ref, cell_m):
    slots = cell_ref.shape[3]
    cell = jnp.concatenate([cell_ref[0, 0]] * 2, axis=1)
    place = (iota((shape.lanes, 2 * slots), 0) == cell % shape.lanes).astype(F32)
    cell_m[...] = twice(place).astype(BF)
    return iota((shape.cells, 2 * slots), 0) == cell // shape.lanes


def base_kernel(shape, with_flux, *refs):
    refs = list(refs)
    take = lambda count: [refs.pop(0) for _ in range(count)]
    field_ref, load_ref, weight, near_m, line_m = take(5)
    end_refs = take(shape.ends)
    if with_flux:
        phi, cell_ref = take(2)
    (base_ref,) = take(1)
    if with_flux:
        (source_ref,) = take(1)
    (lines,) = take(1)
    if with_flux:
        cell_m, placed = take(2)
        cell_mask = build_cells(shape, cell_ref, cell_m)

    cells, lanes = shape.cells, shape.lanes
    weights = weight[...]
    mask = z_mask(shape, 1)
    even = lax.axis_index("gz") % 2 == 0
    filled = (iota((shape.block, 2 * cells), 1) < cells) == even
    for step in range(shape.sides // shape.block):
        sides = slice(step * shape.block, (step + 1) * shape.block)
        at = step * shape.block * cells
        zs = 0.0
        for turn in range(shape.ends):
            wanted = (filled == (turn == 0)) & has_neighbour("gz", turn)
            zs = jnp.where(wanted, end_refs[turn][sides, :].astype(F32), zs)
        values = field_ref[at : at + shape.block * cells, :]
        left = jnp.concatenate([beside(values), expand(shape, zs, mask)], axis=1)
        lines[step] = dot(left, line_m[...])
        if with_flux:
            placed[step] = dot_nt(expand(shape, phi[sides, :], cell_mask), cell_m[...])
        for index in range(shape.half // shape.chunk):
            offset = index * shape.rows
            here = slice(offset, offset + shape.rows)
            spans = [
                slice(at + start, at + start + shape.rows)
                for start in (offset, offset + shape.half_rows)
            ]
            stack = jnp.concatenate([field_ref[span, :] for span in spans], axis=1)
            near = dot(near_m[:, : shape.rows], stack) + lines[step, here, :]
            for part, span in enumerate(spans):
                cols = slice(part * lanes, (part + 1) * lanes)
                source = load_ref[span, :].astype(F32)
                if with_flux:
                    source = source + placed[step, here, cols]
                    source_ref[span, :] = source.astype(BF)
                centre = field_ref[span, :].astype(F32)
                base_ref[span, :] = (1.0 - OMEGA) * centre + weights * (source + near[:, cols])


def sweep_base(shape, field, load, tables, ends, phi=None, flux_cell=None):
    steps = shape.sides // shape.block
    half = (steps, shape.half_rows, 2 * shape.lanes)
    operands = [field, load, *tables[:3], *ends]
    shapes = [jax.ShapeDtypeStruct(field.shape, F32)]
    scratch = [pltpu.VMEM(half, F32)]
    if phi is not None:
        operands += [phi, flux_cell]
        shapes.append(jax.ShapeDtypeStruct(field.shape, BF))
        scratch.append(pltpu.VMEM((2 * shape.lanes, 2 * phi.shape[1]), BF))
        scratch.append(pltpu.VMEM(half, F32))
    return pl.pallas_call(
        functools.partial(base_kernel, shape, phi is not None),
        in_specs=[WHOLE] * len(operands),
        out_specs=[WHOLE] * len(shapes),
        out_shape=shapes,
        scratch_shapes=scratch,
        compiler_params=params(),
        cost_estimate=pl.CostEstimate(
            flops=6 * field.size * 128, bytes_accessed=8 * field.size, transcendentals=0
        ),
    )(*operands)


def finish_kernel(shape, recvs, last, *refs):
    with_flux = recvs > 0
    refs = list(refs)
    take = lambda count: [refs.pop(0) for _ in range(count)]
    base_ref, weight, near_m, ends_m, rsum = take(5)
    halo_refs = take(len(shape.faces))
    if with_flux:
        (cell_ref,) = take(1)
        recv_refs = take(recvs)
    (out_ref,) = take(1)
    if not last:
        face_refs = take(len(shape.faces))
        (z_ref,) = take(1)
    if with_flux:
        phi, flux_ref = take(2)
    if last:
        result_ref = out_ref
        out_ref, out_sems = take(2)
    else:
        (tall,) = take(1)
    if with_flux:
        cell_m, placed = take(2)

    cells, lanes = shape.cells, shape.lanes

    if with_flux:
        slots = cell_ref.shape[3]
        cell_mask = build_cells(shape, cell_ref, cell_m)
        owned = recv_refs[0][...]
        for ref in recv_refs[1:]:
            owned = owned + ref[...]
        flux_ref[...] = owned[slots:, : flux_ref.shape[1]]
        owned = owned[:slots]
        high = owned.astype(BF).astype(F32)
        phi[...] = jnp.concatenate([high, owned - high], axis=0).T

    weights = weight[...]

    def work(step):
        at = step * shape.block
        if with_flux:
            sides = slice(at, at + shape.block)
            placed[step] = dot_nt(expand(shape, phi[sides, :], cell_mask), cell_m[...])
        for index in range(shape.half // shape.chunk):
            offset = index * shape.rows
            starts = (offset, offset + shape.half_rows)
            stacks = []
            for start in starts:
                stack = []
                for face, ref in zip(shape.faces, halo_refs):
                    length = shape.face_len(face)
                    first = at * length + start // cells * length
                    stack.append(ref[first : first + shape.chunk * length, :])
                stacks.append(jnp.concatenate(stack, axis=0))
            near = dot(near_m[:, shape.rows :], jnp.concatenate(stacks, axis=1))
            if with_flux:
                near = near + placed[step, offset : offset + shape.rows, :]
            for part, start in enumerate(starts):
                rows = slice(at * cells + start, at * cells + start + shape.rows)
                fresh = base_ref[rows, :] + weights * near[:, part * lanes : (part + 1) * lanes]
                out_ref[rows, :] = fresh.astype(BF)
                if not last:
                    tall[step, start : start + shape.rows, :] = fresh

    def emit(step):
        at, size = step * shape.block, shape.block * cells
        fresh = out_ref[at * cells : at * cells + size, :]
        cut_faces(shape, shape.faces, at, shape.block, tall.at[step], face_refs)
        cut_ends(shape, at, fresh, z_ref, ends_m, rsum)

    steps = shape.sides // shape.block
    copies = []
    for step in range(steps):
        work(step)
        if last:
            span = pl.ds(step * shape.block * cells, shape.block * cells)
            copies.append(
                pltpu.make_async_copy(out_ref.at[span], result_ref.at[span], out_sems.at[step])
            )
            copies[-1].start()
        elif step > 0:
            emit(step - 1)
    for copy in copies:
        copy.wait()
    if not last:
        emit(steps - 1)


def sweep_finish(shape, base, tables, halos, flux_cell=None, recv=(), last=False):
    lanes, cells = shape.lanes, shape.cells
    steps = shape.sides // shape.block
    weight, near_m, _, ends_m, rsum = tables
    operands = [base, weight, near_m, ends_m, rsum, *halos]
    out_shapes = [jax.ShapeDtypeStruct(base.shape, BF)]
    if last:
        scratch = [pltpu.VMEM(base.shape, BF), pltpu.SemaphoreType.DMA((steps,))]
    else:
        out_shapes += face_shapes(shape, shape.faces)
        out_shapes.append(jax.ShapeDtypeStruct((shape.sides, 2 * cells), BF))
        scratch = [pltpu.VMEM((steps, shape.block * cells, lanes), F32)]
    if recv:
        slots = flux_cell.shape[3]
        operands += [flux_cell, *recv]
        out_shapes += [
            jax.ShapeDtypeStruct((shape.sides, 2 * slots), F32),
            jax.ShapeDtypeStruct((recv[0].shape[0] - slots, slots * lax.axis_size("gz")), F32),
        ]
        scratch += [
            pltpu.VMEM((2 * lanes, 4 * slots), BF),
            pltpu.VMEM((steps, shape.half_rows, 2 * lanes), F32),
        ]
    out_specs = [WHOLE] * len(out_shapes)
    if last:
        out_specs = [pl.BlockSpec(memory_space=pltpu.HBM)]
    return pl.pallas_call(
        functools.partial(finish_kernel, shape, len(recv), last),
        in_specs=[WHOLE] * len(operands),
        out_specs=out_specs,
        out_shape=out_shapes,
        scratch_shapes=scratch,
        compiler_params=params(),
        cost_estimate=pl.CostEstimate(
            flops=4 * base.size * 128, bytes_accessed=8 * base.size, transcendentals=0
        ),
    )(*operands)


def swap_faces(faces, values):
    return [swap(value, *face) for face, value in zip(faces, values)]


def swap_ends(shape, ends):
    return [swap(ends, "gz", turn) for turn in range(shape.ends)]


def exchange(shape, faces, ends):
    count = len(shape.outer)
    tips = swap_ends(shape, ends)
    along_col = swap_faces(shape.outer, faces[:count])
    inner, tips[0] = lax.optimization_barrier((faces[count:], tips[0]))
    return along_col + swap_faces(shape.inner, inner), tips


def row_gather(trace, hidden):
    peers = lax.axis_size("row")
    held = {0: trace}
    bit = peers // 2
    while bit:
        pairs = [(i, i ^ bit) for i in range(peers)]
        fresh = {key ^ bit: lax.ppermute(held[key], "row", pairs) for key in sorted(held, reverse=True)}
        if bit == peers // 2:
            held, fresh, hidden = lax.optimization_barrier((held, fresh, hidden))
        held.update(fresh)
        bit //= 2
    return [held[key] for key in range(peers)], hidden


def per_device(volume_field, volume_load, coefficient, surface_block, trace_cell, flux_cell):
    sides, first, second, lanes = volume_field.shape
    cells = first * second
    shape = Shape(sides, first, second, lanes)
    field = volume_field.reshape(sides * cells, lanes)
    load = volume_load.reshape(sides * cells, lanes)
    coef = coefficient.reshape(cells, lanes)

    slots = trace_cell.shape[3]
    trace, *outer = traces(
        shape, volume_field.reshape(sides, cells, lanes), trace_cell, min(32, sides)
    )
    firsts = first_faces(shape, field, surface_block, coef, slots)
    layers = len(shape.faces)
    count = len(shape.inner) + 1
    inner, held, tables = firsts[:count], firsts[count], firsts[count + 1 :]
    *inner, ends = inner
    along_col = swap_faces(shape.outer, outer)
    parts, (inner, along_col) = row_gather(trace, (inner, along_col))
    along_row = swap_faces(shape.inner, inner)
    recv, ends = flux_sums(parts, held, along_row, ends)
    tips = swap_ends(shape, ends)

    (base,) = sweep_base(shape, field, load, tables, tips)
    current, *faces, ends, phi, surface_flux = sweep_finish(
        shape, base, tables, along_col + along_row, flux_cell=flux_cell, recv=recv
    )
    halos, tips = exchange(shape, faces, ends)
    base, source = sweep_base(shape, current, load, tables, tips, phi, flux_cell)
    current, *faces, ends = sweep_finish(shape, base, tables, halos)
    halos, tips = exchange(shape, faces, ends)
    (base,) = sweep_base(shape, current, source, tables, tips)
    (current,) = sweep_finish(shape, base, tables, halos, last=True)
    return current.reshape(volume_field.shape), surface_flux


def solution(mesh):
    in_specs = (
        P(None, "row", "col", "gz"),
        P(None, "row", "col", "gz"),
        P("row", "col", "gz"),
        P("row", "col"),
        P("row", "col", "gz", None),
        P("row", "col", "gz", None),
    )
    out_specs = (P(None, "row", "col", "gz"), P("gz", ("row", "col")))
    return jax.shard_map(
        per_device, mesh=mesh, in_specs=in_specs, out_specs=out_specs, check_vma=False
    )
```

```python
import functools

import jax
import jax.numpy as jnp
from jax import lax
from jax.experimental import pallas as pl
from jax.experimental.pallas import tpu as pltpu
from jax.sharding import PartitionSpec as P

OMEGA = 0.8
BF = jnp.bfloat16
F32 = jnp.float32
WHOLE = pl.BlockSpec(memory_space=pltpu.VMEM)


def aligned(start, unit):
    return start if isinstance(start, int) else pl.multiple_of(start, unit)


def iota(shape, dim):
    return lax.broadcasted_iota(jnp.int32, shape, dim)


def dot(a, b):
    return jnp.dot(a, b, preferred_element_type=F32)


def dot_nt(a, b):
    return lax.dot_general(a, b, (((1,), (1,)), ((), ())), preferred_element_type=F32)


FACES_MIB = 50


def params(mebibytes=24):
    return pltpu.CompilerParams(vmem_limit_bytes=mebibytes * 1024 * 1024)


def trace_kernel(shape, stride, block, field_ref, cell_ref, out_ref, *refs):
    *face_refs, field, cell_v, tall, near, place, picked, sems = refs
    sides, rows, lanes = field.shape
    slots = cell_ref.shape[3]
    per_row = lanes // stride
    width = near.shape[0]
    parts = slots // width
    cell_copy = pltpu.make_async_copy(cell_ref, cell_v, sems.at[sides // block])
    cell_copy.start()
    copies = []
    for step in range(sides // block):
        span = pl.ds(step * block, block)
        copies.append(pltpu.make_async_copy(field_ref.at[span], field.at[span], sems.at[step]))
        copies[-1].start()

    cell_copy.wait()
    cell = cell_v[0, 0]
    run = cell // stride
    digit = jnp.zeros_like(cell)
    for part in range(parts):
        digit = jnp.where(run // width == part, (cell % stride) * stride**part, digit)
    hit = iota((width, slots), 0) == run % width
    near[...] = hit.astype(BF)
    digits = jnp.sum(jnp.where(hit, digit.astype(F32), 0.0), axis=1, keepdims=True)
    digits = jnp.broadcast_to(digits, (width, 128)).T[0:8].astype(jnp.int32)
    first = iota((8, width), 1) % per_row * stride
    for part in range(parts):
        place[:, part * width : (part + 1) * width] = first + digits // stride**part % stride

    together = 128 // per_row
    group = iota((8, 128), 1) // per_row
    for step in range(sides // block):
        copies[step].wait()
        span = field[step * block : (step + 1) * block]
        tall[step] = span.reshape(block * rows, lanes).astype(F32)
        cut_faces(shape, shape.outer, step * block, block, tall.at[step], face_refs)

        for batch in range(block // 8):
            for tile in range(rows // together):
                cols = slice(tile * 128, (tile + 1) * 128)
                where = place[:, cols]
                found = None
                for row in range(together):
                    start = batch * 8 * rows + tile * together + row
                    line = tall[step, pl.ds(start, 8, stride=rows), :]
                    line = jnp.take_along_axis(line, where, axis=1)
                    found = line if found is None else jnp.where(group == row, line, found)
                at = step * block + batch * 8
                picked[at : at + 8, cols] = found

    total = jnp.zeros((sides, slots), F32)
    for part in range(parts):
        sorted_runs = picked[:, part * width : (part + 1) * width].astype(BF)
        total = jnp.where(run // width == part, dot(sorted_runs, near[...]), total)
    out_ref[...] = total.T.astype(BF)


def traces(shape, field, trace_cell, block):
    sides, rows, lanes = field.shape
    slots = trace_cell.shape[3]
    stride = rows * lanes // slots
    width = min(slots, 256)
    hbm = pl.BlockSpec(memory_space=pltpu.HBM)
    return pl.pallas_call(
        functools.partial(trace_kernel, shape, stride, block),
        in_specs=[hbm, hbm],
        out_specs=[WHOLE] * (1 + len(shape.outer)),
        out_shape=[jax.ShapeDtypeStruct((slots, sides), BF)] + face_shapes(shape, shape.outer),
        scratch_shapes=[
            pltpu.VMEM(field.shape, BF),
            pltpu.VMEM(trace_cell.shape, jnp.int32),
            pltpu.VMEM((sides // block, block * rows, lanes), F32),
            pltpu.VMEM((width, slots), BF),
            pltpu.VMEM((8, slots), jnp.int32),
            pltpu.VMEM((sides, slots), F32),
            pltpu.SemaphoreType.DMA((sides // block + 1,)),
        ],
        compiler_params=params(62),
        cost_estimate=pl.CostEstimate(
            flops=4 * sides * rows * lanes * 128, bytes_accessed=field.size * 2, transcendentals=0
        ),
    )(field, trace_cell)


def fetch_columns(block_ref, held, sems, slots):
    me, group, gzs = lax.axis_index("row"), lax.axis_index("gz"), lax.axis_size("gz")
    copies = []
    for key in range(held.shape[0]):
        start = pl.multiple_of((jnp.bitwise_xor(me, key) * gzs + group) * slots, slots)
        copies.append(
            pltpu.make_async_copy(block_ref.at[:, pl.ds(start, slots)], held.at[key], sems.at[key])
        )
        copies[-1].start()
    return copies


def surface_kernel(halves, *refs):
    ins, total = refs[:-1], refs[-1]
    outs = ins[len(ins) - halves :]
    *parts, held = ins[: len(ins) - halves]
    value = None
    for key, part in enumerate(parts):
        term = dot(held[key], part[...])
        value = term if value is None else value + term
    if halves == 1:
        outs[0][...] = value
        return
    total[...] = value
    count = outs[0].shape[0]
    mine = lax.axis_index("col")
    for key, out in enumerate(outs):
        out[...] = total[pl.ds(pl.multiple_of((mine ^ key) * count, 8), count), :]


def surface(parts, held, halves):
    sides = parts[0].shape[1]
    lines = held.shape[1]
    return pl.pallas_call(
        functools.partial(surface_kernel, halves),
        in_specs=[WHOLE] * (len(parts) + 1),
        out_specs=[WHOLE] * halves,
        out_shape=[jax.ShapeDtypeStruct((lines // halves, sides), F32)] * halves,
        scratch_shapes=[pltpu.VMEM((lines, sides), F32)],
        compiler_params=params(),
        cost_estimate=pl.CostEstimate(
            flops=2 * sides * held.size, bytes_accessed=2 * held.size, transcendentals=0
        ),
    )(*parts, held)


def share_kernel(peers, mine_ref, other_ref, *refs):
    *outs, total, turned = refs
    total[...] = mine_ref[...] + other_ref[...]
    turned[...] = total[...].T
    lines, sides = total.shape
    group = lax.axis_index("gz")
    for key, out in enumerate(outs):
        peer = group ^ key
        rows, some = lines // peers, sides // peers
        out[:rows, :] = total[pl.ds(pl.multiple_of(peer * rows, 8), rows), :]
        out[rows:, :] = turned[pl.ds(pl.multiple_of(peer * some, 8), some), :]


def shares(mine, other):
    peers = lax.axis_size("gz")
    lines, sides = mine.shape
    out = jax.ShapeDtypeStruct(((lines + sides) // peers, sides), F32)
    return pl.pallas_call(
        functools.partial(share_kernel, peers),
        in_specs=[WHOLE] * 2,
        out_specs=[WHOLE] * peers,
        out_shape=[out] * peers,
        scratch_shapes=[pltpu.VMEM((lines, sides), F32), pltpu.VMEM((sides, lines), F32)],
        compiler_params=params(),
        cost_estimate=pl.CostEstimate(
            flops=lines * sides, bytes_accessed=16 * lines * sides, transcendentals=0
        ),
    )(mine, other)


def flux_sums(parts, held, late, after):
    cols, gzs = lax.axis_size("col"), lax.axis_size("gz")
    sides = parts[0].shape[1]
    lines = held.shape[1]
    if cols == 2 and gzs & (gzs - 1) == 0 and lines // cols == sides and sides // gzs % 8 == 0:
        mine, other = surface(parts, held, 2)
        mine, other, after = lax.optimization_barrier((mine, other, after))
        other = lax.ppermute(other, "col", [(0, 1), (1, 0)])
        other, late = lax.optimization_barrier((other, late))
        sent = shares(mine, other)
        recv = [sent[0]]
        for key in range(gzs - 1, 0, -1):
            recv.append(lax.ppermute(sent[key], "gz", [(i, i ^ key) for i in range(gzs)]))
        return recv, after
    (total,) = surface(parts, held, 1)
    rows = lax.psum_scatter(total, "col", scatter_dimension=0, tiled=True)
    owned = lax.psum_scatter(rows, "gz", scatter_dimension=0, tiled=True)
    flux = lax.psum_scatter(rows.T, "gz", scatter_dimension=0, tiled=True)
    flux = jnp.pad(flux, ((0, 0), (0, sides - flux.shape[1])))
    return [jnp.concatenate([owned, flux], axis=0)], after


def turns(axis):
    return 1 if lax.axis_size(axis) == 2 else 2


def partner(index, turn):
    return jnp.where(index % 2 == turn, index + 1, index - 1)


def has_neighbour(axis, turn):
    other = partner(lax.axis_index(axis), turn)
    return (other >= 0) & (other < lax.axis_size(axis))


def swap(value, axis, turn):
    axes = ("row", "col", "gz")
    sizes = [lax.axis_size(name) for name in axes]
    along = axes.index(axis)
    spare = 0 if axis == "gz" else 2
    pairs = []
    for r in range(sizes[0]):
        for c in range(sizes[1]):
            for g in range(sizes[2]):
                here = [r, c, g]
                there = [r, c, g]
                there[along] += 1 if here[along] % 2 == turn else -1
                if not 0 <= there[along] < sizes[along]:
                    there[along] = here[along]
                    if here[spare] ^ 1 < sizes[spare]:
                        there[spare] ^= 1
                flat = [(at[0] * sizes[1] + at[1]) * sizes[2] + at[2] for at in (here, there)]
                pairs.append(tuple(flat))
    return lax.ppermute(value, axes, pairs)


class Shape:
    def __init__(self, sides, first, second, lanes):
        self.sides, self.x, self.y, self.lanes = sides, first, second, lanes
        self.cells = first * second
        self.chunk = max(1, 128 // self.cells)
        self.rows = self.chunk * self.cells
        self.block = min(sides, 32)
        self.half = self.block // 2
        self.half_rows = self.half * self.cells
        self.outer = [("col", i) for i in range(turns("col"))]
        self.inner = [("row", i) for i in reversed(range(turns("row")))]
        self.faces = self.outer + self.inner
        self.ends = turns("gz")

    def face_len(self, face):
        return self.y if face[0] == "row" else self.x

    def halo_rows(self):
        return sum(self.chunk * self.face_len(face) for face in self.faces)

    def edge(self, face):
        axis, turn = face
        last = (self.x if axis == "row" else self.y) - 1
        return jnp.where(lax.axis_index(axis) % 2 == turn, last, 0)


def halo_place(shape):
    dims = (shape.rows, shape.halo_rows())
    row, col = iota(dims, 0), iota(dims, 1)
    side, cell = row // shape.cells, row % shape.cells
    x, y = cell // shape.y, cell % shape.y
    hit, base = None, 0
    for face in shape.faces:
        length = shape.face_len(face)
        along, across = (y, x) if face[0] == "row" else (x, y)
        place = (across == shape.edge(face)) & (col - base == side * length + along)
        place = place & has_neighbour(*face)
        hit = place if hit is None else hit | place
        base += shape.chunk * length
    return hit.astype(BF)


def z_mask(shape, count):
    dims = (count * shape.cells, 2 * shape.cells)
    return iota(dims, 1) % shape.cells == iota(dims, 0) % shape.cells


def twice(matrix):
    zero = jnp.zeros_like(matrix)
    return jnp.concatenate(
        [jnp.concatenate([matrix, zero], axis=1), jnp.concatenate([zero, matrix], axis=1)], axis=0
    )


def beside(values):
    half = values.shape[0] // 2
    return jnp.concatenate([values[:half], values[half:]], axis=1)


def build_out(shape, ends_m, rsum):
    dims = (shape.lanes, 2 * shape.cells)
    edge = jnp.where(iota(dims, 1) < shape.cells, 0, shape.lanes - 1)
    ends_m[...] = twice((iota(dims, 0) == edge).astype(F32)).astype(BF)
    dims = rsum.shape
    rsum[...] = (iota(dims, 1) // shape.cells == iota(dims, 0)).astype(BF)


def cut_faces(shape, faces, at, block, tall, face_refs):
    for face, ref in zip(faces, face_refs):
        length, edge = shape.face_len(face), shape.edge(face)
        lines = []
        for side in range(block):
            start = side * shape.cells
            if face[0] == "row":
                lines.append(tall[pl.ds(aligned(start + edge * length, 8), length), :])
            else:
                lines.append(tall[pl.ds(start + edge, length, stride=shape.y), :])
        span = slice(at * length, (at + block) * length)
        ref[span, :] = jnp.concatenate(lines, axis=0).astype(BF)


def cut_ends(shape, at, values, z_ref, ends_m, rsum):
    mask = jnp.concatenate([z_mask(shape, shape.half)] * 2, axis=1)
    tips = jnp.where(mask, dot(beside(values), ends_m[...]), 0.0).astype(BF)
    tips = dot(rsum[...], tips)[: shape.half]
    tips = jnp.concatenate([tips[:, : 2 * shape.cells], tips[:, 2 * shape.cells :]], axis=0)
    z_ref[at : at + shape.block, :] = tips.astype(BF)


def build_tables(shape, coef_ref, weight, near_m, line_m, ends_m, rsum):
    cells, lanes = shape.cells, shape.lanes
    weight[...] = jnp.concatenate([OMEGA / (6.0 + coef_ref[...])] * shape.chunk, axis=0)
    dims = (shape.rows, shape.rows)
    row, col = iota(dims, 0), iota(dims, 1)
    x, y = row % cells // shape.y, row % shape.y
    x2, y2 = col % cells // shape.y, col % shape.y
    near = ((x == x2) & (jnp.abs(y - y2) == 1)) | ((y == y2) & (jnp.abs(x - x2) == 1))
    near_m[:, : shape.rows] = (near & (row // cells == col // cells)).astype(BF)
    near_m[:, shape.rows :] = halo_place(shape)
    dims = (lanes, lanes)
    line = (jnp.abs(iota(dims, 0) - iota(dims, 1)) == 1).astype(F32)
    line_m[: 2 * lanes, :] = twice(line).astype(BF)
    dims = (2 * cells, lanes)
    edge = jnp.where(iota(dims, 0) < cells, lanes - 1, 0)
    line_m[2 * lanes :, :] = twice((iota(dims, 1) == edge).astype(F32)).astype(BF)
    build_out(shape, ends_m, rsum)


def table_shapes(shape):
    lanes, cells = shape.lanes, shape.cells
    return [
        jax.ShapeDtypeStruct((shape.rows, lanes), F32),
        jax.ShapeDtypeStruct((shape.rows, shape.rows + shape.halo_rows()), BF),
        jax.ShapeDtypeStruct((2 * lanes + 4 * cells, 2 * lanes), BF),
        jax.ShapeDtypeStruct((2 * lanes, 4 * cells), BF),
        jax.ShapeDtypeStruct((max(8, shape.half), shape.half_rows), BF),
    ]


def faces_kernel(shape, slots, field_ref, block_ref, coef_ref, *refs):
    refs = list(refs)
    face_refs = [refs.pop(0) for _ in shape.inner]
    z_ref, held, *tables, field, tall, sems, field_sems = refs
    size = shape.block * shape.cells
    steps = shape.sides // shape.block
    copies = []
    for step in range(steps):
        span = pl.ds(step * size, size)
        copies.append(
            pltpu.make_async_copy(field_ref.at[span], field.at[span], field_sems.at[step])
        )
        copies[-1].start()
    columns = fetch_columns(block_ref, held, sems, slots)
    build_tables(shape, coef_ref, *tables)
    ends_m, rsum = tables[-2:]
    for step in range(steps):
        copies[step].wait()
        values = field[step * size : (step + 1) * size, :]
        tall[step] = values.astype(F32)
        cut_faces(shape, shape.inner, step * shape.block, shape.block, tall.at[step], face_refs)
        cut_ends(shape, step * shape.block, values, z_ref, ends_m, rsum)
    for copy in columns:
        copy.wait()


def face_shapes(shape, faces):
    return [
        jax.ShapeDtypeStruct((shape.sides * shape.face_len(face), shape.lanes), BF)
        for face in faces
    ]


def first_faces(shape, field, block, coef, slots):
    peers = lax.axis_size("row")
    steps = shape.sides // shape.block
    shapes = face_shapes(shape, shape.inner)
    shapes.append(jax.ShapeDtypeStruct((shape.sides, 2 * shape.cells), BF))
    shapes.append(jax.ShapeDtypeStruct((peers, block.shape[0], slots), BF))
    shapes += table_shapes(shape)
    hbm = pl.BlockSpec(memory_space=pltpu.HBM)
    return pl.pallas_call(
        functools.partial(faces_kernel, shape, slots),
        in_specs=[hbm, hbm, WHOLE],
        out_specs=[WHOLE] * len(shapes),
        out_shape=shapes,
        scratch_shapes=[
            pltpu.VMEM(field.shape, BF),
            pltpu.VMEM((steps, shape.block * shape.cells, shape.lanes), F32),
            pltpu.SemaphoreType.DMA((peers,)),
            pltpu.SemaphoreType.DMA((steps,)),
        ],
        compiler_params=params(FACES_MIB),
        cost_estimate=pl.CostEstimate(
            flops=field.size * 128, bytes_accessed=4 * field.size, transcendentals=0
        ),
    )(field, block, coef)


def expand(shape, lines, where):
    rows = []
    for side in range(shape.block):
        line = jnp.broadcast_to(lines[side : side + 1], where.shape)
        rows.append(jnp.where(where, line, 0.0))
    return beside(jnp.concatenate(rows, axis=0).astype(BF))


def halo_ends(shape, end_refs, sides):
    even = lax.axis_index("gz") % 2 == 0
    filled = (iota((shape.block, 2 * shape.cells), 1) < shape.cells) == even
    zs = 0.0
    for turn in range(shape.ends):
        wanted = (filled == (turn == 0)) & has_neighbour("gz", turn)
        zs = jnp.where(wanted, end_refs[turn][sides, :].astype(F32), zs)
    return expand(shape, zs, z_mask(shape, 1))


def build_cells(shape, cell_ref, cell_m):
    slots = cell_ref.shape[3]
    cell = jnp.concatenate([cell_ref[0, 0]] * 2, axis=1)
    place = (iota((shape.lanes, 2 * slots), 0) == cell % shape.lanes).astype(F32)
    cell_m[...] = twice(place).astype(BF)
    return iota((shape.cells, 2 * slots), 0) == cell // shape.lanes


def base_kernel(shape, ends, with_flux, *refs):
    refs = list(refs)
    take = lambda count: [refs.pop(0) for _ in range(count)]
    field_ref, load_ref, weight, near_m, line_m = take(5)
    end_refs = take(ends)
    if with_flux:
        phi, cell_ref = take(2)
    (base_ref,) = take(1)
    if with_flux:
        (source_ref,) = take(1)
    (lines,) = take(1)
    if with_flux:
        cell_m, placed = take(2)
        cell_mask = build_cells(shape, cell_ref, cell_m)

    cells, lanes = shape.cells, shape.lanes
    weights = weight[...]
    for step in range(shape.sides // shape.block):
        sides = slice(step * shape.block, (step + 1) * shape.block)
        at = step * shape.block * cells
        left = beside(field_ref[at : at + shape.block * cells, :])
        if ends:
            left = jnp.concatenate([left, halo_ends(shape, end_refs, sides)], axis=1)
        lines[step] = dot(left, line_m[: left.shape[1], :])
        if with_flux:
            placed[step] = dot_nt(expand(shape, phi[sides, :], cell_mask), cell_m[...])
        for index in range(shape.half // shape.chunk):
            offset = index * shape.rows
            here = slice(offset, offset + shape.rows)
            spans = [
                slice(at + start, at + start + shape.rows)
                for start in (offset, offset + shape.half_rows)
            ]
            stack = jnp.concatenate([field_ref[span, :] for span in spans], axis=1)
            near = dot(near_m[:, : shape.rows], stack) + lines[step, here, :]
            for part, span in enumerate(spans):
                cols = slice(part * lanes, (part + 1) * lanes)
                source = load_ref[span, :].astype(F32)
                if with_flux:
                    source = source + placed[step, here, cols]
                    source_ref[span, :] = source.astype(BF)
                centre = field_ref[span, :].astype(F32)
                base_ref[span, :] = (1.0 - OMEGA) * centre + weights * (source + near[:, cols])


def sweep_base(shape, field, load, tables, ends=(), phi=None, flux_cell=None):
    steps = shape.sides // shape.block
    half = (steps, shape.half_rows, 2 * shape.lanes)
    operands = [field, load, *tables[:3], *ends]
    shapes = [jax.ShapeDtypeStruct(field.shape, F32)]
    scratch = [pltpu.VMEM(half, F32)]
    if phi is not None:
        operands += [phi, flux_cell]
        shapes.append(jax.ShapeDtypeStruct(field.shape, BF))
        scratch.append(pltpu.VMEM((2 * shape.lanes, 2 * phi.shape[1]), BF))
        scratch.append(pltpu.VMEM(half, F32))
    return pl.pallas_call(
        functools.partial(base_kernel, shape, len(ends), phi is not None),
        in_specs=[WHOLE] * len(operands),
        out_specs=[WHOLE] * len(shapes),
        out_shape=shapes,
        scratch_shapes=scratch,
        compiler_params=params(),
        cost_estimate=pl.CostEstimate(
            flops=6 * field.size * 128, bytes_accessed=8 * field.size, transcendentals=0
        ),
    )(*operands)


def finish_kernel(shape, ends, recvs, last, *refs):
    with_flux = recvs > 0
    refs = list(refs)
    take = lambda count: [refs.pop(0) for _ in range(count)]
    base_ref, weight, near_m, line_m, ends_m, rsum = take(6)
    halo_refs = take(len(shape.faces))
    end_refs = take(ends)
    if with_flux:
        (cell_ref,) = take(1)
        recv_refs = take(recvs)
    (out_ref,) = take(1)
    if not last:
        face_refs = take(len(shape.faces))
        (z_ref,) = take(1)
    if with_flux:
        phi, flux_ref = take(2)
    if last:
        result_ref = out_ref
        out_ref, out_sems = take(2)
    else:
        (tall,) = take(1)
    if ends:
        (lines,) = take(1)
    if with_flux:
        cell_m, placed = take(2)

    cells, lanes = shape.cells, shape.lanes

    if with_flux:
        slots = cell_ref.shape[3]
        cell_mask = build_cells(shape, cell_ref, cell_m)
        owned = recv_refs[0][...]
        for ref in recv_refs[1:]:
            owned = owned + ref[...]
        flux_ref[...] = owned[slots:, : flux_ref.shape[1]]
        owned = owned[:slots]
        high = owned.astype(BF).astype(F32)
        phi[...] = jnp.concatenate([high, owned - high], axis=0).T

    weights = weight[...]

    def work(step):
        at = step * shape.block
        sides = slice(at, at + shape.block)
        if ends:
            lines[step] = dot(halo_ends(shape, end_refs, sides), line_m[2 * lanes :, :])
        if with_flux:
            placed[step] = dot_nt(expand(shape, phi[sides, :], cell_mask), cell_m[...])
        for index in range(shape.half // shape.chunk):
            offset = index * shape.rows
            starts = (offset, offset + shape.half_rows)
            stacks = []
            for start in starts:
                stack = []
                for face, ref in zip(shape.faces, halo_refs):
                    length = shape.face_len(face)
                    first = at * length + start // cells * length
                    stack.append(ref[first : first + shape.chunk * length, :])
                stacks.append(jnp.concatenate(stack, axis=0))
            near = dot(near_m[:, shape.rows :], jnp.concatenate(stacks, axis=1))
            if ends:
                near = near + lines[step, offset : offset + shape.rows, :]
            if with_flux:
                near = near + placed[step, offset : offset + shape.rows, :]
            for part, start in enumerate(starts):
                rows = slice(at * cells + start, at * cells + start + shape.rows)
                fresh = base_ref[rows, :] + weights * near[:, part * lanes : (part + 1) * lanes]
                out_ref[rows, :] = fresh.astype(BF)
                if not last:
                    tall[step, start : start + shape.rows, :] = fresh

    def emit(step):
        at, size = step * shape.block, shape.block * cells
        fresh = out_ref[at * cells : at * cells + size, :]
        cut_faces(shape, shape.faces, at, shape.block, tall.at[step], face_refs)
        cut_ends(shape, at, fresh, z_ref, ends_m, rsum)

    steps = shape.sides // shape.block
    copies = []
    for step in range(steps):
        work(step)
        if last:
            span = pl.ds(step * shape.block * cells, shape.block * cells)
            copies.append(
                pltpu.make_async_copy(out_ref.at[span], result_ref.at[span], out_sems.at[step])
            )
            copies[-1].start()
        elif step > 0:
            emit(step - 1)
    for copy in copies:
        copy.wait()
    if not last:
        emit(steps - 1)


def sweep_finish(shape, base, tables, halos, ends=(), flux_cell=None, recv=(), last=False):
    lanes, cells = shape.lanes, shape.cells
    steps = shape.sides // shape.block
    half = (steps, shape.half_rows, 2 * lanes)
    operands = [base, *tables, *halos, *ends]
    out_shapes = [jax.ShapeDtypeStruct(base.shape, BF)]
    if last:
        scratch = [pltpu.VMEM(base.shape, BF), pltpu.SemaphoreType.DMA((steps,))]
    else:
        out_shapes += face_shapes(shape, shape.faces)
        out_shapes.append(jax.ShapeDtypeStruct((shape.sides, 2 * cells), BF))
        scratch = [pltpu.VMEM((steps, shape.block * cells, lanes), F32)]
    if ends:
        scratch.append(pltpu.VMEM(half, F32))
    if recv:
        slots = flux_cell.shape[3]
        operands += [flux_cell, *recv]
        out_shapes += [
            jax.ShapeDtypeStruct((shape.sides, 2 * slots), F32),
            jax.ShapeDtypeStruct((recv[0].shape[0] - slots, slots * lax.axis_size("gz")), F32),
        ]
        scratch += [
            pltpu.VMEM((2 * lanes, 4 * slots), BF),
            pltpu.VMEM(half, F32),
        ]
    out_specs = [WHOLE] * len(out_shapes)
    if last:
        out_specs = [pl.BlockSpec(memory_space=pltpu.HBM)]
    return pl.pallas_call(
        functools.partial(finish_kernel, shape, len(ends), len(recv), last),
        in_specs=[WHOLE] * len(operands),
        out_specs=out_specs,
        out_shape=out_shapes,
        scratch_shapes=scratch,
        compiler_params=params(),
        cost_estimate=pl.CostEstimate(
            flops=4 * base.size * 128, bytes_accessed=8 * base.size, transcendentals=0
        ),
    )(*operands)


def swap_faces(faces, values):
    return [swap(value, *face) for face, value in zip(faces, values)]


def swap_ends(shape, ends):
    return [swap(ends, "gz", turn) for turn in range(shape.ends)]


def row_gather(trace, hidden, late):
    peers = lax.axis_size("row")
    held = {0: trace}
    bit = peers // 2
    while bit:
        pairs = [(i, i ^ bit) for i in range(peers)]
        fresh = {key ^ bit: lax.ppermute(held[key], "row", pairs) for key in sorted(held, reverse=True)}
        if bit == peers // 2:
            fresh, hidden = lax.optimization_barrier((fresh, hidden))
            fresh, late = lax.optimization_barrier((fresh, late))
        held.update(fresh)
        bit //= 2
    return [held[key] for key in range(peers)], hidden, late


def per_device(volume_field, volume_load, coefficient, surface_block, trace_cell, flux_cell):
    sides, first, second, lanes = volume_field.shape
    cells = first * second
    shape = Shape(sides, first, second, lanes)
    field = volume_field.reshape(sides * cells, lanes)
    load = volume_load.reshape(sides * cells, lanes)
    coef = coefficient.reshape(cells, lanes)

    slots = trace_cell.shape[3]
    trace, *outer = traces(
        shape, volume_field.reshape(sides, cells, lanes), trace_cell, min(32, sides)
    )
    firsts = first_faces(shape, field, surface_block, coef, slots)
    layers = len(shape.faces)
    count = len(shape.inner) + 1
    inner, held, tables = firsts[:count], firsts[count], firsts[count + 1 :]
    *inner, ends = inner
    along_col = swap_faces(shape.outer, outer)
    parts, inner, along_col = row_gather(trace, inner, along_col)
    along_row = swap_faces(shape.inner, inner)
    recv, ends = flux_sums(parts, held, along_row, ends)
    tips = swap_ends(shape, ends)

    (base,) = sweep_base(shape, field, load, tables, tips)
    current, *faces, ends, phi, surface_flux = sweep_finish(
        shape, base, tables, along_col + along_row, flux_cell=flux_cell, recv=recv
    )
    halos, tips = swap_faces(shape.faces, faces), swap_ends(shape, ends)
    base, source = sweep_base(shape, current, load, tables, phi=phi, flux_cell=flux_cell)
    current, *faces, ends = sweep_finish(shape, base, tables, halos, tips)
    halos, tips = swap_faces(shape.faces, faces), swap_ends(shape, ends)
    (base,) = sweep_base(shape, current, source, tables)
    (current,) = sweep_finish(shape, base, tables, halos, tips, last=True)
    return current.reshape(volume_field.shape), surface_flux


def solution(mesh):
    in_specs = (
        P(None, "row", "col", "gz"),
        P(None, "row", "col", "gz"),
        P("row", "col", "gz"),
        P("row", "col"),
        P("row", "col", "gz", None),
        P("row", "col", "gz", None),
    )
    out_specs = (P(None, "row", "col", "gz"), P("gz", ("row", "col")))
    return jax.shard_map(
        per_device, mesh=mesh, in_specs=in_specs, out_specs=out_specs, check_vma=False
    )
```

```python
import functools

import jax
import jax.numpy as jnp
from jax import lax
from jax.experimental import pallas as pl
from jax.experimental.pallas import tpu as pltpu
from jax.sharding import PartitionSpec as P

OMEGA = 0.8
BF = jnp.bfloat16
F32 = jnp.float32
WHOLE = pl.BlockSpec(memory_space=pltpu.VMEM)


def aligned(start, unit):
    return start if isinstance(start, int) else pl.multiple_of(start, unit)


def iota(shape, dim):
    return lax.broadcasted_iota(jnp.int32, shape, dim)


def dot(a, b):
    return jnp.dot(a, b, preferred_element_type=F32)


def dot_nt(a, b):
    return lax.dot_general(a, b, (((1,), (1,)), ((), ())), preferred_element_type=F32)


FACES_MIB = 50


def params(mebibytes=24):
    return pltpu.CompilerParams(vmem_limit_bytes=mebibytes * 1024 * 1024)


def trace_kernel(shape, stride, block, field_ref, cell_ref, out_ref, *refs):
    *face_refs, field, cell_v, tall, near, place, picked, sems = refs
    sides, rows, lanes = field.shape
    slots = cell_ref.shape[3]
    per_row = lanes // stride
    width = near.shape[0]
    parts = slots // width
    cell_copy = pltpu.make_async_copy(cell_ref, cell_v, sems.at[sides // block])
    cell_copy.start()
    copies = []
    for step in range(sides // block):
        span = pl.ds(step * block, block)
        copies.append(pltpu.make_async_copy(field_ref.at[span], field.at[span], sems.at[step]))
        copies[-1].start()

    cell_copy.wait()
    cell = cell_v[0, 0]
    run = cell // stride
    digit = jnp.zeros_like(cell)
    for part in range(parts):
        digit = jnp.where(run // width == part, (cell % stride) * stride**part, digit)
    hit = iota((width, slots), 0) == run % width
    near[...] = hit.astype(BF)
    digits = jnp.sum(jnp.where(hit, digit.astype(F32), 0.0), axis=1, keepdims=True)
    digits = jnp.broadcast_to(digits, (width, 128)).T[0:8].astype(jnp.int32)
    first = iota((8, width), 1) % per_row * stride
    for part in range(parts):
        place[:, part * width : (part + 1) * width] = first + digits // stride**part % stride

    together = 128 // per_row
    group = iota((8, 128), 1) // per_row
    for step in range(sides // block):
        copies[step].wait()
        span = field[step * block : (step + 1) * block]
        tall[step] = span.reshape(block * rows, lanes).astype(F32)
        cut_faces(shape, shape.outer, step * block, block, tall.at[step], face_refs)

        for batch in range(block // 8):
            for tile in range(rows // together):
                cols = slice(tile * 128, (tile + 1) * 128)
                where = place[:, cols]
                found = None
                for row in range(together):
                    start = batch * 8 * rows + tile * together + row
                    line = tall[step, pl.ds(start, 8, stride=rows), :]
                    line = jnp.take_along_axis(line, where, axis=1)
                    found = line if found is None else jnp.where(group == row, line, found)
                at = step * block + batch * 8
                picked[at : at + 8, cols] = found

    total = jnp.zeros((sides, slots), F32)
    for part in range(parts):
        sorted_runs = picked[:, part * width : (part + 1) * width].astype(BF)
        total = jnp.where(run // width == part, dot(sorted_runs, near[...]), total)
    out_ref[...] = total.T.astype(BF)


def traces(shape, field, trace_cell, block):
    sides, rows, lanes = field.shape
    slots = trace_cell.shape[3]
    stride = rows * lanes // slots
    width = min(slots, 256)
    hbm = pl.BlockSpec(memory_space=pltpu.HBM)
    return pl.pallas_call(
        functools.partial(trace_kernel, shape, stride, block),
        in_specs=[hbm, hbm],
        out_specs=[WHOLE] * (1 + len(shape.outer)),
        out_shape=[jax.ShapeDtypeStruct((slots, sides), BF)] + face_shapes(shape, shape.outer),
        scratch_shapes=[
            pltpu.VMEM(field.shape, BF),
            pltpu.VMEM(trace_cell.shape, jnp.int32),
            pltpu.VMEM((sides // block, block * rows, lanes), F32),
            pltpu.VMEM((width, slots), BF),
            pltpu.VMEM((8, slots), jnp.int32),
            pltpu.VMEM((sides, slots), F32),
            pltpu.SemaphoreType.DMA((sides // block + 1,)),
        ],
        compiler_params=params(62),
        cost_estimate=pl.CostEstimate(
            flops=4 * sides * rows * lanes * 128, bytes_accessed=field.size * 2, transcendentals=0
        ),
    )(field, trace_cell)


def fetch_columns(block_ref, held, sems, slots):
    me, group, gzs = lax.axis_index("row"), lax.axis_index("gz"), lax.axis_size("gz")
    copies = []
    for key in range(held.shape[0]):
        start = pl.multiple_of((jnp.bitwise_xor(me, key) * gzs + group) * slots, slots)
        copies.append(
            pltpu.make_async_copy(block_ref.at[:, pl.ds(start, slots)], held.at[key], sems.at[key])
        )
        copies[-1].start()
    return copies


def surface_kernel(halves, *refs):
    ins, total = refs[:-1], refs[-1]
    outs = ins[len(ins) - halves :]
    *parts, held = ins[: len(ins) - halves]
    value = None
    for key, part in enumerate(parts):
        term = dot(held[key], part[...])
        value = term if value is None else value + term
    if halves == 1:
        outs[0][...] = value
        return
    total[...] = value
    count = outs[0].shape[0]
    mine = lax.axis_index("col")
    for key, out in enumerate(outs):
        out[...] = total[pl.ds(pl.multiple_of((mine ^ key) * count, 8), count), :]


def surface(parts, held, halves):
    sides = parts[0].shape[1]
    lines = held.shape[1]
    return pl.pallas_call(
        functools.partial(surface_kernel, halves),
        in_specs=[WHOLE] * (len(parts) + 1),
        out_specs=[WHOLE] * halves,
        out_shape=[jax.ShapeDtypeStruct((lines // halves, sides), F32)] * halves,
        scratch_shapes=[pltpu.VMEM((lines, sides), F32)],
        compiler_params=params(),
        cost_estimate=pl.CostEstimate(
            flops=2 * sides * held.size, bytes_accessed=2 * held.size, transcendentals=0
        ),
    )(*parts, held)


def share_kernel(peers, mine_ref, other_ref, *refs):
    *outs, total, turned = refs
    total[...] = mine_ref[...] + other_ref[...]
    turned[...] = total[...].T
    lines, sides = total.shape
    group = lax.axis_index("gz")
    for key, out in enumerate(outs):
        peer = group ^ key
        rows, some = lines // peers, sides // peers
        out[:rows, :] = total[pl.ds(pl.multiple_of(peer * rows, 8), rows), :]
        out[rows:, :] = turned[pl.ds(pl.multiple_of(peer * some, 8), some), :]


def shares(mine, other):
    peers = lax.axis_size("gz")
    lines, sides = mine.shape
    out = jax.ShapeDtypeStruct(((lines + sides) // peers, sides), F32)
    return pl.pallas_call(
        functools.partial(share_kernel, peers),
        in_specs=[WHOLE] * 2,
        out_specs=[WHOLE] * peers,
        out_shape=[out] * peers,
        scratch_shapes=[pltpu.VMEM((lines, sides), F32), pltpu.VMEM((sides, lines), F32)],
        compiler_params=params(),
        cost_estimate=pl.CostEstimate(
            flops=lines * sides, bytes_accessed=16 * lines * sides, transcendentals=0
        ),
    )(mine, other)


def flux_sums(parts, held, late, after):
    cols, gzs = lax.axis_size("col"), lax.axis_size("gz")
    sides = parts[0].shape[1]
    lines = held.shape[1]
    if cols == 2 and gzs & (gzs - 1) == 0 and lines // cols == sides and sides // gzs % 8 == 0:
        mine, other = surface(parts, held, 2)
        mine, other, after = lax.optimization_barrier((mine, other, after))
        other = lax.ppermute(other, "col", [(0, 1), (1, 0)])
        other, late = lax.optimization_barrier((other, late))
        sent = shares(mine, other)
        recv = [sent[0]]
        for key in range(gzs - 1, 0, -1):
            recv.append(lax.ppermute(sent[key], "gz", [(i, i ^ key) for i in range(gzs)]))
        return recv, after
    (total,) = surface(parts, held, 1)
    rows = lax.psum_scatter(total, "col", scatter_dimension=0, tiled=True)
    owned = lax.psum_scatter(rows, "gz", scatter_dimension=0, tiled=True)
    flux = lax.psum_scatter(rows.T, "gz", scatter_dimension=0, tiled=True)
    flux = jnp.pad(flux, ((0, 0), (0, sides - flux.shape[1])))
    return [jnp.concatenate([owned, flux], axis=0)], after


def turns(axis):
    return 1 if lax.axis_size(axis) == 2 else 2


def partner(index, turn):
    return jnp.where(index % 2 == turn, index + 1, index - 1)


def has_neighbour(axis, turn):
    other = partner(lax.axis_index(axis), turn)
    return (other >= 0) & (other < lax.axis_size(axis))


def swap(value, axis, turn):
    axes = ("row", "col", "gz")
    sizes = [lax.axis_size(name) for name in axes]
    along = axes.index(axis)
    spare = 0 if axis == "gz" else 2
    pairs = []
    for r in range(sizes[0]):
        for c in range(sizes[1]):
            for g in range(sizes[2]):
                here = [r, c, g]
                there = [r, c, g]
                there[along] += 1 if here[along] % 2 == turn else -1
                if not 0 <= there[along] < sizes[along]:
                    there[along] = here[along]
                    if here[spare] ^ 1 < sizes[spare]:
                        there[spare] ^= 1
                flat = [(at[0] * sizes[1] + at[1]) * sizes[2] + at[2] for at in (here, there)]
                pairs.append(tuple(flat))
    return lax.ppermute(value, axes, pairs)


class Shape:
    def __init__(self, sides, first, second, lanes):
        self.sides, self.x, self.y, self.lanes = sides, first, second, lanes
        self.cells = first * second
        self.chunk = max(1, 128 // self.cells)
        self.rows = self.chunk * self.cells
        self.block = min(sides, 32)
        self.half = self.block // 2
        self.half_rows = self.half * self.cells
        self.outer = [("col", i) for i in range(turns("col"))]
        self.inner = [("row", i) for i in reversed(range(turns("row")))]
        self.faces = self.outer + self.inner
        self.ends = turns("gz")

    def face_len(self, face):
        return self.y if face[0] == "row" else self.x

    def halo_rows(self):
        return sum(self.chunk * self.face_len(face) for face in self.faces)

    def edge(self, face):
        axis, turn = face
        last = (self.x if axis == "row" else self.y) - 1
        return jnp.where(lax.axis_index(axis) % 2 == turn, last, 0)


def halo_place(shape):
    dims = (shape.rows, shape.halo_rows())
    row, col = iota(dims, 0), iota(dims, 1)
    side, cell = row // shape.cells, row % shape.cells
    x, y = cell // shape.y, cell % shape.y
    hit, base = None, 0
    for face in shape.faces:
        length = shape.face_len(face)
        along, across = (y, x) if face[0] == "row" else (x, y)
        place = (across == shape.edge(face)) & (col - base == side * length + along)
        place = place & has_neighbour(*face)
        hit = place if hit is None else hit | place
        base += shape.chunk * length
    return hit.astype(BF)


def z_mask(shape, count):
    dims = (count * shape.cells, 2 * shape.cells)
    return iota(dims, 1) % shape.cells == iota(dims, 0) % shape.cells


def twice(matrix):
    zero = jnp.zeros_like(matrix)
    return jnp.concatenate(
        [jnp.concatenate([matrix, zero], axis=1), jnp.concatenate([zero, matrix], axis=1)], axis=0
    )


def beside(values):
    half = values.shape[0] // 2
    return jnp.concatenate([values[:half], values[half:]], axis=1)


def build_out(shape, ends_m, rsum):
    dims = (shape.lanes, 2 * shape.cells)
    edge = jnp.where(iota(dims, 1) < shape.cells, 0, shape.lanes - 1)
    ends_m[...] = twice((iota(dims, 0) == edge).astype(F32)).astype(BF)
    dims = rsum.shape
    rsum[...] = (iota(dims, 1) // shape.cells == iota(dims, 0)).astype(BF)


def cut_faces(shape, faces, at, block, tall, face_refs):
    for face, ref in zip(faces, face_refs):
        length, edge = shape.face_len(face), shape.edge(face)
        lines = []
        for side in range(block):
            start = side * shape.cells
            if face[0] == "row":
                lines.append(tall[pl.ds(aligned(start + edge * length, 8), length), :])
            else:
                lines.append(tall[pl.ds(start + edge, length, stride=shape.y), :])
        span = slice(at * length, (at + block) * length)
        ref[span, :] = jnp.concatenate(lines, axis=0).astype(BF)


def cut_ends(shape, at, values, z_ref, ends_m, rsum):
    mask = jnp.concatenate([z_mask(shape, shape.half)] * 2, axis=1)
    tips = jnp.where(mask, dot(beside(values), ends_m[...]), 0.0).astype(BF)
    tips = dot(rsum[...], tips)[: shape.half]
    tips = jnp.concatenate([tips[:, : 2 * shape.cells], tips[:, 2 * shape.cells :]], axis=0)
    z_ref[at : at + shape.block, :] = tips.astype(BF)


def build_tables(shape, coef_ref, weight, near_m, line_m, ends_m, rsum):
    cells, lanes = shape.cells, shape.lanes
    weight[...] = jnp.concatenate([OMEGA / (6.0 + coef_ref[...])] * shape.chunk, axis=0)
    dims = (shape.rows, shape.rows)
    row, col = iota(dims, 0), iota(dims, 1)
    x, y = row % cells // shape.y, row % shape.y
    x2, y2 = col % cells // shape.y, col % shape.y
    near = ((x == x2) & (jnp.abs(y - y2) == 1)) | ((y == y2) & (jnp.abs(x - x2) == 1))
    near_m[:, : shape.rows] = (near & (row // cells == col // cells)).astype(BF)
    near_m[:, shape.rows :] = halo_place(shape)
    dims = (lanes, lanes)
    line = (jnp.abs(iota(dims, 0) - iota(dims, 1)) == 1).astype(F32)
    line_m[: 2 * lanes, :] = twice(line).astype(BF)
    dims = (2 * cells, lanes)
    edge = jnp.where(iota(dims, 0) < cells, lanes - 1, 0)
    line_m[2 * lanes :, :] = twice((iota(dims, 1) == edge).astype(F32)).astype(BF)
    build_out(shape, ends_m, rsum)


def table_shapes(shape):
    lanes, cells = shape.lanes, shape.cells
    return [
        jax.ShapeDtypeStruct((shape.rows, lanes), F32),
        jax.ShapeDtypeStruct((shape.rows, shape.rows + shape.halo_rows()), BF),
        jax.ShapeDtypeStruct((2 * lanes + 4 * cells, 2 * lanes), BF),
        jax.ShapeDtypeStruct((2 * lanes, 4 * cells), BF),
        jax.ShapeDtypeStruct((max(8, shape.half), shape.half_rows), BF),
    ]


def faces_kernel(shape, slots, field_ref, block_ref, coef_ref, *refs):
    refs = list(refs)
    face_refs = [refs.pop(0) for _ in shape.inner]
    z_ref, held, *tables, field, tall, sems, field_sems = refs
    size = shape.block * shape.cells
    steps = shape.sides // shape.block
    copies = []
    for step in range(steps):
        span = pl.ds(step * size, size)
        copies.append(
            pltpu.make_async_copy(field_ref.at[span], field.at[span], field_sems.at[step])
        )
        copies[-1].start()
    columns = fetch_columns(block_ref, held, sems, slots)
    build_tables(shape, coef_ref, *tables)
    ends_m, rsum = tables[-2:]
    for step in range(steps):
        copies[step].wait()
        values = field[step * size : (step + 1) * size, :]
        tall[step] = values.astype(F32)
        cut_faces(shape, shape.inner, step * shape.block, shape.block, tall.at[step], face_refs)
        cut_ends(shape, step * shape.block, values, z_ref, ends_m, rsum)
    for copy in columns:
        copy.wait()


def face_shapes(shape, faces):
    return [
        jax.ShapeDtypeStruct((shape.sides * shape.face_len(face), shape.lanes), BF)
        for face in faces
    ]


def first_faces(shape, field, block, coef, slots):
    peers = lax.axis_size("row")
    steps = shape.sides // shape.block
    shapes = face_shapes(shape, shape.inner)
    shapes.append(jax.ShapeDtypeStruct((shape.sides, 2 * shape.cells), BF))
    shapes.append(jax.ShapeDtypeStruct((peers, block.shape[0], slots), BF))
    shapes += table_shapes(shape)
    hbm = pl.BlockSpec(memory_space=pltpu.HBM)
    return pl.pallas_call(
        functools.partial(faces_kernel, shape, slots),
        in_specs=[hbm, hbm, WHOLE],
        out_specs=[WHOLE] * len(shapes),
        out_shape=shapes,
        scratch_shapes=[
            pltpu.VMEM(field.shape, BF),
            pltpu.VMEM((steps, shape.block * shape.cells, shape.lanes), F32),
            pltpu.SemaphoreType.DMA((peers,)),
            pltpu.SemaphoreType.DMA((steps,)),
        ],
        compiler_params=params(FACES_MIB),
        cost_estimate=pl.CostEstimate(
            flops=field.size * 128, bytes_accessed=4 * field.size, transcendentals=0
        ),
    )(field, block, coef)


def expand(shape, lines, where):
    rows = []
    for side in range(shape.block):
        line = jnp.broadcast_to(lines[side : side + 1], where.shape)
        rows.append(jnp.where(where, line, 0.0))
    return beside(jnp.concatenate(rows, axis=0).astype(BF))


def halo_ends(shape, end_refs, sides):
    even = lax.axis_index("gz") % 2 == 0
    filled = (iota((shape.block, 2 * shape.cells), 1) < shape.cells) == even
    zs = 0.0
    for turn in range(shape.ends):
        wanted = (filled == (turn == 0)) & has_neighbour("gz", turn)
        zs = jnp.where(wanted, end_refs[-1 - turn][sides, :].astype(F32), zs)
    return expand(shape, zs, z_mask(shape, 1))


def build_cells(shape, cell_ref, cell_m):
    slots = cell_ref.shape[3]
    cell = jnp.concatenate([cell_ref[0, 0]] * 2, axis=1)
    place = (iota((shape.lanes, 2 * slots), 0) == cell % shape.lanes).astype(F32)
    cell_m[...] = twice(place).astype(BF)
    return iota((shape.cells, 2 * slots), 0) == cell // shape.lanes


def base_kernel(shape, ends, with_flux, *refs):
    refs = list(refs)
    take = lambda count: [refs.pop(0) for _ in range(count)]
    field_ref, load_ref, weight, near_m, line_m = take(5)
    end_refs = take(ends)
    if with_flux:
        phi, cell_ref = take(2)
    (base_ref,) = take(1)
    if with_flux:
        (source_ref,) = take(1)
    (lines,) = take(1)
    if with_flux:
        cell_m, placed = take(2)
        cell_mask = build_cells(shape, cell_ref, cell_m)

    cells, lanes = shape.cells, shape.lanes
    weights = weight[...]
    for step in range(shape.sides // shape.block):
        sides = slice(step * shape.block, (step + 1) * shape.block)
        at = step * shape.block * cells
        left = beside(field_ref[at : at + shape.block * cells, :])
        if ends:
            left = jnp.concatenate([left, halo_ends(shape, end_refs, sides)], axis=1)
        lines[step] = dot(left, line_m[: left.shape[1], :])
        if with_flux:
            placed[step] = dot_nt(expand(shape, phi[sides, :], cell_mask), cell_m[...])
        for index in range(shape.half // shape.chunk):
            offset = index * shape.rows
            here = slice(offset, offset + shape.rows)
            spans = [
                slice(at + start, at + start + shape.rows)
                for start in (offset, offset + shape.half_rows)
            ]
            stack = jnp.concatenate([field_ref[span, :] for span in spans], axis=1)
            near = dot(near_m[:, : shape.rows], stack) + lines[step, here, :]
            for part, span in enumerate(spans):
                cols = slice(part * lanes, (part + 1) * lanes)
                source = load_ref[span, :].astype(F32)
                if with_flux:
                    source = source + placed[step, here, cols]
                    source_ref[span, :] = source.astype(BF)
                centre = field_ref[span, :].astype(F32)
                base_ref[span, :] = (1.0 - OMEGA) * centre + weights * (source + near[:, cols])


def sweep_base(shape, field, load, tables, ends=(), phi=None, flux_cell=None):
    steps = shape.sides // shape.block
    half = (steps, shape.half_rows, 2 * shape.lanes)
    operands = [field, load, *tables[:3], *ends]
    shapes = [jax.ShapeDtypeStruct(field.shape, F32)]
    scratch = [pltpu.VMEM(half, F32)]
    if phi is not None:
        operands += [phi, flux_cell]
        shapes.append(jax.ShapeDtypeStruct(field.shape, BF))
        scratch.append(pltpu.VMEM((2 * shape.lanes, 2 * phi.shape[1]), BF))
        scratch.append(pltpu.VMEM(half, F32))
    return pl.pallas_call(
        functools.partial(base_kernel, shape, len(ends), phi is not None),
        in_specs=[WHOLE] * len(operands),
        out_specs=[WHOLE] * len(shapes),
        out_shape=shapes,
        scratch_shapes=scratch,
        compiler_params=params(),
        cost_estimate=pl.CostEstimate(
            flops=6 * field.size * 128, bytes_accessed=8 * field.size, transcendentals=0
        ),
    )(*operands)


def finish_kernel(shape, ends, recvs, last, *refs):
    with_flux = recvs > 0
    refs = list(refs)
    take = lambda count: [refs.pop(0) for _ in range(count)]
    base_ref, weight, near_m, line_m, ends_m, rsum = take(6)
    halo_refs = take(len(shape.faces))
    end_refs = take(ends)
    if with_flux:
        (cell_ref,) = take(1)
        recv_refs = take(recvs)
    (out_ref,) = take(1)
    if not last:
        face_refs = take(len(shape.faces))
        (z_ref,) = take(1)
    if with_flux:
        phi, flux_ref = take(2)
    if last:
        result_ref = out_ref
        out_ref, out_sems = take(2)
    else:
        (tall,) = take(1)
    if ends:
        (lines,) = take(1)
    if with_flux:
        cell_m, placed = take(2)

    cells, lanes = shape.cells, shape.lanes

    if with_flux:
        slots = cell_ref.shape[3]
        cell_mask = build_cells(shape, cell_ref, cell_m)
        owned = recv_refs[0][...]
        for ref in recv_refs[1:]:
            owned = owned + ref[...]
        flux_ref[...] = owned[slots:, : flux_ref.shape[1]]
        owned = owned[:slots]
        high = owned.astype(BF).astype(F32)
        phi[...] = jnp.concatenate([high, owned - high], axis=0).T

    weights = weight[...]

    def work(step):
        at = step * shape.block
        sides = slice(at, at + shape.block)
        if ends:
            lines[step] = dot(halo_ends(shape, end_refs, sides), line_m[2 * lanes :, :])
        if with_flux:
            placed[step] = dot_nt(expand(shape, phi[sides, :], cell_mask), cell_m[...])
        for index in range(shape.half // shape.chunk):
            offset = index * shape.rows
            starts = (offset, offset + shape.half_rows)
            stacks = []
            for start in starts:
                stack = []
                for face, ref in zip(shape.faces, halo_refs):
                    length = shape.face_len(face)
                    first = at * length + start // cells * length
                    stack.append(ref[first : first + shape.chunk * length, :])
                stacks.append(jnp.concatenate(stack, axis=0))
            near = dot(near_m[:, shape.rows :], jnp.concatenate(stacks, axis=1))
            if ends:
                near = near + lines[step, offset : offset + shape.rows, :]
            if with_flux:
                near = near + placed[step, offset : offset + shape.rows, :]
            for part, start in enumerate(starts):
                rows = slice(at * cells + start, at * cells + start + shape.rows)
                fresh = base_ref[rows, :] + weights * near[:, part * lanes : (part + 1) * lanes]
                out_ref[rows, :] = fresh.astype(BF)
                if not last:
                    tall[step, start : start + shape.rows, :] = fresh

    def emit(step):
        at, size = step * shape.block, shape.block * cells
        fresh = out_ref[at * cells : at * cells + size, :]
        cut_faces(shape, shape.faces, at, shape.block, tall.at[step], face_refs)
        cut_ends(shape, at, fresh, z_ref, ends_m, rsum)

    steps = shape.sides // shape.block
    copies = []
    for step in range(steps):
        work(step)
        if last:
            span = pl.ds(step * shape.block * cells, shape.block * cells)
            copies.append(
                pltpu.make_async_copy(out_ref.at[span], result_ref.at[span], out_sems.at[step])
            )
            copies[-1].start()
        elif step > 0:
            emit(step - 1)
    for copy in copies:
        copy.wait()
    if not last:
        emit(steps - 1)


def sweep_finish(shape, base, tables, halos, ends=(), flux_cell=None, recv=(), last=False):
    lanes, cells = shape.lanes, shape.cells
    steps = shape.sides // shape.block
    half = (steps, shape.half_rows, 2 * lanes)
    operands = [base, *tables, *halos, *ends]
    out_shapes = [jax.ShapeDtypeStruct(base.shape, BF)]
    if last:
        scratch = [pltpu.VMEM(base.shape, BF), pltpu.SemaphoreType.DMA((steps,))]
    else:
        out_shapes += face_shapes(shape, shape.faces)
        out_shapes.append(jax.ShapeDtypeStruct((shape.sides, 2 * cells), BF))
        scratch = [pltpu.VMEM((steps, shape.block * cells, lanes), F32)]
    if ends:
        scratch.append(pltpu.VMEM(half, F32))
    if recv:
        slots = flux_cell.shape[3]
        operands += [flux_cell, *recv]
        out_shapes += [
            jax.ShapeDtypeStruct((shape.sides, 2 * slots), F32),
            jax.ShapeDtypeStruct((recv[0].shape[0] - slots, slots * lax.axis_size("gz")), F32),
        ]
        scratch += [
            pltpu.VMEM((2 * lanes, 4 * slots), BF),
            pltpu.VMEM(half, F32),
        ]
    out_specs = [WHOLE] * len(out_shapes)
    if last:
        out_specs = [pl.BlockSpec(memory_space=pltpu.HBM)]
    return pl.pallas_call(
        functools.partial(finish_kernel, shape, len(ends), len(recv), last),
        in_specs=[WHOLE] * len(operands),
        out_specs=out_specs,
        out_shape=out_shapes,
        scratch_shapes=scratch,
        compiler_params=params(),
        cost_estimate=pl.CostEstimate(
            flops=4 * base.size * 128, bytes_accessed=8 * base.size, transcendentals=0
        ),
    )(*operands)


def swap_faces(faces, values):
    return [swap(value, *face) for face, value in zip(faces, values)]


def swap_ends(shape, ends):
    return [swap(ends, "gz", turn) for turn in reversed(range(shape.ends))]


def row_gather(trace, hidden, late):
    peers = lax.axis_size("row")
    held = {0: trace}
    bit = peers // 2
    while bit:
        pairs = [(i, i ^ bit) for i in range(peers)]
        fresh = {key ^ bit: lax.ppermute(held[key], "row", pairs) for key in sorted(held, reverse=True)}
        if bit == peers // 2:
            fresh, hidden = lax.optimization_barrier((fresh, hidden))
        held.update(fresh)
        bit //= 2
    parts, late = lax.optimization_barrier(([held[key] for key in range(peers)], late))
    return parts, hidden, late


def per_device(volume_field, volume_load, coefficient, surface_block, trace_cell, flux_cell):
    sides, first, second, lanes = volume_field.shape
    cells = first * second
    shape = Shape(sides, first, second, lanes)
    field = volume_field.reshape(sides * cells, lanes)
    load = volume_load.reshape(sides * cells, lanes)
    coef = coefficient.reshape(cells, lanes)

    slots = trace_cell.shape[3]
    trace, *outer = traces(
        shape, volume_field.reshape(sides, cells, lanes), trace_cell, min(32, sides)
    )
    firsts = first_faces(shape, field, surface_block, coef, slots)
    layers = len(shape.faces)
    count = len(shape.inner) + 1
    inner, held, tables = firsts[:count], firsts[count], firsts[count + 1 :]
    *inner, ends = inner
    along_col = swap_faces(shape.outer, outer)
    parts, inner, along_col = row_gather(trace, inner, along_col)
    along_row = swap_faces(shape.inner, inner)
    recv, ends = flux_sums(parts, held, along_row, ends)
    tips = swap_ends(shape, ends)

    (base,) = sweep_base(shape, field, load, tables, tips)
    current, *faces, ends, phi, surface_flux = sweep_finish(
        shape, base, tables, along_col + along_row, flux_cell=flux_cell, recv=recv
    )
    halos, tips = swap_faces(shape.faces, faces), swap_ends(shape, ends)
    base, source = sweep_base(shape, current, load, tables, phi=phi, flux_cell=flux_cell)
    current, *faces, ends = sweep_finish(shape, base, tables, halos, tips)
    halos, tips = swap_faces(shape.faces, faces), swap_ends(shape, ends)
    (base,) = sweep_base(shape, current, source, tables)
    (current,) = sweep_finish(shape, base, tables, halos, tips, last=True)
    return current.reshape(volume_field.shape), surface_flux


def solution(mesh):
    in_specs = (
        P(None, "row", "col", "gz"),
        P(None, "row", "col", "gz"),
        P("row", "col", "gz"),
        P("row", "col"),
        P("row", "col", "gz", None),
        P("row", "col", "gz", None),
    )
    out_specs = (P(None, "row", "col", "gz"), P("gz", ("row", "col")))
    return jax.shard_map(
        per_device, mesh=mesh, in_specs=in_specs, out_specs=out_specs, check_vma=False
    )
```

```python
import functools

import jax
import jax.numpy as jnp
from jax import lax
from jax.experimental import pallas as pl
from jax.experimental.pallas import tpu as pltpu
from jax.sharding import PartitionSpec as P

OMEGA = 0.8
BF = jnp.bfloat16
F32 = jnp.float32
WHOLE = pl.BlockSpec(memory_space=pltpu.VMEM)


def aligned(start, unit):
    return start if isinstance(start, int) else pl.multiple_of(start, unit)


def iota(shape, dim):
    return lax.broadcasted_iota(jnp.int32, shape, dim)


def dot(a, b):
    return jnp.dot(a, b, preferred_element_type=F32)


def dot_nt(a, b):
    return lax.dot_general(a, b, (((1,), (1,)), ((), ())), preferred_element_type=F32)


FACES_MIB = 50
TRACE_MIB = 52


def params(mebibytes=24):
    return pltpu.CompilerParams(vmem_limit_bytes=mebibytes * 1024 * 1024)


def trace_kernel(shape, stride, block, field_ref, cell_ref, out_ref, *refs):
    *face_refs, field, cell_v, tall, near, place, picked, sems = refs
    sides, rows, lanes = field.shape
    slots = cell_ref.shape[3]
    per_row = lanes // stride
    width = near.shape[0]
    parts = slots // width
    cell_copy = pltpu.make_async_copy(cell_ref, cell_v, sems.at[sides // block])
    cell_copy.start()
    copies = []
    for step in range(sides // block):
        span = pl.ds(step * block, block)
        copies.append(pltpu.make_async_copy(field_ref.at[span], field.at[span], sems.at[step]))
        copies[-1].start()

    cell_copy.wait()
    cell = cell_v[0, 0]
    run = cell // stride
    digit = jnp.zeros_like(cell)
    for part in range(parts):
        digit = jnp.where(run // width == part, (cell % stride) * stride**part, digit)
    hit = iota((width, slots), 0) == run % width
    near[...] = hit.astype(BF)
    digits = jnp.sum(jnp.where(hit, digit.astype(F32), 0.0), axis=1, keepdims=True)
    digits = jnp.broadcast_to(digits, (width, 128)).T[0:8].astype(jnp.int32)
    first = iota((8, width), 1) % per_row * stride
    for part in range(parts):
        place[:, part * width : (part + 1) * width] = first + digits // stride**part % stride

    together = 128 // per_row
    group = iota((8, 128), 1) // per_row
    for step in range(sides // block):
        copies[step].wait()
        span = field[step * block : (step + 1) * block]
        tall[step] = span.reshape(block * rows, lanes).astype(F32)
        cut_faces(shape, shape.outer, step * block, block, tall.at[step], face_refs)

        for batch in range(block // 8):
            for tile in range(rows // together):
                cols = slice(tile * 128, (tile + 1) * 128)
                where = place[:, cols]
                found = None
                for row in range(together):
                    start = batch * 8 * rows + tile * together + row
                    line = tall[step, pl.ds(start, 8, stride=rows), :]
                    line = jnp.take_along_axis(line, where, axis=1)
                    found = line if found is None else jnp.where(group == row, line, found)
                at = step * block + batch * 8
                picked[at : at + 8, cols] = found

    total = jnp.zeros((sides, slots), F32)
    for part in range(parts):
        sorted_runs = picked[:, part * width : (part + 1) * width].astype(BF)
        total = jnp.where(run // width == part, dot(sorted_runs, near[...]), total)
    out_ref[...] = total.T.astype(BF)


def traces(shape, field, trace_cell, block):
    sides, rows, lanes = field.shape
    slots = trace_cell.shape[3]
    stride = rows * lanes // slots
    width = min(slots, 256)
    hbm = pl.BlockSpec(memory_space=pltpu.HBM)
    return pl.pallas_call(
        functools.partial(trace_kernel, shape, stride, block),
        in_specs=[hbm, hbm],
        out_specs=[WHOLE] * (1 + len(shape.outer)),
        out_shape=[jax.ShapeDtypeStruct((slots, sides), BF)] + face_shapes(shape, shape.outer),
        scratch_shapes=[
            pltpu.VMEM(field.shape, BF),
            pltpu.VMEM(trace_cell.shape, jnp.int32),
            pltpu.VMEM((sides // block, block * rows, lanes), F32),
            pltpu.VMEM((width, slots), BF),
            pltpu.VMEM((8, slots), jnp.int32),
            pltpu.VMEM((sides, slots), F32),
            pltpu.SemaphoreType.DMA((sides // block + 1,)),
        ],
        compiler_params=params(TRACE_MIB),
        cost_estimate=pl.CostEstimate(
            flops=4 * sides * rows * lanes * 128, bytes_accessed=field.size * 2, transcendentals=0
        ),
    )(field, trace_cell)


def fetch_columns(block_ref, held, sems, slots):
    me, group, gzs = lax.axis_index("row"), lax.axis_index("gz"), lax.axis_size("gz")
    copies = []
    for key in range(held.shape[0]):
        start = pl.multiple_of((jnp.bitwise_xor(me, key) * gzs + group) * slots, slots)
        copies.append(
            pltpu.make_async_copy(block_ref.at[:, pl.ds(start, slots)], held.at[key], sems.at[key])
        )
        copies[-1].start()
    return copies


def surface_kernel(halves, *refs):
    ins, total = refs[:-1], refs[-1]
    outs = ins[len(ins) - halves :]
    *parts, held = ins[: len(ins) - halves]
    value = None
    for key, part in enumerate(parts):
        term = dot(held[key], part[...])
        value = term if value is None else value + term
    if halves == 1:
        outs[0][...] = value
        return
    total[...] = value
    count = outs[0].shape[0]
    mine = lax.axis_index("col")
    for key, out in enumerate(outs):
        out[...] = total[pl.ds(pl.multiple_of((mine ^ key) * count, 8), count), :]


def surface(parts, held, halves):
    sides = parts[0].shape[1]
    lines = held.shape[1]
    return pl.pallas_call(
        functools.partial(surface_kernel, halves),
        in_specs=[WHOLE] * (len(parts) + 1),
        out_specs=[WHOLE] * halves,
        out_shape=[jax.ShapeDtypeStruct((lines // halves, sides), F32)] * halves,
        scratch_shapes=[pltpu.VMEM((lines, sides), F32)],
        compiler_params=params(),
        cost_estimate=pl.CostEstimate(
            flops=2 * sides * held.size, bytes_accessed=2 * held.size, transcendentals=0
        ),
    )(*parts, held)


def share_kernel(peers, mine_ref, other_ref, *refs):
    *outs, total, turned = refs
    total[...] = mine_ref[...] + other_ref[...]
    turned[...] = total[...].T
    lines, sides = total.shape
    group = lax.axis_index("gz")
    for key, out in enumerate(outs):
        peer = group ^ key
        rows, some = lines // peers, sides // peers
        out[:rows, :] = total[pl.ds(pl.multiple_of(peer * rows, 8), rows), :]
        out[rows:, :] = turned[pl.ds(pl.multiple_of(peer * some, 8), some), :]


def shares(mine, other):
    peers = lax.axis_size("gz")
    lines, sides = mine.shape
    out = jax.ShapeDtypeStruct(((lines + sides) // peers, sides), F32)
    return pl.pallas_call(
        functools.partial(share_kernel, peers),
        in_specs=[WHOLE] * 2,
        out_specs=[WHOLE] * peers,
        out_shape=[out] * peers,
        scratch_shapes=[pltpu.VMEM((lines, sides), F32), pltpu.VMEM((sides, lines), F32)],
        compiler_params=params(),
        cost_estimate=pl.CostEstimate(
            flops=lines * sides, bytes_accessed=16 * lines * sides, transcendentals=0
        ),
    )(mine, other)


def flux_sums(parts, held, late, after):
    cols, gzs = lax.axis_size("col"), lax.axis_size("gz")
    sides = parts[0].shape[1]
    lines = held.shape[1]
    if cols == 2 and gzs & (gzs - 1) == 0 and lines // cols == sides and sides // gzs % 8 == 0:
        mine, other = surface(parts, held, 2)
        mine, other, after = lax.optimization_barrier((mine, other, after))
        other = lax.ppermute(other, "col", [(0, 1), (1, 0)])
        other, late = lax.optimization_barrier((other, late))
        sent = shares(mine, other)
        recv = [sent[0]]
        for key in range(gzs - 1, 0, -1):
            recv.append(lax.ppermute(sent[key], "gz", [(i, i ^ key) for i in range(gzs)]))
        return recv, after
    (total,) = surface(parts, held, 1)
    rows = lax.psum_scatter(total, "col", scatter_dimension=0, tiled=True)
    owned = lax.psum_scatter(rows, "gz", scatter_dimension=0, tiled=True)
    flux = lax.psum_scatter(rows.T, "gz", scatter_dimension=0, tiled=True)
    flux = jnp.pad(flux, ((0, 0), (0, sides - flux.shape[1])))
    return [jnp.concatenate([owned, flux], axis=0)], after


def turns(axis):
    return 1 if lax.axis_size(axis) == 2 else 2


def partner(index, turn):
    return jnp.where(index % 2 == turn, index + 1, index - 1)


def has_neighbour(axis, turn):
    other = partner(lax.axis_index(axis), turn)
    return (other >= 0) & (other < lax.axis_size(axis))


def swap(value, axis, turn):
    axes = ("row", "col", "gz")
    sizes = [lax.axis_size(name) for name in axes]
    along = axes.index(axis)
    spare = 0 if axis == "gz" else 2
    pairs = []
    for r in range(sizes[0]):
        for c in range(sizes[1]):
            for g in range(sizes[2]):
                here = [r, c, g]
                there = [r, c, g]
                there[along] += 1 if here[along] % 2 == turn else -1
                if not 0 <= there[along] < sizes[along]:
                    there[along] = here[along]
                    if here[spare] ^ 1 < sizes[spare]:
                        there[spare] ^= 1
                flat = [(at[0] * sizes[1] + at[1]) * sizes[2] + at[2] for at in (here, there)]
                pairs.append(tuple(flat))
    return lax.ppermute(value, axes, pairs)


class Shape:
    def __init__(self, sides, first, second, lanes):
        self.sides, self.x, self.y, self.lanes = sides, first, second, lanes
        self.cells = first * second
        self.chunk = max(1, 128 // self.cells)
        self.rows = self.chunk * self.cells
        self.block = min(sides, 32)
        self.half = self.block // 2
        self.half_rows = self.half * self.cells
        self.outer = [("col", i) for i in range(turns("col"))]
        self.inner = [("row", i) for i in reversed(range(turns("row")))]
        self.faces = self.outer + self.inner
        self.ends = turns("gz")

    def face_len(self, face):
        return self.y if face[0] == "row" else self.x

    def halo_rows(self):
        return sum(self.chunk * self.face_len(face) for face in self.faces)

    def edge(self, face):
        axis, turn = face
        last = (self.x if axis == "row" else self.y) - 1
        return jnp.where(lax.axis_index(axis) % 2 == turn, last, 0)


def halo_place(shape):
    dims = (shape.rows, shape.halo_rows())
    row, col = iota(dims, 0), iota(dims, 1)
    side, cell = row // shape.cells, row % shape.cells
    x, y = cell // shape.y, cell % shape.y
    hit, base = None, 0
    for face in shape.faces:
        length = shape.face_len(face)
        along, across = (y, x) if face[0] == "row" else (x, y)
        place = (across == shape.edge(face)) & (col - base == side * length + along)
        place = place & has_neighbour(*face)
        hit = place if hit is None else hit | place
        base += shape.chunk * length
    return hit.astype(BF)


def z_mask(shape, count):
    dims = (count * shape.cells, 2 * shape.cells)
    return iota(dims, 1) % shape.cells == iota(dims, 0) % shape.cells


def twice(matrix):
    zero = jnp.zeros_like(matrix)
    return jnp.concatenate(
        [jnp.concatenate([matrix, zero], axis=1), jnp.concatenate([zero, matrix], axis=1)], axis=0
    )


def beside(values):
    half = values.shape[0] // 2
    return jnp.concatenate([values[:half], values[half:]], axis=1)


def build_out(shape, ends_m, rsum):
    dims = (shape.lanes, 2 * shape.cells)
    edge = jnp.where(iota(dims, 1) < shape.cells, 0, shape.lanes - 1)
    ends_m[...] = twice((iota(dims, 0) == edge).astype(F32)).astype(BF)
    dims = rsum.shape
    rsum[...] = (iota(dims, 1) // shape.cells == iota(dims, 0)).astype(BF)


def cut_faces(shape, faces, at, block, tall, face_refs):
    for face, ref in zip(faces, face_refs):
        length, edge = shape.face_len(face), shape.edge(face)
        lines = []
        for side in range(block):
            start = side * shape.cells
            if face[0] == "row":
                lines.append(tall[pl.ds(aligned(start + edge * length, 8), length), :])
            else:
                lines.append(tall[pl.ds(start + edge, length, stride=shape.y), :])
        span = slice(at * length, (at + block) * length)
        ref[span, :] = jnp.concatenate(lines, axis=0).astype(BF)


def cut_ends(shape, at, values, z_ref, ends_m, rsum):
    mask = jnp.concatenate([z_mask(shape, shape.half)] * 2, axis=1)
    tips = jnp.where(mask, dot(beside(values), ends_m[...]), 0.0).astype(BF)
    tips = dot(rsum[...], tips)[: shape.half]
    tips = jnp.concatenate([tips[:, : 2 * shape.cells], tips[:, 2 * shape.cells :]], axis=0)
    z_ref[at : at + shape.block, :] = tips.astype(BF)


def build_tables(shape, coef_ref, weight, near_m, line_m, ends_m, rsum):
    cells, lanes = shape.cells, shape.lanes
    weight[...] = jnp.concatenate([OMEGA / (6.0 + coef_ref[...])] * shape.chunk, axis=0)
    dims = (shape.rows, shape.rows)
    row, col = iota(dims, 0), iota(dims, 1)
    x, y = row % cells // shape.y, row % shape.y
    x2, y2 = col % cells // shape.y, col % shape.y
    near = ((x == x2) & (jnp.abs(y - y2) == 1)) | ((y == y2) & (jnp.abs(x - x2) == 1))
    near_m[:, : shape.rows] = (near & (row // cells == col // cells)).astype(BF)
    near_m[:, shape.rows :] = halo_place(shape)
    dims = (lanes, lanes)
    line = (jnp.abs(iota(dims, 0) - iota(dims, 1)) == 1).astype(F32)
    line_m[: 2 * lanes, :] = twice(line).astype(BF)
    dims = (2 * cells, lanes)
    edge = jnp.where(iota(dims, 0) < cells, lanes - 1, 0)
    line_m[2 * lanes :, :] = twice((iota(dims, 1) == edge).astype(F32)).astype(BF)
    build_out(shape, ends_m, rsum)


def table_shapes(shape):
    lanes, cells = shape.lanes, shape.cells
    return [
        jax.ShapeDtypeStruct((shape.rows, lanes), F32),
        jax.ShapeDtypeStruct((shape.rows, shape.rows + shape.halo_rows()), BF),
        jax.ShapeDtypeStruct((2 * lanes + 4 * cells, 2 * lanes), BF),
        jax.ShapeDtypeStruct((2 * lanes, 4 * cells), BF),
        jax.ShapeDtypeStruct((max(8, shape.half), shape.half_rows), BF),
    ]


def faces_kernel(shape, slots, field_ref, block_ref, coef_ref, *refs):
    refs = list(refs)
    face_refs = [refs.pop(0) for _ in shape.inner]
    z_ref, held, *tables, field, tall, sems, field_sems = refs
    size = shape.block * shape.cells
    steps = shape.sides // shape.block
    copies = []
    for step in range(steps):
        span = pl.ds(step * size, size)
        copies.append(
            pltpu.make_async_copy(field_ref.at[span], field.at[span], field_sems.at[step])
        )
        copies[-1].start()
    columns = fetch_columns(block_ref, held, sems, slots)
    build_tables(shape, coef_ref, *tables)
    ends_m, rsum = tables[-2:]
    for step in range(steps):
        copies[step].wait()
        values = field[step * size : (step + 1) * size, :]
        tall[step] = values.astype(F32)
        cut_faces(shape, shape.inner, step * shape.block, shape.block, tall.at[step], face_refs)
        cut_ends(shape, step * shape.block, values, z_ref, ends_m, rsum)
    for copy in columns:
        copy.wait()


def face_shapes(shape, faces):
    return [
        jax.ShapeDtypeStruct((shape.sides * shape.face_len(face), shape.lanes), BF)
        for face in faces
    ]


def first_faces(shape, field, block, coef, slots):
    peers = lax.axis_size("row")
    steps = shape.sides // shape.block
    shapes = face_shapes(shape, shape.inner)
    shapes.append(jax.ShapeDtypeStruct((shape.sides, 2 * shape.cells), BF))
    shapes.append(jax.ShapeDtypeStruct((peers, block.shape[0], slots), BF))
    shapes += table_shapes(shape)
    hbm = pl.BlockSpec(memory_space=pltpu.HBM)
    return pl.pallas_call(
        functools.partial(faces_kernel, shape, slots),
        in_specs=[hbm, hbm, WHOLE],
        out_specs=[WHOLE] * len(shapes),
        out_shape=shapes,
        scratch_shapes=[
            pltpu.VMEM(field.shape, BF),
            pltpu.VMEM((steps, shape.block * shape.cells, shape.lanes), F32),
            pltpu.SemaphoreType.DMA((peers,)),
            pltpu.SemaphoreType.DMA((steps,)),
        ],
        compiler_params=params(FACES_MIB),
        cost_estimate=pl.CostEstimate(
            flops=field.size * 128, bytes_accessed=4 * field.size, transcendentals=0
        ),
    )(field, block, coef)


def expand(shape, lines, where):
    rows = []
    for side in range(shape.block):
        line = jnp.broadcast_to(lines[side : side + 1], where.shape)
        rows.append(jnp.where(where, line, 0.0))
    return beside(jnp.concatenate(rows, axis=0).astype(BF))


def halo_ends(shape, end_refs, sides):
    even = lax.axis_index("gz") % 2 == 0
    filled = (iota((shape.block, 2 * shape.cells), 1) < shape.cells) == even
    zs = 0.0
    for turn in range(shape.ends):
        wanted = (filled == (turn == 0)) & has_neighbour("gz", turn)
        zs = jnp.where(wanted, end_refs[-1 - turn][sides, :].astype(F32), zs)
    return expand(shape, zs, z_mask(shape, 1))


def flux_width(slots):
    return (2 * slots + 127) // 128 * 128


def build_cells(shape, cell_ref, cell_m):
    slots = cell_ref.shape[3]
    width = flux_width(slots)
    cell = cell_ref[0, 0]
    none = jnp.full((1, width - 2 * slots), -shape.lanes, jnp.int32)
    cell = jnp.concatenate([cell, cell, none], axis=1)
    place = (iota((shape.lanes, width), 0) == cell % shape.lanes).astype(F32)
    cell_m[...] = twice(place).astype(BF)
    return iota((shape.cells, width), 0) == cell // shape.lanes


def base_kernel(shape, ends, with_flux, *refs):
    refs = list(refs)
    take = lambda count: [refs.pop(0) for _ in range(count)]
    field_ref, load_ref, weight, near_m, line_m = take(5)
    end_refs = take(ends)
    if with_flux:
        phi, cell_ref = take(2)
    (base_ref,) = take(1)
    if with_flux:
        (source_ref,) = take(1)
    (lines,) = take(1)
    if with_flux:
        cell_m, placed = take(2)
        cell_mask = build_cells(shape, cell_ref, cell_m)

    cells, lanes = shape.cells, shape.lanes
    weights = weight[...]
    for step in range(shape.sides // shape.block):
        sides = slice(step * shape.block, (step + 1) * shape.block)
        at = step * shape.block * cells
        left = beside(field_ref[at : at + shape.block * cells, :])
        if ends:
            left = jnp.concatenate([left, halo_ends(shape, end_refs, sides)], axis=1)
        lines[step] = dot(left, line_m[: left.shape[1], :])
        if with_flux:
            placed[step] = dot_nt(expand(shape, phi[sides, :], cell_mask), cell_m[...])
        for index in range(shape.half // shape.chunk):
            offset = index * shape.rows
            here = slice(offset, offset + shape.rows)
            spans = [
                slice(at + start, at + start + shape.rows)
                for start in (offset, offset + shape.half_rows)
            ]
            stack = jnp.concatenate([field_ref[span, :] for span in spans], axis=1)
            near = dot(near_m[:, : shape.rows], stack) + lines[step, here, :]
            for part, span in enumerate(spans):
                cols = slice(part * lanes, (part + 1) * lanes)
                source = load_ref[span, :].astype(F32)
                if with_flux:
                    source = source + placed[step, here, cols]
                    source_ref[span, :] = source.astype(BF)
                centre = field_ref[span, :].astype(F32)
                base_ref[span, :] = (1.0 - OMEGA) * centre + weights * (source + near[:, cols])


def sweep_base(shape, field, load, tables, ends=(), phi=None, flux_cell=None):
    steps = shape.sides // shape.block
    half = (steps, shape.half_rows, 2 * shape.lanes)
    operands = [field, load, *tables[:3], *ends]
    shapes = [jax.ShapeDtypeStruct(field.shape, F32)]
    scratch = [pltpu.VMEM(half, F32)]
    if phi is not None:
        operands += [phi, flux_cell]
        shapes.append(jax.ShapeDtypeStruct(field.shape, BF))
        scratch.append(pltpu.VMEM((2 * shape.lanes, 2 * phi.shape[1]), BF))
        scratch.append(pltpu.VMEM(half, F32))
    return pl.pallas_call(
        functools.partial(base_kernel, shape, len(ends), phi is not None),
        in_specs=[WHOLE] * len(operands),
        out_specs=[WHOLE] * len(shapes),
        out_shape=shapes,
        scratch_shapes=scratch,
        compiler_params=params(),
        cost_estimate=pl.CostEstimate(
            flops=6 * field.size * 128, bytes_accessed=8 * field.size, transcendentals=0
        ),
    )(*operands)


def finish_kernel(shape, ends, recvs, last, *refs):
    with_flux = recvs > 0
    refs = list(refs)
    take = lambda count: [refs.pop(0) for _ in range(count)]
    base_ref, weight, near_m, line_m, ends_m, rsum = take(6)
    halo_refs = take(len(shape.faces))
    end_refs = take(ends)
    if with_flux:
        (cell_ref,) = take(1)
        recv_refs = take(recvs)
    (out_ref,) = take(1)
    if not last:
        face_refs = take(len(shape.faces))
        (z_ref,) = take(1)
    if with_flux:
        phi, flux_ref = take(2)
    if last:
        result_ref = out_ref
        out_ref, out_sems = take(2)
    else:
        (tall,) = take(1)
    if ends:
        (lines,) = take(1)
    if with_flux:
        cell_m, placed = take(2)

    cells, lanes = shape.cells, shape.lanes

    if with_flux:
        slots = cell_ref.shape[3]
        cell_mask = build_cells(shape, cell_ref, cell_m)
        owned = recv_refs[0][...]
        for ref in recv_refs[1:]:
            owned = owned + ref[...]
        flux_ref[...] = owned[slots:, : flux_ref.shape[1]]
        owned = owned[:slots]
        high = owned.astype(BF).astype(F32)
        none = jnp.zeros((phi.shape[1] - 2 * slots, phi.shape[0]), F32)
        phi[...] = jnp.concatenate([high, owned - high, none], axis=0).T

    weights = weight[...]

    def work(step):
        at = step * shape.block
        sides = slice(at, at + shape.block)
        if ends:
            lines[step] = dot(halo_ends(shape, end_refs, sides), line_m[2 * lanes :, :])
        if with_flux:
            placed[step] = dot_nt(expand(shape, phi[sides, :], cell_mask), cell_m[...])
        for index in range(shape.half // shape.chunk):
            offset = index * shape.rows
            starts = (offset, offset + shape.half_rows)
            stacks = []
            for start in starts:
                stack = []
                for face, ref in zip(shape.faces, halo_refs):
                    length = shape.face_len(face)
                    first = at * length + start // cells * length
                    stack.append(ref[first : first + shape.chunk * length, :])
                stacks.append(jnp.concatenate(stack, axis=0))
            near = dot(near_m[:, shape.rows :], jnp.concatenate(stacks, axis=1))
            if ends:
                near = near + lines[step, offset : offset + shape.rows, :]
            if with_flux:
                near = near + placed[step, offset : offset + shape.rows, :]
            for part, start in enumerate(starts):
                rows = slice(at * cells + start, at * cells + start + shape.rows)
                fresh = base_ref[rows, :] + weights * near[:, part * lanes : (part + 1) * lanes]
                out_ref[rows, :] = fresh.astype(BF)
                if not last:
                    tall[step, start : start + shape.rows, :] = fresh

    def emit(step):
        at, size = step * shape.block, shape.block * cells
        fresh = out_ref[at * cells : at * cells + size, :]
        cut_faces(shape, shape.faces, at, shape.block, tall.at[step], face_refs)
        cut_ends(shape, at, fresh, z_ref, ends_m, rsum)

    steps = shape.sides // shape.block
    copies = []
    for step in range(steps):
        work(step)
        if last:
            span = pl.ds(step * shape.block * cells, shape.block * cells)
            copies.append(
                pltpu.make_async_copy(out_ref.at[span], result_ref.at[span], out_sems.at[step])
            )
            copies[-1].start()
        elif step > 0:
            emit(step - 1)
    for copy in copies:
        copy.wait()
    if not last:
        emit(steps - 1)


def sweep_finish(shape, base, tables, halos, ends=(), flux_cell=None, recv=(), last=False):
    lanes, cells = shape.lanes, shape.cells
    steps = shape.sides // shape.block
    half = (steps, shape.half_rows, 2 * lanes)
    operands = [base, *tables, *halos, *ends]
    out_shapes = [jax.ShapeDtypeStruct(base.shape, BF)]
    if last:
        scratch = [pltpu.VMEM(base.shape, BF), pltpu.SemaphoreType.DMA((steps,))]
    else:
        out_shapes += face_shapes(shape, shape.faces)
        out_shapes.append(jax.ShapeDtypeStruct((shape.sides, 2 * cells), BF))
        scratch = [pltpu.VMEM((steps, shape.block * cells, lanes), F32)]
    if ends:
        scratch.append(pltpu.VMEM(half, F32))
    if recv:
        slots = flux_cell.shape[3]
        operands += [flux_cell, *recv]
        out_shapes += [
            jax.ShapeDtypeStruct((shape.sides, flux_width(slots)), F32),
            jax.ShapeDtypeStruct((recv[0].shape[0] - slots, slots * lax.axis_size("gz")), F32),
        ]
        scratch += [
            pltpu.VMEM((2 * lanes, 2 * flux_width(slots)), BF),
            pltpu.VMEM(half, F32),
        ]
    out_specs = [WHOLE] * len(out_shapes)
    if last:
        out_specs = [pl.BlockSpec(memory_space=pltpu.HBM)]
    return pl.pallas_call(
        functools.partial(finish_kernel, shape, len(ends), len(recv), last),
        in_specs=[WHOLE] * len(operands),
        out_specs=out_specs,
        out_shape=out_shapes,
        scratch_shapes=scratch,
        compiler_params=params(),
        cost_estimate=pl.CostEstimate(
            flops=4 * base.size * 128, bytes_accessed=8 * base.size, transcendentals=0
        ),
    )(*operands)


def swap_faces(faces, values):
    return [swap(value, *face) for face, value in zip(faces, values)]


def swap_ends(shape, ends):
    return [swap(ends, "gz", turn) for turn in reversed(range(shape.ends))]


def row_gather(trace, hidden, late):
    peers = lax.axis_size("row")
    held = {0: trace}
    bit = peers // 2
    while bit:
        pairs = [(i, i ^ bit) for i in range(peers)]
        fresh = {key ^ bit: lax.ppermute(held[key], "row", pairs) for key in sorted(held, reverse=True)}
        if bit == peers // 2:
            fresh, hidden = lax.optimization_barrier((fresh, hidden))
        held.update(fresh)
        bit //= 2
    parts, late = lax.optimization_barrier(([held[key] for key in range(peers)], late))
    return parts, hidden, late


def per_device(volume_field, volume_load, coefficient, surface_block, trace_cell, flux_cell):
    sides, first, second, lanes = volume_field.shape
    cells = first * second
    shape = Shape(sides, first, second, lanes)
    field = volume_field.reshape(sides * cells, lanes)
    load = volume_load.reshape(sides * cells, lanes)
    coef = coefficient.reshape(cells, lanes)

    slots = trace_cell.shape[3]
    trace, *outer = traces(
        shape, volume_field.reshape(sides, cells, lanes), trace_cell, min(32, sides)
    )
    firsts = first_faces(shape, field, surface_block, coef, slots)
    layers = len(shape.faces)
    count = len(shape.inner) + 1
    inner, held, tables = firsts[:count], firsts[count], firsts[count + 1 :]
    *inner, ends = inner
    along_col = swap_faces(shape.outer, outer)
    parts, inner, along_col = row_gather(trace, inner, along_col)
    along_row = swap_faces(shape.inner, inner)
    recv, ends = flux_sums(parts, held, along_row, ends)
    tips = swap_ends(shape, ends)

    (base,) = sweep_base(shape, field, load, tables, tips)
    current, *faces, ends, phi, surface_flux = sweep_finish(
        shape, base, tables, along_col + along_row, flux_cell=flux_cell, recv=recv
    )
    halos, tips = swap_faces(shape.faces, faces), swap_ends(shape, ends)
    base, source = sweep_base(shape, current, load, tables, phi=phi, flux_cell=flux_cell)
    current, *faces, ends = sweep_finish(shape, base, tables, halos, tips)
    halos, tips = swap_faces(shape.faces, faces), swap_ends(shape, ends)
    (base,) = sweep_base(shape, current, source, tables)
    (current,) = sweep_finish(shape, base, tables, halos, tips, last=True)
    return current.reshape(volume_field.shape), surface_flux


def solution(mesh):
    in_specs = (
        P(None, "row", "col", "gz"),
        P(None, "row", "col", "gz"),
        P("row", "col", "gz"),
        P("row", "col"),
        P("row", "col", "gz", None),
        P("row", "col", "gz", None),
    )
    out_specs = (P(None, "row", "col", "gz"), P("gz", ("row", "col")))
    return jax.shard_map(
        per_device, mesh=mesh, in_specs=in_specs, out_specs=out_specs, check_vma=False
    )
```

```python
import functools

import jax
import jax.numpy as jnp
from jax import lax
from jax.experimental import pallas as pl
from jax.experimental.pallas import tpu as pltpu
from jax.sharding import PartitionSpec as P

OMEGA = 0.8
BF = jnp.bfloat16
F32 = jnp.float32
WHOLE = pl.BlockSpec(memory_space=pltpu.VMEM)


def aligned(start, unit):
    return start if isinstance(start, int) else pl.multiple_of(start, unit)


def iota(shape, dim):
    return lax.broadcasted_iota(jnp.int32, shape, dim)


def dot(a, b):
    return jnp.dot(a, b, preferred_element_type=F32)


def dot_nt(a, b):
    return lax.dot_general(a, b, (((1,), (1,)), ((), ())), preferred_element_type=F32)


FACES_MIB = 50
TRACE_MIB = 52


def params(mebibytes=24):
    return pltpu.CompilerParams(vmem_limit_bytes=mebibytes * 1024 * 1024)


def trace_kernel(shape, stride, block, field_ref, cell_ref, out_ref, *refs):
    *face_refs, field, cell_v, tall, near, place, picked, sems = refs
    sides, rows, lanes = field.shape
    slots = cell_ref.shape[3]
    per_row = lanes // stride
    width = near.shape[0]
    parts = slots // width
    cell_copy = pltpu.make_async_copy(cell_ref, cell_v, sems.at[sides // block])
    cell_copy.start()
    copies = []
    for step in range(sides // block):
        span = pl.ds(step * block, block)
        copies.append(pltpu.make_async_copy(field_ref.at[span], field.at[span], sems.at[step]))
        copies[-1].start()

    cell_copy.wait()
    cell = cell_v[0, 0]
    run = cell // stride
    digit = jnp.zeros_like(cell)
    for part in range(parts):
        digit = jnp.where(run // width == part, (cell % stride) * stride**part, digit)
    hit = iota((width, slots), 0) == run % width
    near[...] = hit.astype(BF)
    digits = jnp.sum(jnp.where(hit, digit.astype(F32), 0.0), axis=1, keepdims=True)
    digits = jnp.broadcast_to(digits, (width, 128)).T[0:8].astype(jnp.int32)
    first = iota((8, width), 1) % per_row * stride
    for part in range(parts):
        place[:, part * width : (part + 1) * width] = first + digits // stride**part % stride

    pitch = rows + 1
    together = 128 // per_row
    group = iota((8, 128), 1) // per_row
    for step in range(sides // block):
        copies[step].wait()
        span = field[step * block : (step + 1) * block]
        for side in range(block):
            start = side * pitch
            tall[step, start : start + rows, :] = span[side].astype(F32)
        cut_faces(shape, shape.outer, step * block, block, tall.at[step], face_refs, pitch)

        for batch in range(block // 8):
            for tile in range(rows // together):
                cols = slice(tile * 128, (tile + 1) * 128)
                where = place[:, cols]
                found = None
                for row in range(together):
                    start = batch * 8 * pitch + tile * together + row
                    line = tall[step, pl.ds(start, 8, stride=pitch), :]
                    line = jnp.take_along_axis(line, where, axis=1)
                    found = line if found is None else jnp.where(group == row, line, found)
                at = step * block + batch * 8
                picked[at : at + 8, cols] = found

    total = jnp.zeros((sides, slots), F32)
    for part in range(parts):
        sorted_runs = picked[:, part * width : (part + 1) * width].astype(BF)
        total = jnp.where(run // width == part, dot(sorted_runs, near[...]), total)
    out_ref[...] = total.T.astype(BF)


def traces(shape, field, trace_cell, block):
    sides, rows, lanes = field.shape
    slots = trace_cell.shape[3]
    stride = rows * lanes // slots
    width = min(slots, 256)
    hbm = pl.BlockSpec(memory_space=pltpu.HBM)
    return pl.pallas_call(
        functools.partial(trace_kernel, shape, stride, block),
        in_specs=[hbm, hbm],
        out_specs=[WHOLE] * (1 + len(shape.outer)),
        out_shape=[jax.ShapeDtypeStruct((slots, sides), BF)] + face_shapes(shape, shape.outer),
        scratch_shapes=[
            pltpu.VMEM(field.shape, BF),
            pltpu.VMEM(trace_cell.shape, jnp.int32),
            pltpu.VMEM((sides // block, block * (rows + 1), lanes), F32),
            pltpu.VMEM((width, slots), BF),
            pltpu.VMEM((8, slots), jnp.int32),
            pltpu.VMEM((sides, slots), F32),
            pltpu.SemaphoreType.DMA((sides // block + 1,)),
        ],
        compiler_params=params(TRACE_MIB),
        cost_estimate=pl.CostEstimate(
            flops=4 * sides * rows * lanes * 128, bytes_accessed=field.size * 2, transcendentals=0
        ),
    )(field, trace_cell)


def fetch_columns(block_ref, held, sems, slots):
    me, group, gzs = lax.axis_index("row"), lax.axis_index("gz"), lax.axis_size("gz")
    copies = []
    for key in range(held.shape[0]):
        start = pl.multiple_of((jnp.bitwise_xor(me, key) * gzs + group) * slots, slots)
        copies.append(
            pltpu.make_async_copy(block_ref.at[:, pl.ds(start, slots)], held.at[key], sems.at[key])
        )
        copies[-1].start()
    return copies


def surface_kernel(halves, *refs):
    ins, total = refs[:-1], refs[-1]
    outs = ins[len(ins) - halves :]
    *parts, held = ins[: len(ins) - halves]
    value = None
    for key, part in enumerate(parts):
        term = dot(held[key], part[...])
        value = term if value is None else value + term
    if halves == 1:
        outs[0][...] = value
        return
    total[...] = value
    count = outs[0].shape[0]
    mine = lax.axis_index("col")
    for key, out in enumerate(outs):
        out[...] = total[pl.ds(pl.multiple_of((mine ^ key) * count, 8), count), :]


def surface(parts, held, halves):
    sides = parts[0].shape[1]
    lines = held.shape[1]
    return pl.pallas_call(
        functools.partial(surface_kernel, halves),
        in_specs=[WHOLE] * (len(parts) + 1),
        out_specs=[WHOLE] * halves,
        out_shape=[jax.ShapeDtypeStruct((lines // halves, sides), F32)] * halves,
        scratch_shapes=[pltpu.VMEM((lines, sides), F32)],
        compiler_params=params(),
        cost_estimate=pl.CostEstimate(
            flops=2 * sides * held.size, bytes_accessed=2 * held.size, transcendentals=0
        ),
    )(*parts, held)


def share_kernel(peers, mine_ref, other_ref, *refs):
    *outs, total, turned = refs
    total[...] = mine_ref[...] + other_ref[...]
    turned[...] = total[...].T
    lines, sides = total.shape
    group = lax.axis_index("gz")
    for key, out in enumerate(outs):
        peer = group ^ key
        rows, some = lines // peers, sides // peers
        out[:rows, :] = total[pl.ds(pl.multiple_of(peer * rows, 8), rows), :]
        out[rows:, :] = turned[pl.ds(pl.multiple_of(peer * some, 8), some), :]


def shares(mine, other):
    peers = lax.axis_size("gz")
    lines, sides = mine.shape
    out = jax.ShapeDtypeStruct(((lines + sides) // peers, sides), F32)
    return pl.pallas_call(
        functools.partial(share_kernel, peers),
        in_specs=[WHOLE] * 2,
        out_specs=[WHOLE] * peers,
        out_shape=[out] * peers,
        scratch_shapes=[pltpu.VMEM((lines, sides), F32), pltpu.VMEM((sides, lines), F32)],
        compiler_params=params(),
        cost_estimate=pl.CostEstimate(
            flops=lines * sides, bytes_accessed=16 * lines * sides, transcendentals=0
        ),
    )(mine, other)


def flux_sums(parts, held, late, after):
    cols, gzs = lax.axis_size("col"), lax.axis_size("gz")
    sides = parts[0].shape[1]
    lines = held.shape[1]
    if cols == 2 and gzs & (gzs - 1) == 0 and lines // cols == sides and sides // gzs % 8 == 0:
        mine, other = surface(parts, held, 2)
        mine, other, after = lax.optimization_barrier((mine, other, after))
        other = lax.ppermute(other, "col", [(0, 1), (1, 0)])
        other, late = lax.optimization_barrier((other, late))
        sent = shares(mine, other)
        recv = [sent[0]]
        for key in range(gzs - 1, 0, -1):
            recv.append(lax.ppermute(sent[key], "gz", [(i, i ^ key) for i in range(gzs)]))
        return recv, after
    (total,) = surface(parts, held, 1)
    rows = lax.psum_scatter(total, "col", scatter_dimension=0, tiled=True)
    owned = lax.psum_scatter(rows, "gz", scatter_dimension=0, tiled=True)
    flux = lax.psum_scatter(rows.T, "gz", scatter_dimension=0, tiled=True)
    flux = jnp.pad(flux, ((0, 0), (0, sides - flux.shape[1])))
    return [jnp.concatenate([owned, flux], axis=0)], after


def turns(axis):
    return 1 if lax.axis_size(axis) == 2 else 2


def partner(index, turn):
    return jnp.where(index % 2 == turn, index + 1, index - 1)


def has_neighbour(axis, turn):
    other = partner(lax.axis_index(axis), turn)
    return (other >= 0) & (other < lax.axis_size(axis))


def swap(value, axis, turn):
    axes = ("row", "col", "gz")
    sizes = [lax.axis_size(name) for name in axes]
    along = axes.index(axis)
    spare = 0 if axis == "gz" else 2
    pairs = []
    for r in range(sizes[0]):
        for c in range(sizes[1]):
            for g in range(sizes[2]):
                here = [r, c, g]
                there = [r, c, g]
                there[along] += 1 if here[along] % 2 == turn else -1
                if not 0 <= there[along] < sizes[along]:
                    there[along] = here[along]
                    if here[spare] ^ 1 < sizes[spare]:
                        there[spare] ^= 1
                flat = [(at[0] * sizes[1] + at[1]) * sizes[2] + at[2] for at in (here, there)]
                pairs.append(tuple(flat))
    return lax.ppermute(value, axes, pairs)


class Shape:
    def __init__(self, sides, first, second, lanes):
        self.sides, self.x, self.y, self.lanes = sides, first, second, lanes
        self.cells = first * second
        self.chunk = max(1, 128 // self.cells)
        self.rows = self.chunk * self.cells
        self.block = min(sides, 32)
        self.half = self.block // 2
        self.half_rows = self.half * self.cells
        self.outer = [("col", i) for i in range(turns("col"))]
        self.inner = [("row", i) for i in reversed(range(turns("row")))]
        self.faces = self.outer + self.inner
        self.ends = turns("gz")

    def face_len(self, face):
        return self.y if face[0] == "row" else self.x

    def halo_rows(self):
        return sum(self.chunk * self.face_len(face) for face in self.faces)

    def edge(self, face):
        axis, turn = face
        last = (self.x if axis == "row" else self.y) - 1
        return jnp.where(lax.axis_index(axis) % 2 == turn, last, 0)


def halo_place(shape):
    dims = (shape.rows, shape.halo_rows())
    row, col = iota(dims, 0), iota(dims, 1)
    side, cell = row // shape.cells, row % shape.cells
    x, y = cell // shape.y, cell % shape.y
    hit, base = None, 0
    for face in shape.faces:
        length = shape.face_len(face)
        along, across = (y, x) if face[0] == "row" else (x, y)
        place = (across == shape.edge(face)) & (col - base == side * length + along)
        place = place & has_neighbour(*face)
        hit = place if hit is None else hit | place
        base += shape.chunk * length
    return hit.astype(BF)


def z_mask(shape, count):
    dims = (count * shape.cells, 2 * shape.cells)
    return iota(dims, 1) % shape.cells == iota(dims, 0) % shape.cells


def twice(matrix):
    zero = jnp.zeros_like(matrix)
    return jnp.concatenate(
        [jnp.concatenate([matrix, zero], axis=1), jnp.concatenate([zero, matrix], axis=1)], axis=0
    )


def beside(values):
    half = values.shape[0] // 2
    return jnp.concatenate([values[:half], values[half:]], axis=1)


def build_out(shape, ends_m, rsum):
    dims = (shape.lanes, 2 * shape.cells)
    edge = jnp.where(iota(dims, 1) < shape.cells, 0, shape.lanes - 1)
    ends_m[...] = twice((iota(dims, 0) == edge).astype(F32)).astype(BF)
    dims = rsum.shape
    rsum[...] = (iota(dims, 1) // shape.cells == iota(dims, 0)).astype(BF)


def cut_faces(shape, faces, at, block, tall, face_refs, pitch=None):
    for face, ref in zip(faces, face_refs):
        length, edge = shape.face_len(face), shape.edge(face)
        lines = []
        for side in range(block):
            start = side * (pitch or shape.cells)
            if face[0] == "row":
                lines.append(tall[pl.ds(aligned(start + edge * length, 8), length), :])
            else:
                lines.append(tall[pl.ds(start + edge, length, stride=shape.y), :])
        span = slice(at * length, (at + block) * length)
        ref[span, :] = jnp.concatenate(lines, axis=0).astype(BF)


def cut_ends(shape, at, values, z_ref, ends_m, rsum):
    mask = jnp.concatenate([z_mask(shape, shape.half)] * 2, axis=1)
    tips = jnp.where(mask, dot(beside(values), ends_m[...]), 0.0).astype(BF)
    tips = dot(rsum[...], tips)[: shape.half]
    tips = jnp.concatenate([tips[:, : 2 * shape.cells], tips[:, 2 * shape.cells :]], axis=0)
    z_ref[at : at + shape.block, :] = tips.astype(BF)


def build_tables(shape, coef_ref, weight, near_m, line_m, ends_m, rsum):
    cells, lanes = shape.cells, shape.lanes
    weight[...] = jnp.concatenate([OMEGA / (6.0 + coef_ref[...])] * shape.chunk, axis=0)
    dims = (shape.rows, shape.rows)
    row, col = iota(dims, 0), iota(dims, 1)
    x, y = row % cells // shape.y, row % shape.y
    x2, y2 = col % cells // shape.y, col % shape.y
    near = ((x == x2) & (jnp.abs(y - y2) == 1)) | ((y == y2) & (jnp.abs(x - x2) == 1))
    near_m[:, : shape.rows] = (near & (row // cells == col // cells)).astype(BF)
    near_m[:, shape.rows :] = halo_place(shape)
    dims = (lanes, lanes)
    line = (jnp.abs(iota(dims, 0) - iota(dims, 1)) == 1).astype(F32)
    line_m[: 2 * lanes, :] = twice(line).astype(BF)
    dims = (2 * cells, lanes)
    edge = jnp.where(iota(dims, 0) < cells, lanes - 1, 0)
    line_m[2 * lanes :, :] = twice((iota(dims, 1) == edge).astype(F32)).astype(BF)
    build_out(shape, ends_m, rsum)


def table_shapes(shape):
    lanes, cells = shape.lanes, shape.cells
    return [
        jax.ShapeDtypeStruct((shape.rows, lanes), F32),
        jax.ShapeDtypeStruct((shape.rows, shape.rows + shape.halo_rows()), BF),
        jax.ShapeDtypeStruct((2 * lanes + 4 * cells, 2 * lanes), BF),
        jax.ShapeDtypeStruct((2 * lanes, 4 * cells), BF),
        jax.ShapeDtypeStruct((max(8, shape.half), shape.half_rows), BF),
    ]


def faces_kernel(shape, slots, field_ref, block_ref, coef_ref, *refs):
    refs = list(refs)
    face_refs = [refs.pop(0) for _ in shape.inner]
    z_ref, held, *tables, field, tall, sems, field_sems = refs
    size = shape.block * shape.cells
    steps = shape.sides // shape.block
    copies = []
    for step in range(steps):
        span = pl.ds(step * size, size)
        copies.append(
            pltpu.make_async_copy(field_ref.at[span], field.at[span], field_sems.at[step])
        )
        copies[-1].start()
    columns = fetch_columns(block_ref, held, sems, slots)
    build_tables(shape, coef_ref, *tables)
    ends_m, rsum = tables[-2:]
    for step in range(steps):
        copies[step].wait()
        values = field[step * size : (step + 1) * size, :]
        tall[step] = values.astype(F32)
        cut_faces(shape, shape.inner, step * shape.block, shape.block, tall.at[step], face_refs)
        cut_ends(shape, step * shape.block, values, z_ref, ends_m, rsum)
    for copy in columns:
        copy.wait()


def face_shapes(shape, faces):
    return [
        jax.ShapeDtypeStruct((shape.sides * shape.face_len(face), shape.lanes), BF)
        for face in faces
    ]


def first_faces(shape, field, block, coef, slots):
    peers = lax.axis_size("row")
    steps = shape.sides // shape.block
    shapes = face_shapes(shape, shape.inner)
    shapes.append(jax.ShapeDtypeStruct((shape.sides, 2 * shape.cells), BF))
    shapes.append(jax.ShapeDtypeStruct((peers, block.shape[0], slots), BF))
    shapes += table_shapes(shape)
    hbm = pl.BlockSpec(memory_space=pltpu.HBM)
    return pl.pallas_call(
        functools.partial(faces_kernel, shape, slots),
        in_specs=[hbm, hbm, WHOLE],
        out_specs=[WHOLE] * len(shapes),
        out_shape=shapes,
        scratch_shapes=[
            pltpu.VMEM(field.shape, BF),
            pltpu.VMEM((steps, shape.block * shape.cells, shape.lanes), F32),
            pltpu.SemaphoreType.DMA((peers,)),
            pltpu.SemaphoreType.DMA((steps,)),
        ],
        compiler_params=params(FACES_MIB),
        cost_estimate=pl.CostEstimate(
            flops=field.size * 128, bytes_accessed=4 * field.size, transcendentals=0
        ),
    )(field, block, coef)


def expand(shape, lines, where):
    rows = []
    for side in range(shape.block):
        line = jnp.broadcast_to(lines[side : side + 1], where.shape)
        rows.append(jnp.where(where, line, 0.0))
    return beside(jnp.concatenate(rows, axis=0).astype(BF))


def halo_ends(shape, end_refs, sides):
    even = lax.axis_index("gz") % 2 == 0
    filled = (iota((shape.block, 2 * shape.cells), 1) < shape.cells) == even
    zs = 0.0
    for turn in range(shape.ends):
        wanted = (filled == (turn == 0)) & has_neighbour("gz", turn)
        zs = jnp.where(wanted, end_refs[-1 - turn][sides, :].astype(F32), zs)
    return expand(shape, zs, z_mask(shape, 1))


def flux_width(slots):
    return (2 * slots + 127) // 128 * 128


def build_cells(shape, cell_ref, cell_m):
    slots = cell_ref.shape[3]
    width = flux_width(slots)
    cell = cell_ref[0, 0]
    none = jnp.full((1, width - 2 * slots), -shape.lanes, jnp.int32)
    cell = jnp.concatenate([cell, cell, none], axis=1)
    place = (iota((shape.lanes, width), 0) == cell % shape.lanes).astype(F32)
    cell_m[...] = twice(place).astype(BF)
    return iota((shape.cells, width), 0) == cell // shape.lanes


def base_kernel(shape, ends, with_flux, *refs):
    refs = list(refs)
    take = lambda count: [refs.pop(0) for _ in range(count)]
    field_ref, load_ref, weight, near_m, line_m = take(5)
    end_refs = take(ends)
    if with_flux:
        phi, cell_ref = take(2)
    (base_ref,) = take(1)
    if with_flux:
        (source_ref,) = take(1)
    (lines,) = take(1)
    if with_flux:
        cell_m, placed = take(2)
        cell_mask = build_cells(shape, cell_ref, cell_m)

    cells, lanes = shape.cells, shape.lanes
    weights = weight[...]
    for step in range(shape.sides // shape.block):
        sides = slice(step * shape.block, (step + 1) * shape.block)
        at = step * shape.block * cells
        left = beside(field_ref[at : at + shape.block * cells, :])
        if ends:
            left = jnp.concatenate([left, halo_ends(shape, end_refs, sides)], axis=1)
        lines[step] = dot(left, line_m[: left.shape[1], :])
        if with_flux:
            placed[step] = dot_nt(expand(shape, phi[sides, :], cell_mask), cell_m[...])
        for index in range(shape.half // shape.chunk):
            offset = index * shape.rows
            here = slice(offset, offset + shape.rows)
            spans = [
                slice(at + start, at + start + shape.rows)
                for start in (offset, offset + shape.half_rows)
            ]
            stack = jnp.concatenate([field_ref[span, :] for span in spans], axis=1)
            near = dot(near_m[:, : shape.rows], stack) + lines[step, here, :]
            for part, span in enumerate(spans):
                cols = slice(part * lanes, (part + 1) * lanes)
                source = load_ref[span, :].astype(F32)
                if with_flux:
                    source = source + placed[step, here, cols]
                    source_ref[span, :] = source.astype(BF)
                centre = field_ref[span, :].astype(F32)
                base_ref[span, :] = (1.0 - OMEGA) * centre + weights * (source + near[:, cols])


def sweep_base(shape, field, load, tables, ends=(), phi=None, flux_cell=None):
    steps = shape.sides // shape.block
    half = (steps, shape.half_rows, 2 * shape.lanes)
    operands = [field, load, *tables[:3], *ends]
    shapes = [jax.ShapeDtypeStruct(field.shape, F32)]
    scratch = [pltpu.VMEM(half, F32)]
    if phi is not None:
        operands += [phi, flux_cell]
        shapes.append(jax.ShapeDtypeStruct(field.shape, BF))
        scratch.append(pltpu.VMEM((2 * shape.lanes, 2 * phi.shape[1]), BF))
        scratch.append(pltpu.VMEM(half, F32))
    return pl.pallas_call(
        functools.partial(base_kernel, shape, len(ends), phi is not None),
        in_specs=[WHOLE] * len(operands),
        out_specs=[WHOLE] * len(shapes),
        out_shape=shapes,
        scratch_shapes=scratch,
        compiler_params=params(),
        cost_estimate=pl.CostEstimate(
            flops=6 * field.size * 128, bytes_accessed=8 * field.size, transcendentals=0
        ),
    )(*operands)


def finish_kernel(shape, ends, recvs, last, *refs):
    with_flux = recvs > 0
    refs = list(refs)
    take = lambda count: [refs.pop(0) for _ in range(count)]
    base_ref, weight, near_m, line_m, ends_m, rsum = take(6)
    halo_refs = take(len(shape.faces))
    end_refs = take(ends)
    if with_flux:
        (cell_ref,) = take(1)
        recv_refs = take(recvs)
    (out_ref,) = take(1)
    if not last:
        face_refs = take(len(shape.faces))
        (z_ref,) = take(1)
    if with_flux:
        phi, flux_ref = take(2)
    if last:
        result_ref = out_ref
        out_ref, out_sems = take(2)
    else:
        (tall,) = take(1)
    if ends:
        (lines,) = take(1)
    if with_flux:
        cell_m, placed = take(2)

    cells, lanes = shape.cells, shape.lanes

    if with_flux:
        slots = cell_ref.shape[3]
        cell_mask = build_cells(shape, cell_ref, cell_m)
        owned = recv_refs[0][...]
        for ref in recv_refs[1:]:
            owned = owned + ref[...]
        flux_ref[...] = owned[slots:, : flux_ref.shape[1]]
        owned = owned[:slots]
        high = owned.astype(BF).astype(F32)
        none = jnp.zeros((phi.shape[1] - 2 * slots, phi.shape[0]), F32)
        phi[...] = jnp.concatenate([high, owned - high, none], axis=0).T

    weights = weight[...]

    def work(step):
        at = step * shape.block
        sides = slice(at, at + shape.block)
        if ends:
            lines[step] = dot(halo_ends(shape, end_refs, sides), line_m[2 * lanes :, :])
        if with_flux:
            placed[step] = dot_nt(expand(shape, phi[sides, :], cell_mask), cell_m[...])
        for index in range(shape.half // shape.chunk):
            offset = index * shape.rows
            starts = (offset, offset + shape.half_rows)
            stacks = []
            for start in starts:
                stack = []
                for face, ref in zip(shape.faces, halo_refs):
                    length = shape.face_len(face)
                    first = at * length + start // cells * length
                    stack.append(ref[first : first + shape.chunk * length, :])
                stacks.append(jnp.concatenate(stack, axis=0))
            near = dot(near_m[:, shape.rows :], jnp.concatenate(stacks, axis=1))
            if ends:
                near = near + lines[step, offset : offset + shape.rows, :]
            if with_flux:
                near = near + placed[step, offset : offset + shape.rows, :]
            for part, start in enumerate(starts):
                rows = slice(at * cells + start, at * cells + start + shape.rows)
                fresh = base_ref[rows, :] + weights * near[:, part * lanes : (part + 1) * lanes]
                out_ref[rows, :] = fresh.astype(BF)
                if not last:
                    tall[step, start : start + shape.rows, :] = fresh

    def emit(step):
        at, size = step * shape.block, shape.block * cells
        fresh = out_ref[at * cells : at * cells + size, :]
        cut_faces(shape, shape.faces, at, shape.block, tall.at[step], face_refs)
        cut_ends(shape, at, fresh, z_ref, ends_m, rsum)

    steps = shape.sides // shape.block
    copies = []
    for step in range(steps):
        work(step)
        if last:
            span = pl.ds(step * shape.block * cells, shape.block * cells)
            copies.append(
                pltpu.make_async_copy(out_ref.at[span], result_ref.at[span], out_sems.at[step])
            )
            copies[-1].start()
        elif step > 0:
            emit(step - 1)
    for copy in copies:
        copy.wait()
    if not last:
        emit(steps - 1)


def sweep_finish(shape, base, tables, halos, ends=(), flux_cell=None, recv=(), last=False):
    lanes, cells = shape.lanes, shape.cells
    steps = shape.sides // shape.block
    half = (steps, shape.half_rows, 2 * lanes)
    operands = [base, *tables, *halos, *ends]
    out_shapes = [jax.ShapeDtypeStruct(base.shape, BF)]
    if last:
        scratch = [pltpu.VMEM(base.shape, BF), pltpu.SemaphoreType.DMA((steps,))]
    else:
        out_shapes += face_shapes(shape, shape.faces)
        out_shapes.append(jax.ShapeDtypeStruct((shape.sides, 2 * cells), BF))
        scratch = [pltpu.VMEM((steps, shape.block * cells, lanes), F32)]
    if ends:
        scratch.append(pltpu.VMEM(half, F32))
    if recv:
        slots = flux_cell.shape[3]
        operands += [flux_cell, *recv]
        out_shapes += [
            jax.ShapeDtypeStruct((shape.sides, flux_width(slots)), F32),
            jax.ShapeDtypeStruct((recv[0].shape[0] - slots, slots * lax.axis_size("gz")), F32),
        ]
        scratch += [
            pltpu.VMEM((2 * lanes, 2 * flux_width(slots)), BF),
            pltpu.VMEM(half, F32),
        ]
    out_specs = [WHOLE] * len(out_shapes)
    if last:
        out_specs = [pl.BlockSpec(memory_space=pltpu.HBM)]
    return pl.pallas_call(
        functools.partial(finish_kernel, shape, len(ends), len(recv), last),
        in_specs=[WHOLE] * len(operands),
        out_specs=out_specs,
        out_shape=out_shapes,
        scratch_shapes=scratch,
        compiler_params=params(),
        cost_estimate=pl.CostEstimate(
            flops=4 * base.size * 128, bytes_accessed=8 * base.size, transcendentals=0
        ),
    )(*operands)


def swap_faces(faces, values):
    return [swap(value, *face) for face, value in zip(faces, values)]


def swap_ends(shape, ends):
    return [swap(ends, "gz", turn) for turn in reversed(range(shape.ends))]


def row_gather(trace, hidden, late):
    peers = lax.axis_size("row")
    held = {0: trace}
    bit = peers // 2
    while bit:
        pairs = [(i, i ^ bit) for i in range(peers)]
        fresh = {key ^ bit: lax.ppermute(held[key], "row", pairs) for key in sorted(held, reverse=True)}
        if bit == peers // 2:
            fresh, hidden = lax.optimization_barrier((fresh, hidden))
        held.update(fresh)
        bit //= 2
    parts, late = lax.optimization_barrier(([held[key] for key in range(peers)], late))
    return parts, hidden, late


def per_device(volume_field, volume_load, coefficient, surface_block, trace_cell, flux_cell):
    sides, first, second, lanes = volume_field.shape
    cells = first * second
    shape = Shape(sides, first, second, lanes)
    field = volume_field.reshape(sides * cells, lanes)
    load = volume_load.reshape(sides * cells, lanes)
    coef = coefficient.reshape(cells, lanes)

    slots = trace_cell.shape[3]
    trace, *outer = traces(
        shape, volume_field.reshape(sides, cells, lanes), trace_cell, min(32, sides)
    )
    firsts = first_faces(shape, field, surface_block, coef, slots)
    layers = len(shape.faces)
    count = len(shape.inner) + 1
    inner, held, tables = firsts[:count], firsts[count], firsts[count + 1 :]
    *inner, ends = inner
    along_col = swap_faces(shape.outer, outer)
    parts, inner, along_col = row_gather(trace, inner, along_col)
    along_row = swap_faces(shape.inner, inner)
    recv, ends = flux_sums(parts, held, along_row, ends)
    tips = swap_ends(shape, ends)

    (base,) = sweep_base(shape, field, load, tables, tips)
    current, *faces, ends, phi, surface_flux = sweep_finish(
        shape, base, tables, along_col + along_row, flux_cell=flux_cell, recv=recv
    )
    halos, tips = swap_faces(shape.faces, faces), swap_ends(shape, ends)
    base, source = sweep_base(shape, current, load, tables, phi=phi, flux_cell=flux_cell)
    current, *faces, ends = sweep_finish(shape, base, tables, halos, tips)
    halos, tips = swap_faces(shape.faces, faces), swap_ends(shape, ends)
    (base,) = sweep_base(shape, current, source, tables)
    (current,) = sweep_finish(shape, base, tables, halos, tips, last=True)
    return current.reshape(volume_field.shape), surface_flux


def solution(mesh):
    in_specs = (
        P(None, "row", "col", "gz"),
        P(None, "row", "col", "gz"),
        P("row", "col", "gz"),
        P("row", "col"),
        P("row", "col", "gz", None),
        P("row", "col", "gz", None),
    )
    out_specs = (P(None, "row", "col", "gz"), P("gz", ("row", "col")))
    return jax.shard_map(
        per_device, mesh=mesh, in_specs=in_specs, out_specs=out_specs, check_vma=False
    )
```

```python
import functools

import jax
import jax.numpy as jnp
from jax import lax
from jax.experimental import pallas as pl
from jax.experimental.pallas import tpu as pltpu
from jax.sharding import PartitionSpec as P

OMEGA = 0.8
BF = jnp.bfloat16
F32 = jnp.float32
WHOLE = pl.BlockSpec(memory_space=pltpu.VMEM)


def aligned(start, unit):
    return start if isinstance(start, int) else pl.multiple_of(start, unit)


def iota(shape, dim):
    return lax.broadcasted_iota(jnp.int32, shape, dim)


def dot(a, b):
    return jnp.dot(a, b, preferred_element_type=F32)


def dot_nt(a, b):
    return lax.dot_general(a, b, (((1,), (1,)), ((), ())), preferred_element_type=F32)


FACES_MIB = 50
TRACE_MIB = 52


def params(mebibytes=24):
    return pltpu.CompilerParams(vmem_limit_bytes=mebibytes * 1024 * 1024)


def trace_kernel(shape, stride, block, field_ref, cell_ref, out_ref, *refs):
    *face_refs, field, cell_v, tall, near, place, picked, sems = refs
    sides, rows, lanes = field.shape
    slots = cell_ref.shape[3]
    per_row = lanes // stride
    width = near.shape[0]
    parts = slots // width
    cell_copy = pltpu.make_async_copy(cell_ref, cell_v, sems.at[sides // block])
    cell_copy.start()
    copies = []
    for step in range(sides // block):
        span = pl.ds(step * block, block)
        copies.append(pltpu.make_async_copy(field_ref.at[span], field.at[span], sems.at[step]))
        copies[-1].start()

    cell_copy.wait()
    cell = cell_v[0, 0]
    run = cell // stride
    digit = jnp.zeros_like(cell)
    for part in range(parts):
        digit = jnp.where(run // width == part, (cell % stride) * stride**part, digit)
    hit = iota((width, slots), 0) == run % width
    near[...] = hit.astype(BF)
    digits = jnp.sum(jnp.where(hit, digit.astype(F32), 0.0), axis=1, keepdims=True)
    digits = jnp.broadcast_to(digits, (width, 128)).T[0:8].astype(jnp.int32)
    first = iota((8, width), 1) % per_row * stride
    for part in range(parts):
        place[:, part * width : (part + 1) * width] = first + digits // stride**part % stride

    pitch = rows + 1
    together = 128 // per_row
    group = iota((8, 128), 1) // per_row
    for step in range(sides // block):
        copies[step].wait()
        span = field[step * block : (step + 1) * block]
        for side in range(block):
            start = side * pitch
            tall[step, start : start + rows, :] = span[side].astype(F32)
        cut_faces(shape, shape.outer, step * block, block, tall.at[step], face_refs, pitch)

        for batch in range(block // 8):
            for tile in range(rows // together):
                cols = slice(tile * 128, (tile + 1) * 128)
                where = place[:, cols]
                found = None
                for row in range(together):
                    start = batch * 8 * pitch + tile * together + row
                    line = tall[step, pl.ds(start, 8, stride=pitch), :]
                    line = jnp.take_along_axis(line, where, axis=1)
                    found = line if found is None else jnp.where(group == row, line, found)
                at = step * block + batch * 8
                picked[at : at + 8, cols] = found

    total = jnp.zeros((sides, slots), F32)
    for part in range(parts):
        sorted_runs = picked[:, part * width : (part + 1) * width].astype(BF)
        total = jnp.where(run // width == part, dot(sorted_runs, near[...]), total)
    out_ref[...] = total.T.astype(BF)


def traces(shape, field, trace_cell, block):
    sides, rows, lanes = field.shape
    slots = trace_cell.shape[3]
    stride = rows * lanes // slots
    width = min(slots, 256)
    hbm = pl.BlockSpec(memory_space=pltpu.HBM)
    return pl.pallas_call(
        functools.partial(trace_kernel, shape, stride, block),
        in_specs=[hbm, hbm],
        out_specs=[WHOLE] * (1 + len(shape.outer)),
        out_shape=[jax.ShapeDtypeStruct((slots, sides), BF)] + face_shapes(shape, shape.outer),
        scratch_shapes=[
            pltpu.VMEM(field.shape, BF),
            pltpu.VMEM(trace_cell.shape, jnp.int32),
            pltpu.VMEM((sides // block, block * (rows + 1), lanes), F32),
            pltpu.VMEM((width, slots), BF),
            pltpu.VMEM((8, slots), jnp.int32),
            pltpu.VMEM((sides, slots), F32),
            pltpu.SemaphoreType.DMA((sides // block + 1,)),
        ],
        compiler_params=params(TRACE_MIB),
        cost_estimate=pl.CostEstimate(
            flops=4 * sides * rows * lanes * 128, bytes_accessed=field.size * 2, transcendentals=0
        ),
    )(field, trace_cell)


def fetch_columns(block_ref, held, sems, slots):
    me, group, gzs = lax.axis_index("row"), lax.axis_index("gz"), lax.axis_size("gz")
    copies = []
    for key in range(held.shape[0]):
        start = pl.multiple_of((jnp.bitwise_xor(me, key) * gzs + group) * slots, slots)
        copies.append(
            pltpu.make_async_copy(block_ref.at[:, pl.ds(start, slots)], held.at[key], sems.at[key])
        )
        copies[-1].start()
    return copies


def surface_kernel(halves, *refs):
    ins, total = refs[:-1], refs[-1]
    outs = ins[len(ins) - halves :]
    *parts, held = ins[: len(ins) - halves]
    value = None
    for key, part in enumerate(parts):
        term = dot(held[key], part[...])
        value = term if value is None else value + term
    if halves == 1:
        outs[0][...] = value
        return
    total[...] = value
    count = outs[0].shape[0]
    mine = lax.axis_index("col")
    for key, out in enumerate(outs):
        out[...] = total[pl.ds(pl.multiple_of((mine ^ key) * count, 8), count), :]


def surface(parts, held, halves):
    sides = parts[0].shape[1]
    lines = held.shape[1]
    return pl.pallas_call(
        functools.partial(surface_kernel, halves),
        in_specs=[WHOLE] * (len(parts) + 1),
        out_specs=[WHOLE] * halves,
        out_shape=[jax.ShapeDtypeStruct((lines // halves, sides), F32)] * halves,
        scratch_shapes=[pltpu.VMEM((lines, sides), F32)],
        compiler_params=params(),
        cost_estimate=pl.CostEstimate(
            flops=2 * sides * held.size, bytes_accessed=2 * held.size, transcendentals=0
        ),
    )(*parts, held)


def share_kernel(peers, mine_ref, other_ref, *refs):
    *outs, total, turned = refs
    total[...] = mine_ref[...] + other_ref[...]
    turned[...] = total[...].T
    lines, sides = total.shape
    group = lax.axis_index("gz")
    for key, out in enumerate(outs):
        peer = group ^ key
        rows, some = lines // peers, sides // peers
        out[:rows, :] = total[pl.ds(pl.multiple_of(peer * rows, 8), rows), :]
        out[rows:, :] = turned[pl.ds(pl.multiple_of(peer * some, 8), some), :]


def shares(mine, other):
    peers = lax.axis_size("gz")
    lines, sides = mine.shape
    out = jax.ShapeDtypeStruct(((lines + sides) // peers, sides), F32)
    return pl.pallas_call(
        functools.partial(share_kernel, peers),
        in_specs=[WHOLE] * 2,
        out_specs=[WHOLE] * peers,
        out_shape=[out] * peers,
        scratch_shapes=[pltpu.VMEM((lines, sides), F32), pltpu.VMEM((sides, lines), F32)],
        compiler_params=params(),
        cost_estimate=pl.CostEstimate(
            flops=lines * sides, bytes_accessed=16 * lines * sides, transcendentals=0
        ),
    )(mine, other)


def flux_sums(parts, held, late, after):
    cols, gzs = lax.axis_size("col"), lax.axis_size("gz")
    sides = parts[0].shape[1]
    lines = held.shape[1]
    if cols == 2 and gzs & (gzs - 1) == 0 and lines // cols == sides and sides // gzs % 8 == 0:
        mine, other = surface(parts, held, 2)
        mine, other, after = lax.optimization_barrier((mine, other, after))
        other = lax.ppermute(other, "col", [(0, 1), (1, 0)])
        other, late = lax.optimization_barrier((other, late))
        sent = shares(mine, other)
        recv = [sent[0]]
        for key in range(gzs - 1, 0, -1):
            recv.append(lax.ppermute(sent[key], "gz", [(i, i ^ key) for i in range(gzs)]))
        return recv, after
    (total,) = surface(parts, held, 1)
    rows = lax.psum_scatter(total, "col", scatter_dimension=0, tiled=True)
    owned = lax.psum_scatter(rows, "gz", scatter_dimension=0, tiled=True)
    flux = lax.psum_scatter(rows.T, "gz", scatter_dimension=0, tiled=True)
    flux = jnp.pad(flux, ((0, 0), (0, sides - flux.shape[1])))
    return [jnp.concatenate([owned, flux], axis=0)], after


def turns(axis):
    return 1 if lax.axis_size(axis) == 2 else 2


def partner(index, turn):
    return jnp.where(index % 2 == turn, index + 1, index - 1)


def has_neighbour(axis, turn):
    other = partner(lax.axis_index(axis), turn)
    return (other >= 0) & (other < lax.axis_size(axis))


def swap(value, axis, turn):
    axes = ("row", "col", "gz")
    sizes = [lax.axis_size(name) for name in axes]
    along = axes.index(axis)
    pairs = []
    for r in range(sizes[0]):
        for c in range(sizes[1]):
            for g in range(sizes[2]):
                here = [r, c, g]
                there = [r, c, g]
                there[along] += 1 if here[along] % 2 == turn else -1
                if not 0 <= there[along] < sizes[along]:
                    there[along] = here[along]
                    if axis != "row" and r ^ 1 < sizes[0]:
                        there[0] ^= 1
                flat = [(at[0] * sizes[1] + at[1]) * sizes[2] + at[2] for at in (here, there)]
                pairs.append(tuple(flat))
    return lax.ppermute(value, axes, pairs)


class Shape:
    def __init__(self, sides, first, second, lanes):
        self.sides, self.x, self.y, self.lanes = sides, first, second, lanes
        self.cells = first * second
        self.chunk = max(1, 128 // self.cells)
        self.rows = self.chunk * self.cells
        self.block = min(sides, 32)
        self.half = self.block // 2
        self.half_rows = self.half * self.cells
        self.outer = [("col", i) for i in range(turns("col"))]
        self.inner = [("row", i) for i in reversed(range(turns("row")))]
        self.faces = self.outer + self.inner
        self.ends = turns("gz")

    def face_len(self, face):
        return self.y if face[0] == "row" else self.x

    def halo_rows(self):
        return sum(self.chunk * self.face_len(face) for face in self.faces)

    def edge(self, face):
        axis, turn = face
        last = (self.x if axis == "row" else self.y) - 1
        return jnp.where(lax.axis_index(axis) % 2 == turn, last, 0)


def halo_place(shape):
    dims = (shape.rows, shape.halo_rows())
    row, col = iota(dims, 0), iota(dims, 1)
    side, cell = row // shape.cells, row % shape.cells
    x, y = cell // shape.y, cell % shape.y
    hit, base = None, 0
    for face in shape.faces:
        length = shape.face_len(face)
        along, across = (y, x) if face[0] == "row" else (x, y)
        place = (across == shape.edge(face)) & (col - base == side * length + along)
        place = place & has_neighbour(*face)
        hit = place if hit is None else hit | place
        base += shape.chunk * length
    return hit.astype(BF)


def z_mask(shape, count):
    dims = (count * shape.cells, 2 * shape.cells)
    return iota(dims, 1) % shape.cells == iota(dims, 0) % shape.cells


def twice(matrix):
    zero = jnp.zeros_like(matrix)
    return jnp.concatenate(
        [jnp.concatenate([matrix, zero], axis=1), jnp.concatenate([zero, matrix], axis=1)], axis=0
    )


def beside(values):
    half = values.shape[0] // 2
    return jnp.concatenate([values[:half], values[half:]], axis=1)


def build_out(shape, ends_m, rsum):
    dims = (shape.lanes, 2 * shape.cells)
    edge = jnp.where(iota(dims, 1) < shape.cells, 0, shape.lanes - 1)
    ends_m[...] = twice((iota(dims, 0) == edge).astype(F32)).astype(BF)
    dims = rsum.shape
    rsum[...] = (iota(dims, 1) // shape.cells == iota(dims, 0)).astype(BF)


def cut_faces(shape, faces, at, block, tall, face_refs, pitch=None):
    for face, ref in zip(faces, face_refs):
        length, edge = shape.face_len(face), shape.edge(face)
        lines = []
        for side in range(block):
            start = side * (pitch or shape.cells)
            if face[0] == "row":
                lines.append(tall[pl.ds(aligned(start + edge * length, 8), length), :])
            else:
                lines.append(tall[pl.ds(start + edge, length, stride=shape.y), :])
        span = slice(at * length, (at + block) * length)
        ref[span, :] = jnp.concatenate(lines, axis=0).astype(BF)


def cut_ends(shape, at, values, z_ref, ends_m, rsum):
    mask = jnp.concatenate([z_mask(shape, shape.half)] * 2, axis=1)
    tips = jnp.where(mask, dot(beside(values), ends_m[...]), 0.0).astype(BF)
    tips = dot(rsum[...], tips)[: shape.half]
    tips = jnp.concatenate([tips[:, : 2 * shape.cells], tips[:, 2 * shape.cells :]], axis=0)
    z_ref[at : at + shape.block, :] = tips.astype(BF)


def build_tables(shape, coef_ref, weight, near_m, line_m, ends_m, rsum):
    cells, lanes = shape.cells, shape.lanes
    weight[...] = jnp.concatenate([OMEGA / (6.0 + coef_ref[...])] * shape.chunk, axis=0)
    dims = (shape.rows, shape.rows)
    row, col = iota(dims, 0), iota(dims, 1)
    x, y = row % cells // shape.y, row % shape.y
    x2, y2 = col % cells // shape.y, col % shape.y
    near = ((x == x2) & (jnp.abs(y - y2) == 1)) | ((y == y2) & (jnp.abs(x - x2) == 1))
    near_m[:, : shape.rows] = (near & (row // cells == col // cells)).astype(BF)
    near_m[:, shape.rows :] = halo_place(shape)
    dims = (lanes, lanes)
    line = (jnp.abs(iota(dims, 0) - iota(dims, 1)) == 1).astype(F32)
    line_m[: 2 * lanes, :] = twice(line).astype(BF)
    dims = (2 * cells, lanes)
    edge = jnp.where(iota(dims, 0) < cells, lanes - 1, 0)
    line_m[2 * lanes :, :] = twice((iota(dims, 1) == edge).astype(F32)).astype(BF)
    build_out(shape, ends_m, rsum)


def table_shapes(shape):
    lanes, cells = shape.lanes, shape.cells
    return [
        jax.ShapeDtypeStruct((shape.rows, lanes), F32),
        jax.ShapeDtypeStruct((shape.rows, shape.rows + shape.halo_rows()), BF),
        jax.ShapeDtypeStruct((2 * lanes + 4 * cells, 2 * lanes), BF),
        jax.ShapeDtypeStruct((2 * lanes, 4 * cells), BF),
        jax.ShapeDtypeStruct((max(8, shape.half), shape.half_rows), BF),
    ]


def faces_kernel(shape, slots, field_ref, block_ref, coef_ref, *refs):
    refs = list(refs)
    face_refs = [refs.pop(0) for _ in shape.inner]
    z_ref, held, *tables, field, tall, sems, field_sems = refs
    size = shape.block * shape.cells
    steps = shape.sides // shape.block
    copies = []
    for step in range(steps):
        span = pl.ds(step * size, size)
        copies.append(
            pltpu.make_async_copy(field_ref.at[span], field.at[span], field_sems.at[step])
        )
        copies[-1].start()
    columns = fetch_columns(block_ref, held, sems, slots)
    build_tables(shape, coef_ref, *tables)
    ends_m, rsum = tables[-2:]
    for step in range(steps):
        copies[step].wait()
        values = field[step * size : (step + 1) * size, :]
        tall[step] = values.astype(F32)
        cut_faces(shape, shape.inner, step * shape.block, shape.block, tall.at[step], face_refs)
        cut_ends(shape, step * shape.block, values, z_ref, ends_m, rsum)
    for copy in columns:
        copy.wait()


def face_shapes(shape, faces):
    return [
        jax.ShapeDtypeStruct((shape.sides * shape.face_len(face), shape.lanes), BF)
        for face in faces
    ]


def first_faces(shape, field, block, coef, slots):
    peers = lax.axis_size("row")
    steps = shape.sides // shape.block
    shapes = face_shapes(shape, shape.inner)
    shapes.append(jax.ShapeDtypeStruct((shape.sides, 2 * shape.cells), BF))
    shapes.append(jax.ShapeDtypeStruct((peers, block.shape[0], slots), BF))
    shapes += table_shapes(shape)
    hbm = pl.BlockSpec(memory_space=pltpu.HBM)
    return pl.pallas_call(
        functools.partial(faces_kernel, shape, slots),
        in_specs=[hbm, hbm, WHOLE],
        out_specs=[WHOLE] * len(shapes),
        out_shape=shapes,
        scratch_shapes=[
            pltpu.VMEM(field.shape, BF),
            pltpu.VMEM((steps, shape.block * shape.cells, shape.lanes), F32),
            pltpu.SemaphoreType.DMA((peers,)),
            pltpu.SemaphoreType.DMA((steps,)),
        ],
        compiler_params=params(FACES_MIB),
        cost_estimate=pl.CostEstimate(
            flops=field.size * 128, bytes_accessed=4 * field.size, transcendentals=0
        ),
    )(field, block, coef)


def expand(shape, lines, where):
    rows = []
    for side in range(shape.block):
        line = jnp.broadcast_to(lines[side : side + 1], where.shape)
        rows.append(jnp.where(where, line, 0.0))
    return beside(jnp.concatenate(rows, axis=0).astype(BF))


def halo_ends(shape, end_refs, sides):
    even = lax.axis_index("gz") % 2 == 0
    filled = (iota((shape.block, 2 * shape.cells), 1) < shape.cells) == even
    zs = 0.0
    for turn in range(shape.ends):
        wanted = (filled == (turn == 0)) & has_neighbour("gz", turn)
        zs = jnp.where(wanted, end_refs[-1 - turn][sides, :].astype(F32), zs)
    return expand(shape, zs, z_mask(shape, 1))


def flux_width(slots):
    return (2 * slots + 127) // 128 * 128


def build_cells(shape, cell_ref, cell_m):
    slots = cell_ref.shape[3]
    width = flux_width(slots)
    cell = cell_ref[0, 0]
    none = jnp.full((1, width - 2 * slots), -shape.lanes, jnp.int32)
    cell = jnp.concatenate([cell, cell, none], axis=1)
    place = (iota((shape.lanes, width), 0) == cell % shape.lanes).astype(F32)
    cell_m[...] = twice(place).astype(BF)
    return iota((shape.cells, width), 0) == cell // shape.lanes


def base_kernel(shape, ends, with_flux, *refs):
    refs = list(refs)
    take = lambda count: [refs.pop(0) for _ in range(count)]
    field_ref, load_ref, weight, near_m, line_m = take(5)
    end_refs = take(ends)
    if with_flux:
        phi, cell_ref = take(2)
    (base_ref,) = take(1)
    if with_flux:
        (source_ref,) = take(1)
    (lines,) = take(1)
    if with_flux:
        cell_m, placed = take(2)
        cell_mask = build_cells(shape, cell_ref, cell_m)

    cells, lanes = shape.cells, shape.lanes
    weights = weight[...]
    for step in range(shape.sides // shape.block):
        sides = slice(step * shape.block, (step + 1) * shape.block)
        at = step * shape.block * cells
        left = beside(field_ref[at : at + shape.block * cells, :])
        if ends:
            left = jnp.concatenate([left, halo_ends(shape, end_refs, sides)], axis=1)
        lines[step] = dot(left, line_m[: left.shape[1], :])
        if with_flux:
            placed[step] = dot_nt(expand(shape, phi[sides, :], cell_mask), cell_m[...])
        for index in range(shape.half // shape.chunk):
            offset = index * shape.rows
            here = slice(offset, offset + shape.rows)
            spans = [
                slice(at + start, at + start + shape.rows)
                for start in (offset, offset + shape.half_rows)
            ]
            stack = jnp.concatenate([field_ref[span, :] for span in spans], axis=1)
            near = dot(near_m[:, : shape.rows], stack) + lines[step, here, :]
            for part, span in enumerate(spans):
                cols = slice(part * lanes, (part + 1) * lanes)
                source = load_ref[span, :].astype(F32)
                if with_flux:
                    source = source + placed[step, here, cols]
                    source_ref[span, :] = source.astype(BF)
                centre = field_ref[span, :].astype(F32)
                base_ref[span, :] = (1.0 - OMEGA) * centre + weights * (source + near[:, cols])


def sweep_base(shape, field, load, tables, ends=(), phi=None, flux_cell=None):
    steps = shape.sides // shape.block
    half = (steps, shape.half_rows, 2 * shape.lanes)
    operands = [field, load, *tables[:3], *ends]
    shapes = [jax.ShapeDtypeStruct(field.shape, F32)]
    scratch = [pltpu.VMEM(half, F32)]
    if phi is not None:
        operands += [phi, flux_cell]
        shapes.append(jax.ShapeDtypeStruct(field.shape, BF))
        scratch.append(pltpu.VMEM((2 * shape.lanes, 2 * phi.shape[1]), BF))
        scratch.append(pltpu.VMEM(half, F32))
    return pl.pallas_call(
        functools.partial(base_kernel, shape, len(ends), phi is not None),
        in_specs=[WHOLE] * len(operands),
        out_specs=[WHOLE] * len(shapes),
        out_shape=shapes,
        scratch_shapes=scratch,
        compiler_params=params(),
        cost_estimate=pl.CostEstimate(
            flops=6 * field.size * 128, bytes_accessed=8 * field.size, transcendentals=0
        ),
    )(*operands)


def finish_kernel(shape, ends, recvs, last, *refs):
    with_flux = recvs > 0
    refs = list(refs)
    take = lambda count: [refs.pop(0) for _ in range(count)]
    base_ref, weight, near_m, line_m, ends_m, rsum = take(6)
    halo_refs = take(len(shape.faces))
    end_refs = take(ends)
    if with_flux:
        (cell_ref,) = take(1)
        recv_refs = take(recvs)
    (out_ref,) = take(1)
    if not last:
        face_refs = take(len(shape.faces))
        (z_ref,) = take(1)
    if with_flux:
        phi, flux_ref = take(2)
    if last:
        result_ref = out_ref
        out_ref, out_sems = take(2)
    else:
        (tall,) = take(1)
    if ends:
        (lines,) = take(1)
    if with_flux:
        cell_m, placed = take(2)

    cells, lanes = shape.cells, shape.lanes

    if with_flux:
        slots = cell_ref.shape[3]
        cell_mask = build_cells(shape, cell_ref, cell_m)
        owned = recv_refs[0][...]
        for ref in recv_refs[1:]:
            owned = owned + ref[...]
        flux_ref[...] = owned[slots:, : flux_ref.shape[1]]
        owned = owned[:slots]
        high = owned.astype(BF).astype(F32)
        none = jnp.zeros((phi.shape[1] - 2 * slots, phi.shape[0]), F32)
        phi[...] = jnp.concatenate([high, owned - high, none], axis=0).T

    weights = weight[...]

    def work(step):
        at = step * shape.block
        sides = slice(at, at + shape.block)
        if ends:
            lines[step] = dot(halo_ends(shape, end_refs, sides), line_m[2 * lanes :, :])
        if with_flux:
            placed[step] = dot_nt(expand(shape, phi[sides, :], cell_mask), cell_m[...])
        for index in range(shape.half // shape.chunk):
            offset = index * shape.rows
            starts = (offset, offset + shape.half_rows)
            stacks = []
            for start in starts:
                stack = []
                for face, ref in zip(shape.faces, halo_refs):
                    length = shape.face_len(face)
                    first = at * length + start // cells * length
                    stack.append(ref[first : first + shape.chunk * length, :])
                stacks.append(jnp.concatenate(stack, axis=0))
            near = dot(near_m[:, shape.rows :], jnp.concatenate(stacks, axis=1))
            if ends:
                near = near + lines[step, offset : offset + shape.rows, :]
            if with_flux:
                near = near + placed[step, offset : offset + shape.rows, :]
            for part, start in enumerate(starts):
                rows = slice(at * cells + start, at * cells + start + shape.rows)
                fresh = base_ref[rows, :] + weights * near[:, part * lanes : (part + 1) * lanes]
                out_ref[rows, :] = fresh.astype(BF)
                if not last:
                    tall[step, start : start + shape.rows, :] = fresh

    def emit(step):
        at, size = step * shape.block, shape.block * cells
        fresh = out_ref[at * cells : at * cells + size, :]
        cut_faces(shape, shape.faces, at, shape.block, tall.at[step], face_refs)
        cut_ends(shape, at, fresh, z_ref, ends_m, rsum)

    steps = shape.sides // shape.block
    copies = []
    for step in range(steps):
        work(step)
        if last:
            span = pl.ds(step * shape.block * cells, shape.block * cells)
            copies.append(
                pltpu.make_async_copy(out_ref.at[span], result_ref.at[span], out_sems.at[step])
            )
            copies[-1].start()
        elif step > 0:
            emit(step - 1)
    for copy in copies:
        copy.wait()
    if not last:
        emit(steps - 1)


def sweep_finish(shape, base, tables, halos, ends=(), flux_cell=None, recv=(), last=False):
    lanes, cells = shape.lanes, shape.cells
    steps = shape.sides // shape.block
    half = (steps, shape.half_rows, 2 * lanes)
    operands = [base, *tables, *halos, *ends]
    out_shapes = [jax.ShapeDtypeStruct(base.shape, BF)]
    if last:
        scratch = [pltpu.VMEM(base.shape, BF), pltpu.SemaphoreType.DMA((steps,))]
    else:
        out_shapes += face_shapes(shape, shape.faces)
        out_shapes.append(jax.ShapeDtypeStruct((shape.sides, 2 * cells), BF))
        scratch = [pltpu.VMEM((steps, shape.block * cells, lanes), F32)]
    if ends:
        scratch.append(pltpu.VMEM(half, F32))
    if recv:
        slots = flux_cell.shape[3]
        operands += [flux_cell, *recv]
        out_shapes += [
            jax.ShapeDtypeStruct((shape.sides, flux_width(slots)), F32),
            jax.ShapeDtypeStruct((recv[0].shape[0] - slots, slots * lax.axis_size("gz")), F32),
        ]
        scratch += [
            pltpu.VMEM((2 * lanes, 2 * flux_width(slots)), BF),
            pltpu.VMEM(half, F32),
        ]
    out_specs = [WHOLE] * len(out_shapes)
    if last:
        out_specs = [pl.BlockSpec(memory_space=pltpu.HBM)]
    return pl.pallas_call(
        functools.partial(finish_kernel, shape, len(ends), len(recv), last),
        in_specs=[WHOLE] * len(operands),
        out_specs=out_specs,
        out_shape=out_shapes,
        scratch_shapes=scratch,
        compiler_params=params(),
        cost_estimate=pl.CostEstimate(
            flops=4 * base.size * 128, bytes_accessed=8 * base.size, transcendentals=0
        ),
    )(*operands)


def swap_faces(faces, values):
    return [swap(value, *face) for face, value in zip(faces, values)]


def swap_ends(shape, ends):
    return [swap(ends, "gz", turn) for turn in reversed(range(shape.ends))]


def row_gather(trace, hidden, late):
    peers = lax.axis_size("row")
    held = {0: trace}
    bit = peers // 2
    while bit:
        pairs = [(i, i ^ bit) for i in range(peers)]
        fresh = {key ^ bit: lax.ppermute(held[key], "row", pairs) for key in sorted(held, reverse=True)}
        if bit == peers // 2:
            fresh, hidden = lax.optimization_barrier((fresh, hidden))
        held.update(fresh)
        bit //= 2
    parts, late = lax.optimization_barrier(([held[key] for key in range(peers)], late))
    return parts, hidden, late


def per_device(volume_field, volume_load, coefficient, surface_block, trace_cell, flux_cell):
    sides, first, second, lanes = volume_field.shape
    cells = first * second
    shape = Shape(sides, first, second, lanes)
    field = volume_field.reshape(sides * cells, lanes)
    load = volume_load.reshape(sides * cells, lanes)
    coef = coefficient.reshape(cells, lanes)

    slots = trace_cell.shape[3]
    trace, *outer = traces(
        shape, volume_field.reshape(sides, cells, lanes), trace_cell, min(32, sides)
    )
    firsts = first_faces(shape, field, surface_block, coef, slots)
    layers = len(shape.faces)
    count = len(shape.inner) + 1
    inner, held, tables = firsts[:count], firsts[count], firsts[count + 1 :]
    *inner, ends = inner
    along_col = swap_faces(shape.outer, outer)
    parts, inner, along_col = row_gather(trace, inner, along_col)
    along_row = swap_faces(shape.inner, inner)
    recv, ends = flux_sums(parts, held, along_row, ends)
    tips = swap_ends(shape, ends)

    (base,) = sweep_base(shape, field, load, tables, tips)
    current, *faces, ends, phi, surface_flux = sweep_finish(
        shape, base, tables, along_col + along_row, flux_cell=flux_cell, recv=recv
    )
    halos, tips = swap_faces(shape.faces, faces), swap_ends(shape, ends)
    base, source = sweep_base(shape, current, load, tables, phi=phi, flux_cell=flux_cell)
    current, *faces, ends = sweep_finish(shape, base, tables, halos, tips)
    halos, tips = swap_faces(shape.faces, faces), swap_ends(shape, ends)
    (base,) = sweep_base(shape, current, source, tables)
    (current,) = sweep_finish(shape, base, tables, halos, tips, last=True)
    return current.reshape(volume_field.shape), surface_flux


def solution(mesh):
    in_specs = (
        P(None, "row", "col", "gz"),
        P(None, "row", "col", "gz"),
        P("row", "col", "gz"),
        P("row", "col"),
        P("row", "col", "gz", None),
        P("row", "col", "gz", None),
    )
    out_specs = (P(None, "row", "col", "gz"), P("gz", ("row", "col")))
    return jax.shard_map(
        per_device, mesh=mesh, in_specs=in_specs, out_specs=out_specs, check_vma=False
    )
```

```python
import functools

import jax
import jax.numpy as jnp
from jax import lax
from jax.experimental import pallas as pl
from jax.experimental.pallas import tpu as pltpu
from jax.sharding import PartitionSpec as P

OMEGA = 0.8
BF = jnp.bfloat16
F32 = jnp.float32
WHOLE = pl.BlockSpec(memory_space=pltpu.VMEM)


def aligned(start, unit):
    return start if isinstance(start, int) else pl.multiple_of(start, unit)


def iota(shape, dim):
    return lax.broadcasted_iota(jnp.int32, shape, dim)


def dot(a, b):
    return jnp.dot(a, b, preferred_element_type=F32)


def dot_nt(a, b):
    return lax.dot_general(a, b, (((1,), (1,)), ((), ())), preferred_element_type=F32)


FACES_MIB = 50
TRACE_MIB = 52


def params(mebibytes=24):
    return pltpu.CompilerParams(vmem_limit_bytes=mebibytes * 1024 * 1024)


def trace_kernel(shape, stride, block, field_ref, cell_ref, out_ref, *refs):
    *face_refs, field, cell_v, tall, near, place, picked, sems = refs
    sides, rows, lanes = field.shape
    slots = cell_ref.shape[3]
    per_row = lanes // stride
    width = near.shape[0]
    parts = slots // width
    cell_copy = pltpu.make_async_copy(cell_ref, cell_v, sems.at[sides // block])
    cell_copy.start()
    copies = []
    for step in range(sides // block):
        span = pl.ds(step * block, block)
        copies.append(pltpu.make_async_copy(field_ref.at[span], field.at[span], sems.at[step]))
        copies[-1].start()

    cell_copy.wait()
    cell = cell_v[0, 0]
    run = cell // stride
    digit = jnp.zeros_like(cell)
    for part in range(parts):
        digit = jnp.where(run // width == part, (cell % stride) * stride**part, digit)
    hit = iota((width, slots), 0) == run % width
    near[...] = hit.astype(BF)
    digits = jnp.sum(jnp.where(hit, digit.astype(F32), 0.0), axis=1, keepdims=True)
    digits = jnp.broadcast_to(digits, (width, 128)).T[0:8].astype(jnp.int32)
    first = iota((8, width), 1) % per_row * stride
    for part in range(parts):
        place[:, part * width : (part + 1) * width] = first + digits // stride**part % stride

    pitch = rows + 1
    together = 128 // per_row
    group = iota((8, 128), 1) // per_row
    for step in range(sides // block):
        copies[step].wait()
        span = field[step * block : (step + 1) * block]
        for side in range(block):
            start = side * pitch
            tall[step, start : start + rows, :] = span[side].astype(F32)
        cut_faces(shape, shape.outer, step * block, block, tall.at[step], face_refs, pitch)

        for batch in range(block // 8):
            for tile in range(rows // together):
                cols = slice(tile * 128, (tile + 1) * 128)
                where = place[:, cols]
                found = None
                for row in range(together):
                    start = batch * 8 * pitch + tile * together + row
                    line = tall[step, pl.ds(start, 8, stride=pitch), :]
                    line = jnp.take_along_axis(line, where, axis=1)
                    found = line if found is None else jnp.where(group == row, line, found)
                at = step * block + batch * 8
                picked[at : at + 8, cols] = found

    total = jnp.zeros((sides, slots), F32)
    for part in range(parts):
        sorted_runs = picked[:, part * width : (part + 1) * width].astype(BF)
        total = jnp.where(run // width == part, dot(sorted_runs, near[...]), total)
    out_ref[...] = total.T.astype(BF)


def traces(shape, field, trace_cell, block):
    sides, rows, lanes = field.shape
    slots = trace_cell.shape[3]
    stride = rows * lanes // slots
    width = min(slots, 256)
    hbm = pl.BlockSpec(memory_space=pltpu.HBM)
    return pl.pallas_call(
        functools.partial(trace_kernel, shape, stride, block),
        in_specs=[hbm, hbm],
        out_specs=[WHOLE] * (1 + len(shape.outer)),
        out_shape=[jax.ShapeDtypeStruct((slots, sides), BF)] + face_shapes(shape, shape.outer),
        scratch_shapes=[
            pltpu.VMEM(field.shape, BF),
            pltpu.VMEM(trace_cell.shape, jnp.int32),
            pltpu.VMEM((sides // block, block * (rows + 1), lanes), F32),
            pltpu.VMEM((width, slots), BF),
            pltpu.VMEM((8, slots), jnp.int32),
            pltpu.VMEM((sides, slots), F32),
            pltpu.SemaphoreType.DMA((sides // block + 1,)),
        ],
        compiler_params=params(TRACE_MIB),
        cost_estimate=pl.CostEstimate(
            flops=4 * sides * rows * lanes * 128, bytes_accessed=field.size * 2, transcendentals=0
        ),
    )(field, trace_cell)


def fetch_columns(block_ref, held, sems, slots):
    me, group, gzs = lax.axis_index("row"), lax.axis_index("gz"), lax.axis_size("gz")
    copies = []
    for key in range(held.shape[0]):
        start = pl.multiple_of((jnp.bitwise_xor(me, key) * gzs + group) * slots, slots)
        copies.append(
            pltpu.make_async_copy(block_ref.at[:, pl.ds(start, slots)], held.at[key], sems.at[key])
        )
        copies[-1].start()
    return copies


def surface_kernel(halves, *refs):
    ins, total = refs[:-1], refs[-1]
    outs = ins[len(ins) - halves :]
    *parts, held = ins[: len(ins) - halves]
    value = None
    for key, part in enumerate(parts):
        term = dot(held[key], part[...])
        value = term if value is None else value + term
    if halves == 1:
        outs[0][...] = value
        return
    total[...] = value
    count = outs[0].shape[0]
    mine = lax.axis_index("col")
    for key, out in enumerate(outs):
        out[...] = total[pl.ds(pl.multiple_of((mine ^ key) * count, 8), count), :]


def surface(parts, held, halves):
    sides = parts[0].shape[1]
    lines = held.shape[1]
    return pl.pallas_call(
        functools.partial(surface_kernel, halves),
        in_specs=[WHOLE] * (len(parts) + 1),
        out_specs=[WHOLE] * halves,
        out_shape=[jax.ShapeDtypeStruct((lines // halves, sides), F32)] * halves,
        scratch_shapes=[pltpu.VMEM((lines, sides), F32)],
        compiler_params=params(),
        cost_estimate=pl.CostEstimate(
            flops=2 * sides * held.size, bytes_accessed=2 * held.size, transcendentals=0
        ),
    )(*parts, held)


def share_kernel(peers, mine_ref, other_ref, *refs):
    *outs, total, turned = refs
    total[...] = mine_ref[...] + other_ref[...]
    turned[...] = total[...].T
    lines, sides = total.shape
    group = lax.axis_index("gz")
    for key, out in enumerate(outs):
        peer = group ^ key
        rows, some = lines // peers, sides // peers
        out[:rows, :] = total[pl.ds(pl.multiple_of(peer * rows, 8), rows), :]
        out[rows:, :] = turned[pl.ds(pl.multiple_of(peer * some, 8), some), :]


def shares(mine, other):
    peers = lax.axis_size("gz")
    lines, sides = mine.shape
    out = jax.ShapeDtypeStruct(((lines + sides) // peers, sides), F32)
    return pl.pallas_call(
        functools.partial(share_kernel, peers),
        in_specs=[WHOLE] * 2,
        out_specs=[WHOLE] * peers,
        out_shape=[out] * peers,
        scratch_shapes=[pltpu.VMEM((lines, sides), F32), pltpu.VMEM((sides, lines), F32)],
        compiler_params=params(),
        cost_estimate=pl.CostEstimate(
            flops=lines * sides, bytes_accessed=16 * lines * sides, transcendentals=0
        ),
    )(mine, other)


def flux_sums(parts, held, late, after):
    cols, gzs = lax.axis_size("col"), lax.axis_size("gz")
    sides = parts[0].shape[1]
    lines = held.shape[1]
    if cols == 2 and gzs & (gzs - 1) == 0 and lines // cols == sides and sides // gzs % 8 == 0:
        mine, other = surface(parts, held, 2)
        mine, other, after = lax.optimization_barrier((mine, other, after))
        other = lax.ppermute(other, "col", [(0, 1), (1, 0)])
        other, late = lax.optimization_barrier((other, late))
        sent = shares(mine, other)
        recv = [sent[0]]
        for key in range(gzs - 1, 0, -1):
            recv.append(lax.ppermute(sent[key], "gz", [(i, i ^ key) for i in range(gzs)]))
        return recv, after
    (total,) = surface(parts, held, 1)
    rows = lax.psum_scatter(total, "col", scatter_dimension=0, tiled=True)
    owned = lax.psum_scatter(rows, "gz", scatter_dimension=0, tiled=True)
    flux = lax.psum_scatter(rows.T, "gz", scatter_dimension=0, tiled=True)
    flux = jnp.pad(flux, ((0, 0), (0, sides - flux.shape[1])))
    return [jnp.concatenate([owned, flux], axis=0)], after


def turns(axis):
    return 1 if lax.axis_size(axis) == 2 else 2


def partner(index, turn):
    return jnp.where(index % 2 == turn, index + 1, index - 1)


def has_neighbour(axis, turn):
    other = partner(lax.axis_index(axis), turn)
    return (other >= 0) & (other < lax.axis_size(axis))


def swap(value, axis, turn):
    axes = ("row", "col", "gz")
    sizes = [lax.axis_size(name) for name in axes]
    along = axes.index(axis)
    pairs = []
    for r in range(sizes[0]):
        for c in range(sizes[1]):
            for g in range(sizes[2]):
                here = [r, c, g]
                there = [r, c, g]
                there[along] += 1 if here[along] % 2 == turn else -1
                if not 0 <= there[along] < sizes[along]:
                    there[along] = here[along]
                    if axis != "row" and r ^ 1 < sizes[0]:
                        there[0] ^= 1
                flat = [(at[0] * sizes[1] + at[1]) * sizes[2] + at[2] for at in (here, there)]
                pairs.append(tuple(flat))
    return lax.ppermute(value, axes, pairs)


class Shape:
    def __init__(self, sides, first, second, lanes):
        self.sides, self.x, self.y, self.lanes = sides, first, second, lanes
        self.cells = first * second
        self.chunk = max(1, 128 // self.cells)
        self.rows = self.chunk * self.cells
        self.block = min(sides, 32)
        self.half = self.block // 2
        self.half_rows = self.half * self.cells
        self.outer = [("col", i) for i in range(turns("col"))]
        self.inner = [("row", i) for i in range(turns("row"))]
        self.faces = self.outer + self.inner
        self.ends = turns("gz")

    def face_len(self, face):
        return self.y if face[0] == "row" else self.x

    def halo_rows(self):
        return sum(self.chunk * self.face_len(face) for face in self.faces)

    def edge(self, face):
        axis, turn = face
        last = (self.x if axis == "row" else self.y) - 1
        return jnp.where(lax.axis_index(axis) % 2 == turn, last, 0)


def halo_place(shape):
    dims = (shape.rows, shape.halo_rows())
    row, col = iota(dims, 0), iota(dims, 1)
    side, cell = row // shape.cells, row % shape.cells
    x, y = cell // shape.y, cell % shape.y
    hit, base = None, 0
    for face in shape.faces:
        length = shape.face_len(face)
        along, across = (y, x) if face[0] == "row" else (x, y)
        place = (across == shape.edge(face)) & (col - base == side * length + along)
        place = place & has_neighbour(*face)
        hit = place if hit is None else hit | place
        base += shape.chunk * length
    return hit.astype(BF)


def z_mask(shape, count):
    dims = (count * shape.cells, 2 * shape.cells)
    return iota(dims, 1) % shape.cells == iota(dims, 0) % shape.cells


def twice(matrix):
    zero = jnp.zeros_like(matrix)
    return jnp.concatenate(
        [jnp.concatenate([matrix, zero], axis=1), jnp.concatenate([zero, matrix], axis=1)], axis=0
    )


def beside(values):
    half = values.shape[0] // 2
    return jnp.concatenate([values[:half], values[half:]], axis=1)


def build_out(shape, ends_m, rsum):
    dims = (shape.lanes, 2 * shape.cells)
    edge = jnp.where(iota(dims, 1) < shape.cells, 0, shape.lanes - 1)
    ends_m[...] = twice((iota(dims, 0) == edge).astype(F32)).astype(BF)
    dims = rsum.shape
    rsum[...] = (iota(dims, 1) // shape.cells == iota(dims, 0)).astype(BF)


def cut_faces(shape, faces, at, block, tall, face_refs, pitch=None):
    for face, ref in zip(faces, face_refs):
        length, edge = shape.face_len(face), shape.edge(face)
        lines = []
        for side in range(block):
            start = side * (pitch or shape.cells)
            if face[0] == "row":
                lines.append(tall[pl.ds(aligned(start + edge * length, 8), length), :])
            else:
                lines.append(tall[pl.ds(start + edge, length, stride=shape.y), :])
        span = slice(at * length, (at + block) * length)
        ref[span, :] = jnp.concatenate(lines, axis=0).astype(BF)


def cut_ends(shape, at, values, z_ref, ends_m, rsum):
    mask = jnp.concatenate([z_mask(shape, shape.half)] * 2, axis=1)
    tips = jnp.where(mask, dot(beside(values), ends_m[...]), 0.0).astype(BF)
    tips = dot(rsum[...], tips)[: shape.half]
    tips = jnp.concatenate([tips[:, : 2 * shape.cells], tips[:, 2 * shape.cells :]], axis=0)
    z_ref[at : at + shape.block, :] = tips.astype(BF)


def build_tables(shape, coef_ref, weight, near_m, line_m, ends_m, rsum):
    cells, lanes = shape.cells, shape.lanes
    weight[...] = jnp.concatenate([OMEGA / (6.0 + coef_ref[...])] * shape.chunk, axis=0)
    dims = (shape.rows, shape.rows)
    row, col = iota(dims, 0), iota(dims, 1)
    x, y = row % cells // shape.y, row % shape.y
    x2, y2 = col % cells // shape.y, col % shape.y
    near = ((x == x2) & (jnp.abs(y - y2) == 1)) | ((y == y2) & (jnp.abs(x - x2) == 1))
    near_m[:, : shape.rows] = (near & (row // cells == col // cells)).astype(BF)
    near_m[:, shape.rows :] = halo_place(shape)
    dims = (lanes, lanes)
    line = (jnp.abs(iota(dims, 0) - iota(dims, 1)) == 1).astype(F32)
    line_m[: 2 * lanes, :] = twice(line).astype(BF)
    dims = (2 * cells, lanes)
    edge = jnp.where(iota(dims, 0) < cells, lanes - 1, 0)
    line_m[2 * lanes :, :] = twice((iota(dims, 1) == edge).astype(F32)).astype(BF)
    build_out(shape, ends_m, rsum)


def table_shapes(shape):
    lanes, cells = shape.lanes, shape.cells
    return [
        jax.ShapeDtypeStruct((shape.rows, lanes), F32),
        jax.ShapeDtypeStruct((shape.rows, shape.rows + shape.halo_rows()), BF),
        jax.ShapeDtypeStruct((2 * lanes + 4 * cells, 2 * lanes), BF),
        jax.ShapeDtypeStruct((2 * lanes, 4 * cells), BF),
        jax.ShapeDtypeStruct((max(8, shape.half), shape.half_rows), BF),
    ]


def faces_kernel(shape, slots, field_ref, block_ref, coef_ref, *refs):
    refs = list(refs)
    face_refs = [refs.pop(0) for _ in shape.inner]
    z_ref, held, *tables, field, tall, sems, field_sems = refs
    size = shape.block * shape.cells
    steps = shape.sides // shape.block
    copies = []
    for step in range(steps):
        span = pl.ds(step * size, size)
        copies.append(
            pltpu.make_async_copy(field_ref.at[span], field.at[span], field_sems.at[step])
        )
        copies[-1].start()
    columns = fetch_columns(block_ref, held, sems, slots)
    build_tables(shape, coef_ref, *tables)
    ends_m, rsum = tables[-2:]
    for step in range(steps):
        copies[step].wait()
        values = field[step * size : (step + 1) * size, :]
        tall[step] = values.astype(F32)
        cut_faces(shape, shape.inner, step * shape.block, shape.block, tall.at[step], face_refs)
        cut_ends(shape, step * shape.block, values, z_ref, ends_m, rsum)
    for copy in columns:
        copy.wait()


def face_shapes(shape, faces):
    return [
        jax.ShapeDtypeStruct((shape.sides * shape.face_len(face), shape.lanes), BF)
        for face in faces
    ]


def first_faces(shape, field, block, coef, slots):
    peers = lax.axis_size("row")
    steps = shape.sides // shape.block
    shapes = face_shapes(shape, shape.inner)
    shapes.append(jax.ShapeDtypeStruct((shape.sides, 2 * shape.cells), BF))
    shapes.append(jax.ShapeDtypeStruct((peers, block.shape[0], slots), BF))
    shapes += table_shapes(shape)
    hbm = pl.BlockSpec(memory_space=pltpu.HBM)
    return pl.pallas_call(
        functools.partial(faces_kernel, shape, slots),
        in_specs=[hbm, hbm, WHOLE],
        out_specs=[WHOLE] * len(shapes),
        out_shape=shapes,
        scratch_shapes=[
            pltpu.VMEM(field.shape, BF),
            pltpu.VMEM((steps, shape.block * shape.cells, shape.lanes), F32),
            pltpu.SemaphoreType.DMA((peers,)),
            pltpu.SemaphoreType.DMA((steps,)),
        ],
        compiler_params=params(FACES_MIB),
        cost_estimate=pl.CostEstimate(
            flops=field.size * 128, bytes_accessed=4 * field.size, transcendentals=0
        ),
    )(field, block, coef)


def expand(shape, lines, where):
    rows = []
    for side in range(shape.block):
        line = jnp.broadcast_to(lines[side : side + 1], where.shape)
        rows.append(jnp.where(where, line, 0.0))
    return beside(jnp.concatenate(rows, axis=0).astype(BF))


def halo_ends(shape, end_refs, sides):
    even = lax.axis_index("gz") % 2 == 0
    filled = (iota((shape.block, 2 * shape.cells), 1) < shape.cells) == even
    zs = 0.0
    for turn in range(shape.ends):
        wanted = (filled == (turn == 0)) & has_neighbour("gz", turn)
        zs = jnp.where(wanted, end_refs[-1 - turn][sides, :].astype(F32), zs)
    return expand(shape, zs, z_mask(shape, 1))


def flux_width(slots):
    return (2 * slots + 127) // 128 * 128


def build_cells(shape, cell_ref, cell_m):
    slots = cell_ref.shape[3]
    width = flux_width(slots)
    cell = cell_ref[0, 0]
    none = jnp.full((1, width - 2 * slots), -shape.lanes, jnp.int32)
    cell = jnp.concatenate([cell, cell, none], axis=1)
    place = (iota((shape.lanes, width), 0) == cell % shape.lanes).astype(F32)
    cell_m[...] = twice(place).astype(BF)
    return iota((shape.cells, width), 0) == cell // shape.lanes


def base_kernel(shape, ends, with_flux, *refs):
    refs = list(refs)
    take = lambda count: [refs.pop(0) for _ in range(count)]
    field_ref, load_ref, weight, near_m, line_m = take(5)
    end_refs = take(ends)
    if with_flux:
        phi, cell_ref = take(2)
    (base_ref,) = take(1)
    if with_flux:
        (source_ref,) = take(1)
    (lines,) = take(1)
    if with_flux:
        cell_m, placed = take(2)
        cell_mask = build_cells(shape, cell_ref, cell_m)

    cells, lanes = shape.cells, shape.lanes
    weights = weight[...]
    for step in range(shape.sides // shape.block):
        sides = slice(step * shape.block, (step + 1) * shape.block)
        at = step * shape.block * cells
        left = beside(field_ref[at : at + shape.block * cells, :])
        if ends:
            left = jnp.concatenate([left, halo_ends(shape, end_refs, sides)], axis=1)
        lines[step] = dot(left, line_m[: left.shape[1], :])
        if with_flux:
            placed[step] = dot_nt(expand(shape, phi[sides, :], cell_mask), cell_m[...])
        for index in range(shape.half // shape.chunk):
            offset = index * shape.rows
            here = slice(offset, offset + shape.rows)
            spans = [
                slice(at + start, at + start + shape.rows)
                for start in (offset, offset + shape.half_rows)
            ]
            stack = jnp.concatenate([field_ref[span, :] for span in spans], axis=1)
            near = dot(near_m[:, : shape.rows], stack) + lines[step, here, :]
            for part, span in enumerate(spans):
                cols = slice(part * lanes, (part + 1) * lanes)
                source = load_ref[span, :].astype(F32)
                if with_flux:
                    source = source + placed[step, here, cols]
                    source_ref[span, :] = source.astype(BF)
                centre = field_ref[span, :].astype(F32)
                base_ref[span, :] = (1.0 - OMEGA) * centre + weights * (source + near[:, cols])


def sweep_base(shape, field, load, tables, ends=(), phi=None, flux_cell=None):
    steps = shape.sides // shape.block
    half = (steps, shape.half_rows, 2 * shape.lanes)
    operands = [field, load, *tables[:3], *ends]
    shapes = [jax.ShapeDtypeStruct(field.shape, F32)]
    scratch = [pltpu.VMEM(half, F32)]
    if phi is not None:
        operands += [phi, flux_cell]
        shapes.append(jax.ShapeDtypeStruct(field.shape, BF))
        scratch.append(pltpu.VMEM((2 * shape.lanes, 2 * phi.shape[1]), BF))
        scratch.append(pltpu.VMEM(half, F32))
    return pl.pallas_call(
        functools.partial(base_kernel, shape, len(ends), phi is not None),
        in_specs=[WHOLE] * len(operands),
        out_specs=[WHOLE] * len(shapes),
        out_shape=shapes,
        scratch_shapes=scratch,
        compiler_params=params(),
        cost_estimate=pl.CostEstimate(
            flops=6 * field.size * 128, bytes_accessed=8 * field.size, transcendentals=0
        ),
    )(*operands)


def finish_kernel(shape, ends, recvs, last, *refs):
    with_flux = recvs > 0
    refs = list(refs)
    take = lambda count: [refs.pop(0) for _ in range(count)]
    base_ref, weight, near_m, line_m, ends_m, rsum = take(6)
    halo_refs = take(len(shape.faces))
    end_refs = take(ends)
    if with_flux:
        (cell_ref,) = take(1)
        recv_refs = take(recvs)
    (out_ref,) = take(1)
    if not last:
        face_refs = take(len(shape.faces))
        (z_ref,) = take(1)
    if with_flux:
        phi, flux_ref = take(2)
    if last:
        result_ref = out_ref
        out_ref, out_sems = take(2)
    else:
        (tall,) = take(1)
    if ends:
        (lines,) = take(1)
    if with_flux:
        cell_m, placed = take(2)

    cells, lanes = shape.cells, shape.lanes

    if with_flux:
        slots = cell_ref.shape[3]
        cell_mask = build_cells(shape, cell_ref, cell_m)
        owned = recv_refs[0][...]
        for ref in recv_refs[1:]:
            owned = owned + ref[...]
        flux_ref[...] = owned[slots:, : flux_ref.shape[1]]
        owned = owned[:slots]
        high = owned.astype(BF).astype(F32)
        none = jnp.zeros((phi.shape[1] - 2 * slots, phi.shape[0]), F32)
        phi[...] = jnp.concatenate([high, owned - high, none], axis=0).T

    weights = weight[...]

    def work(step):
        at = step * shape.block
        sides = slice(at, at + shape.block)
        if ends:
            lines[step] = dot(halo_ends(shape, end_refs, sides), line_m[2 * lanes :, :])
        if with_flux:
            placed[step] = dot_nt(expand(shape, phi[sides, :], cell_mask), cell_m[...])
        for index in range(shape.half // shape.chunk):
            offset = index * shape.rows
            starts = (offset, offset + shape.half_rows)
            stacks = []
            for start in starts:
                stack = []
                for face, ref in zip(shape.faces, halo_refs):
                    length = shape.face_len(face)
                    first = at * length + start // cells * length
                    stack.append(ref[first : first + shape.chunk * length, :])
                stacks.append(jnp.concatenate(stack, axis=0))
            near = dot(near_m[:, shape.rows :], jnp.concatenate(stacks, axis=1))
            if ends:
                near = near + lines[step, offset : offset + shape.rows, :]
            if with_flux:
                near = near + placed[step, offset : offset + shape.rows, :]
            for part, start in enumerate(starts):
                rows = slice(at * cells + start, at * cells + start + shape.rows)
                fresh = base_ref[rows, :] + weights * near[:, part * lanes : (part + 1) * lanes]
                out_ref[rows, :] = fresh.astype(BF)
                if not last:
                    tall[step, start : start + shape.rows, :] = fresh

    def emit(step):
        at, size = step * shape.block, shape.block * cells
        fresh = out_ref[at * cells : at * cells + size, :]
        cut_faces(shape, shape.faces, at, shape.block, tall.at[step], face_refs)
        cut_ends(shape, at, fresh, z_ref, ends_m, rsum)

    steps = shape.sides // shape.block
    copies = []
    for step in range(steps):
        work(step)
        if last:
            span = pl.ds(step * shape.block * cells, shape.block * cells)
            copies.append(
                pltpu.make_async_copy(out_ref.at[span], result_ref.at[span], out_sems.at[step])
            )
            copies[-1].start()
        elif step > 0:
            emit(step - 1)
    for copy in copies:
        copy.wait()
    if not last:
        emit(steps - 1)


def sweep_finish(shape, base, tables, halos, ends=(), flux_cell=None, recv=(), last=False):
    lanes, cells = shape.lanes, shape.cells
    steps = shape.sides // shape.block
    half = (steps, shape.half_rows, 2 * lanes)
    operands = [base, *tables, *halos, *ends]
    out_shapes = [jax.ShapeDtypeStruct(base.shape, BF)]
    if last:
        scratch = [pltpu.VMEM(base.shape, BF), pltpu.SemaphoreType.DMA((steps,))]
    else:
        out_shapes += face_shapes(shape, shape.faces)
        out_shapes.append(jax.ShapeDtypeStruct((shape.sides, 2 * cells), BF))
        scratch = [pltpu.VMEM((steps, shape.block * cells, lanes), F32)]
    if ends:
        scratch.append(pltpu.VMEM(half, F32))
    if recv:
        slots = flux_cell.shape[3]
        operands += [flux_cell, *recv]
        out_shapes += [
            jax.ShapeDtypeStruct((shape.sides, flux_width(slots)), F32),
            jax.ShapeDtypeStruct((recv[0].shape[0] - slots, slots * lax.axis_size("gz")), F32),
        ]
        scratch += [
            pltpu.VMEM((2 * lanes, 2 * flux_width(slots)), BF),
            pltpu.VMEM(half, F32),
        ]
    out_specs = [WHOLE] * len(out_shapes)
    if last:
        out_specs = [pl.BlockSpec(memory_space=pltpu.HBM)]
    return pl.pallas_call(
        functools.partial(finish_kernel, shape, len(ends), len(recv), last),
        in_specs=[WHOLE] * len(operands),
        out_specs=out_specs,
        out_shape=out_shapes,
        scratch_shapes=scratch,
        compiler_params=params(),
        cost_estimate=pl.CostEstimate(
            flops=4 * base.size * 128, bytes_accessed=8 * base.size, transcendentals=0
        ),
    )(*operands)


def swap_faces(faces, values):
    return [swap(value, *face) for face, value in zip(faces, values)]


def swap_ends(shape, ends):
    return [swap(ends, "gz", turn) for turn in reversed(range(shape.ends))]


def row_gather(trace, hidden, late):
    peers = lax.axis_size("row")
    held = {0: trace}
    bit = peers // 2
    while bit:
        pairs = [(i, i ^ bit) for i in range(peers)]
        fresh = {key ^ bit: lax.ppermute(held[key], "row", pairs) for key in sorted(held, reverse=True)}
        if bit == peers // 2:
            fresh, hidden = lax.optimization_barrier((fresh, hidden))
        held.update(fresh)
        bit //= 2
    parts, late = lax.optimization_barrier(([held[key] for key in range(peers)], late))
    return parts, hidden, late


def per_device(volume_field, volume_load, coefficient, surface_block, trace_cell, flux_cell):
    sides, first, second, lanes = volume_field.shape
    cells = first * second
    shape = Shape(sides, first, second, lanes)
    field = volume_field.reshape(sides * cells, lanes)
    load = volume_load.reshape(sides * cells, lanes)
    coef = coefficient.reshape(cells, lanes)

    slots = trace_cell.shape[3]
    trace, *outer = traces(
        shape, volume_field.reshape(sides, cells, lanes), trace_cell, min(32, sides)
    )
    firsts = first_faces(shape, field, surface_block, coef, slots)
    layers = len(shape.faces)
    count = len(shape.inner) + 1
    inner, held, tables = firsts[:count], firsts[count], firsts[count + 1 :]
    *inner, ends = inner
    along_col = swap_faces(shape.outer, outer)
    parts, inner, along_col = row_gather(trace, inner, along_col)
    along_row = swap_faces(shape.inner, inner)
    recv, ends = flux_sums(parts, held, along_row, ends)
    tips = swap_ends(shape, ends)

    (base,) = sweep_base(shape, field, load, tables, tips)
    current, *faces, ends, phi, surface_flux = sweep_finish(
        shape, base, tables, along_col + along_row, flux_cell=flux_cell, recv=recv
    )
    halos, tips = swap_faces(shape.faces, faces), swap_ends(shape, ends)
    base, source = sweep_base(shape, current, load, tables, phi=phi, flux_cell=flux_cell)
    current, *faces, ends = sweep_finish(shape, base, tables, halos, tips)
    halos, tips = swap_faces(shape.faces, faces), swap_ends(shape, ends)
    (base,) = sweep_base(shape, current, source, tables)
    (current,) = sweep_finish(shape, base, tables, halos, tips, last=True)
    return current.reshape(volume_field.shape), surface_flux


def solution(mesh):
    in_specs = (
        P(None, "row", "col", "gz"),
        P(None, "row", "col", "gz"),
        P("row", "col", "gz"),
        P("row", "col"),
        P("row", "col", "gz", None),
        P("row", "col", "gz", None),
    )
    out_specs = (P(None, "row", "col", "gz"), P("gz", ("row", "col")))
    return jax.shard_map(
        per_device, mesh=mesh, in_specs=in_specs, out_specs=out_specs, check_vma=False
    )
```

```python
import functools

import jax
import jax.numpy as jnp
from jax import lax
from jax.experimental import pallas as pl
from jax.experimental.pallas import tpu as pltpu
from jax.sharding import PartitionSpec as P

OMEGA = 0.8
BF = jnp.bfloat16
F32 = jnp.float32
WHOLE = pl.BlockSpec(memory_space=pltpu.VMEM)


def aligned(start, unit):
    return start if isinstance(start, int) else pl.multiple_of(start, unit)


def iota(shape, dim):
    return lax.broadcasted_iota(jnp.int32, shape, dim)


def dot(a, b):
    return jnp.dot(a, b, preferred_element_type=F32)


def dot_nt(a, b):
    return lax.dot_general(a, b, (((1,), (1,)), ((), ())), preferred_element_type=F32)


FACES_MIB = 50
TRACE_MIB = 52


def params(mebibytes=24):
    return pltpu.CompilerParams(vmem_limit_bytes=mebibytes * 1024 * 1024)


def trace_kernel(shape, stride, block, field_ref, cell_ref, out_ref, *refs):
    *face_refs, field, cell_v, tall, near, place, picked, sems = refs
    sides, rows, lanes = field.shape
    slots = cell_ref.shape[3]
    per_row = lanes // stride
    width = near.shape[0]
    parts = slots // width
    cell_copy = pltpu.make_async_copy(cell_ref, cell_v, sems.at[sides // block])
    cell_copy.start()
    copies = []
    for step in range(sides // block):
        span = pl.ds(step * block, block)
        copies.append(pltpu.make_async_copy(field_ref.at[span], field.at[span], sems.at[step]))
        copies[-1].start()

    cell_copy.wait()
    cell = cell_v[0, 0]
    run = cell // stride
    digit = jnp.zeros_like(cell)
    for part in range(parts):
        digit = jnp.where(run // width == part, (cell % stride) * stride**part, digit)
    hit = iota((width, slots), 0) == run % width
    near[...] = hit.astype(BF)
    digits = jnp.sum(jnp.where(hit, digit.astype(F32), 0.0), axis=1, keepdims=True)
    digits = jnp.broadcast_to(digits, (width, 128)).T[0:8].astype(jnp.int32)
    first = iota((8, width), 1) % per_row * stride
    for part in range(parts):
        place[:, part * width : (part + 1) * width] = first + digits // stride**part % stride

    pitch = rows + 1
    together = 128 // per_row
    group = iota((8, 128), 1) // per_row
    for step in range(sides // block):
        copies[step].wait()
        span = field[step * block : (step + 1) * block]
        for side in range(block):
            start = side * pitch
            tall[step, start : start + rows, :] = span[side].astype(F32)
        cut_faces(shape, shape.outer, step * block, block, tall.at[step], face_refs, pitch)

        for batch in range(block // 8):
            for tile in range(rows // together):
                cols = slice(tile * 128, (tile + 1) * 128)
                where = place[:, cols]
                found = None
                for row in range(together):
                    start = batch * 8 * pitch + tile * together + row
                    line = tall[step, pl.ds(start, 8, stride=pitch), :]
                    line = jnp.take_along_axis(line, where, axis=1)
                    found = line if found is None else jnp.where(group == row, line, found)
                at = step * block + batch * 8
                picked[at : at + 8, cols] = found

    total = jnp.zeros((sides, slots), F32)
    for part in range(parts):
        sorted_runs = picked[:, part * width : (part + 1) * width].astype(BF)
        total = jnp.where(run // width == part, dot(sorted_runs, near[...]), total)
    out_ref[...] = total.T.astype(BF)


def traces(shape, field, trace_cell, block):
    sides, rows, lanes = field.shape
    slots = trace_cell.shape[3]
    stride = rows * lanes // slots
    width = min(slots, 256)
    hbm = pl.BlockSpec(memory_space=pltpu.HBM)
    return pl.pallas_call(
        functools.partial(trace_kernel, shape, stride, block),
        in_specs=[hbm, hbm],
        out_specs=[WHOLE] * (1 + len(shape.outer)),
        out_shape=[jax.ShapeDtypeStruct((slots, sides), BF)] + face_shapes(shape, shape.outer),
        scratch_shapes=[
            pltpu.VMEM(field.shape, BF),
            pltpu.VMEM(trace_cell.shape, jnp.int32),
            pltpu.VMEM((sides // block, block * (rows + 1), lanes), F32),
            pltpu.VMEM((width, slots), BF),
            pltpu.VMEM((8, slots), jnp.int32),
            pltpu.VMEM((sides, slots), F32),
            pltpu.SemaphoreType.DMA((sides // block + 1,)),
        ],
        compiler_params=params(TRACE_MIB),
        cost_estimate=pl.CostEstimate(
            flops=4 * sides * rows * lanes * 128, bytes_accessed=field.size * 2, transcendentals=0
        ),
    )(field, trace_cell)


def fetch_columns(block_ref, held, sems, slots):
    me, group, gzs = lax.axis_index("row"), lax.axis_index("gz"), lax.axis_size("gz")
    copies = []
    for key in range(held.shape[0]):
        start = pl.multiple_of((jnp.bitwise_xor(me, key) * gzs + group) * slots, slots)
        copies.append(
            pltpu.make_async_copy(block_ref.at[:, pl.ds(start, slots)], held.at[key], sems.at[key])
        )
        copies[-1].start()
    return copies


def surface_kernel(halves, *refs):
    ins, total = refs[:-1], refs[-1]
    outs = ins[len(ins) - halves :]
    *parts, held = ins[: len(ins) - halves]
    value = None
    for key, part in enumerate(parts):
        term = dot(held[key], part[...])
        value = term if value is None else value + term
    if halves == 1:
        outs[0][...] = value
        return
    total[...] = value
    count = outs[0].shape[0]
    mine = lax.axis_index("col")
    for key, out in enumerate(outs):
        out[...] = total[pl.ds(pl.multiple_of((mine ^ key) * count, 8), count), :]


def surface(parts, held, halves):
    sides = parts[0].shape[1]
    lines = held.shape[1]
    return pl.pallas_call(
        functools.partial(surface_kernel, halves),
        in_specs=[WHOLE] * (len(parts) + 1),
        out_specs=[WHOLE] * halves,
        out_shape=[jax.ShapeDtypeStruct((lines // halves, sides), F32)] * halves,
        scratch_shapes=[pltpu.VMEM((lines, sides), F32)],
        compiler_params=params(),
        cost_estimate=pl.CostEstimate(
            flops=2 * sides * held.size, bytes_accessed=2 * held.size, transcendentals=0
        ),
    )(*parts, held)


def share_kernel(peers, mine_ref, other_ref, *refs):
    *outs, total, turned = refs
    total[...] = mine_ref[...] + other_ref[...]
    turned[...] = total[...].T
    lines, sides = total.shape
    group = lax.axis_index("gz")
    for key, out in enumerate(outs):
        peer = group ^ key
        rows, some = lines // peers, sides // peers
        out[:rows, :] = total[pl.ds(pl.multiple_of(peer * rows, 8), rows), :]
        out[rows:, :] = turned[pl.ds(pl.multiple_of(peer * some, 8), some), :]


def shares(mine, other):
    peers = lax.axis_size("gz")
    lines, sides = mine.shape
    out = jax.ShapeDtypeStruct(((lines + sides) // peers, sides), F32)
    return pl.pallas_call(
        functools.partial(share_kernel, peers),
        in_specs=[WHOLE] * 2,
        out_specs=[WHOLE] * peers,
        out_shape=[out] * peers,
        scratch_shapes=[pltpu.VMEM((lines, sides), F32), pltpu.VMEM((sides, lines), F32)],
        compiler_params=params(),
        cost_estimate=pl.CostEstimate(
            flops=lines * sides, bytes_accessed=16 * lines * sides, transcendentals=0
        ),
    )(mine, other)


def flux_sums(parts, held, late, after):
    cols, gzs = lax.axis_size("col"), lax.axis_size("gz")
    sides = parts[0].shape[1]
    lines = held.shape[1]
    if cols == 2 and gzs & (gzs - 1) == 0 and lines // cols == sides and sides // gzs % 8 == 0:
        mine, other = surface(parts, held, 2)
        mine, other, after = lax.optimization_barrier((mine, other, after))
        other = lax.ppermute(other, "col", [(0, 1), (1, 0)])
        other, late = lax.optimization_barrier((other, late))
        sent = shares(mine, other)
        recv = [sent[0]]
        for key in range(gzs - 1, 0, -1):
            recv.append(lax.ppermute(sent[key], "gz", [(i, i ^ key) for i in range(gzs)]))
        return recv, after
    (total,) = surface(parts, held, 1)
    rows = lax.psum_scatter(total, "col", scatter_dimension=0, tiled=True)
    owned = lax.psum_scatter(rows, "gz", scatter_dimension=0, tiled=True)
    flux = lax.psum_scatter(rows.T, "gz", scatter_dimension=0, tiled=True)
    flux = jnp.pad(flux, ((0, 0), (0, sides - flux.shape[1])))
    return [jnp.concatenate([owned, flux], axis=0)], after


def turns(axis):
    return 1 if lax.axis_size(axis) == 2 else 2


def partner(index, turn):
    return jnp.where(index % 2 == turn, index + 1, index - 1)


def has_neighbour(axis, turn):
    other = partner(lax.axis_index(axis), turn)
    return (other >= 0) & (other < lax.axis_size(axis))


def swap(value, axis, turn):
    axes = ("row", "col", "gz")
    sizes = [lax.axis_size(name) for name in axes]
    along = axes.index(axis)
    pairs = []
    for r in range(sizes[0]):
        for c in range(sizes[1]):
            for g in range(sizes[2]):
                here = [r, c, g]
                there = [r, c, g]
                there[along] += 1 if here[along] % 2 == turn else -1
                if not 0 <= there[along] < sizes[along]:
                    there[along] = here[along]
                    if axis == "row" and sizes[0] % 2 == 0:
                        there[0] = sizes[0] - 1 - r
                    elif axis != "row" and r ^ 1 < sizes[0]:
                        there[0] ^= 1
                flat = [(at[0] * sizes[1] + at[1]) * sizes[2] + at[2] for at in (here, there)]
                pairs.append(tuple(flat))
    return lax.ppermute(value, axes, pairs)


class Shape:
    def __init__(self, sides, first, second, lanes):
        self.sides, self.x, self.y, self.lanes = sides, first, second, lanes
        self.cells = first * second
        self.chunk = max(1, 128 // self.cells)
        self.rows = self.chunk * self.cells
        self.block = min(sides, 32)
        self.half = self.block // 2
        self.half_rows = self.half * self.cells
        self.outer = [("col", i) for i in range(turns("col"))]
        self.inner = [("row", i) for i in reversed(range(turns("row")))]
        self.faces = self.outer + self.inner
        self.ends = turns("gz")

    def face_len(self, face):
        return self.y if face[0] == "row" else self.x

    def halo_rows(self):
        return sum(self.chunk * self.face_len(face) for face in self.faces)

    def edge(self, face):
        axis, turn = face
        last = (self.x if axis == "row" else self.y) - 1
        return jnp.where(lax.axis_index(axis) % 2 == turn, last, 0)


def halo_place(shape):
    dims = (shape.rows, shape.halo_rows())
    row, col = iota(dims, 0), iota(dims, 1)
    side, cell = row // shape.cells, row % shape.cells
    x, y = cell // shape.y, cell % shape.y
    hit, base = None, 0
    for face in shape.faces:
        length = shape.face_len(face)
        along, across = (y, x) if face[0] == "row" else (x, y)
        place = (across == shape.edge(face)) & (col - base == side * length + along)
        place = place & has_neighbour(*face)
        hit = place if hit is None else hit | place
        base += shape.chunk * length
    return hit.astype(BF)


def z_mask(shape, count):
    dims = (count * shape.cells, 2 * shape.cells)
    return iota(dims, 1) % shape.cells == iota(dims, 0) % shape.cells


def twice(matrix):
    zero = jnp.zeros_like(matrix)
    return jnp.concatenate(
        [jnp.concatenate([matrix, zero], axis=1), jnp.concatenate([zero, matrix], axis=1)], axis=0
    )


def beside(values):
    half = values.shape[0] // 2
    return jnp.concatenate([values[:half], values[half:]], axis=1)


def build_out(shape, ends_m, rsum):
    dims = (shape.lanes, 2 * shape.cells)
    edge = jnp.where(iota(dims, 1) < shape.cells, 0, shape.lanes - 1)
    ends_m[...] = twice((iota(dims, 0) == edge).astype(F32)).astype(BF)
    dims = rsum.shape
    rsum[...] = (iota(dims, 1) // shape.cells == iota(dims, 0)).astype(BF)


def cut_faces(shape, faces, at, block, tall, face_refs, pitch=None):
    for face, ref in zip(faces, face_refs):
        length, edge = shape.face_len(face), shape.edge(face)
        lines = []
        for side in range(block):
            start = side * (pitch or shape.cells)
            if face[0] == "row":
                lines.append(tall[pl.ds(aligned(start + edge * length, 8), length), :])
            else:
                lines.append(tall[pl.ds(start + edge, length, stride=shape.y), :])
        span = slice(at * length, (at + block) * length)
        ref[span, :] = jnp.concatenate(lines, axis=0).astype(BF)


def cut_ends(shape, at, values, z_ref, ends_m, rsum):
    mask = jnp.concatenate([z_mask(shape, shape.half)] * 2, axis=1)
    tips = jnp.where(mask, dot(beside(values), ends_m[...]), 0.0).astype(BF)
    tips = dot(rsum[...], tips)[: shape.half]
    tips = jnp.concatenate([tips[:, : 2 * shape.cells], tips[:, 2 * shape.cells :]], axis=0)
    z_ref[at : at + shape.block, :] = tips.astype(BF)


def build_tables(shape, coef_ref, weight, near_m, line_m, ends_m, rsum):
    cells, lanes = shape.cells, shape.lanes
    weight[...] = jnp.concatenate([OMEGA / (6.0 + coef_ref[...])] * shape.chunk, axis=0)
    dims = (shape.rows, shape.rows)
    row, col = iota(dims, 0), iota(dims, 1)
    x, y = row % cells // shape.y, row % shape.y
    x2, y2 = col % cells // shape.y, col % shape.y
    near = ((x == x2) & (jnp.abs(y - y2) == 1)) | ((y == y2) & (jnp.abs(x - x2) == 1))
    near_m[:, : shape.rows] = (near & (row // cells == col // cells)).astype(BF)
    near_m[:, shape.rows :] = halo_place(shape)
    dims = (lanes, lanes)
    line = (jnp.abs(iota(dims, 0) - iota(dims, 1)) == 1).astype(F32)
    line_m[: 2 * lanes, :] = twice(line).astype(BF)
    dims = (2 * cells, lanes)
    edge = jnp.where(iota(dims, 0) < cells, lanes - 1, 0)
    line_m[2 * lanes :, :] = twice((iota(dims, 1) == edge).astype(F32)).astype(BF)
    build_out(shape, ends_m, rsum)


def table_shapes(shape):
    lanes, cells = shape.lanes, shape.cells
    return [
        jax.ShapeDtypeStruct((shape.rows, lanes), F32),
        jax.ShapeDtypeStruct((shape.rows, shape.rows + shape.halo_rows()), BF),
        jax.ShapeDtypeStruct((2 * lanes + 4 * cells, 2 * lanes), BF),
        jax.ShapeDtypeStruct((2 * lanes, 4 * cells), BF),
        jax.ShapeDtypeStruct((max(8, shape.half), shape.half_rows), BF),
    ]


def faces_kernel(shape, slots, field_ref, block_ref, coef_ref, *refs):
    refs = list(refs)
    face_refs = [refs.pop(0) for _ in shape.inner]
    z_ref, held, *tables, field, tall, sems, field_sems = refs
    size = shape.block * shape.cells
    steps = shape.sides // shape.block
    copies = []
    for step in range(steps):
        span = pl.ds(step * size, size)
        copies.append(
            pltpu.make_async_copy(field_ref.at[span], field.at[span], field_sems.at[step])
        )
        copies[-1].start()
    columns = fetch_columns(block_ref, held, sems, slots)
    build_tables(shape, coef_ref, *tables)
    ends_m, rsum = tables[-2:]
    for step in range(steps):
        copies[step].wait()
        values = field[step * size : (step + 1) * size, :]
        tall[step] = values.astype(F32)
        cut_faces(shape, shape.inner, step * shape.block, shape.block, tall.at[step], face_refs)
        cut_ends(shape, step * shape.block, values, z_ref, ends_m, rsum)
    for copy in columns:
        copy.wait()


def face_shapes(shape, faces):
    return [
        jax.ShapeDtypeStruct((shape.sides * shape.face_len(face), shape.lanes), BF)
        for face in faces
    ]


def first_faces(shape, field, block, coef, slots):
    peers = lax.axis_size("row")
    steps = shape.sides // shape.block
    shapes = face_shapes(shape, shape.inner)
    shapes.append(jax.ShapeDtypeStruct((shape.sides, 2 * shape.cells), BF))
    shapes.append(jax.ShapeDtypeStruct((peers, block.shape[0], slots), BF))
    shapes += table_shapes(shape)
    hbm = pl.BlockSpec(memory_space=pltpu.HBM)
    return pl.pallas_call(
        functools.partial(faces_kernel, shape, slots),
        in_specs=[hbm, hbm, WHOLE],
        out_specs=[WHOLE] * len(shapes),
        out_shape=shapes,
        scratch_shapes=[
            pltpu.VMEM(field.shape, BF),
            pltpu.VMEM((steps, shape.block * shape.cells, shape.lanes), F32),
            pltpu.SemaphoreType.DMA((peers,)),
            pltpu.SemaphoreType.DMA((steps,)),
        ],
        compiler_params=params(FACES_MIB),
        cost_estimate=pl.CostEstimate(
            flops=field.size * 128, bytes_accessed=4 * field.size, transcendentals=0
        ),
    )(field, block, coef)


def expand(shape, lines, where):
    rows = []
    for side in range(shape.block):
        line = jnp.broadcast_to(lines[side : side + 1], where.shape)
        rows.append(jnp.where(where, line, 0.0))
    return beside(jnp.concatenate(rows, axis=0).astype(BF))


def halo_ends(shape, end_refs, sides):
    even = lax.axis_index("gz") % 2 == 0
    filled = (iota((shape.block, 2 * shape.cells), 1) < shape.cells) == even
    zs = 0.0
    for turn in range(shape.ends):
        wanted = (filled == (turn == 0)) & has_neighbour("gz", turn)
        zs = jnp.where(wanted, end_refs[-1 - turn][sides, :].astype(F32), zs)
    return expand(shape, zs, z_mask(shape, 1))


def flux_width(slots):
    return (2 * slots + 127) // 128 * 128


def build_cells(shape, cell_ref, cell_m):
    slots = cell_ref.shape[3]
    width = flux_width(slots)
    cell = cell_ref[0, 0]
    none = jnp.full((1, width - 2 * slots), -shape.lanes, jnp.int32)
    cell = jnp.concatenate([cell, cell, none], axis=1)
    place = (iota((shape.lanes, width), 0) == cell % shape.lanes).astype(F32)
    cell_m[...] = twice(place).astype(BF)
    return iota((shape.cells, width), 0) == cell // shape.lanes


def base_kernel(shape, ends, with_flux, *refs):
    refs = list(refs)
    take = lambda count: [refs.pop(0) for _ in range(count)]
    field_ref, load_ref, weight, near_m, line_m = take(5)
    end_refs = take(ends)
    if with_flux:
        phi, cell_ref = take(2)
    (base_ref,) = take(1)
    if with_flux:
        (source_ref,) = take(1)
    (lines,) = take(1)
    if with_flux:
        cell_m, placed = take(2)
        cell_mask = build_cells(shape, cell_ref, cell_m)

    cells, lanes = shape.cells, shape.lanes
    weights = weight[...]
    for step in range(shape.sides // shape.block):
        sides = slice(step * shape.block, (step + 1) * shape.block)
        at = step * shape.block * cells
        left = beside(field_ref[at : at + shape.block * cells, :])
        if ends:
            left = jnp.concatenate([left, halo_ends(shape, end_refs, sides)], axis=1)
        lines[step] = dot(left, line_m[: left.shape[1], :])
        if with_flux:
            placed[step] = dot_nt(expand(shape, phi[sides, :], cell_mask), cell_m[...])
        for index in range(shape.half // shape.chunk):
            offset = index * shape.rows
            here = slice(offset, offset + shape.rows)
            spans = [
                slice(at + start, at + start + shape.rows)
                for start in (offset, offset + shape.half_rows)
            ]
            stack = jnp.concatenate([field_ref[span, :] for span in spans], axis=1)
            near = dot(near_m[:, : shape.rows], stack) + lines[step, here, :]
            for part, span in enumerate(spans):
                cols = slice(part * lanes, (part + 1) * lanes)
                source = load_ref[span, :].astype(F32)
                if with_flux:
                    source = source + placed[step, here, cols]
                    source_ref[span, :] = source.astype(BF)
                centre = field_ref[span, :].astype(F32)
                base_ref[span, :] = (1.0 - OMEGA) * centre + weights * (source + near[:, cols])


def sweep_base(shape, field, load, tables, ends=(), phi=None, flux_cell=None):
    steps = shape.sides // shape.block
    half = (steps, shape.half_rows, 2 * shape.lanes)
    operands = [field, load, *tables[:3], *ends]
    shapes = [jax.ShapeDtypeStruct(field.shape, F32)]
    scratch = [pltpu.VMEM(half, F32)]
    if phi is not None:
        operands += [phi, flux_cell]
        shapes.append(jax.ShapeDtypeStruct(field.shape, BF))
        scratch.append(pltpu.VMEM((2 * shape.lanes, 2 * phi.shape[1]), BF))
        scratch.append(pltpu.VMEM(half, F32))
    return pl.pallas_call(
        functools.partial(base_kernel, shape, len(ends), phi is not None),
        in_specs=[WHOLE] * len(operands),
        out_specs=[WHOLE] * len(shapes),
        out_shape=shapes,
        scratch_shapes=scratch,
        compiler_params=params(),
        cost_estimate=pl.CostEstimate(
            flops=6 * field.size * 128, bytes_accessed=8 * field.size, transcendentals=0
        ),
    )(*operands)


def finish_kernel(shape, ends, recvs, last, *refs):
    with_flux = recvs > 0
    refs = list(refs)
    take = lambda count: [refs.pop(0) for _ in range(count)]
    base_ref, weight, near_m, line_m, ends_m, rsum = take(6)
    halo_refs = take(len(shape.faces))
    end_refs = take(ends)
    if with_flux:
        (cell_ref,) = take(1)
        recv_refs = take(recvs)
    (out_ref,) = take(1)
    if not last:
        face_refs = take(len(shape.faces))
        (z_ref,) = take(1)
    if with_flux:
        phi, flux_ref = take(2)
    if last:
        result_ref = out_ref
        out_ref, out_sems = take(2)
    else:
        (tall,) = take(1)
    if ends:
        (lines,) = take(1)
    if with_flux:
        cell_m, placed = take(2)

    cells, lanes = shape.cells, shape.lanes

    if with_flux:
        slots = cell_ref.shape[3]
        cell_mask = build_cells(shape, cell_ref, cell_m)
        owned = recv_refs[0][...]
        for ref in recv_refs[1:]:
            owned = owned + ref[...]
        flux_ref[...] = owned[slots:, : flux_ref.shape[1]]
        owned = owned[:slots]
        high = owned.astype(BF).astype(F32)
        none = jnp.zeros((phi.shape[1] - 2 * slots, phi.shape[0]), F32)
        phi[...] = jnp.concatenate([high, owned - high, none], axis=0).T

    weights = weight[...]

    def work(step):
        at = step * shape.block
        sides = slice(at, at + shape.block)
        if ends:
            lines[step] = dot(halo_ends(shape, end_refs, sides), line_m[2 * lanes :, :])
        if with_flux:
            placed[step] = dot_nt(expand(shape, phi[sides, :], cell_mask), cell_m[...])
        for index in range(shape.half // shape.chunk):
            offset = index * shape.rows
            starts = (offset, offset + shape.half_rows)
            stacks = []
            for start in starts:
                stack = []
                for face, ref in zip(shape.faces, halo_refs):
                    length = shape.face_len(face)
                    first = at * length + start // cells * length
                    stack.append(ref[first : first + shape.chunk * length, :])
                stacks.append(jnp.concatenate(stack, axis=0))
            near = dot(near_m[:, shape.rows :], jnp.concatenate(stacks, axis=1))
            if ends:
                near = near + lines[step, offset : offset + shape.rows, :]
            if with_flux:
                near = near + placed[step, offset : offset + shape.rows, :]
            for part, start in enumerate(starts):
                rows = slice(at * cells + start, at * cells + start + shape.rows)
                fresh = base_ref[rows, :] + weights * near[:, part * lanes : (part + 1) * lanes]
                out_ref[rows, :] = fresh.astype(BF)
                if not last:
                    tall[step, start : start + shape.rows, :] = fresh

    def emit(step):
        at, size = step * shape.block, shape.block * cells
        fresh = out_ref[at * cells : at * cells + size, :]
        cut_faces(shape, shape.faces, at, shape.block, tall.at[step], face_refs)
        cut_ends(shape, at, fresh, z_ref, ends_m, rsum)

    steps = shape.sides // shape.block
    copies = []
    for step in range(steps):
        work(step)
        if last:
            span = pl.ds(step * shape.block * cells, shape.block * cells)
            copies.append(
                pltpu.make_async_copy(out_ref.at[span], result_ref.at[span], out_sems.at[step])
            )
            copies[-1].start()
        elif step > 0:
            emit(step - 1)
    for copy in copies:
        copy.wait()
    if not last:
        emit(steps - 1)


def sweep_finish(shape, base, tables, halos, ends=(), flux_cell=None, recv=(), last=False):
    lanes, cells = shape.lanes, shape.cells
    steps = shape.sides // shape.block
    half = (steps, shape.half_rows, 2 * lanes)
    operands = [base, *tables, *halos, *ends]
    out_shapes = [jax.ShapeDtypeStruct(base.shape, BF)]
    if last:
        scratch = [pltpu.VMEM(base.shape, BF), pltpu.SemaphoreType.DMA((steps,))]
    else:
        out_shapes += face_shapes(shape, shape.faces)
        out_shapes.append(jax.ShapeDtypeStruct((shape.sides, 2 * cells), BF))
        scratch = [pltpu.VMEM((steps, shape.block * cells, lanes), F32)]
    if ends:
        scratch.append(pltpu.VMEM(half, F32))
    if recv:
        slots = flux_cell.shape[3]
        operands += [flux_cell, *recv]
        out_shapes += [
            jax.ShapeDtypeStruct((shape.sides, flux_width(slots)), F32),
            jax.ShapeDtypeStruct((recv[0].shape[0] - slots, slots * lax.axis_size("gz")), F32),
        ]
        scratch += [
            pltpu.VMEM((2 * lanes, 2 * flux_width(slots)), BF),
            pltpu.VMEM(half, F32),
        ]
    out_specs = [WHOLE] * len(out_shapes)
    if last:
        out_specs = [pl.BlockSpec(memory_space=pltpu.HBM)]
    return pl.pallas_call(
        functools.partial(finish_kernel, shape, len(ends), len(recv), last),
        in_specs=[WHOLE] * len(operands),
        out_specs=out_specs,
        out_shape=out_shapes,
        scratch_shapes=scratch,
        compiler_params=params(),
        cost_estimate=pl.CostEstimate(
            flops=4 * base.size * 128, bytes_accessed=8 * base.size, transcendentals=0
        ),
    )(*operands)


def swap_faces(faces, values):
    return [swap(value, *face) for face, value in zip(faces, values)]


def swap_ends(shape, ends):
    return [swap(ends, "gz", turn) for turn in reversed(range(shape.ends))]


def row_gather(trace, hidden, late):
    peers = lax.axis_size("row")
    held = {0: trace}
    bit = peers // 2
    while bit:
        pairs = [(i, i ^ bit) for i in range(peers)]
        fresh = {key ^ bit: lax.ppermute(held[key], "row", pairs) for key in sorted(held, reverse=True)}
        if bit == peers // 2:
            fresh, hidden = lax.optimization_barrier((fresh, hidden))
        held.update(fresh)
        bit //= 2
    parts, late = lax.optimization_barrier(([held[key] for key in range(peers)], late))
    return parts, hidden, late


def per_device(volume_field, volume_load, coefficient, surface_block, trace_cell, flux_cell):
    sides, first, second, lanes = volume_field.shape
    cells = first * second
    shape = Shape(sides, first, second, lanes)
    field = volume_field.reshape(sides * cells, lanes)
    load = volume_load.reshape(sides * cells, lanes)
    coef = coefficient.reshape(cells, lanes)

    slots = trace_cell.shape[3]
    trace, *outer = traces(
        shape, volume_field.reshape(sides, cells, lanes), trace_cell, min(32, sides)
    )
    firsts = first_faces(shape, field, surface_block, coef, slots)
    layers = len(shape.faces)
    count = len(shape.inner) + 1
    inner, held, tables = firsts[:count], firsts[count], firsts[count + 1 :]
    *inner, ends = inner
    along_col = swap_faces(shape.outer, outer)
    parts, inner, along_col = row_gather(trace, inner, along_col)
    along_row = swap_faces(shape.inner, inner)
    recv, ends = flux_sums(parts, held, along_row, ends)
    tips = swap_ends(shape, ends)

    (base,) = sweep_base(shape, field, load, tables, tips)
    current, *faces, ends, phi, surface_flux = sweep_finish(
        shape, base, tables, along_col + along_row, flux_cell=flux_cell, recv=recv
    )
    halos, tips = swap_faces(shape.faces, faces), swap_ends(shape, ends)
    base, source = sweep_base(shape, current, load, tables, phi=phi, flux_cell=flux_cell)
    current, *faces, ends = sweep_finish(shape, base, tables, halos, tips)
    halos, tips = swap_faces(shape.faces, faces), swap_ends(shape, ends)
    (base,) = sweep_base(shape, current, source, tables)
    (current,) = sweep_finish(shape, base, tables, halos, tips, last=True)
    return current.reshape(volume_field.shape), surface_flux


def solution(mesh):
    in_specs = (
        P(None, "row", "col", "gz"),
        P(None, "row", "col", "gz"),
        P("row", "col", "gz"),
        P("row", "col"),
        P("row", "col", "gz", None),
        P("row", "col", "gz", None),
    )
    out_specs = (P(None, "row", "col", "gz"), P("gz", ("row", "col")))
    return jax.shard_map(
        per_device, mesh=mesh, in_specs=in_specs, out_specs=out_specs, check_vma=False
    )
```

```python
import functools

import jax
import jax.numpy as jnp
from jax import lax
from jax.experimental import pallas as pl
from jax.experimental.pallas import tpu as pltpu
from jax.sharding import PartitionSpec as P

OMEGA = 0.8
BF = jnp.bfloat16
F32 = jnp.float32
WHOLE = pl.BlockSpec(memory_space=pltpu.VMEM)


def aligned(start, unit):
    return start if isinstance(start, int) else pl.multiple_of(start, unit)


def iota(shape, dim):
    return lax.broadcasted_iota(jnp.int32, shape, dim)


def dot(a, b):
    return jnp.dot(a, b, preferred_element_type=F32)


def dot_nt(a, b):
    return lax.dot_general(a, b, (((1,), (1,)), ((), ())), preferred_element_type=F32)


FACES_MIB = 50
TRACE_MIB = 52


def params(mebibytes=24):
    return pltpu.CompilerParams(vmem_limit_bytes=mebibytes * 1024 * 1024)


def trace_kernel(shape, stride, block, field_ref, cell_ref, out_ref, *refs):
    *face_refs, field, cell_v, tall, near, place, picked, sems = refs
    sides, rows, lanes = field.shape
    slots = cell_ref.shape[3]
    per_row = lanes // stride
    width = near.shape[0]
    parts = slots // width
    cell_copy = pltpu.make_async_copy(cell_ref, cell_v, sems.at[sides // block])
    cell_copy.start()
    copies = []
    for step in range(sides // block):
        span = pl.ds(step * block, block)
        copies.append(pltpu.make_async_copy(field_ref.at[span], field.at[span], sems.at[step]))
        copies[-1].start()

    cell_copy.wait()
    cell = cell_v[0, 0]
    run = cell // stride
    digit = jnp.zeros_like(cell)
    for part in range(parts):
        digit = jnp.where(run // width == part, (cell % stride) * stride**part, digit)
    hit = iota((width, slots), 0) == run % width
    near[...] = hit.astype(BF)
    digits = jnp.sum(jnp.where(hit, digit.astype(F32), 0.0), axis=1, keepdims=True)
    digits = jnp.broadcast_to(digits, (width, 128)).T[0:8].astype(jnp.int32)
    first = iota((8, width), 1) % per_row * stride
    for part in range(parts):
        place[:, part * width : (part + 1) * width] = first + digits // stride**part % stride

    pitch = rows + 1
    together = 128 // per_row
    group = iota((8, 128), 1) // per_row
    for step in range(sides // block):
        copies[step].wait()
        span = field[step * block : (step + 1) * block]
        for side in range(block):
            start = side * pitch
            tall[step, start : start + rows, :] = span[side].astype(F32)
        cut_faces(shape, shape.outer, step * block, block, tall.at[step], face_refs, pitch)

        for batch in range(block // 8):
            for tile in range(rows // together):
                cols = slice(tile * 128, (tile + 1) * 128)
                where = place[:, cols]
                found = None
                for row in range(together):
                    start = batch * 8 * pitch + tile * together + row
                    line = tall[step, pl.ds(start, 8, stride=pitch), :]
                    line = jnp.take_along_axis(line, where, axis=1)
                    found = line if found is None else jnp.where(group == row, line, found)
                at = step * block + batch * 8
                picked[at : at + 8, cols] = found

    total = jnp.zeros((sides, slots), F32)
    for part in range(parts):
        sorted_runs = picked[:, part * width : (part + 1) * width].astype(BF)
        total = jnp.where(run // width == part, dot(sorted_runs, near[...]), total)
    out_ref[...] = total.T.astype(BF)


def traces(shape, field, trace_cell, block):
    sides, rows, lanes = field.shape
    slots = trace_cell.shape[3]
    stride = rows * lanes // slots
    width = min(slots, 256)
    hbm = pl.BlockSpec(memory_space=pltpu.HBM)
    return pl.pallas_call(
        functools.partial(trace_kernel, shape, stride, block),
        in_specs=[hbm, hbm],
        out_specs=[WHOLE] * (1 + len(shape.outer)),
        out_shape=[jax.ShapeDtypeStruct((slots, sides), BF)] + face_shapes(shape, shape.outer),
        scratch_shapes=[
            pltpu.VMEM(field.shape, BF),
            pltpu.VMEM(trace_cell.shape, jnp.int32),
            pltpu.VMEM((sides // block, block * (rows + 1), lanes), F32),
            pltpu.VMEM((width, slots), BF),
            pltpu.VMEM((8, slots), jnp.int32),
            pltpu.VMEM((sides, slots), F32),
            pltpu.SemaphoreType.DMA((sides // block + 1,)),
        ],
        compiler_params=params(TRACE_MIB),
        cost_estimate=pl.CostEstimate(
            flops=4 * sides * rows * lanes * 128, bytes_accessed=field.size * 2, transcendentals=0
        ),
    )(field, trace_cell)


def fetch_columns(block_ref, held, sems, slots):
    me, group, gzs = lax.axis_index("row"), lax.axis_index("gz"), lax.axis_size("gz")
    copies = []
    for key in range(held.shape[0]):
        start = pl.multiple_of((jnp.bitwise_xor(me, key) * gzs + group) * slots, slots)
        copies.append(
            pltpu.make_async_copy(block_ref.at[:, pl.ds(start, slots)], held.at[key], sems.at[key])
        )
        copies[-1].start()
    return copies


def surface_kernel(halves, *refs):
    ins, total = refs[:-1], refs[-1]
    outs = ins[len(ins) - halves :]
    *parts, held = ins[: len(ins) - halves]
    value = None
    for key, part in enumerate(parts):
        term = dot(held[key], part[...])
        value = term if value is None else value + term
    if halves == 1:
        outs[0][...] = value
        return
    total[...] = value
    count = outs[0].shape[0]
    mine = lax.axis_index("col")
    for key, out in enumerate(outs):
        out[...] = total[pl.ds(pl.multiple_of((mine ^ key) * count, 8), count), :]


def surface(parts, held, halves):
    sides = parts[0].shape[1]
    lines = held.shape[1]
    return pl.pallas_call(
        functools.partial(surface_kernel, halves),
        in_specs=[WHOLE] * (len(parts) + 1),
        out_specs=[WHOLE] * halves,
        out_shape=[jax.ShapeDtypeStruct((lines // halves, sides), F32)] * halves,
        scratch_shapes=[pltpu.VMEM((lines, sides), F32)],
        compiler_params=params(),
        cost_estimate=pl.CostEstimate(
            flops=2 * sides * held.size, bytes_accessed=2 * held.size, transcendentals=0
        ),
    )(*parts, held)


def share_kernel(peers, mine_ref, other_ref, *refs):
    *outs, total, turned = refs
    total[...] = mine_ref[...] + other_ref[...]
    turned[...] = total[...].T
    lines, sides = total.shape
    group = lax.axis_index("gz")
    for key, out in enumerate(outs):
        peer = group ^ key
        rows, some = lines // peers, sides // peers
        out[:rows, :] = total[pl.ds(pl.multiple_of(peer * rows, 8), rows), :]
        out[rows:, :] = turned[pl.ds(pl.multiple_of(peer * some, 8), some), :]


def shares(mine, other):
    peers = lax.axis_size("gz")
    lines, sides = mine.shape
    out = jax.ShapeDtypeStruct(((lines + sides) // peers, sides), F32)
    return pl.pallas_call(
        functools.partial(share_kernel, peers),
        in_specs=[WHOLE] * 2,
        out_specs=[WHOLE] * peers,
        out_shape=[out] * peers,
        scratch_shapes=[pltpu.VMEM((lines, sides), F32), pltpu.VMEM((sides, lines), F32)],
        compiler_params=params(),
        cost_estimate=pl.CostEstimate(
            flops=lines * sides, bytes_accessed=16 * lines * sides, transcendentals=0
        ),
    )(mine, other)


def flux_sums(parts, held, late, after):
    cols, gzs = lax.axis_size("col"), lax.axis_size("gz")
    sides = parts[0].shape[1]
    lines = held.shape[1]
    if cols == 2 and gzs & (gzs - 1) == 0 and lines // cols == sides and sides // gzs % 8 == 0:
        mine, other = surface(parts, held, 2)
        mine, other, after = lax.optimization_barrier((mine, other, after))
        other = lax.ppermute(other, "col", [(0, 1), (1, 0)])
        other, late = lax.optimization_barrier((other, late))
        sent = shares(mine, other)
        recv = [sent[0]]
        for key in range(1, gzs):
            recv.append(lax.ppermute(sent[key], "gz", [(i, i ^ key) for i in range(gzs)]))
        return recv, after
    (total,) = surface(parts, held, 1)
    rows = lax.psum_scatter(total, "col", scatter_dimension=0, tiled=True)
    owned = lax.psum_scatter(rows, "gz", scatter_dimension=0, tiled=True)
    flux = lax.psum_scatter(rows.T, "gz", scatter_dimension=0, tiled=True)
    flux = jnp.pad(flux, ((0, 0), (0, sides - flux.shape[1])))
    return [jnp.concatenate([owned, flux], axis=0)], after


def turns(axis):
    return 1 if lax.axis_size(axis) == 2 else 2


def partner(index, turn):
    return jnp.where(index % 2 == turn, index + 1, index - 1)


def has_neighbour(axis, turn):
    other = partner(lax.axis_index(axis), turn)
    return (other >= 0) & (other < lax.axis_size(axis))


def swap(value, axis, turn):
    axes = ("row", "col", "gz")
    sizes = [lax.axis_size(name) for name in axes]
    along = axes.index(axis)
    spare = 0 if axis == "gz" else 2
    pairs = []
    for r in range(sizes[0]):
        for c in range(sizes[1]):
            for g in range(sizes[2]):
                here = [r, c, g]
                there = [r, c, g]
                there[along] += 1 if here[along] % 2 == turn else -1
                if not 0 <= there[along] < sizes[along]:
                    there[along] = here[along]
                    if here[spare] ^ 1 < sizes[spare]:
                        there[spare] ^= 1
                flat = [(at[0] * sizes[1] + at[1]) * sizes[2] + at[2] for at in (here, there)]
                pairs.append(tuple(flat))
    return lax.ppermute(value, axes, pairs)


class Shape:
    def __init__(self, sides, first, second, lanes):
        self.sides, self.x, self.y, self.lanes = sides, first, second, lanes
        self.cells = first * second
        self.chunk = max(1, 128 // self.cells)
        self.rows = self.chunk * self.cells
        self.block = min(sides, 32)
        self.half = self.block // 2
        self.half_rows = self.half * self.cells
        self.outer = [("col", i) for i in range(turns("col"))]
        self.inner = [("row", i) for i in reversed(range(turns("row")))]
        self.faces = self.outer + self.inner
        self.ends = turns("gz")

    def face_len(self, face):
        return self.y if face[0] == "row" else self.x

    def halo_rows(self):
        return sum(self.chunk * self.face_len(face) for face in self.faces)

    def edge(self, face):
        axis, turn = face
        last = (self.x if axis == "row" else self.y) - 1
        return jnp.where(lax.axis_index(axis) % 2 == turn, last, 0)


def halo_place(shape):
    dims = (shape.rows, shape.halo_rows())
    row, col = iota(dims, 0), iota(dims, 1)
    side, cell = row // shape.cells, row % shape.cells
    x, y = cell // shape.y, cell % shape.y
    hit, base = None, 0
    for face in shape.faces:
        length = shape.face_len(face)
        along, across = (y, x) if face[0] == "row" else (x, y)
        place = (across == shape.edge(face)) & (col - base == side * length + along)
        place = place & has_neighbour(*face)
        hit = place if hit is None else hit | place
        base += shape.chunk * length
    return hit.astype(BF)


def z_mask(shape, count):
    dims = (count * shape.cells, 2 * shape.cells)
    return iota(dims, 1) % shape.cells == iota(dims, 0) % shape.cells


def twice(matrix):
    zero = jnp.zeros_like(matrix)
    return jnp.concatenate(
        [jnp.concatenate([matrix, zero], axis=1), jnp.concatenate([zero, matrix], axis=1)], axis=0
    )


def beside(values):
    half = values.shape[0] // 2
    return jnp.concatenate([values[:half], values[half:]], axis=1)


def build_out(shape, ends_m, rsum):
    dims = (shape.lanes, 2 * shape.cells)
    edge = jnp.where(iota(dims, 1) < shape.cells, 0, shape.lanes - 1)
    ends_m[...] = twice((iota(dims, 0) == edge).astype(F32)).astype(BF)
    dims = rsum.shape
    rsum[...] = (iota(dims, 1) // shape.cells == iota(dims, 0)).astype(BF)


def cut_faces(shape, faces, at, block, tall, face_refs, pitch=None):
    for face, ref in zip(faces, face_refs):
        length, edge = shape.face_len(face), shape.edge(face)
        lines = []
        for side in range(block):
            start = side * (pitch or shape.cells)
            if face[0] == "row":
                lines.append(tall[pl.ds(aligned(start + edge * length, 8), length), :])
            else:
                lines.append(tall[pl.ds(start + edge, length, stride=shape.y), :])
        span = slice(at * length, (at + block) * length)
        ref[span, :] = jnp.concatenate(lines, axis=0).astype(BF)


def cut_ends(shape, at, values, z_ref, ends_m, rsum):
    mask = jnp.concatenate([z_mask(shape, shape.half)] * 2, axis=1)
    tips = jnp.where(mask, dot(beside(values), ends_m[...]), 0.0).astype(BF)
    tips = dot(rsum[...], tips)[: shape.half]
    tips = jnp.concatenate([tips[:, : 2 * shape.cells], tips[:, 2 * shape.cells :]], axis=0)
    z_ref[at : at + shape.block, :] = tips.astype(BF)


def build_tables(shape, coef_ref, weight, near_m, line_m, ends_m, rsum):
    cells, lanes = shape.cells, shape.lanes
    weight[...] = jnp.concatenate([OMEGA / (6.0 + coef_ref[...])] * shape.chunk, axis=0)
    dims = (shape.rows, shape.rows)
    row, col = iota(dims, 0), iota(dims, 1)
    x, y = row % cells // shape.y, row % shape.y
    x2, y2 = col % cells // shape.y, col % shape.y
    near = ((x == x2) & (jnp.abs(y - y2) == 1)) | ((y == y2) & (jnp.abs(x - x2) == 1))
    near_m[:, : shape.rows] = (near & (row // cells == col // cells)).astype(BF)
    near_m[:, shape.rows :] = halo_place(shape)
    dims = (lanes, lanes)
    line = (jnp.abs(iota(dims, 0) - iota(dims, 1)) == 1).astype(F32)
    line_m[: 2 * lanes, :] = twice(line).astype(BF)
    dims = (2 * cells, lanes)
    edge = jnp.where(iota(dims, 0) < cells, lanes - 1, 0)
    line_m[2 * lanes :, :] = twice((iota(dims, 1) == edge).astype(F32)).astype(BF)
    build_out(shape, ends_m, rsum)


def table_shapes(shape):
    lanes, cells = shape.lanes, shape.cells
    return [
        jax.ShapeDtypeStruct((shape.rows, lanes), F32),
        jax.ShapeDtypeStruct((shape.rows, shape.rows + shape.halo_rows()), BF),
        jax.ShapeDtypeStruct((2 * lanes + 4 * cells, 2 * lanes), BF),
        jax.ShapeDtypeStruct((2 * lanes, 4 * cells), BF),
        jax.ShapeDtypeStruct((max(8, shape.half), shape.half_rows), BF),
    ]


def faces_kernel(shape, slots, field_ref, block_ref, coef_ref, *refs):
    refs = list(refs)
    face_refs = [refs.pop(0) for _ in shape.inner]
    z_ref, held, *tables, field, tall, sems, field_sems = refs
    size = shape.block * shape.cells
    steps = shape.sides // shape.block
    copies = []
    for step in range(steps):
        span = pl.ds(step * size, size)
        copies.append(
            pltpu.make_async_copy(field_ref.at[span], field.at[span], field_sems.at[step])
        )
        copies[-1].start()
    columns = fetch_columns(block_ref, held, sems, slots)
    build_tables(shape, coef_ref, *tables)
    ends_m, rsum = tables[-2:]
    for step in range(steps):
        copies[step].wait()
        values = field[step * size : (step + 1) * size, :]
        tall[step] = values.astype(F32)
        cut_faces(shape, shape.inner, step * shape.block, shape.block, tall.at[step], face_refs)
        cut_ends(shape, step * shape.block, values, z_ref, ends_m, rsum)
    for copy in columns:
        copy.wait()


def face_shapes(shape, faces):
    return [
        jax.ShapeDtypeStruct((shape.sides * shape.face_len(face), shape.lanes), BF)
        for face in faces
    ]


def first_faces(shape, field, block, coef, slots):
    peers = lax.axis_size("row")
    steps = shape.sides // shape.block
    shapes = face_shapes(shape, shape.inner)
    shapes.append(jax.ShapeDtypeStruct((shape.sides, 2 * shape.cells), BF))
    shapes.append(jax.ShapeDtypeStruct((peers, block.shape[0], slots), BF))
    shapes += table_shapes(shape)
    hbm = pl.BlockSpec(memory_space=pltpu.HBM)
    return pl.pallas_call(
        functools.partial(faces_kernel, shape, slots),
        in_specs=[hbm, hbm, WHOLE],
        out_specs=[WHOLE] * len(shapes),
        out_shape=shapes,
        scratch_shapes=[
            pltpu.VMEM(field.shape, BF),
            pltpu.VMEM((steps, shape.block * shape.cells, shape.lanes), F32),
            pltpu.SemaphoreType.DMA((peers,)),
            pltpu.SemaphoreType.DMA((steps,)),
        ],
        compiler_params=params(FACES_MIB),
        cost_estimate=pl.CostEstimate(
            flops=field.size * 128, bytes_accessed=4 * field.size, transcendentals=0
        ),
    )(field, block, coef)


def expand(shape, lines, where):
    rows = []
    for side in range(shape.block):
        line = jnp.broadcast_to(lines[side : side + 1], where.shape)
        rows.append(jnp.where(where, line, 0.0))
    return beside(jnp.concatenate(rows, axis=0).astype(BF))


def halo_ends(shape, end_refs, sides):
    even = lax.axis_index("gz") % 2 == 0
    filled = (iota((shape.block, 2 * shape.cells), 1) < shape.cells) == even
    zs = 0.0
    for turn in range(shape.ends):
        wanted = (filled == (turn == 0)) & has_neighbour("gz", turn)
        zs = jnp.where(wanted, end_refs[-1 - turn][sides, :].astype(F32), zs)
    return expand(shape, zs, z_mask(shape, 1))


def flux_width(slots):
    return (2 * slots + 127) // 128 * 128


def build_cells(shape, cell_ref, cell_m):
    slots = cell_ref.shape[3]
    width = flux_width(slots)
    cell = cell_ref[0, 0]
    none = jnp.full((1, width - 2 * slots), -shape.lanes, jnp.int32)
    cell = jnp.concatenate([cell, cell, none], axis=1)
    place = (iota((shape.lanes, width), 0) == cell % shape.lanes).astype(F32)
    cell_m[...] = twice(place).astype(BF)
    return iota((shape.cells, width), 0) == cell // shape.lanes


def base_kernel(shape, ends, with_flux, *refs):
    refs = list(refs)
    take = lambda count: [refs.pop(0) for _ in range(count)]
    field_ref, load_ref, weight, near_m, line_m = take(5)
    end_refs = take(ends)
    if with_flux:
        phi, cell_ref = take(2)
    (base_ref,) = take(1)
    if with_flux:
        (source_ref,) = take(1)
    (lines,) = take(1)
    if with_flux:
        cell_m, placed = take(2)
        cell_mask = build_cells(shape, cell_ref, cell_m)

    cells, lanes = shape.cells, shape.lanes
    weights = weight[...]
    for step in range(shape.sides // shape.block):
        sides = slice(step * shape.block, (step + 1) * shape.block)
        at = step * shape.block * cells
        left = beside(field_ref[at : at + shape.block * cells, :])
        if ends:
            left = jnp.concatenate([left, halo_ends(shape, end_refs, sides)], axis=1)
        lines[step] = dot(left, line_m[: left.shape[1], :])
        if with_flux:
            placed[step] = dot_nt(expand(shape, phi[sides, :], cell_mask), cell_m[...])
        for index in range(shape.half // shape.chunk):
            offset = index * shape.rows
            here = slice(offset, offset + shape.rows)
            spans = [
                slice(at + start, at + start + shape.rows)
                for start in (offset, offset + shape.half_rows)
            ]
            stack = jnp.concatenate([field_ref[span, :] for span in spans], axis=1)
            near = dot(near_m[:, : shape.rows], stack) + lines[step, here, :]
            for part, span in enumerate(spans):
                cols = slice(part * lanes, (part + 1) * lanes)
                source = load_ref[span, :].astype(F32)
                if with_flux:
                    source = source + placed[step, here, cols]
                    source_ref[span, :] = source.astype(BF)
                centre = field_ref[span, :].astype(F32)
                base_ref[span, :] = (1.0 - OMEGA) * centre + weights * (source + near[:, cols])


def sweep_base(shape, field, load, tables, ends=(), phi=None, flux_cell=None):
    steps = shape.sides // shape.block
    half = (steps, shape.half_rows, 2 * shape.lanes)
    operands = [field, load, *tables[:3], *ends]
    shapes = [jax.ShapeDtypeStruct(field.shape, F32)]
    scratch = [pltpu.VMEM(half, F32)]
    if phi is not None:
        operands += [phi, flux_cell]
        shapes.append(jax.ShapeDtypeStruct(field.shape, BF))
        scratch.append(pltpu.VMEM((2 * shape.lanes, 2 * phi.shape[1]), BF))
        scratch.append(pltpu.VMEM(half, F32))
    return pl.pallas_call(
        functools.partial(base_kernel, shape, len(ends), phi is not None),
        in_specs=[WHOLE] * len(operands),
        out_specs=[WHOLE] * len(shapes),
        out_shape=shapes,
        scratch_shapes=scratch,
        compiler_params=params(),
        cost_estimate=pl.CostEstimate(
            flops=6 * field.size * 128, bytes_accessed=8 * field.size, transcendentals=0
        ),
    )(*operands)


def finish_kernel(shape, ends, recvs, last, *refs):
    with_flux = recvs > 0
    refs = list(refs)
    take = lambda count: [refs.pop(0) for _ in range(count)]
    base_ref, weight, near_m, line_m, ends_m, rsum = take(6)
    halo_refs = take(len(shape.faces))
    end_refs = take(ends)
    if with_flux:
        (cell_ref,) = take(1)
        recv_refs = take(recvs)
    (out_ref,) = take(1)
    if not last:
        face_refs = take(len(shape.faces))
        (z_ref,) = take(1)
    if with_flux:
        phi, flux_ref = take(2)
    if last:
        result_ref = out_ref
        out_ref, out_sems = take(2)
    else:
        (tall,) = take(1)
    if ends:
        (lines,) = take(1)
    if with_flux:
        cell_m, placed = take(2)

    cells, lanes = shape.cells, shape.lanes

    if with_flux:
        slots = cell_ref.shape[3]
        cell_mask = build_cells(shape, cell_ref, cell_m)
        owned = recv_refs[0][...]
        for ref in recv_refs[1:]:
            owned = owned + ref[...]
        flux_ref[...] = owned[slots:, : flux_ref.shape[1]]
        owned = owned[:slots]
        high = owned.astype(BF).astype(F32)
        none = jnp.zeros((phi.shape[1] - 2 * slots, phi.shape[0]), F32)
        phi[...] = jnp.concatenate([high, owned - high, none], axis=0).T

    weights = weight[...]

    def work(step):
        at = step * shape.block
        sides = slice(at, at + shape.block)
        if ends:
            lines[step] = dot(halo_ends(shape, end_refs, sides), line_m[2 * lanes :, :])
        if with_flux:
            placed[step] = dot_nt(expand(shape, phi[sides, :], cell_mask), cell_m[...])
        for index in range(shape.half // shape.chunk):
            offset = index * shape.rows
            starts = (offset, offset + shape.half_rows)
            stacks = []
            for start in starts:
                stack = []
                for face, ref in zip(shape.faces, halo_refs):
                    length = shape.face_len(face)
                    first = at * length + start // cells * length
                    stack.append(ref[first : first + shape.chunk * length, :])
                stacks.append(jnp.concatenate(stack, axis=0))
            near = dot(near_m[:, shape.rows :], jnp.concatenate(stacks, axis=1))
            if ends:
                near = near + lines[step, offset : offset + shape.rows, :]
            if with_flux:
                near = near + placed[step, offset : offset + shape.rows, :]
            for part, start in enumerate(starts):
                rows = slice(at * cells + start, at * cells + start + shape.rows)
                fresh = base_ref[rows, :] + weights * near[:, part * lanes : (part + 1) * lanes]
                out_ref[rows, :] = fresh.astype(BF)
                if not last:
                    tall[step, start : start + shape.rows, :] = fresh

    def emit(step):
        at, size = step * shape.block, shape.block * cells
        fresh = out_ref[at * cells : at * cells + size, :]
        cut_faces(shape, shape.faces, at, shape.block, tall.at[step], face_refs)
        cut_ends(shape, at, fresh, z_ref, ends_m, rsum)

    steps = shape.sides // shape.block
    copies = []
    for step in range(steps):
        work(step)
        if last:
            span = pl.ds(step * shape.block * cells, shape.block * cells)
            copies.append(
                pltpu.make_async_copy(out_ref.at[span], result_ref.at[span], out_sems.at[step])
            )
            copies[-1].start()
        elif step > 0:
            emit(step - 1)
    for copy in copies:
        copy.wait()
    if not last:
        emit(steps - 1)


def sweep_finish(shape, base, tables, halos, ends=(), flux_cell=None, recv=(), last=False):
    lanes, cells = shape.lanes, shape.cells
    steps = shape.sides // shape.block
    half = (steps, shape.half_rows, 2 * lanes)
    operands = [base, *tables, *halos, *ends]
    out_shapes = [jax.ShapeDtypeStruct(base.shape, BF)]
    if last:
        scratch = [pltpu.VMEM(base.shape, BF), pltpu.SemaphoreType.DMA((steps,))]
    else:
        out_shapes += face_shapes(shape, shape.faces)
        out_shapes.append(jax.ShapeDtypeStruct((shape.sides, 2 * cells), BF))
        scratch = [pltpu.VMEM((steps, shape.block * cells, lanes), F32)]
    if ends:
        scratch.append(pltpu.VMEM(half, F32))
    if recv:
        slots = flux_cell.shape[3]
        operands += [flux_cell, *recv]
        out_shapes += [
            jax.ShapeDtypeStruct((shape.sides, flux_width(slots)), F32),
            jax.ShapeDtypeStruct((recv[0].shape[0] - slots, slots * lax.axis_size("gz")), F32),
        ]
        scratch += [
            pltpu.VMEM((2 * lanes, 2 * flux_width(slots)), BF),
            pltpu.VMEM(half, F32),
        ]
    out_specs = [WHOLE] * len(out_shapes)
    if last:
        out_specs = [pl.BlockSpec(memory_space=pltpu.HBM)]
    return pl.pallas_call(
        functools.partial(finish_kernel, shape, len(ends), len(recv), last),
        in_specs=[WHOLE] * len(operands),
        out_specs=out_specs,
        out_shape=out_shapes,
        scratch_shapes=scratch,
        compiler_params=params(),
        cost_estimate=pl.CostEstimate(
            flops=4 * base.size * 128, bytes_accessed=8 * base.size, transcendentals=0
        ),
    )(*operands)


def swap_faces(faces, values):
    return [swap(value, *face) for face, value in zip(faces, values)]


def swap_ends(shape, ends):
    return [swap(ends, "gz", turn) for turn in reversed(range(shape.ends))]


def row_gather(trace, hidden, late):
    peers = lax.axis_size("row")
    held = {0: trace}
    bit = peers // 2
    while bit:
        pairs = [(i, i ^ bit) for i in range(peers)]
        fresh = {key ^ bit: lax.ppermute(held[key], "row", pairs) for key in sorted(held, reverse=True)}
        if bit == peers // 2:
            fresh, hidden = lax.optimization_barrier((fresh, hidden))
        held.update(fresh)
        bit //= 2
    parts, late = lax.optimization_barrier(([held[key] for key in range(peers)], late))
    return parts, hidden, late


def per_device(volume_field, volume_load, coefficient, surface_block, trace_cell, flux_cell):
    sides, first, second, lanes = volume_field.shape
    cells = first * second
    shape = Shape(sides, first, second, lanes)
    field = volume_field.reshape(sides * cells, lanes)
    load = volume_load.reshape(sides * cells, lanes)
    coef = coefficient.reshape(cells, lanes)

    slots = trace_cell.shape[3]
    trace, *outer = traces(
        shape, volume_field.reshape(sides, cells, lanes), trace_cell, min(32, sides)
    )
    firsts = first_faces(shape, field, surface_block, coef, slots)
    layers = len(shape.faces)
    count = len(shape.inner) + 1
    inner, held, tables = firsts[:count], firsts[count], firsts[count + 1 :]
    *inner, ends = inner
    along_col = swap_faces(shape.outer, outer)
    parts, inner, along_col = row_gather(trace, inner, along_col)
    along_row = swap_faces(shape.inner, inner)
    recv, ends = flux_sums(parts, held, along_row, ends)
    tips = swap_ends(shape, ends)

    (base,) = sweep_base(shape, field, load, tables, tips)
    current, *faces, ends, phi, surface_flux = sweep_finish(
        shape, base, tables, along_col + along_row, flux_cell=flux_cell, recv=recv
    )
    halos, tips = swap_faces(shape.faces, faces), swap_ends(shape, ends)
    base, source = sweep_base(shape, current, load, tables, phi=phi, flux_cell=flux_cell)
    current, *faces, ends = sweep_finish(shape, base, tables, halos, tips)
    halos, tips = swap_faces(shape.faces, faces), swap_ends(shape, ends)
    (base,) = sweep_base(shape, current, source, tables)
    (current,) = sweep_finish(shape, base, tables, halos, tips, last=True)
    return current.reshape(volume_field.shape), surface_flux


def solution(mesh):
    in_specs = (
        P(None, "row", "col", "gz"),
        P(None, "row", "col", "gz"),
        P("row", "col", "gz"),
        P("row", "col"),
        P("row", "col", "gz", None),
        P("row", "col", "gz", None),
    )
    out_specs = (P(None, "row", "col", "gz"), P("gz", ("row", "col")))
    return jax.shard_map(
        per_device, mesh=mesh, in_specs=in_specs, out_specs=out_specs, check_vma=False
    )
```

```python
import functools

import jax
import jax.numpy as jnp
from jax import lax
from jax.experimental import pallas as pl
from jax.experimental.pallas import tpu as pltpu
from jax.sharding import PartitionSpec as P

OMEGA = 0.8
BF = jnp.bfloat16
F32 = jnp.float32
WHOLE = pl.BlockSpec(memory_space=pltpu.VMEM)


def aligned(start, unit):
    return start if isinstance(start, int) else pl.multiple_of(start, unit)


def iota(shape, dim):
    return lax.broadcasted_iota(jnp.int32, shape, dim)


def dot(a, b):
    return jnp.dot(a, b, preferred_element_type=F32)


def dot_nt(a, b):
    return lax.dot_general(a, b, (((1,), (1,)), ((), ())), preferred_element_type=F32)


FACES_MIB = 50
TRACE_MIB = 52


def params(mebibytes=24):
    return pltpu.CompilerParams(vmem_limit_bytes=mebibytes * 1024 * 1024)


def trace_kernel(shape, stride, block, field_ref, cell_ref, out_ref, *refs):
    *face_refs, field, cell_v, tall, near, place, picked, sems = refs
    sides, rows, lanes = field.shape
    slots = cell_ref.shape[3]
    per_row = lanes // stride
    width = near.shape[0]
    parts = slots // width
    cell_copy = pltpu.make_async_copy(cell_ref, cell_v, sems.at[sides // block])
    cell_copy.start()
    copies = []
    for step in range(sides // block):
        span = pl.ds(step * block, block)
        copies.append(pltpu.make_async_copy(field_ref.at[span], field.at[span], sems.at[step]))
        copies[-1].start()

    cell_copy.wait()
    cell = cell_v[0, 0]
    run = cell // stride
    digit = jnp.zeros_like(cell)
    for part in range(parts):
        digit = jnp.where(run // width == part, (cell % stride) * stride**part, digit)
    hit = iota((width, slots), 0) == run % width
    near[...] = hit.astype(BF)
    digits = jnp.sum(jnp.where(hit, digit.astype(F32), 0.0), axis=1, keepdims=True)
    digits = jnp.broadcast_to(digits, (width, 128)).T[0:8].astype(jnp.int32)
    first = iota((8, width), 1) % per_row * stride
    for part in range(parts):
        place[:, part * width : (part + 1) * width] = first + digits // stride**part % stride

    pitch = rows + 1
    together = 128 // per_row
    group = iota((8, 128), 1) // per_row
    for step in range(sides // block):
        copies[step].wait()
        span = field[step * block : (step + 1) * block]
        for side in range(block):
            start = side * pitch
            tall[step, start : start + rows, :] = span[side].astype(F32)
        cut_faces(shape, shape.outer, step * block, block, tall.at[step], face_refs, pitch)

        for batch in range(block // 8):
            for tile in range(rows // together):
                cols = slice(tile * 128, (tile + 1) * 128)
                where = place[:, cols]
                found = None
                for row in range(together):
                    start = batch * 8 * pitch + tile * together + row
                    line = tall[step, pl.ds(start, 8, stride=pitch), :]
                    line = jnp.take_along_axis(line, where, axis=1)
                    found = line if found is None else jnp.where(group == row, line, found)
                at = step * block + batch * 8
                picked[at : at + 8, cols] = found

    total = jnp.zeros((sides, slots), F32)
    for part in range(parts):
        sorted_runs = picked[:, part * width : (part + 1) * width].astype(BF)
        total = jnp.where(run // width == part, dot(sorted_runs, near[...]), total)
    out_ref[...] = total.T.astype(BF)


def traces(shape, field, trace_cell, block):
    sides, rows, lanes = field.shape
    slots = trace_cell.shape[3]
    stride = rows * lanes // slots
    width = min(slots, 256)
    hbm = pl.BlockSpec(memory_space=pltpu.HBM)
    return pl.pallas_call(
        functools.partial(trace_kernel, shape, stride, block),
        in_specs=[hbm, hbm],
        out_specs=[WHOLE] * (1 + len(shape.outer)),
        out_shape=[jax.ShapeDtypeStruct((slots, sides), BF)] + face_shapes(shape, shape.outer),
        scratch_shapes=[
            pltpu.VMEM(field.shape, BF),
            pltpu.VMEM(trace_cell.shape, jnp.int32),
            pltpu.VMEM((sides // block, block * (rows + 1), lanes), F32),
            pltpu.VMEM((width, slots), BF),
            pltpu.VMEM((8, slots), jnp.int32),
            pltpu.VMEM((sides, slots), F32),
            pltpu.SemaphoreType.DMA((sides // block + 1,)),
        ],
        compiler_params=params(TRACE_MIB),
        cost_estimate=pl.CostEstimate(
            flops=4 * sides * rows * lanes * 128, bytes_accessed=field.size * 2, transcendentals=0
        ),
    )(field, trace_cell)


def fetch_columns(block_ref, held, sems, slots):
    me, group, gzs = lax.axis_index("row"), lax.axis_index("gz"), lax.axis_size("gz")
    copies = []
    for key in range(held.shape[0]):
        start = pl.multiple_of((jnp.bitwise_xor(me, key) * gzs + group) * slots, slots)
        copies.append(
            pltpu.make_async_copy(block_ref.at[:, pl.ds(start, slots)], held.at[key], sems.at[key])
        )
        copies[-1].start()
    return copies


def surface_kernel(halves, *refs):
    ins, total = refs[:-1], refs[-1]
    outs = ins[len(ins) - halves :]
    *parts, held = ins[: len(ins) - halves]
    value = None
    for key, part in enumerate(parts):
        term = dot(held[key], part[...])
        value = term if value is None else value + term
    if halves == 1:
        outs[0][...] = value
        return
    total[...] = value
    count = outs[0].shape[0]
    mine = lax.axis_index("col")
    for key, out in enumerate(outs):
        out[...] = total[pl.ds(pl.multiple_of((mine ^ key) * count, 8), count), :]


def surface(parts, held, halves):
    sides = parts[0].shape[1]
    lines = held.shape[1]
    return pl.pallas_call(
        functools.partial(surface_kernel, halves),
        in_specs=[WHOLE] * (len(parts) + 1),
        out_specs=[WHOLE] * halves,
        out_shape=[jax.ShapeDtypeStruct((lines // halves, sides), F32)] * halves,
        scratch_shapes=[pltpu.VMEM((lines, sides), F32)],
        compiler_params=params(),
        cost_estimate=pl.CostEstimate(
            flops=2 * sides * held.size, bytes_accessed=2 * held.size, transcendentals=0
        ),
    )(*parts, held)


def share_kernel(peers, mine_ref, other_ref, *refs):
    *outs, total, turned = refs
    total[...] = mine_ref[...] + other_ref[...]
    turned[...] = total[...].T
    lines, sides = total.shape
    group = lax.axis_index("gz")
    for key, out in enumerate(outs):
        peer = group ^ key
        rows, some = lines // peers, sides // peers
        out[:rows, :] = total[pl.ds(pl.multiple_of(peer * rows, 8), rows), :]
        out[rows:, :] = turned[pl.ds(pl.multiple_of(peer * some, 8), some), :]


def shares(mine, other):
    peers = lax.axis_size("gz")
    lines, sides = mine.shape
    out = jax.ShapeDtypeStruct(((lines + sides) // peers, sides), F32)
    return pl.pallas_call(
        functools.partial(share_kernel, peers),
        in_specs=[WHOLE] * 2,
        out_specs=[WHOLE] * peers,
        out_shape=[out] * peers,
        scratch_shapes=[pltpu.VMEM((lines, sides), F32), pltpu.VMEM((sides, lines), F32)],
        compiler_params=params(),
        cost_estimate=pl.CostEstimate(
            flops=lines * sides, bytes_accessed=16 * lines * sides, transcendentals=0
        ),
    )(mine, other)


def flux_sums(parts, held, late, after):
    cols, gzs = lax.axis_size("col"), lax.axis_size("gz")
    sides = parts[0].shape[1]
    lines = held.shape[1]
    if cols == 2 and gzs & (gzs - 1) == 0 and lines // cols == sides and sides // gzs % 8 == 0:
        mine, other = surface(parts, held, 2)
        mine, other, after = lax.optimization_barrier((mine, other, after))
        other = lax.ppermute(other, "col", [(0, 1), (1, 0)])
        other, late = lax.optimization_barrier((other, late))
        sent = shares(mine, other)
        recv = [sent[0]]
        for key in range(gzs - 1, 0, -1):
            recv.append(lax.ppermute(sent[key], "gz", [(i, i ^ key) for i in range(gzs)]))
        return recv, after
    (total,) = surface(parts, held, 1)
    rows = lax.psum_scatter(total, "col", scatter_dimension=0, tiled=True)
    owned = lax.psum_scatter(rows, "gz", scatter_dimension=0, tiled=True)
    flux = lax.psum_scatter(rows.T, "gz", scatter_dimension=0, tiled=True)
    flux = jnp.pad(flux, ((0, 0), (0, sides - flux.shape[1])))
    return [jnp.concatenate([owned, flux], axis=0)], after


def turns(axis):
    return 1 if lax.axis_size(axis) == 2 else 2


def partner(index, turn):
    return jnp.where(index % 2 == turn, index + 1, index - 1)


def has_neighbour(axis, turn):
    other = partner(lax.axis_index(axis), turn)
    return (other >= 0) & (other < lax.axis_size(axis))


def swap(value, axis, turn):
    axes = ("row", "col", "gz")
    sizes = [lax.axis_size(name) for name in axes]
    along = axes.index(axis)
    spare = 0 if axis == "gz" else 2
    pairs = []
    for r in range(sizes[0]):
        for c in range(sizes[1]):
            for g in range(sizes[2]):
                here = [r, c, g]
                there = [r, c, g]
                there[along] += 1 if here[along] % 2 == turn else -1
                if not 0 <= there[along] < sizes[along]:
                    there[along] = here[along]
                    if here[spare] ^ 1 < sizes[spare]:
                        there[spare] ^= 1
                flat = [(at[0] * sizes[1] + at[1]) * sizes[2] + at[2] for at in (here, there)]
                pairs.append(tuple(flat))
    return lax.ppermute(value, axes, pairs)


class Shape:
    def __init__(self, sides, first, second, lanes):
        self.sides, self.x, self.y, self.lanes = sides, first, second, lanes
        self.cells = first * second
        self.chunk = max(1, 128 // self.cells)
        self.rows = self.chunk * self.cells
        self.block = min(sides, 16)
        self.half = self.block // 2
        self.half_rows = self.half * self.cells
        self.outer = [("col", i) for i in range(turns("col"))]
        self.inner = [("row", i) for i in reversed(range(turns("row")))]
        self.faces = self.outer + self.inner
        self.ends = turns("gz")

    def face_len(self, face):
        return self.y if face[0] == "row" else self.x

    def halo_rows(self):
        return sum(self.chunk * self.face_len(face) for face in self.faces)

    def edge(self, face):
        axis, turn = face
        last = (self.x if axis == "row" else self.y) - 1
        return jnp.where(lax.axis_index(axis) % 2 == turn, last, 0)


def halo_place(shape):
    dims = (shape.rows, shape.halo_rows())
    row, col = iota(dims, 0), iota(dims, 1)
    side, cell = row // shape.cells, row % shape.cells
    x, y = cell // shape.y, cell % shape.y
    hit, base = None, 0
    for face in shape.faces:
        length = shape.face_len(face)
        along, across = (y, x) if face[0] == "row" else (x, y)
        place = (across == shape.edge(face)) & (col - base == side * length + along)
        place = place & has_neighbour(*face)
        hit = place if hit is None else hit | place
        base += shape.chunk * length
    return hit.astype(BF)


def z_mask(shape, count):
    dims = (count * shape.cells, 2 * shape.cells)
    return iota(dims, 1) % shape.cells == iota(dims, 0) % shape.cells


def twice(matrix):
    zero = jnp.zeros_like(matrix)
    return jnp.concatenate(
        [jnp.concatenate([matrix, zero], axis=1), jnp.concatenate([zero, matrix], axis=1)], axis=0
    )


def beside(values):
    half = values.shape[0] // 2
    return jnp.concatenate([values[:half], values[half:]], axis=1)


def build_out(shape, ends_m, rsum):
    dims = (shape.lanes, 2 * shape.cells)
    edge = jnp.where(iota(dims, 1) < shape.cells, 0, shape.lanes - 1)
    ends_m[...] = twice((iota(dims, 0) == edge).astype(F32)).astype(BF)
    dims = rsum.shape
    rsum[...] = (iota(dims, 1) // shape.cells == iota(dims, 0)).astype(BF)


def cut_faces(shape, faces, at, block, tall, face_refs, pitch=None):
    for face, ref in zip(faces, face_refs):
        length, edge = shape.face_len(face), shape.edge(face)
        lines = []
        for side in range(block):
            start = side * (pitch or shape.cells)
            if face[0] == "row":
                lines.append(tall[pl.ds(aligned(start + edge * length, 8), length), :])
            else:
                lines.append(tall[pl.ds(start + edge, length, stride=shape.y), :])
        span = slice(at * length, (at + block) * length)
        ref[span, :] = jnp.concatenate(lines, axis=0).astype(BF)


def cut_ends(shape, at, values, z_ref, ends_m, rsum):
    mask = jnp.concatenate([z_mask(shape, shape.half)] * 2, axis=1)
    tips = jnp.where(mask, dot(beside(values), ends_m[...]), 0.0).astype(BF)
    tips = dot(rsum[...], tips)[: shape.half]
    tips = jnp.concatenate([tips[:, : 2 * shape.cells], tips[:, 2 * shape.cells :]], axis=0)
    z_ref[at : at + shape.block, :] = tips.astype(BF)


def build_tables(shape, coef_ref, weight, near_m, line_m, ends_m, rsum):
    cells, lanes = shape.cells, shape.lanes
    weight[...] = jnp.concatenate([OMEGA / (6.0 + coef_ref[...])] * shape.chunk, axis=0)
    dims = (shape.rows, shape.rows)
    row, col = iota(dims, 0), iota(dims, 1)
    x, y = row % cells // shape.y, row % shape.y
    x2, y2 = col % cells // shape.y, col % shape.y
    near = ((x == x2) & (jnp.abs(y - y2) == 1)) | ((y == y2) & (jnp.abs(x - x2) == 1))
    near_m[:, : shape.rows] = (near & (row // cells == col // cells)).astype(BF)
    near_m[:, shape.rows :] = halo_place(shape)
    dims = (lanes, lanes)
    line = (jnp.abs(iota(dims, 0) - iota(dims, 1)) == 1).astype(F32)
    line_m[: 2 * lanes, :] = twice(line).astype(BF)
    dims = (2 * cells, lanes)
    edge = jnp.where(iota(dims, 0) < cells, lanes - 1, 0)
    line_m[2 * lanes :, :] = twice((iota(dims, 1) == edge).astype(F32)).astype(BF)
    build_out(shape, ends_m, rsum)


def table_shapes(shape):
    lanes, cells = shape.lanes, shape.cells
    return [
        jax.ShapeDtypeStruct((shape.rows, lanes), F32),
        jax.ShapeDtypeStruct((shape.rows, shape.rows + shape.halo_rows()), BF),
        jax.ShapeDtypeStruct((2 * lanes + 4 * cells, 2 * lanes), BF),
        jax.ShapeDtypeStruct((2 * lanes, 4 * cells), BF),
        jax.ShapeDtypeStruct((max(8, shape.half), shape.half_rows), BF),
    ]


def faces_kernel(shape, slots, field_ref, block_ref, coef_ref, *refs):
    refs = list(refs)
    face_refs = [refs.pop(0) for _ in shape.inner]
    z_ref, held, *tables, field, tall, sems, field_sems = refs
    size = shape.block * shape.cells
    steps = shape.sides // shape.block
    copies = []
    for step in range(steps):
        span = pl.ds(step * size, size)
        copies.append(
            pltpu.make_async_copy(field_ref.at[span], field.at[span], field_sems.at[step])
        )
        copies[-1].start()
    columns = fetch_columns(block_ref, held, sems, slots)
    build_tables(shape, coef_ref, *tables)
    ends_m, rsum = tables[-2:]
    for step in range(steps):
        copies[step].wait()
        values = field[step * size : (step + 1) * size, :]
        tall[step] = values.astype(F32)
        cut_faces(shape, shape.inner, step * shape.block, shape.block, tall.at[step], face_refs)
        cut_ends(shape, step * shape.block, values, z_ref, ends_m, rsum)
    for copy in columns:
        copy.wait()


def face_shapes(shape, faces):
    return [
        jax.ShapeDtypeStruct((shape.sides * shape.face_len(face), shape.lanes), BF)
        for face in faces
    ]


def first_faces(shape, field, block, coef, slots):
    peers = lax.axis_size("row")
    steps = shape.sides // shape.block
    shapes = face_shapes(shape, shape.inner)
    shapes.append(jax.ShapeDtypeStruct((shape.sides, 2 * shape.cells), BF))
    shapes.append(jax.ShapeDtypeStruct((peers, block.shape[0], slots), BF))
    shapes += table_shapes(shape)
    hbm = pl.BlockSpec(memory_space=pltpu.HBM)
    return pl.pallas_call(
        functools.partial(faces_kernel, shape, slots),
        in_specs=[hbm, hbm, WHOLE],
        out_specs=[WHOLE] * len(shapes),
        out_shape=shapes,
        scratch_shapes=[
            pltpu.VMEM(field.shape, BF),
            pltpu.VMEM((steps, shape.block * shape.cells, shape.lanes), F32),
            pltpu.SemaphoreType.DMA((peers,)),
            pltpu.SemaphoreType.DMA((steps,)),
        ],
        compiler_params=params(FACES_MIB),
        cost_estimate=pl.CostEstimate(
            flops=field.size * 128, bytes_accessed=4 * field.size, transcendentals=0
        ),
    )(field, block, coef)


def expand(shape, lines, where):
    rows = []
    for side in range(shape.block):
        line = jnp.broadcast_to(lines[side : side + 1], where.shape)
        rows.append(jnp.where(where, line, 0.0))
    return beside(jnp.concatenate(rows, axis=0).astype(BF))


def halo_ends(shape, end_refs, sides):
    even = lax.axis_index("gz") % 2 == 0
    filled = (iota((shape.block, 2 * shape.cells), 1) < shape.cells) == even
    zs = 0.0
    for turn in range(shape.ends):
        wanted = (filled == (turn == 0)) & has_neighbour("gz", turn)
        zs = jnp.where(wanted, end_refs[-1 - turn][sides, :].astype(F32), zs)
    return expand(shape, zs, z_mask(shape, 1))


def flux_width(slots):
    return (2 * slots + 127) // 128 * 128


def build_cells(shape, cell_ref, cell_m):
    slots = cell_ref.shape[3]
    width = flux_width(slots)
    cell = cell_ref[0, 0]
    none = jnp.full((1, width - 2 * slots), -shape.lanes, jnp.int32)
    cell = jnp.concatenate([cell, cell, none], axis=1)
    place = (iota((shape.lanes, width), 0) == cell % shape.lanes).astype(F32)
    cell_m[...] = twice(place).astype(BF)
    return iota((shape.cells, width), 0) == cell // shape.lanes


def base_kernel(shape, ends, with_flux, *refs):
    refs = list(refs)
    take = lambda count: [refs.pop(0) for _ in range(count)]
    field_ref, load_ref, weight, near_m, line_m = take(5)
    end_refs = take(ends)
    if with_flux:
        phi, cell_ref = take(2)
    (base_ref,) = take(1)
    if with_flux:
        (source_ref,) = take(1)
    (lines,) = take(1)
    if with_flux:
        cell_m, placed = take(2)
        cell_mask = build_cells(shape, cell_ref, cell_m)

    cells, lanes = shape.cells, shape.lanes
    weights = weight[...]
    for step in range(shape.sides // shape.block):
        sides = slice(step * shape.block, (step + 1) * shape.block)
        at = step * shape.block * cells
        left = beside(field_ref[at : at + shape.block * cells, :])
        if ends:
            left = jnp.concatenate([left, halo_ends(shape, end_refs, sides)], axis=1)
        lines[step] = dot(left, line_m[: left.shape[1], :])
        if with_flux:
            placed[step] = dot_nt(expand(shape, phi[sides, :], cell_mask), cell_m[...])
        for index in range(shape.half // shape.chunk):
            offset = index * shape.rows
            here = slice(offset, offset + shape.rows)
            spans = [
                slice(at + start, at + start + shape.rows)
                for start in (offset, offset + shape.half_rows)
            ]
            stack = jnp.concatenate([field_ref[span, :] for span in spans], axis=1)
            near = dot(near_m[:, : shape.rows], stack) + lines[step, here, :]
            for part, span in enumerate(spans):
                cols = slice(part * lanes, (part + 1) * lanes)
                source = load_ref[span, :].astype(F32)
                if with_flux:
                    source = source + placed[step, here, cols]
                    source_ref[span, :] = source.astype(BF)
                centre = field_ref[span, :].astype(F32)
                base_ref[span, :] = (1.0 - OMEGA) * centre + weights * (source + near[:, cols])


def sweep_base(shape, field, load, tables, ends=(), phi=None, flux_cell=None):
    steps = shape.sides // shape.block
    half = (steps, shape.half_rows, 2 * shape.lanes)
    operands = [field, load, *tables[:3], *ends]
    shapes = [jax.ShapeDtypeStruct(field.shape, F32)]
    scratch = [pltpu.VMEM(half, F32)]
    if phi is not None:
        operands += [phi, flux_cell]
        shapes.append(jax.ShapeDtypeStruct(field.shape, BF))
        scratch.append(pltpu.VMEM((2 * shape.lanes, 2 * phi.shape[1]), BF))
        scratch.append(pltpu.VMEM(half, F32))
    return pl.pallas_call(
        functools.partial(base_kernel, shape, len(ends), phi is not None),
        in_specs=[WHOLE] * len(operands),
        out_specs=[WHOLE] * len(shapes),
        out_shape=shapes,
        scratch_shapes=scratch,
        compiler_params=params(),
        cost_estimate=pl.CostEstimate(
            flops=6 * field.size * 128, bytes_accessed=8 * field.size, transcendentals=0
        ),
    )(*operands)


def finish_kernel(shape, ends, recvs, last, *refs):
    with_flux = recvs > 0
    refs = list(refs)
    take = lambda count: [refs.pop(0) for _ in range(count)]
    base_ref, weight, near_m, line_m, ends_m, rsum = take(6)
    halo_refs = take(len(shape.faces))
    end_refs = take(ends)
    if with_flux:
        (cell_ref,) = take(1)
        recv_refs = take(recvs)
    (out_ref,) = take(1)
    if not last:
        face_refs = take(len(shape.faces))
        (z_ref,) = take(1)
    if with_flux:
        phi, flux_ref = take(2)
    if last:
        result_ref = out_ref
        out_ref, out_sems = take(2)
    else:
        (tall,) = take(1)
    if ends:
        (lines,) = take(1)
    if with_flux:
        cell_m, placed = take(2)

    cells, lanes = shape.cells, shape.lanes

    if with_flux:
        slots = cell_ref.shape[3]
        cell_mask = build_cells(shape, cell_ref, cell_m)
        owned = recv_refs[0][...]
        for ref in recv_refs[1:]:
            owned = owned + ref[...]
        flux_ref[...] = owned[slots:, : flux_ref.shape[1]]
        owned = owned[:slots]
        high = owned.astype(BF).astype(F32)
        none = jnp.zeros((phi.shape[1] - 2 * slots, phi.shape[0]), F32)
        phi[...] = jnp.concatenate([high, owned - high, none], axis=0).T

    weights = weight[...]

    def work(step):
        at = step * shape.block
        sides = slice(at, at + shape.block)
        if ends:
            lines[step] = dot(halo_ends(shape, end_refs, sides), line_m[2 * lanes :, :])
        if with_flux:
            placed[step] = dot_nt(expand(shape, phi[sides, :], cell_mask), cell_m[...])
        for index in range(shape.half // shape.chunk):
            offset = index * shape.rows
            starts = (offset, offset + shape.half_rows)
            stacks = []
            for start in starts:
                stack = []
                for face, ref in zip(shape.faces, halo_refs):
                    length = shape.face_len(face)
                    first = at * length + start // cells * length
                    stack.append(ref[first : first + shape.chunk * length, :])
                stacks.append(jnp.concatenate(stack, axis=0))
            near = dot(near_m[:, shape.rows :], jnp.concatenate(stacks, axis=1))
            if ends:
                near = near + lines[step, offset : offset + shape.rows, :]
            if with_flux:
                near = near + placed[step, offset : offset + shape.rows, :]
            for part, start in enumerate(starts):
                rows = slice(at * cells + start, at * cells + start + shape.rows)
                fresh = base_ref[rows, :] + weights * near[:, part * lanes : (part + 1) * lanes]
                out_ref[rows, :] = fresh.astype(BF)
                if not last:
                    tall[step, start : start + shape.rows, :] = fresh

    def emit(step):
        at, size = step * shape.block, shape.block * cells
        fresh = out_ref[at * cells : at * cells + size, :]
        cut_faces(shape, shape.faces, at, shape.block, tall.at[step], face_refs)
        cut_ends(shape, at, fresh, z_ref, ends_m, rsum)

    steps = shape.sides // shape.block
    copies = []
    for step in range(steps):
        work(step)
        if last:
            span = pl.ds(step * shape.block * cells, shape.block * cells)
            copies.append(
                pltpu.make_async_copy(out_ref.at[span], result_ref.at[span], out_sems.at[step])
            )
            copies[-1].start()
        elif step > 0:
            emit(step - 1)
    for copy in copies:
        copy.wait()
    if not last:
        emit(steps - 1)


def sweep_finish(shape, base, tables, halos, ends=(), flux_cell=None, recv=(), last=False):
    lanes, cells = shape.lanes, shape.cells
    steps = shape.sides // shape.block
    half = (steps, shape.half_rows, 2 * lanes)
    operands = [base, *tables, *halos, *ends]
    out_shapes = [jax.ShapeDtypeStruct(base.shape, BF)]
    if last:
        scratch = [pltpu.VMEM(base.shape, BF), pltpu.SemaphoreType.DMA((steps,))]
    else:
        out_shapes += face_shapes(shape, shape.faces)
        out_shapes.append(jax.ShapeDtypeStruct((shape.sides, 2 * cells), BF))
        scratch = [pltpu.VMEM((steps, shape.block * cells, lanes), F32)]
    if ends:
        scratch.append(pltpu.VMEM(half, F32))
    if recv:
        slots = flux_cell.shape[3]
        operands += [flux_cell, *recv]
        out_shapes += [
            jax.ShapeDtypeStruct((shape.sides, flux_width(slots)), F32),
            jax.ShapeDtypeStruct((recv[0].shape[0] - slots, slots * lax.axis_size("gz")), F32),
        ]
        scratch += [
            pltpu.VMEM((2 * lanes, 2 * flux_width(slots)), BF),
            pltpu.VMEM(half, F32),
        ]
    out_specs = [WHOLE] * len(out_shapes)
    if last:
        out_specs = [pl.BlockSpec(memory_space=pltpu.HBM)]
    return pl.pallas_call(
        functools.partial(finish_kernel, shape, len(ends), len(recv), last),
        in_specs=[WHOLE] * len(operands),
        out_specs=out_specs,
        out_shape=out_shapes,
        scratch_shapes=scratch,
        compiler_params=params(),
        cost_estimate=pl.CostEstimate(
            flops=4 * base.size * 128, bytes_accessed=8 * base.size, transcendentals=0
        ),
    )(*operands)


def swap_faces(faces, values):
    return [swap(value, *face) for face, value in zip(faces, values)]


def swap_ends(shape, ends):
    return [swap(ends, "gz", turn) for turn in reversed(range(shape.ends))]


def row_gather(trace, hidden, late):
    peers = lax.axis_size("row")
    held = {0: trace}
    bit = peers // 2
    while bit:
        pairs = [(i, i ^ bit) for i in range(peers)]
        fresh = {key ^ bit: lax.ppermute(held[key], "row", pairs) for key in sorted(held, reverse=True)}
        if bit == peers // 2:
            fresh, hidden = lax.optimization_barrier((fresh, hidden))
        held.update(fresh)
        bit //= 2
    parts, late = lax.optimization_barrier(([held[key] for key in range(peers)], late))
    return parts, hidden, late


def per_device(volume_field, volume_load, coefficient, surface_block, trace_cell, flux_cell):
    sides, first, second, lanes = volume_field.shape
    cells = first * second
    shape = Shape(sides, first, second, lanes)
    field = volume_field.reshape(sides * cells, lanes)
    load = volume_load.reshape(sides * cells, lanes)
    coef = coefficient.reshape(cells, lanes)

    slots = trace_cell.shape[3]
    trace, *outer = traces(
        shape, volume_field.reshape(sides, cells, lanes), trace_cell, min(32, sides)
    )
    firsts = first_faces(shape, field, surface_block, coef, slots)
    layers = len(shape.faces)
    count = len(shape.inner) + 1
    inner, held, tables = firsts[:count], firsts[count], firsts[count + 1 :]
    *inner, ends = inner
    along_col = swap_faces(shape.outer, outer)
    parts, inner, along_col = row_gather(trace, inner, along_col)
    along_row = swap_faces(shape.inner, inner)
    recv, ends = flux_sums(parts, held, along_row, ends)
    tips = swap_ends(shape, ends)

    (base,) = sweep_base(shape, field, load, tables, tips)
    current, *faces, ends, phi, surface_flux = sweep_finish(
        shape, base, tables, along_col + along_row, flux_cell=flux_cell, recv=recv
    )
    halos, tips = swap_faces(shape.faces, faces), swap_ends(shape, ends)
    base, source = sweep_base(shape, current, load, tables, phi=phi, flux_cell=flux_cell)
    current, *faces, ends = sweep_finish(shape, base, tables, halos, tips)
    halos, tips = swap_faces(shape.faces, faces), swap_ends(shape, ends)
    (base,) = sweep_base(shape, current, source, tables)
    (current,) = sweep_finish(shape, base, tables, halos, tips, last=True)
    return current.reshape(volume_field.shape), surface_flux


def solution(mesh):
    in_specs = (
        P(None, "row", "col", "gz"),
        P(None, "row", "col", "gz"),
        P("row", "col", "gz"),
        P("row", "col"),
        P("row", "col", "gz", None),
        P("row", "col", "gz", None),
    )
    out_specs = (P(None, "row", "col", "gz"), P("gz", ("row", "col")))
    return jax.shard_map(
        per_device, mesh=mesh, in_specs=in_specs, out_specs=out_specs, check_vma=False
    )
```
